32 devices in a mesh: dp: 8 (over z, x), mp: 4 (over y, core).
Axes of the slice: x: 2, y: 2, z: 4, core: 2. Of those that a mesh axis runs over, the one named last changes fastest.
Arguments:
- text_in: bfloat16 [12288, 768], P(('dp', 'mp')), may hold values from -6 to 6
- image_in: bfloat16 [6144, 1024], P(('dp', 'mp')), may hold values from -6 to 6
- caption_lengths: int32 [192], P('dp'), may hold values from 1 to 64, 7680 in all
- region_lengths: int32 [48, 4], P('dp'), may hold values from 1 to 80, 128 in all within a row
- image_caption: int32 [8, 24], P('dp'), may hold values from 0 to 23, each once within a row
- co_text_qkv: bfloat16 [3, 768, 1024], P(None, None, 'mp'), may hold values from -0.21875 to 0.21875
- co_image_qkv: bfloat16 [3, 1024, 1024], P(None, None, 'mp'), may hold values from -0.1875 to 0.1875
- co_text_out: bfloat16 [1024, 768], P('mp'), may hold values from -1 to 1
- co_image_out: bfloat16 [1024, 1024], P('mp'), may hold values from -1 to 1
- text_up: bfloat16 [768, 3072], P(None, 'mp'), may hold values from -0.21875 to 0.21875
- text_down: bfloat16 [3072, 768], P('mp'), may hold values from -0.109375 to 0.109375
- image_up: bfloat16 [1024, 1024], P(None, 'mp'), may hold values from -0.1875 to 0.1875
- image_down: bfloat16 [1024, 1024], P('mp'), may hold values from -0.1875 to 0.1875
- text_self_qkv: bfloat16 [3, 768, 768], P(None, None, 'mp'), may hold values from -0.21875 to 0.21875
- text_self_out: bfloat16 [768, 768], P('mp'), may hold values from -1 to 1
- image_self_qkv: bfloat16 [3, 1024, 1024], P(None, None, 'mp'), may hold values from -0.1875 to 0.1875
- image_self_out: bfloat16 [1024, 1024], P('mp'), may hold values from -1 to 1
- text_gains: float32 [3, 768], replicated, may hold values from 0.5 to 1.5
- text_shifts: float32 [3, 768], replicated, may hold values from -3 to 3
- image_gains: float32 [3, 1024], replicated, may hold values from 0.5 to 1.5
- image_shifts: float32 [3, 1024], replicated, may hold values from -3 to 3
- text_grad_out: bfloat16 [12288, 768], P(('dp', 'mp')), may hold values from -6 to 6
- image_grad_out: bfloat16 [6144, 1024], P(('dp', 'mp')), may hold values from -6 to 6
Outputs:
- text_out: bfloat16 [12288, 768], P(('dp', 'mp'))
- image_out: bfloat16 [6144, 1024], P(('dp', 'mp'))
- text_in_grad: float32 [12288, 768], P(('dp', 'mp'))
- image_in_grad: float32 [6144, 1024], P(('dp', 'mp'))
- co_text_qkv_grad: float32 [3, 768, 1024], P(None, 'dp', 'mp')
- co_image_qkv_grad: float32 [3, 1024, 1024], P(None, 'dp', 'mp')
- co_text_out_grad: float32 [1024, 768], P('mp', 'dp')
- co_image_out_grad: float32 [1024, 1024], P('mp', 'dp')
- text_up_grad: float32 [768, 3072], P('dp', 'mp')
- text_down_grad: float32 [3072, 768], P('mp', 'dp')
- image_up_grad: float32 [1024, 1024], P('dp', 'mp')
- image_down_grad: float32 [1024, 1024], P('mp', 'dp')
- text_self_qkv_grad: float32 [3, 768, 768], P(None, 'dp', 'mp')
- text_self_out_grad: float32 [768, 768], P('mp', 'dp')
- image_self_qkv_grad: float32 [3, 1024, 1024], P(None, 'dp', 'mp')
- image_self_out_grad: float32 [1024, 1024], P('mp', 'dp')
- text_gains_grad: float32 [3, 768], P(None, ('dp', 'mp'))
- text_shifts_grad: float32 [3, 768], P(None, ('dp', 'mp'))
- image_gains_grad: float32 [3, 1024], P(None, ('dp', 'mp'))
- image_shifts_grad: float32 [3, 1024], P(None, ('dp', 'mp'))
The draws below stay inside these ranges and needn't reach their ends.
Inputs may be any that keep to these rules, and one draw needn't show every extreme that they name: `region_lengths`: each row's 4 counts sum to 128. `image_caption`: each row is a permutation.
All inputs are finite; a program needn't handle non-finite values. No bound on the sum of `caption_lengths` on one device may be relied on, other than what follows from the above.
Results may differ from the reference program's by a relative error of at most 0.04.
Values may be sent and summed in bfloat16 or wider, within the bound.
A program may use at most 192 MiB of HBM per device.

```python
import math
import jax
import jax.numpy as jnp
import numpy as np
from jax import lax

D_TEXT = 768
D_IMAGE = 1024
CO_INNER = 1024
CO_HEADS = 8
FF_TEXT = 3072
FF_IMAGE = 1024
TEXT_HEADS = 12
IMAGE_HEADS = 8
CAP_LEN = 64
ROW_LEN = 128
PER_ROW = 4
REGION_MOST = 80
CAP_GROUP = 24
GROUPS = 8
CAPTIONS = 192
GROUP_TEXT = 1536
GROUP_IMAGE = 768
TEXT_TOKENS = 12288
IMAGE_TOKENS = 6144
IMG_ROWS = 48


def shard_levels(rng, dims, cuts, smallest, high):
    def one(position, shards_of):
        steps = jax.random.uniform(jax.random.fold_in(jax.random.fold_in(rng, 6), position), (shards_of,), jnp.float32, smallest / len(cuts), high / len(cuts))
        return jnp.repeat(jnp.exp(steps), dims[position] // shards_of).reshape((-1,) + (1,) * (len(dims) - position - 1))

    factor_of = one(*cuts[0])
    for cut in cuts[1:]:
        factor_of = factor_of * one(*cut)
    return factor_of


def profile(number_of, total, most, slope):
    weights = [(1 << 20) // math.isqrt(standing ** slope) + 1 for standing in range(2, number_of + 1)]
    surplus, counts = total - most - (number_of - 1), [1] * (number_of - 1)
    while surplus > 0:
        free = [i for i in range(number_of - 1) if counts[i] < most]
        whole, budget = sum([weights[i] for i in free]), surplus
        for i in free:
            more = min(most - counts[i], max(1, budget * weights[i] // whole), surplus)
            counts[i] = counts[i] + more
            surplus = surplus - more
    return np.array([most] + counts)


def uneven_parts(key, amount, total, reach, lean):
    if amount == 2:
        one = jax.random.randint(key, (), max(1, total - reach), min(reach, total - 1) + 1)
        return jnp.stack([one, total - one])
    tallies = jnp.asarray(profile(amount, total, reach, lean), jnp.int32)
    twos = (amount - 1) // 2
    donor, receiver = tallies[1:1 + 2 * twos:2], tallies[2:2 + 2 * twos:2]
    room = jnp.minimum(donor - 1, reach - receiver)
    moved = jax.random.randint(jax.random.fold_in(key, 1), (twos,), 0, 1 << 20) % (room + 1)
    tallies = tallies.at[1:1 + 2 * twos:2].set(donor - moved).at[2:2 + 2 * twos:2].set(receiver + moved)
    return tallies[jax.random.permutation(jax.random.fold_in(key, 2), amount)]


def gaussian(own_key, dims, deviation, limit, cuts=(), held_as=jnp.bfloat16):
    array = deviation * jax.random.normal(own_key, dims, jnp.float32)
    if cuts:
        array = array * shard_levels(own_key, dims, cuts, -0.22, 0.18)
    return jnp.clip(array, -limit, limit).astype(held_as)


def setup_inputs(seed: int = 0) -> dict:
    seeds = jax.random.split(jax.random.key(seed), 24)
    return {
        "text_in": gaussian(seeds[0], (TEXT_TOKENS, D_TEXT), 1.0, 6.0, ((0, 32),)),
        "image_in": gaussian(seeds[1], (IMAGE_TOKENS, D_IMAGE), 1.0, 6.0, ((0, 32),)),
        "caption_lengths": uneven_parts(seeds[2], CAPTIONS, CAPTIONS * (5 * CAP_LEN // 8), CAP_LEN, 2).astype(jnp.int32),
        "region_lengths": jax.vmap(lambda own: uneven_parts(own, PER_ROW, ROW_LEN, REGION_MOST, 2))(jax.random.split(seeds[3], IMG_ROWS)).reshape((IMG_ROWS, PER_ROW)).astype(jnp.int32),
        "image_caption": jax.vmap(lambda own: jax.random.permutation(own, CAP_GROUP))(jax.random.split(seeds[4], GROUPS)).reshape((GROUPS, CAP_GROUP)).astype(jnp.int32),
        "co_text_qkv": gaussian(seeds[5], (3, D_TEXT, CO_INNER), D_TEXT ** -0.5, 0.21875, ((2, 4),)),
        "co_image_qkv": gaussian(seeds[6], (3, D_IMAGE, CO_INNER), D_IMAGE ** -0.5, 0.1875, ((2, 4),)),
        "co_text_out": gaussian(seeds[7], (CO_INNER, D_TEXT), 32 ** -0.5, 1.0, ((0, 4),)),
        "co_image_out": gaussian(seeds[8], (CO_INNER, D_IMAGE), 32 ** -0.5, 1.0, ((0, 4),)),
        "text_up": gaussian(seeds[9], (D_TEXT, FF_TEXT), D_TEXT ** -0.5, 0.21875, ((1, 4),)),
        "text_down": gaussian(seeds[10], (FF_TEXT, D_TEXT), FF_TEXT ** -0.5, 0.109375, ((0, 4),)),
        "image_up": gaussian(seeds[11], (D_IMAGE, FF_IMAGE), D_IMAGE ** -0.5, 0.1875, ((1, 4),)),
        "image_down": gaussian(seeds[12], (FF_IMAGE, D_IMAGE), FF_IMAGE ** -0.5, 0.1875, ((0, 4),)),
        "text_self_qkv": gaussian(seeds[13], (3, D_TEXT, D_TEXT), D_TEXT ** -0.5, 0.21875, ((2, 4),)),
        "text_self_out": gaussian(seeds[14], (D_TEXT, D_TEXT), 32 ** -0.5, 1.0, ((0, 4),)),
        "image_self_qkv": gaussian(seeds[15], (3, D_IMAGE, D_IMAGE), D_IMAGE ** -0.5, 0.1875, ((2, 4),)),
        "image_self_out": gaussian(seeds[16], (D_IMAGE, D_IMAGE), 32 ** -0.5, 1.0, ((0, 4),)),
        "text_gains": jnp.clip(1.0 + 0.1 * jax.random.normal(seeds[17], (3, D_TEXT), jnp.float32), 0.5, 1.5),
        "text_shifts": gaussian(seeds[18], (3, D_TEXT), 0.5, 3.0, (), jnp.float32),
        "image_gains": jnp.clip(1.0 + 0.1 * jax.random.normal(seeds[19], (3, D_IMAGE), jnp.float32), 0.5, 1.5),
        "image_shifts": gaussian(seeds[20], (3, D_IMAGE), 0.5, 3.0, (), jnp.float32),
        "text_grad_out": gaussian(seeds[21], (TEXT_TOKENS, D_TEXT), 1.0, 6.0, ((0, 32),)),
        "image_grad_out": gaussian(seeds[22], (IMAGE_TOKENS, D_IMAGE), 1.0, 6.0, ((0, 32),)),
    }


@jax.custom_vjp
def low(v):
    return lax.optimization_barrier(v.astype(jnp.bfloat16)).astype(jnp.float32)

@jax.custom_vjp
def low_back(v):
    return v

def low_keep(v):
    return (low(v), None)

def low_pass(kept, grad):
    return (grad,)

def back_keep(v):
    return (v, None)

def back_low(kept, grad):
    return (low(grad),)
low.defvjp(low_keep, low_pass)
low_back.defvjp(back_keep, back_low)
epsilon = 1e-05
highest = lax.Precision.HIGHEST

def product(former, latter):
    return jnp.dot(former, latter, precision=highest)

def contract(form, former, latter):
    return jnp.einsum(form, former, latter, precision=highest)

def layer_norm(values, norm_gain, norm_shift):
    centre = values - lax.optimization_barrier(jnp.mean(values, axis=-1, keepdims=True))
    spread = lax.optimization_barrier(jnp.mean(centre * centre, axis=-1, keepdims=True))
    return centre * lax.rsqrt(spread + epsilon) * norm_gain + norm_shift

def gelu_tanh(values):
    return 0.5 * values * (1.0 + jnp.tanh(0.7978845608028654 * (values + 0.044715 * values * values * values)))

def layout(cap_len, reg_len, image_order):
    caption_count = image_order.shape[0]
    row_count = caption_count // PER_ROW
    places = jnp.arange(ROW_LEN, dtype=jnp.int32)
    ends = jnp.cumsum(reg_len, axis=1)
    region_slot = lax.optimization_barrier(jnp.sum((places[None, :, None] >= ends[:, None, :]).astype(jnp.int32), axis=2))
    labels = jnp.arange(caption_count, dtype=jnp.int32)
    inverse = lax.optimization_barrier(jnp.sum(labels[None, :] * (image_order[None, :] == labels[:, None]).astype(jnp.int32), axis=1))
    spots = jnp.arange(PER_ROW * CAP_LEN, dtype=jnp.int32)
    slot_len = jnp.take(cap_len, image_order).reshape(row_count, PER_ROW)
    text_live = (spots % CAP_LEN)[None, :] < jnp.repeat(slot_len, CAP_LEN, axis=1)
    to_image = (spots // CAP_LEN)[None, :, None] == region_slot[:, None, :]
    to_text = jnp.swapaxes(to_image, 1, 2) & text_live[:, None, :]
    among_regions = region_slot[:, :, None] == region_slot[:, None, :]
    pairs = jnp.arange(2 * CAP_LEN, dtype=jnp.int32)
    pair_live = (pairs % CAP_LEN)[None, :] < jnp.repeat(cap_len.reshape(caption_count // 2, 2), CAP_LEN, axis=1)
    same_caption = (pairs // CAP_LEN)[:, None] == (pairs // CAP_LEN)[None, :]
    among_tokens = same_caption[None] & pair_live[:, None, :]
    return (inverse, to_image, to_text, among_regions, among_tokens)

def attend(queries, key_rows, value_rows, key_mask, head_count):
    blocks, query_len, inner_width = queries.shape
    key_len = key_rows.shape[1]
    head_size = inner_width // head_count
    split_q = queries.reshape(blocks, query_len, head_count, head_size)
    split_k = key_rows.reshape(blocks, key_len, head_count, head_size)
    split_v = value_rows.reshape(blocks, key_len, head_count, head_size)
    scores = low_back(contract('bqhd,bkhd->bhqk', split_q, split_k)) * head_size ** (-0.5)
    scores = jnp.where(key_mask[:, None], scores, -1000000000.0)
    row_max = lax.optimization_barrier(jnp.max(scores, axis=-1, keepdims=True))
    exponent = jnp.exp(scores - row_max)
    shares = exponent / lax.optimization_barrier(jnp.sum(exponent, axis=-1, keepdims=True))
    context = contract('bhqk,bkhd->bqhd', low(shares), split_v)
    return low(low_back(context.reshape(blocks, query_len, inner_width)))

def feed(hidden, up_weight, down_weight):
    pre_act = low_back(product(low(hidden), up_weight))
    return low_back(product(low(gelu_tanh(pre_act)), down_weight))

def self_attend(hidden, qkv_weight, out_weight, key_mask, blocks, block_len, head_count):
    rounded = low(hidden)
    pieces = [low(low_back(product(rounded, qkv_weight[member]))).reshape(blocks, block_len, -1) for member in range(3)]
    context = attend(pieces[0], pieces[1], pieces[2], key_mask, head_count)
    return low_back(product(context.reshape(blocks * block_len, -1), out_weight))

def group_pass(text_rows, image_rows, cap_len, reg_len, image_order, weights):
    co_text_qkv, co_image_qkv, co_text_out, co_image_out, text_up, text_down, image_up, image_down, text_self_qkv, text_self_out, image_self_qkv, image_self_out, text_gains, text_shifts, image_gains, image_shifts = weights
    inverse, to_image, to_text, among_regions, among_tokens = layout(cap_len, reg_len, image_order)
    caption_count = image_order.shape[0]
    row_count = caption_count // PER_ROW
    text_order = jnp.take(text_rows.reshape(caption_count, CAP_LEN, D_TEXT), image_order, axis=0).reshape(caption_count * CAP_LEN, D_TEXT)
    text_side = [low(low_back(product(text_order, co_text_qkv[member]))).reshape(row_count, PER_ROW * CAP_LEN, CO_INNER) for member in range(3)]
    image_side = [low(low_back(product(image_rows, co_image_qkv[member]))).reshape(row_count, ROW_LEN, CO_INNER) for member in range(3)]
    text_context = attend(text_side[0], image_side[1], image_side[2], to_image, CO_HEADS)
    image_context = attend(image_side[0], text_side[1], text_side[2], to_text, CO_HEADS)
    text_context = jnp.take(text_context.reshape(caption_count, CAP_LEN, CO_INNER), inverse, axis=0).reshape(caption_count * CAP_LEN, CO_INNER)
    image_context = image_context.reshape(row_count * ROW_LEN, CO_INNER)
    text_first = layer_norm(text_rows + low_back(product(text_context, co_text_out)), text_gains[0], text_shifts[0])
    image_first = layer_norm(image_rows + low_back(product(image_context, co_image_out)), image_gains[0], image_shifts[0])
    text_second = layer_norm(text_first + feed(text_first, text_up, text_down), text_gains[1], text_shifts[1])
    image_second = layer_norm(image_first + feed(image_first, image_up, image_down), image_gains[1], image_shifts[1])
    text_late = self_attend(text_second, text_self_qkv, text_self_out, among_tokens, caption_count // 2, 2 * CAP_LEN, TEXT_HEADS)
    image_late = self_attend(image_second, image_self_qkv, image_self_out, among_regions, row_count, ROW_LEN, IMAGE_HEADS)
    text_third = layer_norm(text_second + text_late, text_gains[2], text_shifts[2])
    image_third = layer_norm(image_second + image_late, image_gains[2], image_shifts[2])
    return (text_third, image_third)

def reference(text_in, image_in, caption_lengths, region_lengths, image_caption, co_text_qkv, co_image_qkv, co_text_out, co_image_out, text_up, text_down, image_up, image_down, text_self_qkv, text_self_out, image_self_qkv, image_self_out, text_gains, text_shifts, image_gains, image_shifts, text_grad_out, image_grad_out):
    weights = tuple((member.astype(jnp.float32) for member in (co_text_qkv, co_image_qkv, co_text_out, co_image_out, text_up, text_down, image_up, image_down, text_self_qkv, text_self_out, image_self_qkv, image_self_out, text_gains, text_shifts, image_gains, image_shifts)))
    group_count = image_caption.shape[0]
    caption_groups = caption_lengths.reshape(group_count, CAP_GROUP)
    region_groups = region_lengths.reshape(group_count, CAP_GROUP // PER_ROW, PER_ROW)

    def forward(text_rows, image_rows, params):

        def advance(running, pieces):
            return (running, jax.checkpoint(group_pass)(pieces[0], pieces[1], pieces[2], pieces[3], pieces[4], params))
        _, (text_third, image_third) = lax.scan(advance, jnp.zeros((), jnp.float32), (text_rows.reshape(group_count, GROUP_TEXT, D_TEXT), image_rows.reshape(group_count, GROUP_IMAGE, D_IMAGE), caption_groups, region_groups, image_caption))
        return (text_third.reshape(group_count * GROUP_TEXT, D_TEXT), image_third.reshape(group_count * GROUP_IMAGE, D_IMAGE))
    (text_third, image_third), pullback = jax.vjp(forward, text_in.astype(jnp.float32), image_in.astype(jnp.float32), weights)
    text_grad, image_grad, grads = pullback((text_grad_out.astype(jnp.float32), image_grad_out.astype(jnp.float32)))
    return (text_third.astype(jnp.bfloat16), image_third.astype(jnp.bfloat16), text_grad, image_grad, grads[0], grads[1], grads[2], grads[3], grads[4], grads[5], grads[6], grads[7], grads[8], grads[9], grads[10], grads[11], grads[12], grads[13], grads[14], grads[15])
```

```python
import functools

import jax
import jax.numpy as jnp
from jax import lax
from jax.experimental import pallas as pl
from jax.experimental.pallas import tpu as pltpu
from jax.sharding import PartitionSpec as P

CO_HEADS = 8
TEXT_HEADS = 12
IMAGE_HEADS = 8
CAP_LEN = 64
ROW_LEN = 128
PER_ROW = 4

epsilon = 1e-05
BF = jnp.bfloat16
F32 = jnp.float32
VMEM_LIMIT = 48 * 1024 * 1024


def product(former, latter):
    return jnp.dot(former, latter, preferred_element_type=F32)


def product_tn(former, latter):
    return lax.dot_general(former, latter, (((0,), (0,)), ((), ())), preferred_element_type=F32)


def product_nt(former, latter):
    return lax.dot_general(former, latter, (((1,), (1,)), ((), ())), preferred_element_type=F32)


def layer_norm(values, norm_gain, norm_shift):
    centre = values - jnp.mean(values, axis=-1, keepdims=True)
    spread = jnp.mean(centre * centre, axis=-1, keepdims=True)
    return centre * lax.rsqrt(spread + epsilon) * norm_gain + norm_shift


def norm_back(values, norm_gain, gradient):
    centre = values - jnp.mean(values, axis=-1, keepdims=True)
    spread = jnp.mean(centre * centre, axis=-1, keepdims=True)
    inverse = lax.rsqrt(spread + epsilon)
    unit = centre * inverse
    scaled = gradient * norm_gain
    back = inverse * (
        scaled
        - jnp.mean(scaled, axis=-1, keepdims=True)
        - unit * jnp.mean(scaled * unit, axis=-1, keepdims=True)
    )
    return back, jnp.sum(gradient * unit, axis=0), jnp.sum(gradient, axis=0)


GELU_A = 0.7978845608028654
GELU_B = 0.044715


def gelu_tanh(values):
    return 0.5 * values * (1.0 + jnp.tanh(GELU_A * (values + GELU_B * values * values * values)))


def gelu_slope(values):
    bent = jnp.tanh(GELU_A * (values + GELU_B * values * values * values))
    return 0.5 * (1.0 + bent) + 0.5 * values * (1.0 - bent * bent) * GELU_A * (
        1.0 + 3.0 * GELU_B * values * values
    )


def softmax_block(scores, mask):
    scores = jnp.where(mask, scores, -1000000000.0)
    exponent = jnp.exp(scores - jnp.max(scores, axis=-1, keepdims=True))
    return (exponent / jnp.sum(exponent, axis=-1, keepdims=True)).astype(BF)


def attend_back(shares, scaling, queries, keys, values, context_grad):
    wide = shares.astype(F32)
    share_grad = product_nt(context_grad, values)
    inner = jnp.sum(share_grad * wide, axis=-1, keepdims=True)
    score_grad = (wide * (share_grad - inner) * scaling).astype(BF)
    return (
        product(score_grad, keys).astype(BF),
        product_tn(score_grad, queries).astype(BF),
        product_tn(shares, context_grad).astype(BF),
    )


def row_ends(region_ref, row):
    ends = [region_ref[row * PER_ROW]]
    for slot in range(1, PER_ROW):
        ends.append(ends[-1] + region_ref[row * PER_ROW + slot])
    return ends


def slot_of(places, ends):
    slot = (places >= ends[0]).astype(jnp.int32)
    for end in ends[1:]:
        slot = slot + (places >= end).astype(jnp.int32)
    return slot


def caption_rows(ref, captions, start, width):
    return jnp.concatenate(
        [
            ref[pl.ds(pl.multiple_of(caption * CAP_LEN, CAP_LEN), CAP_LEN), start : start + width]
            for caption in captions
        ],
        axis=0,
    )


def co_forward_kernel(
    heads, per_step, order_ref, region_ref, length_ref, text_ref, image_ref,
    text_out, image_out, text_shares, image_shares,
):
    inner = text_ref.shape[1] // 3
    size = inner // heads
    scaling = size ** (-0.5)
    span = PER_ROW * CAP_LEN
    for member in range(per_step):
        row = pl.program_id(0) * per_step + member
        captions = [order_ref[row * PER_ROW + slot] for slot in range(PER_ROW)]
        ends = row_ends(region_ref, row)
        token_slot = lax.broadcasted_iota(jnp.int32, (span, ROW_LEN), 0) // CAP_LEN
        to_image = token_slot == slot_of(
            lax.broadcasted_iota(jnp.int32, (span, ROW_LEN), 1), ends
        )
        spots = lax.broadcasted_iota(jnp.int32, (ROW_LEN, span), 1)
        length = jnp.full((ROW_LEN, span), length_ref[captions[0]], jnp.int32)
        for slot in range(1, PER_ROW):
            length = jnp.where(spots >= slot * CAP_LEN, length_ref[captions[slot]], length)
        to_text = (
            slot_of(lax.broadcasted_iota(jnp.int32, (ROW_LEN, span), 0), ends) == spots // CAP_LEN
        ) & (spots % CAP_LEN < length)
        rows = slice(member * ROW_LEN, (member + 1) * ROW_LEN)
        for head in range(heads):
            text = [
                caption_rows(text_ref, captions, part * inner + head * size, size)
                for part in range(3)
            ]
            image = [
                image_ref[rows, part * inner + head * size : part * inner + (head + 1) * size]
                for part in range(3)
            ]
            lanes = slice(head * size, (head + 1) * size)
            shares = softmax_block(product_nt(text[0], image[1]) * scaling, to_image)
            text_shares[member, head] = shares
            context = product(shares, image[2]).astype(BF)
            for slot, caption in enumerate(captions):
                text_out[
                    pl.ds(pl.multiple_of(caption * CAP_LEN, CAP_LEN), CAP_LEN), lanes
                ] = context[slot * CAP_LEN : (slot + 1) * CAP_LEN]
            shares = softmax_block(product_nt(image[0], text[1]) * scaling, to_text)
            image_shares[member, head] = shares
            image_out[rows, lanes] = product(shares, text[2]).astype(BF)


def co_backward_kernel(
    heads, per_step, order_ref, text_ref, image_ref, text_shares, image_shares,
    text_grad, image_grad, text_out, image_out,
):
    inner = text_ref.shape[1] // 3
    size = inner // heads
    scaling = size ** (-0.5)
    for member in range(per_step):
        row = pl.program_id(0) * per_step + member
        captions = [order_ref[row * PER_ROW + slot] for slot in range(PER_ROW)]
        rows = slice(member * ROW_LEN, (member + 1) * ROW_LEN)
        for head in range(heads):
            text = [
                caption_rows(text_ref, captions, part * inner + head * size, size)
                for part in range(3)
            ]
            image = [
                image_ref[rows, part * inner + head * size : part * inner + (head + 1) * size]
                for part in range(3)
            ]
            lanes = slice(head * size, (head + 1) * size)
            from_text = caption_rows(text_grad, captions, head * size, size)
            text_q, image_k, image_v = attend_back(
                text_shares[member, head], scaling, text[0], image[1], image[2], from_text
            )
            image_q, text_k, text_v = attend_back(
                image_shares[member, head], scaling, image[0], text[1], text[2],
                image_grad[rows, lanes],
            )
            for part, grad in enumerate((text_q, text_k, text_v)):
                for slot, caption in enumerate(captions):
                    text_out[
                        pl.ds(pl.multiple_of(caption * CAP_LEN, CAP_LEN), CAP_LEN),
                        part * inner + head * size : part * inner + (head + 1) * size,
                    ] = grad[slot * CAP_LEN : (slot + 1) * CAP_LEN]
            for part, grad in enumerate((image_q, image_k, image_v)):
                image_out[
                    rows, part * inner + head * size : part * inner + (head + 1) * size
                ] = grad


def self_mask_text(length_ref, block):
    shape = (2 * CAP_LEN, 2 * CAP_LEN)
    queries = lax.broadcasted_iota(jnp.int32, shape, 0)
    spots = lax.broadcasted_iota(jnp.int32, shape, 1)
    length = jnp.where(
        spots >= CAP_LEN, length_ref[block * 2 + 1] + CAP_LEN, length_ref[block * 2]
    )
    return (queries // CAP_LEN == spots // CAP_LEN) & (spots < length)


def self_mask_image(region_ref, row):
    ends = row_ends(region_ref, row)
    shape = (ROW_LEN, ROW_LEN)
    return slot_of(lax.broadcasted_iota(jnp.int32, shape, 0), ends) == slot_of(
        lax.broadcasted_iota(jnp.int32, shape, 1), ends
    )


def self_forward_kernel(heads, per_step, masker, count_ref, rows_ref, context_out, shares_out):
    inner = rows_ref.shape[1] // 3
    size = inner // heads
    scaling = size ** (-0.5)
    for member in range(per_step):
        mask = masker(count_ref, pl.program_id(0) * per_step + member)
        rows = slice(member * ROW_LEN, (member + 1) * ROW_LEN)
        contexts = []
        for head in range(heads):
            pieces = [
                rows_ref[rows, part * inner + head * size : part * inner + (head + 1) * size]
                for part in range(3)
            ]
            shares = softmax_block(product_nt(pieces[0], pieces[1]) * scaling, mask)
            shares_out[member, head] = shares
            contexts.append(product(shares, pieces[2]).astype(BF))
        context_out[rows, :] = jnp.concatenate(contexts, axis=1)


def self_backward_kernel(heads, per_step, rows_ref, shares_ref, grad_ref, rows_out):
    inner = rows_ref.shape[1] // 3
    size = inner // heads
    scaling = size ** (-0.5)
    for member in range(per_step):
        rows = slice(member * ROW_LEN, (member + 1) * ROW_LEN)
        grads = []
        for head in range(heads):
            pieces = [
                rows_ref[rows, part * inner + head * size : part * inner + (head + 1) * size]
                for part in range(3)
            ]
            grads.append(
                attend_back(
                    shares_ref[member, head], scaling, *pieces,
                    grad_ref[rows, head * size : (head + 1) * size],
                )
            )
        rows_out[rows, :] = jnp.concatenate(
            [grads[head][part] for part in range(3) for head in range(heads)], axis=1
        )


def shape_of(shape, dtype=BF):
    return jax.ShapeDtypeStruct(shape, dtype)


def cost(flops, moved, exps):
    return pl.CostEstimate(flops=int(flops), bytes_accessed=int(moved), transcendentals=int(exps))


def co_forward(text, image, order, regions, lengths, heads):
    tokens, width = text.shape
    slots = image.shape[0]
    inner = width // 3
    rows = slots // ROW_LEN
    per_step = 2
    span = PER_ROW * CAP_LEN
    whole = lambda i, *_: (0, 0)
    strip = lambda i, *_: (i, 0)
    block = lambda i, *_: (i, 0, 0, 0)
    return pl.pallas_call(
        functools.partial(co_forward_kernel, heads, per_step),
        grid_spec=pltpu.PrefetchScalarGridSpec(
            num_scalar_prefetch=3,
            grid=(rows // per_step,),
            in_specs=[
                pl.BlockSpec((tokens, width), whole),
                pl.BlockSpec((per_step * ROW_LEN, width), strip),
            ],
            out_specs=[
                pl.BlockSpec((tokens, inner), whole),
                pl.BlockSpec((per_step * ROW_LEN, inner), strip),
                pl.BlockSpec((per_step, heads, span, ROW_LEN), block),
                pl.BlockSpec((per_step, heads, ROW_LEN, span), block),
            ],
        ),
        out_shape=[
            shape_of((tokens, inner)),
            shape_of((slots, inner)),
            shape_of((rows, heads, span, ROW_LEN)),
            shape_of((rows, heads, ROW_LEN, span)),
        ],
        compiler_params=pltpu.CompilerParams(vmem_limit_bytes=VMEM_LIMIT),
        cost_estimate=cost(
            8 * rows * inner * span * ROW_LEN, 8e6, 2 * rows * heads * span * ROW_LEN
        ),
        name="co_forward",
    )(order, regions, lengths, text, image)


def co_backward(text, image, text_shares, image_shares, text_grad, image_grad, order, heads):
    tokens, width = text.shape
    slots = image.shape[0]
    inner = width // 3
    rows = slots // ROW_LEN
    per_step = 2
    span = PER_ROW * CAP_LEN
    whole = lambda i, *_: (0, 0)
    strip = lambda i, *_: (i, 0)
    block = lambda i, *_: (i, 0, 0, 0)
    return pl.pallas_call(
        functools.partial(co_backward_kernel, heads, per_step),
        grid_spec=pltpu.PrefetchScalarGridSpec(
            num_scalar_prefetch=1,
            grid=(rows // per_step,),
            in_specs=[
                pl.BlockSpec((tokens, width), whole),
                pl.BlockSpec((per_step * ROW_LEN, width), strip),
                pl.BlockSpec((per_step, heads, span, ROW_LEN), block),
                pl.BlockSpec((per_step, heads, ROW_LEN, span), block),
                pl.BlockSpec((tokens, inner), whole),
                pl.BlockSpec((per_step * ROW_LEN, inner), strip),
            ],
            out_specs=[
                pl.BlockSpec((tokens, width), whole),
                pl.BlockSpec((per_step * ROW_LEN, width), strip),
            ],
        ),
        out_shape=[shape_of((tokens, width)), shape_of((slots, width))],
        compiler_params=pltpu.CompilerParams(vmem_limit_bytes=VMEM_LIMIT),
        cost_estimate=cost(16 * rows * inner * span * ROW_LEN, 12e6, 0),
        name="co_backward",
    )(order, text, image, text_shares, image_shares, text_grad, image_grad)


def self_forward(rows_in, counts, heads, per_step, masker):
    tokens, width = rows_in.shape
    inner = width // 3
    blocks = tokens // ROW_LEN
    strip = lambda i, *_: (i, 0)
    block = lambda i, *_: (i, 0, 0, 0)
    return pl.pallas_call(
        functools.partial(self_forward_kernel, heads, per_step, masker),
        grid_spec=pltpu.PrefetchScalarGridSpec(
            num_scalar_prefetch=1,
            grid=(blocks // per_step,),
            in_specs=[pl.BlockSpec((per_step * ROW_LEN, width), strip)],
            out_specs=[
                pl.BlockSpec((per_step * ROW_LEN, inner), strip),
                pl.BlockSpec((per_step, heads, ROW_LEN, ROW_LEN), block),
            ],
        ),
        out_shape=[
            shape_of((tokens, inner)),
            shape_of((blocks, heads, ROW_LEN, ROW_LEN)),
        ],
        compiler_params=pltpu.CompilerParams(vmem_limit_bytes=VMEM_LIMIT),
        cost_estimate=cost(4 * tokens * inner * ROW_LEN, 6e6, tokens * heads * ROW_LEN),
        name="self_forward",
    )(counts, rows_in)


def self_backward(rows_in, shares, grad, heads, per_step):
    tokens, width = rows_in.shape
    inner = width // 3
    blocks = tokens // ROW_LEN
    strip = lambda i: (i, 0)
    block = lambda i: (i, 0, 0, 0)
    return pl.pallas_call(
        functools.partial(self_backward_kernel, heads, per_step),
        grid=(blocks // per_step,),
        in_specs=[
            pl.BlockSpec((per_step * ROW_LEN, width), strip),
            pl.BlockSpec((per_step, heads, ROW_LEN, ROW_LEN), block),
            pl.BlockSpec((per_step * ROW_LEN, inner), strip),
        ],
        out_specs=pl.BlockSpec((per_step * ROW_LEN, width), strip),
        out_shape=shape_of((tokens, width)),
        compiler_params=pltpu.CompilerParams(vmem_limit_bytes=VMEM_LIMIT),
        cost_estimate=cost(10 * tokens * inner * ROW_LEN, 9e6, 0),
        name="self_backward",
    )(rows_in, shares, grad)


def swap(values, axis, flip):
    return lax.ppermute(values, axis, [(i, i ^ flip) for i in range(lax.axis_size(axis))])


def gather(shard, core):
    other = swap(shard, "mp", 2)
    near = swap(shard, "mp", 1)
    far = swap(other, "mp", 1)
    first = core == 0
    return jnp.concatenate(
        [
            jnp.where(first, shard, near),
            jnp.where(first, near, shard),
            jnp.where(first, other, far),
            jnp.where(first, far, other),
        ],
        axis=0,
    )


def scatter_sum(left, right, core):
    first = core == 0

    def over_cores(half):
        upper, lower = jnp.split(half, 2, axis=0)
        kept = jnp.where(first, upper, lower)
        given = jnp.where(first, lower, upper).astype(BF)
        return kept + swap(given, "mp", 1).astype(F32)

    sent = swap(over_cores(right).astype(BF), "mp", 2)
    return over_cores(left) + sent.astype(F32)


def halves(rows):
    return jnp.split(rows, 2, axis=0)


def blocked(grads, group_count):
    pieces = []
    for grad in grads:
        rows, columns = grad.shape
        for start in range(0, columns, 256):
            pieces.append(
                grad[:, start : start + 256].astype(BF).reshape(group_count, rows // group_count, 256)
            )
    return jnp.concatenate(pieces, axis=1)


def unblocked(summed, shapes, group_count):
    outs = []
    at = 0
    for rows, columns in shapes:
        part = rows // group_count
        pieces = []
        for _ in range(columns // 256):
            pieces.append(summed[at : at + part])
            at += part
        outs.append(jnp.concatenate(pieces, axis=1).astype(F32))
    return outs


def reduce_groups(grads, group_count):
    stacked = blocked(grads, group_count)
    flat = stacked.reshape(-1, 256)
    summed = lax.psum_scatter(flat, "dp", scatter_dimension=0, tiled=True)
    return unblocked(summed, [grad.shape for grad in grads], group_count)


def reduce_halving(grads, group_count, bits):
    current = blocked(grads, group_count)
    tail = current.shape[1:]
    place = lax.axis_index("dp")
    names = list(range(group_count.bit_length() - 1))[::-1]
    current = current.reshape((2,) * len(names) + tail)
    for bit in bits:
        axis = names.index(bit)
        lower = lax.index_in_dim(current, 0, axis, keepdims=False)
        upper = lax.index_in_dim(current, 1, axis, keepdims=False)
        mine = (place >> bit) & 1
        kept = jnp.where(mine == 0, lower, upper)
        given = jnp.where(mine == 0, upper, lower)
        current = (kept.astype(F32) + swap(given, "dp", 1 << bit).astype(F32)).astype(BF)
        names.pop(axis)
    return unblocked(current, [grad.shape for grad in grads], group_count)


def side_by_side(stacked):
    members, height, breadth = stacked.shape
    return jnp.transpose(stacked, (1, 0, 2)).reshape(height, members * breadth)


def apart(grad):
    rows, columns = grad.shape
    return jnp.transpose(grad.reshape(rows, 3, columns // 3), (1, 0, 2))


def per_device(
    text_in,
    image_in,
    caption_lengths,
    region_lengths,
    image_caption,
    co_text_qkv,
    co_image_qkv,
    co_text_out,
    co_image_out,
    text_up,
    text_down,
    image_up,
    image_down,
    text_self_qkv,
    text_self_out,
    image_self_qkv,
    image_self_out,
    text_gains,
    text_shifts,
    image_gains,
    image_shifts,
    text_grad_out,
    image_grad_out,
):
    captions = image_caption.shape[1]
    part_count = lax.axis_size("mp")
    group_count = lax.axis_size("dp")
    spot = lax.axis_index("mp")
    core = spot % 2
    chip = spot // 2
    co_local = CO_HEADS // part_count
    text_local = TEXT_HEADS // part_count
    image_local = IMAGE_HEADS // part_count

    half = captions // 2
    turned = chip == 1
    flip = lambda values: jnp.where(turned, jnp.roll(values, half), values)
    lengths = flip(caption_lengths)
    regions = flip(region_lengths.reshape(-1))
    order = flip(image_caption[0])
    order = jnp.where(turned, (order + half) % captions, order)

    w_co_text = side_by_side(co_text_qkv)
    w_co_image = side_by_side(co_image_qkv)
    w_self_text = side_by_side(text_self_qkv)
    w_self_image = side_by_side(image_self_qkv)

    text_all = gather(text_in, core)
    image_all = gather(image_in, core)
    text_co = product(text_all, w_co_text).astype(BF)
    image_co = product(image_all, w_co_image).astype(BF)
    text_ctx, image_ctx, text_share, image_share = co_forward(
        text_co, image_co, order, regions, lengths, co_local
    )
    text_zero = text_in.astype(F32) + scatter_sum(
        *[product(rows, co_text_out) for rows in halves(text_ctx)], core
    )
    image_zero = image_in.astype(F32) + scatter_sum(
        *[product(rows, co_image_out) for rows in halves(image_ctx)], core
    )
    text_first = layer_norm(text_zero, text_gains[0], text_shifts[0])
    image_first = layer_norm(image_zero, image_gains[0], image_shifts[0])

    text_mlp_in = gather(text_first.astype(BF), core)
    image_mlp_in = gather(image_first.astype(BF), core)
    text_pre = product(text_mlp_in, text_up)
    image_pre = product(image_mlp_in, image_up)
    text_act = gelu_tanh(text_pre).astype(BF)
    image_act = gelu_tanh(image_pre).astype(BF)
    text_mid = text_first + scatter_sum(
        *[product(rows, text_down) for rows in halves(text_act)], core
    )
    image_mid = image_first + scatter_sum(
        *[product(rows, image_down) for rows in halves(image_act)], core
    )
    text_second = layer_norm(text_mid, text_gains[1], text_shifts[1])
    image_second = layer_norm(image_mid, image_gains[1], image_shifts[1])

    text_self_in = gather(text_second.astype(BF), core)
    image_self_in = gather(image_second.astype(BF), core)
    text_parts = product(text_self_in, w_self_text).astype(BF)
    image_parts = product(image_self_in, w_self_image).astype(BF)
    text_self_ctx, text_self_share = self_forward(
        text_parts, lengths, text_local, 3, self_mask_text
    )
    image_self_ctx, image_self_share = self_forward(
        image_parts, regions, image_local, 2, self_mask_image
    )
    text_last = text_second + scatter_sum(
        *[product(rows, text_self_out) for rows in halves(text_self_ctx)], core
    )
    image_last = image_second + scatter_sum(
        *[product(rows, image_self_out) for rows in halves(image_self_ctx)], core
    )
    text_result = layer_norm(text_last, text_gains[2], text_shifts[2]).astype(BF)
    image_result = layer_norm(image_last, image_gains[2], image_shifts[2]).astype(BF)

    text_late_grad, text_gain_c, text_shift_c = norm_back(
        text_last, text_gains[2], text_grad_out.astype(F32)
    )
    image_late_grad, image_gain_c, image_shift_c = norm_back(
        image_last, image_gains[2], image_grad_out.astype(F32)
    )
    text_late_all = gather(text_late_grad.astype(BF), core)
    image_late_all = gather(image_late_grad.astype(BF), core)
    text_parts_grad = self_backward(
        text_parts, text_self_share, product_nt(text_late_all, text_self_out).astype(BF),
        text_local, 3,
    )
    image_parts_grad = self_backward(
        image_parts, image_self_share, product_nt(image_late_all, image_self_out).astype(BF),
        image_local, 2,
    )
    text_back_self = scatter_sum(
        *[product_nt(rows, w_self_text) for rows in halves(text_parts_grad)], core
    )
    image_back_self = scatter_sum(
        *[product_nt(rows, w_self_image) for rows in halves(image_parts_grad)], core
    )
    grads_self = reduce_groups(
        [
            jnp.concatenate(
                [
                    product_tn(text_self_in, text_parts_grad),
                    product_tn(text_late_all, text_self_ctx),
                ],
                axis=1,
            ),
            product_tn(image_self_in, image_parts_grad),
            product_tn(image_late_all, image_self_ctx),
        ],
        group_count,
    )
    text_mid_grad, text_gain_b, text_shift_b = norm_back(
        text_mid, text_gains[1], text_late_grad + text_back_self
    )
    image_mid_grad, image_gain_b, image_shift_b = norm_back(
        image_mid, image_gains[1], image_late_grad + image_back_self
    )

    text_mlp_all = gather(text_mid_grad.astype(BF), core)
    image_mlp_all = gather(image_mid_grad.astype(BF), core)
    text_pre_grad = (product_nt(text_mlp_all, text_down) * gelu_slope(text_pre)).astype(BF)
    image_pre_grad = (product_nt(image_mlp_all, image_down) * gelu_slope(image_pre)).astype(BF)
    text_back_mlp = scatter_sum(
        *[product_nt(rows, text_up) for rows in halves(text_pre_grad)], core
    )
    image_back_mlp = scatter_sum(
        *[product_nt(rows, image_up) for rows in halves(image_pre_grad)], core
    )
    grads_mlp = reduce_groups(
        [
            product_tn(text_mlp_in, text_pre_grad),
            product_tn(text_mlp_all, text_act),
            product_tn(image_mlp_in, image_pre_grad),
            product_tn(image_mlp_all, image_act),
        ],
        group_count,
    )
    text_zero_grad, text_gain_a, text_shift_a = norm_back(
        text_zero, text_gains[0], text_mid_grad + text_back_mlp
    )
    image_zero_grad, image_gain_a, image_shift_a = norm_back(
        image_zero, image_gains[0], image_mid_grad + image_back_mlp
    )

    def norm_columns(*vectors):
        stacked = jnp.stack(vectors)
        for step in (1, 2):
            stacked = stacked + swap(stacked, "mp", step)
        return jnp.pad(stacked.T, ((0, 0), (0, 256 - len(vectors))))

    text_norm = norm_columns(
        text_gain_a, text_gain_b, text_gain_c, text_shift_a, text_shift_b, text_shift_c
    )
    image_norm = norm_columns(
        image_gain_a, image_gain_b, image_gain_c, image_shift_a, image_shift_b, image_shift_c
    )

    text_co_all = gather(text_zero_grad.astype(BF), core)
    image_co_all = gather(image_zero_grad.astype(BF), core)
    text_ctx_grad = product_nt(text_co_all, co_text_out).astype(BF)
    image_ctx_grad = product_nt(image_co_all, co_image_out).astype(BF)
    text_co_grad, image_co_grad = co_backward(
        text_co, image_co, text_share, image_share, text_ctx_grad, image_ctx_grad, order, co_local
    )
    text_in_grad = text_zero_grad + scatter_sum(
        *[product_nt(rows, w_co_text) for rows in halves(text_co_grad)], core
    )
    image_in_grad = image_zero_grad + scatter_sum(
        *[product_nt(rows, w_co_image) for rows in halves(image_co_grad)], core
    )
    bits = list(range(group_count.bit_length() - 1))
    grads_text_co = reduce_halving(
        [product_tn(text_all, text_co_grad), product_tn(text_co_all, text_ctx), text_norm],
        group_count,
        bits,
    )
    grads_image_co = reduce_halving(
        [product_tn(image_all, image_co_grad), product_tn(image_co_all, image_ctx), image_norm],
        group_count,
        bits[1:2] + bits[:1] + bits[2:],
    )

    def norm_part(columns):
        rows = columns.shape[0] // part_count
        mine = lax.dynamic_slice_in_dim(columns, spot * rows, rows, axis=0)[:, :6].T
        return mine[:3], mine[3:]

    text_gain_grad, text_shift_grad = norm_part(grads_text_co[2])
    image_gain_grad, image_shift_grad = norm_part(grads_image_co[2])
    text_self_columns = 3 * text_self_qkv.shape[2]
    return (
        text_result,
        image_result,
        text_in_grad,
        image_in_grad,
        apart(grads_text_co[0]),
        apart(grads_image_co[0]),
        grads_text_co[1].T,
        grads_image_co[1].T,
        grads_mlp[0],
        grads_mlp[1].T,
        grads_mlp[2],
        grads_mlp[3].T,
        apart(grads_self[0][:, :text_self_columns]),
        grads_self[0][:, text_self_columns:].T,
        apart(grads_self[1]),
        grads_self[2].T,
        text_gain_grad,
        text_shift_grad,
        image_gain_grad,
        image_shift_grad,
    )


def solution(mesh):
    tokens = P(("dp", "mp"), None)
    stack_in = P(None, None, "mp")
    rows_in = P("mp", None)
    columns_in = P(None, "mp")
    in_specs = (
        tokens, tokens, P("dp"), P("dp", None), P("dp", None),
        stack_in, stack_in, rows_in, rows_in,
        columns_in, rows_in, columns_in, rows_in,
        stack_in, rows_in, stack_in, rows_in,
        P(), P(), P(), P(),
        tokens, tokens,
    )
    stack_out = P(None, "dp", "mp")
    rows_out = P("mp", "dp")
    columns_out = P("dp", "mp")
    norm_out = P(None, ("dp", "mp"))
    out_specs = (
        tokens, tokens, tokens, tokens,
        stack_out, stack_out, rows_out, rows_out,
        columns_out, rows_out, columns_out, rows_out,
        stack_out, rows_out, stack_out, rows_out,
        norm_out, norm_out, norm_out, norm_out,
    )
    return jax.shard_map(
        per_device, mesh=mesh, in_specs=in_specs, out_specs=out_specs, check_vma=False
    )
```

```python
import functools

import jax
import jax.numpy as jnp
from jax import lax
from jax.experimental import pallas as pl
from jax.experimental.pallas import tpu as pltpu
from jax.sharding import PartitionSpec as P

CO_HEADS = 8
TEXT_HEADS = 12
IMAGE_HEADS = 8
CAP_LEN = 64
ROW_LEN = 128
PER_ROW = 4

epsilon = 1e-05
BF = jnp.bfloat16
F32 = jnp.float32
VMEM_LIMIT = 48 * 1024 * 1024


def product(former, latter):
    return jnp.dot(former, latter, preferred_element_type=F32)


def product_tn(former, latter):
    return lax.dot_general(former, latter, (((0,), (0,)), ((), ())), preferred_element_type=F32)


def product_nt(former, latter):
    return lax.dot_general(former, latter, (((1,), (1,)), ((), ())), preferred_element_type=F32)


def layer_norm(values, norm_gain, norm_shift):
    centre = values - jnp.mean(values, axis=-1, keepdims=True)
    spread = jnp.mean(centre * centre, axis=-1, keepdims=True)
    return centre * lax.rsqrt(spread + epsilon) * norm_gain + norm_shift


def norm_back(values, norm_gain, gradient):
    centre = values - jnp.mean(values, axis=-1, keepdims=True)
    spread = jnp.mean(centre * centre, axis=-1, keepdims=True)
    inverse = lax.rsqrt(spread + epsilon)
    unit = centre * inverse
    scaled = gradient * norm_gain
    back = inverse * (
        scaled
        - jnp.mean(scaled, axis=-1, keepdims=True)
        - unit * jnp.mean(scaled * unit, axis=-1, keepdims=True)
    )
    return back, jnp.sum(gradient * unit, axis=0), jnp.sum(gradient, axis=0)


GELU_A = 0.7978845608028654
GELU_B = 0.044715


def gelu_tanh(values):
    return 0.5 * values * (1.0 + jnp.tanh(GELU_A * (values + GELU_B * values * values * values)))


def gelu_slope(values):
    bent = jnp.tanh(GELU_A * (values + GELU_B * values * values * values))
    return 0.5 * (1.0 + bent) + 0.5 * values * (1.0 - bent * bent) * GELU_A * (
        1.0 + 3.0 * GELU_B * values * values
    )


def softmax_block(scores, mask):
    scores = jnp.where(mask, scores, -1000000000.0)
    exponent = jnp.exp(scores - jnp.max(scores, axis=-1, keepdims=True))
    return (exponent / jnp.sum(exponent, axis=-1, keepdims=True)).astype(BF)


def attend_back(shares, scaling, queries, keys, values, context_grad):
    wide = shares.astype(F32)
    share_grad = product_nt(context_grad, values)
    inner = jnp.sum(share_grad * wide, axis=-1, keepdims=True)
    score_grad = (wide * (share_grad - inner) * scaling).astype(BF)
    return (
        product(score_grad, keys).astype(BF),
        product_tn(score_grad, queries).astype(BF),
        product_tn(shares, context_grad).astype(BF),
    )


def row_ends(region_ref, row):
    ends = [region_ref[row * PER_ROW]]
    for slot in range(1, PER_ROW):
        ends.append(ends[-1] + region_ref[row * PER_ROW + slot])
    return ends


def slot_of(places, ends):
    slot = (places >= ends[0]).astype(jnp.int32)
    for end in ends[1:]:
        slot = slot + (places >= end).astype(jnp.int32)
    return slot


def caption_rows(ref, captions, start, width):
    return jnp.concatenate(
        [
            ref[pl.ds(pl.multiple_of(caption * CAP_LEN, CAP_LEN), CAP_LEN), start : start + width]
            for caption in captions
        ],
        axis=0,
    )


def co_forward_kernel(
    heads, per_step, order_ref, region_ref, length_ref, text_ref, image_ref,
    text_out, image_out, text_shares, image_shares,
):
    inner = text_ref.shape[1] // 3
    size = inner // heads
    scaling = size ** (-0.5)
    span = PER_ROW * CAP_LEN
    for member in range(per_step):
        row = pl.program_id(0) * per_step + member
        captions = [order_ref[row * PER_ROW + slot] for slot in range(PER_ROW)]
        ends = row_ends(region_ref, row)
        token_slot = lax.broadcasted_iota(jnp.int32, (span, ROW_LEN), 0) // CAP_LEN
        to_image = token_slot == slot_of(
            lax.broadcasted_iota(jnp.int32, (span, ROW_LEN), 1), ends
        )
        spots = lax.broadcasted_iota(jnp.int32, (ROW_LEN, span), 1)
        length = jnp.full((ROW_LEN, span), length_ref[captions[0]], jnp.int32)
        for slot in range(1, PER_ROW):
            length = jnp.where(spots >= slot * CAP_LEN, length_ref[captions[slot]], length)
        to_text = (
            slot_of(lax.broadcasted_iota(jnp.int32, (ROW_LEN, span), 0), ends) == spots // CAP_LEN
        ) & (spots % CAP_LEN < length)
        rows = slice(member * ROW_LEN, (member + 1) * ROW_LEN)
        for head in range(heads):
            text = [
                caption_rows(text_ref, captions, part * inner + head * size, size)
                for part in range(3)
            ]
            image = [
                image_ref[rows, part * inner + head * size : part * inner + (head + 1) * size]
                for part in range(3)
            ]
            lanes = slice(head * size, (head + 1) * size)
            shares = softmax_block(product_nt(text[0], image[1]) * scaling, to_image)
            text_shares[member, head] = shares
            context = product(shares, image[2]).astype(BF)
            for slot, caption in enumerate(captions):
                text_out[
                    pl.ds(pl.multiple_of(caption * CAP_LEN, CAP_LEN), CAP_LEN), lanes
                ] = context[slot * CAP_LEN : (slot + 1) * CAP_LEN]
            shares = softmax_block(product_nt(image[0], text[1]) * scaling, to_text)
            image_shares[member, head] = shares
            image_out[rows, lanes] = product(shares, text[2]).astype(BF)


def co_backward_kernel(
    heads, per_step, order_ref, text_ref, image_ref, text_shares, image_shares,
    text_grad, image_grad, text_out, image_out,
):
    inner = text_ref.shape[1] // 3
    size = inner // heads
    scaling = size ** (-0.5)
    for member in range(per_step):
        row = pl.program_id(0) * per_step + member
        captions = [order_ref[row * PER_ROW + slot] for slot in range(PER_ROW)]
        rows = slice(member * ROW_LEN, (member + 1) * ROW_LEN)
        for head in range(heads):
            text = [
                caption_rows(text_ref, captions, part * inner + head * size, size)
                for part in range(3)
            ]
            image = [
                image_ref[rows, part * inner + head * size : part * inner + (head + 1) * size]
                for part in range(3)
            ]
            lanes = slice(head * size, (head + 1) * size)
            from_text = caption_rows(text_grad, captions, head * size, size)
            text_q, image_k, image_v = attend_back(
                text_shares[member, head], scaling, text[0], image[1], image[2], from_text
            )
            image_q, text_k, text_v = attend_back(
                image_shares[member, head], scaling, image[0], text[1], text[2],
                image_grad[rows, lanes],
            )
            for part, grad in enumerate((text_q, text_k, text_v)):
                for slot, caption in enumerate(captions):
                    text_out[
                        pl.ds(pl.multiple_of(caption * CAP_LEN, CAP_LEN), CAP_LEN),
                        part * inner + head * size : part * inner + (head + 1) * size,
                    ] = grad[slot * CAP_LEN : (slot + 1) * CAP_LEN]
            for part, grad in enumerate((image_q, image_k, image_v)):
                image_out[
                    rows, part * inner + head * size : part * inner + (head + 1) * size
                ] = grad


def self_mask_text(length_ref, block):
    shape = (2 * CAP_LEN, 2 * CAP_LEN)
    queries = lax.broadcasted_iota(jnp.int32, shape, 0)
    spots = lax.broadcasted_iota(jnp.int32, shape, 1)
    length = jnp.where(
        spots >= CAP_LEN, length_ref[block * 2 + 1] + CAP_LEN, length_ref[block * 2]
    )
    return (queries // CAP_LEN == spots // CAP_LEN) & (spots < length)


def self_mask_image(region_ref, row):
    ends = row_ends(region_ref, row)
    shape = (ROW_LEN, ROW_LEN)
    return slot_of(lax.broadcasted_iota(jnp.int32, shape, 0), ends) == slot_of(
        lax.broadcasted_iota(jnp.int32, shape, 1), ends
    )


def self_forward_kernel(heads, per_step, masker, count_ref, rows_ref, context_out, shares_out):
    inner = rows_ref.shape[1] // 3
    size = inner // heads
    scaling = size ** (-0.5)
    for member in range(per_step):
        mask = masker(count_ref, pl.program_id(0) * per_step + member)
        rows = slice(member * ROW_LEN, (member + 1) * ROW_LEN)
        contexts = []
        for head in range(heads):
            pieces = [
                rows_ref[rows, part * inner + head * size : part * inner + (head + 1) * size]
                for part in range(3)
            ]
            shares = softmax_block(product_nt(pieces[0], pieces[1]) * scaling, mask)
            shares_out[member, head] = shares
            contexts.append(product(shares, pieces[2]).astype(BF))
        context_out[rows, :] = jnp.concatenate(contexts, axis=1)


def self_backward_kernel(heads, per_step, rows_ref, shares_ref, grad_ref, rows_out):
    inner = rows_ref.shape[1] // 3
    size = inner // heads
    scaling = size ** (-0.5)
    for member in range(per_step):
        rows = slice(member * ROW_LEN, (member + 1) * ROW_LEN)
        grads = []
        for head in range(heads):
            pieces = [
                rows_ref[rows, part * inner + head * size : part * inner + (head + 1) * size]
                for part in range(3)
            ]
            grads.append(
                attend_back(
                    shares_ref[member, head], scaling, *pieces,
                    grad_ref[rows, head * size : (head + 1) * size],
                )
            )
        rows_out[rows, :] = jnp.concatenate(
            [grads[head][part] for part in range(3) for head in range(heads)], axis=1
        )


def shape_of(shape, dtype=BF):
    return jax.ShapeDtypeStruct(shape, dtype)


def cost(flops, moved, exps):
    return pl.CostEstimate(flops=int(flops), bytes_accessed=int(moved), transcendentals=int(exps))


def co_forward(text, image, order, regions, lengths, heads):
    tokens, width = text.shape
    slots = image.shape[0]
    inner = width // 3
    rows = slots // ROW_LEN
    per_step = 2
    span = PER_ROW * CAP_LEN
    whole = lambda i, *_: (0, 0)
    strip = lambda i, *_: (i, 0)
    block = lambda i, *_: (i, 0, 0, 0)
    return pl.pallas_call(
        functools.partial(co_forward_kernel, heads, per_step),
        grid_spec=pltpu.PrefetchScalarGridSpec(
            num_scalar_prefetch=3,
            grid=(rows // per_step,),
            in_specs=[
                pl.BlockSpec((tokens, width), whole),
                pl.BlockSpec((per_step * ROW_LEN, width), strip),
            ],
            out_specs=[
                pl.BlockSpec((tokens, inner), whole),
                pl.BlockSpec((per_step * ROW_LEN, inner), strip),
                pl.BlockSpec((per_step, heads, span, ROW_LEN), block),
                pl.BlockSpec((per_step, heads, ROW_LEN, span), block),
            ],
        ),
        out_shape=[
            shape_of((tokens, inner)),
            shape_of((slots, inner)),
            shape_of((rows, heads, span, ROW_LEN)),
            shape_of((rows, heads, ROW_LEN, span)),
        ],
        compiler_params=pltpu.CompilerParams(vmem_limit_bytes=VMEM_LIMIT),
        cost_estimate=cost(
            8 * rows * inner * span * ROW_LEN, 8e6, 2 * rows * heads * span * ROW_LEN
        ),
        name="co_forward",
    )(order, regions, lengths, text, image)


def co_backward(text, image, text_shares, image_shares, text_grad, image_grad, order, heads):
    tokens, width = text.shape
    slots = image.shape[0]
    inner = width // 3
    rows = slots // ROW_LEN
    per_step = 2
    span = PER_ROW * CAP_LEN
    whole = lambda i, *_: (0, 0)
    strip = lambda i, *_: (i, 0)
    block = lambda i, *_: (i, 0, 0, 0)
    return pl.pallas_call(
        functools.partial(co_backward_kernel, heads, per_step),
        grid_spec=pltpu.PrefetchScalarGridSpec(
            num_scalar_prefetch=1,
            grid=(rows // per_step,),
            in_specs=[
                pl.BlockSpec((tokens, width), whole),
                pl.BlockSpec((per_step * ROW_LEN, width), strip),
                pl.BlockSpec((per_step, heads, span, ROW_LEN), block),
                pl.BlockSpec((per_step, heads, ROW_LEN, span), block),
                pl.BlockSpec((tokens, inner), whole),
                pl.BlockSpec((per_step * ROW_LEN, inner), strip),
            ],
            out_specs=[
                pl.BlockSpec((tokens, width), whole),
                pl.BlockSpec((per_step * ROW_LEN, width), strip),
            ],
        ),
        out_shape=[shape_of((tokens, width)), shape_of((slots, width))],
        compiler_params=pltpu.CompilerParams(vmem_limit_bytes=VMEM_LIMIT),
        cost_estimate=cost(16 * rows * inner * span * ROW_LEN, 12e6, 0),
        name="co_backward",
    )(order, text, image, text_shares, image_shares, text_grad, image_grad)


def self_forward(rows_in, counts, heads, per_step, masker):
    tokens, width = rows_in.shape
    inner = width // 3
    blocks = tokens // ROW_LEN
    strip = lambda i, *_: (i, 0)
    block = lambda i, *_: (i, 0, 0, 0)
    return pl.pallas_call(
        functools.partial(self_forward_kernel, heads, per_step, masker),
        grid_spec=pltpu.PrefetchScalarGridSpec(
            num_scalar_prefetch=1,
            grid=(blocks // per_step,),
            in_specs=[pl.BlockSpec((per_step * ROW_LEN, width), strip)],
            out_specs=[
                pl.BlockSpec((per_step * ROW_LEN, inner), strip),
                pl.BlockSpec((per_step, heads, ROW_LEN, ROW_LEN), block),
            ],
        ),
        out_shape=[
            shape_of((tokens, inner)),
            shape_of((blocks, heads, ROW_LEN, ROW_LEN)),
        ],
        compiler_params=pltpu.CompilerParams(vmem_limit_bytes=VMEM_LIMIT),
        cost_estimate=cost(4 * tokens * inner * ROW_LEN, 6e6, tokens * heads * ROW_LEN),
        name="self_forward",
    )(counts, rows_in)


def self_backward(rows_in, shares, grad, heads, per_step):
    tokens, width = rows_in.shape
    inner = width // 3
    blocks = tokens // ROW_LEN
    strip = lambda i: (i, 0)
    block = lambda i: (i, 0, 0, 0)
    return pl.pallas_call(
        functools.partial(self_backward_kernel, heads, per_step),
        grid=(blocks // per_step,),
        in_specs=[
            pl.BlockSpec((per_step * ROW_LEN, width), strip),
            pl.BlockSpec((per_step, heads, ROW_LEN, ROW_LEN), block),
            pl.BlockSpec((per_step * ROW_LEN, inner), strip),
        ],
        out_specs=pl.BlockSpec((per_step * ROW_LEN, width), strip),
        out_shape=shape_of((tokens, width)),
        compiler_params=pltpu.CompilerParams(vmem_limit_bytes=VMEM_LIMIT),
        cost_estimate=cost(10 * tokens * inner * ROW_LEN, 9e6, 0),
        name="self_backward",
    )(rows_in, shares, grad)


MESH = pl.DeviceIdType.MESH
BIG_LIMIT = 60 * 1024 * 1024


class Bench:
    def __init__(self, refs, fetched, flushed, counts):
        self.refs = refs
        self.fetches = {}
        self.flushes = []
        self.flush_index = {name: i for i, name in enumerate(flushed)}
        self.copies = 0
        for index, name in enumerate(fetched):
            copy = pltpu.make_async_copy(
                refs["in_" + name], refs[name], refs["fetch_sems"].at[index]
            )
            copy.start()
            self.fetches[name] = copy

    def __getattr__(self, name):
        fetches = self.__dict__["fetches"]
        if name in fetches:
            fetches.pop(name).wait()
        return self.__dict__["refs"][name]

    def flush(self, *names):
        for name in names:
            copy = pltpu.make_async_copy(
                self.refs[name],
                self.refs["out_" + name],
                self.refs["flush_sems"].at[self.flush_index.pop(name)],
            )
            copy.start()
            self.flushes.append(copy)

    def remote(self, source, target, peer):
        index = self.copies
        self.copies += 1
        return pltpu.make_async_remote_copy(
            src_ref=source,
            dst_ref=target,
            send_sem=self.refs["send_sems"].at[index],
            recv_sem=self.refs["recv_sems"].at[index],
            device_id=peer,
            device_id_type=MESH,
        )

    def close(self):
        for name in list(self.flush_index):
            self.flush(name)
        for copy in self.flushes:
            copy.wait()


def exchange_kernel(body, name, collective, peers, inputs, outputs, scratch, copies, work):
    fetched = [key for key, (_, kind) in inputs.items() if kind == "hbm"]
    flushed = [key for key, (_, _, kind) in outputs.items() if kind == "hbm"]
    spaces = {"hbm": pl.ANY, "vmem": pltpu.VMEM, "smem": pltpu.SMEM}
    names = [("in_" + key if kind == "hbm" else key) for key, (_, kind) in inputs.items()]
    names += [("out_" + key if kind == "hbm" else key) for key, (_, _, kind) in outputs.items()]
    shapes = []
    for key in fetched:
        names.append(key)
        shapes.append(pltpu.VMEM(inputs[key][0].shape, inputs[key][0].dtype))
    for key in flushed:
        names.append(key)
        shapes.append(pltpu.VMEM(outputs[key][0], outputs[key][1]))
    for key, (shape, dtype) in scratch.items():
        names.append(key)
        shapes.append(pltpu.VMEM(shape, dtype))
    for key, count in (
        ("fetch_sems", len(fetched)), ("flush_sems", len(flushed)),
        ("send_sems", copies), ("recv_sems", copies),
    ):
        names.append(key)
        shapes.append(pltpu.SemaphoreType.DMA((max(count, 1),)))

    def kernel(*refs):
        bench = Bench(dict(zip(names, refs)), fetched, flushed, copies)
        barrier = pltpu.get_barrier_semaphore()
        partners = peers()
        for partner in partners:
            pl.semaphore_signal(barrier, inc=1, device_id=partner, device_id_type=MESH)
        pl.semaphore_wait(barrier, len(partners))
        body(bench)
        bench.close()

    flops, moved, exps = work
    results = pl.pallas_call(
        kernel,
        in_specs=[pl.BlockSpec(memory_space=spaces[kind]) for _, kind in inputs.values()],
        out_specs=[pl.BlockSpec(memory_space=spaces[kind]) for _, _, kind in outputs.values()],
        out_shape=[shape_of(shape, dtype) for shape, dtype, _ in outputs.values()],
        scratch_shapes=shapes,
        compiler_params=pltpu.CompilerParams(
            collective_id=collective, has_side_effects=True, vmem_limit_bytes=BIG_LIMIT
        ),
        cost_estimate=cost(flops, moved, exps),
        name=name,
    )(*[array for array, _ in inputs.values()])
    return dict(zip(outputs, results))


def group_peers():
    spot = lax.axis_index("mp")
    core = lax.rem(spot, 2)
    chip = lax.div(spot, 2)
    return core, {"mp": spot + 1 - 2 * core}, {"mp": spot + 2 - 4 * chip}


class Stream:
    def __init__(self, bench, tag, rows):
        self.bench = bench
        self.rows = rows
        self.core, self.core_peer, self.chip_peer = group_peers()
        self.other = 1 - self.core
        for key in ("give", "got", "send", "recv", "acc"):
            setattr(self, key, getattr(bench, tag + "_" + key))

    def place(self, half, core):
        step = self.rows & -self.rows
        return pl.ds(pl.multiple_of((2 * half + core) * self.rows, step), self.rows)

    def gather(self, full):
        own = full.at[self.place(0, self.core)]
        far = full.at[self.place(1, self.core)]
        self.across = self.bench.remote(own, far, self.chip_peer)
        self.near = self.bench.remote(own, own, self.core_peer)
        self.relay = self.bench.remote(far, far, self.core_peer)
        self.across.start()
        self.near.start()

    def arrive(self, half, project):
        if half == 0:
            project(0, self.core)
            self.near.wait_recv()
            project(0, self.other)
        else:
            self.across.wait_recv()
            self.relay.start()
            project(1, self.core)
            self.relay.wait_recv()
            project(1, self.other)

    def open_sum(self):
        self.hand = [
            self.bench.remote(self.give.at[half], self.got.at[half], self.core_peer)
            for half in (0, 1)
        ]
        self.post = self.bench.remote(self.send, self.recv, self.chip_peer)

    def partial(self, half, output):
        self.give[half] = output(half, self.other).astype(BF)
        self.hand[half].start()
        self.acc[half] = output(half, self.core)
        if half == 1:
            self.hand[1].wait_recv()
            self.send[...] = (self.acc[1] + self.got[1].astype(F32)).astype(BF)
            self.post.start()

    def settle(self, gathered=True):
        self.hand[0].wait_recv()
        self.post.wait_recv()
        self.hand[0].wait_send()
        self.hand[1].wait_send()
        self.post.wait_send()
        if gathered:
            self.finish_gather()

    def finish_gather(self):
        self.across.wait_send()
        self.near.wait_send()
        self.relay.wait_send()

    def piece(self, rows):
        return self.acc[0, rows] + self.got[0, rows].astype(F32) + self.recv[rows].astype(F32)


CHUNK = 32


def chunks(count, step, start):
    def once(index, carry):
        return step(pl.ds(pl.multiple_of(index * CHUNK, CHUNK), CHUNK), carry)

    return lax.fori_loop(0, count // CHUNK, once, start)


def folded(values):
    return jnp.sum(values.reshape(CHUNK // 8, 8, values.shape[-1]), axis=0)


def stream_scratch(tag, rows, width):
    return {
        tag + "_give": ((2, rows, width), BF),
        tag + "_got": ((2, rows, width), BF),
        tag + "_send": ((rows, width), BF),
        tag + "_recv": ((rows, width), BF),
        tag + "_acc": ((2, rows, width), F32),
    }


def at_offset(ref, offset, rows):
    return ref.at[pl.ds(pl.multiple_of(offset + rows.start, CHUNK), rows.size)]


def attend_many(parts_ref, share_ref, context_ref, base, first_block, blocks, heads, masker):
    inner = parts_ref.shape[1] // 3
    size = inner // heads
    scaling = size ** (-0.5)
    rows = [
        pl.ds(pl.multiple_of(base + block * ROW_LEN, CHUNK), ROW_LEN) for block in range(blocks)
    ]
    masks = [masker(first_block + block) for block in range(blocks)]
    scores = []
    for block in range(blocks):
        for head in range(heads):
            queries = parts_ref[rows[block], head * size : (head + 1) * size]
            keys = parts_ref[rows[block], inner + head * size : inner + (head + 1) * size]
            scores.append(jnp.where(masks[block], product_nt(queries, keys) * scaling, -1e9))
    scores = jnp.concatenate(scores, axis=0)
    exponent = jnp.exp(scores - jnp.max(scores, axis=-1, keepdims=True))
    shares = (exponent / jnp.sum(exponent, axis=-1, keepdims=True)).astype(BF)
    for block in range(blocks):
        contexts = []
        for head in range(heads):
            at = (block * heads + head) * ROW_LEN
            piece = shares[at : at + ROW_LEN]
            share_ref[first_block + block, head] = piece
            values = parts_ref[rows[block], 2 * inner + head * size : 2 * inner + (head + 1) * size]
            contexts.append(product(piece, values).astype(BF))
        context_ref[rows[block], :] = jnp.concatenate(contexts, axis=1)


def norm_chunk(values, gain, shift):
    centre = values - jnp.mean(values, axis=-1, keepdims=True)
    spread = jnp.mean(centre * centre, axis=-1, keepdims=True)
    return centre * lax.rsqrt(spread + epsilon) * gain + shift


def forward_kernel(ctx_t, ctx_i, text_in, image_in, weights, norms, text_g, image_g, lengths, regions,
                   text_local, image_local):
    (co_text_out, co_image_out, text_up, text_down, image_up, image_down,
     w_self_text, text_self_out, w_self_image, image_self_out) = weights
    n_t, d_t = text_in.shape
    n_i, d_i = image_in.shape
    ff_t, ff_i = text_up.shape[1], image_up.shape[1]
    in_t, in_i = text_self_out.shape[0], image_self_out.shape[0]
    inputs = {
        "lengths": (lengths, "smem"), "regions": (regions, "smem"),
        "gains_t": (norms[0], "vmem"), "shifts_t": (norms[1], "vmem"),
        "gains_i": (norms[2], "vmem"), "shifts_i": (norms[3], "vmem"),
        "ctx_i": (ctx_i, "hbm"), "w_co_i": (co_image_out, "hbm"),
        "ctx_t": (ctx_t, "hbm"), "w_co_t": (co_text_out, "hbm"),
        "x_i": (image_in, "hbm"), "x_t": (text_in, "hbm"),
        "up_i": (image_up, "hbm"), "down_i": (image_down, "hbm"),
        "up_t": (text_up, "hbm"), "down_t": (text_down, "hbm"),
        "qkv_i": (w_self_image, "hbm"), "so_i": (image_self_out, "hbm"),
        "qkv_t": (w_self_text, "hbm"), "so_t": (text_self_out, "hbm"),
        "g_i": (image_g, "hbm"), "g_t": (text_g, "hbm"),
    }
    outputs = {}
    scratch = {}
    for tag, n, d, ff, inner, heads in (
        ("t", n_t, d_t, ff_t, in_t, text_local), ("i", n_i, d_i, ff_i, in_i, image_local),
    ):
        outputs.update({
            "zero_" + tag: ((n, d), F32, "hbm"),
            "mid_" + tag: ((n, d), F32, "hbm"),
            "mlp_" + tag: ((4 * n, d), BF, "hbm"),
            "act_" + tag: ((4 * n, ff), BF, "hbm"),
            "slope_" + tag: ((4 * n, ff), BF, "hbm"),
            "self_" + tag: ((4 * n, d), BF, "hbm"),
            "parts_" + tag: ((4 * n, 3 * inner), BF, "hbm"),
            "share_" + tag: ((4 * n // ROW_LEN, heads, ROW_LEN, ROW_LEN), BF, "hbm"),
            "ctx2_" + tag: ((4 * n, inner), BF, "hbm"),
            "late_" + tag: ((n, d), F32, "hbm"),
            "result_" + tag: ((n, d), BF, "hbm"),
            "gain_" + tag: ((8, d), F32, "vmem"),
            "shift_" + tag: ((8, d), F32, "vmem"),
        })
        scratch.update(stream_scratch(tag, n, d))
        scratch["first_" + tag] = ((n, d), F32)

    def body(bench):
        streams = {tag: Stream(bench, tag, n) for tag, n in (("i", n_i), ("t", n_t))}
        get = lambda key, tag: getattr(bench, key + "_" + tag)

        for tag, stream in streams.items():
            context, weight = get("ctx", tag), get("w_co", tag)
            output = lambda half, core: product(context[stream.place(half, core)], weight[...])
            stream.open_sum()
            stream.partial(1, output)
            stream.partial(0, output)

        def settle(tag, stage, source, kept, resid, full):
            stream = streams[tag]
            stream.settle(gathered=stage > 0)
            gain = get("gains", tag)[stage : stage + 1]
            shift = get("shifts", tag)[stage : stage + 1]
            base = stream.core * stream.rows

            def step(rows, carry):
                values = source[rows].astype(F32) + stream.piece(rows)
                kept[rows] = values
                normed = norm_chunk(values, gain, shift)
                resid[rows] = normed
                at_offset(full, base, rows)[...] = normed.astype(BF)
                return carry

            chunks(stream.rows, step, 0)
            bench.flush({"zero": "zero_", "mid": "mid_"}["zero" if stage == 0 else "mid"] + tag)
            stream.gather(full)

        for tag in streams:
            settle(tag, 0, get("x", tag), get("zero", tag), get("first", tag), get("mlp", tag))

        def feeds(tag):
            stream = streams[tag]
            full, up, down = get("mlp", tag), get("up", tag), get("down", tag)
            act, slope = get("act", tag), get("slope", tag)

            def project(half, core):
                place = stream.place(half, core)
                pre = product(full[place], up[...])
                cube = GELU_A * (pre + GELU_B * pre * pre * pre)
                bent = jnp.tanh(cube)
                act[place] = (0.5 * pre * (1.0 + bent)).astype(BF)
                slope[place] = (
                    0.5 * (1.0 + bent)
                    + 0.5 * pre * (1.0 - bent * bent) * GELU_A * (1.0 + 3.0 * GELU_B * pre * pre)
                ).astype(BF)

            def output(half, core):
                return product(act[stream.place(half, core)], down[...])

            return project, output

        def layer(work):
            for half in (0, 1):
                for tag, stream in streams.items():
                    hooks = work[tag]
                    if half == 0:
                        stream.open_sum()
                    stream.arrive(half, hooks[0])
                    if len(hooks) > 2:
                        hooks[2](half)
                    stream.partial(half, hooks[1])

        layer({tag: feeds(tag) for tag in streams})
        for tag in streams:
            settle(tag, 1, get("first", tag), get("mid", tag), get("first", tag), get("self", tag))
            bench.flush("mlp_" + tag, "act_" + tag, "slope_" + tag)

        def attends(tag):
            stream = streams[tag]
            full, qkv, out = get("self", tag), get("qkv", tag), get("so", tag)
            parts, share, context = get("parts", tag), get("share", tag), get("ctx2", tag)

            def output(half, core):
                return product(context[stream.place(half, core)], out[...])

            if tag == "t":

                def project(half, core):
                    place = stream.place(half, core)
                    parts[place] = product(full[place], qkv[...]).astype(BF)
                    quad = 2 * half + core
                    attend_many(
                        parts, share, context, quad * n_t, quad * (n_t // ROW_LEN),
                        n_t // ROW_LEN, text_local,
                        functools.partial(self_mask_text, bench.lengths),
                    )

                return project, output

            def project_image(half, core):
                place = stream.place(half, core)
                parts[place] = product(full[place], qkv[...]).astype(BF)

            def middle(half):
                blocks = 2 * n_i // ROW_LEN
                attend_many(
                    parts, share, context, 2 * half * n_i, half * blocks, blocks, image_local,
                    functools.partial(self_mask_image, bench.regions),
                )

            return project_image, output, middle

        layer({tag: attends(tag) for tag in streams})
        for tag, stream in streams.items():
            stream.settle()
            bench.flush("self_" + tag, "parts_" + tag, "share_" + tag, "ctx2_" + tag)
            gain, shift = get("gains", tag)[2:3], get("shifts", tag)[2:3]
            second, result, late, grad = (
                get("first", tag), get("result", tag), get("late", tag), get("g", tag)
            )
            width = second.shape[1]

            def step(rows, carry):
                values = second[rows] + stream.piece(rows)
                back, normed, gains, shifts = norm_pull(values, gain, shift, grad[rows].astype(F32))
                result[rows] = normed.astype(BF)
                late[rows] = back
                return carry[0] + gains, carry[1] + shifts

            start = jnp.zeros((8, width), F32)
            gains, shifts = chunks(stream.rows, step, (start, start))
            get("gain", tag)[...] = gains
            get("shift", tag)[...] = shifts
            bench.flush("result_" + tag, "late_" + tag)

    return exchange_kernel(
        body, "forward_tail", 1, lambda: list(group_peers()[1:]), inputs, outputs, scratch, 32,
        (15e9, 40e6, 1e6),
    )


def norm_pull(values, gain, shift, gradient):
    centre = values - jnp.mean(values, axis=-1, keepdims=True)
    spread = jnp.mean(centre * centre, axis=-1, keepdims=True)
    inverse = lax.rsqrt(spread + epsilon)
    unit = centre * inverse
    scaled = gradient * gain
    back = inverse * (
        scaled
        - jnp.mean(scaled, axis=-1, keepdims=True)
        - unit * jnp.mean(scaled * unit, axis=-1, keepdims=True)
    )
    return back, unit * gain + shift, folded(gradient * unit), folded(gradient)


def swap(values, axis, flip):
    return lax.ppermute(values, axis, [(i, i ^ flip) for i in range(lax.axis_size(axis))])


def gather(shard, core):
    other = swap(shard, "mp", 2)
    near = swap(shard, "mp", 1)
    far = swap(other, "mp", 1)
    first = core == 0
    return jnp.concatenate(
        [
            jnp.where(first, shard, near),
            jnp.where(first, near, shard),
            jnp.where(first, other, far),
            jnp.where(first, far, other),
        ],
        axis=0,
    )


def scatter_sum(left, right, core):
    first = core == 0

    def over_cores(half):
        upper, lower = jnp.split(half, 2, axis=0)
        kept = jnp.where(first, upper, lower)
        given = jnp.where(first, lower, upper).astype(BF)
        return kept + swap(given, "mp", 1).astype(F32)

    sent = swap(over_cores(right).astype(BF), "mp", 2)
    return over_cores(left) + sent.astype(F32)


def halves(rows):
    return jnp.split(rows, 2, axis=0)


def blocked(grads, group_count):
    pieces = []
    for grad in grads:
        rows, columns = grad.shape
        for start in range(0, columns, 256):
            pieces.append(
                grad[:, start : start + 256].astype(BF).reshape(group_count, rows // group_count, 256)
            )
    return jnp.concatenate(pieces, axis=1)


def unblocked(summed, shapes, group_count):
    outs = []
    at = 0
    for rows, columns in shapes:
        part = rows // group_count
        pieces = []
        for _ in range(columns // 256):
            pieces.append(summed[at : at + part])
            at += part
        outs.append(jnp.concatenate(pieces, axis=1).astype(F32))
    return outs


def reduce_groups(grads, group_count):
    stacked = blocked(grads, group_count)
    flat = stacked.reshape(-1, 256)
    summed = lax.psum_scatter(flat, "dp", scatter_dimension=0, tiled=True)
    return unblocked(summed, [grad.shape for grad in grads], group_count)


def reduce_halving(grads, group_count, bits):
    current = blocked(grads, group_count)
    tail = current.shape[1:]
    place = lax.axis_index("dp")
    names = list(range(group_count.bit_length() - 1))[::-1]
    current = current.reshape((2,) * len(names) + tail)
    for bit in bits:
        axis = names.index(bit)
        lower = lax.index_in_dim(current, 0, axis, keepdims=False)
        upper = lax.index_in_dim(current, 1, axis, keepdims=False)
        mine = (place >> bit) & 1
        kept = jnp.where(mine == 0, lower, upper)
        given = jnp.where(mine == 0, upper, lower)
        current = (kept.astype(F32) + swap(given, "dp", 1 << bit).astype(F32)).astype(BF)
        names.pop(axis)
    return unblocked(current, [grad.shape for grad in grads], group_count)


def side_by_side(stacked):
    members, height, breadth = stacked.shape
    return jnp.transpose(stacked, (1, 0, 2)).reshape(height, members * breadth)


def apart(grad):
    rows, columns = grad.shape
    return jnp.transpose(grad.reshape(rows, 3, columns // 3), (1, 0, 2))


def per_device(
    text_in,
    image_in,
    caption_lengths,
    region_lengths,
    image_caption,
    co_text_qkv,
    co_image_qkv,
    co_text_out,
    co_image_out,
    text_up,
    text_down,
    image_up,
    image_down,
    text_self_qkv,
    text_self_out,
    image_self_qkv,
    image_self_out,
    text_gains,
    text_shifts,
    image_gains,
    image_shifts,
    text_grad_out,
    image_grad_out,
):
    captions = image_caption.shape[1]
    part_count = lax.axis_size("mp")
    group_count = lax.axis_size("dp")
    spot = lax.axis_index("mp")
    core = spot % 2
    chip = spot // 2
    co_local = CO_HEADS // part_count
    text_local = TEXT_HEADS // part_count
    image_local = IMAGE_HEADS // part_count

    half = captions // 2
    turned = chip == 1
    flip = lambda values: jnp.where(turned, jnp.roll(values, half), values)
    lengths = flip(caption_lengths)
    regions = flip(region_lengths.reshape(-1))
    order = flip(image_caption[0])
    order = jnp.where(turned, (order + half) % captions, order)

    w_co_text = side_by_side(co_text_qkv)
    w_co_image = side_by_side(co_image_qkv)
    w_self_text = side_by_side(text_self_qkv)
    w_self_image = side_by_side(image_self_qkv)

    text_all = gather(text_in, core)
    image_all = gather(image_in, core)
    text_co = product(text_all, w_co_text).astype(BF)
    image_co = product(image_all, w_co_image).astype(BF)
    text_ctx, image_ctx, text_share, image_share = co_forward(
        text_co, image_co, order, regions, lengths, co_local
    )
    ahead = forward_kernel(
        text_ctx, image_ctx, text_in, image_in,
        (co_text_out, co_image_out, text_up, text_down, image_up, image_down,
         w_self_text, text_self_out, w_self_image, image_self_out),
        (text_gains, text_shifts, image_gains, image_shifts),
        text_grad_out, image_grad_out, lengths, regions, text_local, image_local,
    )
    text_result, image_result = ahead["result_t"], ahead["result_i"]
    text_zero, image_zero = ahead["zero_t"], ahead["zero_i"]
    text_mid, image_mid = ahead["mid_t"], ahead["mid_i"]
    text_mlp_in, image_mlp_in = ahead["mlp_t"], ahead["mlp_i"]
    text_act, image_act = ahead["act_t"], ahead["act_i"]
    text_slope, image_slope = ahead["slope_t"], ahead["slope_i"]
    text_self_in, image_self_in = ahead["self_t"], ahead["self_i"]
    text_parts, image_parts = ahead["parts_t"], ahead["parts_i"]
    text_self_share, image_self_share = ahead["share_t"], ahead["share_i"]
    text_self_ctx, image_self_ctx = ahead["ctx2_t"], ahead["ctx2_i"]
    text_late_grad, image_late_grad = ahead["late_t"], ahead["late_i"]
    text_gain_c, text_shift_c = [jnp.sum(ahead[key], axis=0) for key in ("gain_t", "shift_t")]
    image_gain_c, image_shift_c = [jnp.sum(ahead[key], axis=0) for key in ("gain_i", "shift_i")]

    text_late_all = gather(text_late_grad.astype(BF), core)
    image_late_all = gather(image_late_grad.astype(BF), core)
    text_parts_grad = self_backward(
        text_parts, text_self_share, product_nt(text_late_all, text_self_out).astype(BF),
        text_local, 3,
    )
    image_parts_grad = self_backward(
        image_parts, image_self_share, product_nt(image_late_all, image_self_out).astype(BF),
        image_local, 2,
    )
    text_back_self = scatter_sum(
        *[product_nt(rows, w_self_text) for rows in halves(text_parts_grad)], core
    )
    image_back_self = scatter_sum(
        *[product_nt(rows, w_self_image) for rows in halves(image_parts_grad)], core
    )
    grads_self = reduce_groups(
        [
            jnp.concatenate(
                [
                    product_tn(text_self_in, text_parts_grad),
                    product_tn(text_late_all, text_self_ctx),
                ],
                axis=1,
            ),
            product_tn(image_self_in, image_parts_grad),
            product_tn(image_late_all, image_self_ctx),
        ],
        group_count,
    )
    text_mid_grad, text_gain_b, text_shift_b = norm_back(
        text_mid, text_gains[1], text_late_grad + text_back_self
    )
    image_mid_grad, image_gain_b, image_shift_b = norm_back(
        image_mid, image_gains[1], image_late_grad + image_back_self
    )

    text_mlp_all = gather(text_mid_grad.astype(BF), core)
    image_mlp_all = gather(image_mid_grad.astype(BF), core)
    text_pre_grad = (product_nt(text_mlp_all, text_down) * text_slope.astype(F32)).astype(BF)
    image_pre_grad = (product_nt(image_mlp_all, image_down) * image_slope.astype(F32)).astype(BF)
    text_back_mlp = scatter_sum(
        *[product_nt(rows, text_up) for rows in halves(text_pre_grad)], core
    )
    image_back_mlp = scatter_sum(
        *[product_nt(rows, image_up) for rows in halves(image_pre_grad)], core
    )
    grads_mlp = reduce_groups(
        [
            product_tn(text_mlp_in, text_pre_grad),
            product_tn(text_mlp_all, text_act),
            product_tn(image_mlp_in, image_pre_grad),
            product_tn(image_mlp_all, image_act),
        ],
        group_count,
    )
    text_zero_grad, text_gain_a, text_shift_a = norm_back(
        text_zero, text_gains[0], text_mid_grad + text_back_mlp
    )
    image_zero_grad, image_gain_a, image_shift_a = norm_back(
        image_zero, image_gains[0], image_mid_grad + image_back_mlp
    )

    def norm_columns(*vectors):
        stacked = jnp.stack(vectors)
        for step in (1, 2):
            stacked = stacked + swap(stacked, "mp", step)
        return jnp.pad(stacked.T, ((0, 0), (0, 256 - len(vectors))))

    text_norm = norm_columns(
        text_gain_a, text_gain_b, text_gain_c, text_shift_a, text_shift_b, text_shift_c
    )
    image_norm = norm_columns(
        image_gain_a, image_gain_b, image_gain_c, image_shift_a, image_shift_b, image_shift_c
    )

    text_co_all = gather(text_zero_grad.astype(BF), core)
    image_co_all = gather(image_zero_grad.astype(BF), core)
    text_ctx_grad = product_nt(text_co_all, co_text_out).astype(BF)
    image_ctx_grad = product_nt(image_co_all, co_image_out).astype(BF)
    text_co_grad, image_co_grad = co_backward(
        text_co, image_co, text_share, image_share, text_ctx_grad, image_ctx_grad, order, co_local
    )
    text_in_grad = text_zero_grad + scatter_sum(
        *[product_nt(rows, w_co_text) for rows in halves(text_co_grad)], core
    )
    image_in_grad = image_zero_grad + scatter_sum(
        *[product_nt(rows, w_co_image) for rows in halves(image_co_grad)], core
    )
    bits = list(range(group_count.bit_length() - 1))
    grads_text_co = reduce_halving(
        [product_tn(text_all, text_co_grad), product_tn(text_co_all, text_ctx), text_norm],
        group_count,
        bits,
    )
    grads_image_co = reduce_halving(
        [product_tn(image_all, image_co_grad), product_tn(image_co_all, image_ctx), image_norm],
        group_count,
        bits[1:2] + bits[:1] + bits[2:],
    )

    def norm_part(columns):
        rows = columns.shape[0] // part_count
        mine = lax.dynamic_slice_in_dim(columns, spot * rows, rows, axis=0)[:, :6].T
        return mine[:3], mine[3:]

    text_gain_grad, text_shift_grad = norm_part(grads_text_co[2])
    image_gain_grad, image_shift_grad = norm_part(grads_image_co[2])
    text_self_columns = 3 * text_self_qkv.shape[2]
    return (
        text_result,
        image_result,
        text_in_grad,
        image_in_grad,
        apart(grads_text_co[0]),
        apart(grads_image_co[0]),
        grads_text_co[1].T,
        grads_image_co[1].T,
        grads_mlp[0],
        grads_mlp[1].T,
        grads_mlp[2],
        grads_mlp[3].T,
        apart(grads_self[0][:, :text_self_columns]),
        grads_self[0][:, text_self_columns:].T,
        apart(grads_self[1]),
        grads_self[2].T,
        text_gain_grad,
        text_shift_grad,
        image_gain_grad,
        image_shift_grad,
    )


def solution(mesh):
    tokens = P(("dp", "mp"), None)
    stack_in = P(None, None, "mp")
    rows_in = P("mp", None)
    columns_in = P(None, "mp")
    in_specs = (
        tokens, tokens, P("dp"), P("dp", None), P("dp", None),
        stack_in, stack_in, rows_in, rows_in,
        columns_in, rows_in, columns_in, rows_in,
        stack_in, rows_in, stack_in, rows_in,
        P(), P(), P(), P(),
        tokens, tokens,
    )
    stack_out = P(None, "dp", "mp")
    rows_out = P("mp", "dp")
    columns_out = P("dp", "mp")
    norm_out = P(None, ("dp", "mp"))
    out_specs = (
        tokens, tokens, tokens, tokens,
        stack_out, stack_out, rows_out, rows_out,
        columns_out, rows_out, columns_out, rows_out,
        stack_out, rows_out, stack_out, rows_out,
        norm_out, norm_out, norm_out, norm_out,
    )
    return jax.shard_map(
        per_device, mesh=mesh, in_specs=in_specs, out_specs=out_specs, check_vma=False
    )
```

```python
import functools

import jax
import jax.numpy as jnp
from jax import lax
from jax.experimental import pallas as pl
from jax.experimental.pallas import tpu as pltpu
from jax.sharding import PartitionSpec as P

CO_HEADS = 8
TEXT_HEADS = 12
IMAGE_HEADS = 8
CAP_LEN = 64
ROW_LEN = 128
PER_ROW = 4

epsilon = 1e-05
BF = jnp.bfloat16
F32 = jnp.float32
VMEM_LIMIT = 48 * 1024 * 1024


def product(former, latter):
    return jnp.dot(former, latter, preferred_element_type=F32)


def product_tn(former, latter):
    return lax.dot_general(former, latter, (((0,), (0,)), ((), ())), preferred_element_type=F32)


def product_nt(former, latter):
    return lax.dot_general(former, latter, (((1,), (1,)), ((), ())), preferred_element_type=F32)


def layer_norm(values, norm_gain, norm_shift):
    centre = values - jnp.mean(values, axis=-1, keepdims=True)
    spread = jnp.mean(centre * centre, axis=-1, keepdims=True)
    return centre * lax.rsqrt(spread + epsilon) * norm_gain + norm_shift


def norm_back(values, norm_gain, gradient):
    centre = values - jnp.mean(values, axis=-1, keepdims=True)
    spread = jnp.mean(centre * centre, axis=-1, keepdims=True)
    inverse = lax.rsqrt(spread + epsilon)
    unit = centre * inverse
    scaled = gradient * norm_gain
    back = inverse * (
        scaled
        - jnp.mean(scaled, axis=-1, keepdims=True)
        - unit * jnp.mean(scaled * unit, axis=-1, keepdims=True)
    )
    return back, jnp.sum(gradient * unit, axis=0), jnp.sum(gradient, axis=0)


GELU_A = 0.7978845608028654
GELU_B = 0.044715


def gelu_tanh(values):
    return 0.5 * values * (1.0 + jnp.tanh(GELU_A * (values + GELU_B * values * values * values)))


def gelu_slope(values):
    bent = jnp.tanh(GELU_A * (values + GELU_B * values * values * values))
    return 0.5 * (1.0 + bent) + 0.5 * values * (1.0 - bent * bent) * GELU_A * (
        1.0 + 3.0 * GELU_B * values * values
    )


def softmax_block(scores, mask):
    scores = jnp.where(mask, scores, -1000000000.0)
    exponent = jnp.exp(scores - jnp.max(scores, axis=-1, keepdims=True))
    return (exponent / jnp.sum(exponent, axis=-1, keepdims=True)).astype(BF)


def attend_back(shares, scaling, queries, keys, values, context_grad):
    wide = shares.astype(F32)
    share_grad = product_nt(context_grad, values)
    inner = jnp.sum(share_grad * wide, axis=-1, keepdims=True)
    score_grad = (wide * (share_grad - inner) * scaling).astype(BF)
    return (
        product(score_grad, keys).astype(BF),
        product_tn(score_grad, queries).astype(BF),
        product_tn(shares, context_grad).astype(BF),
    )


def row_ends(region_ref, row):
    ends = [region_ref[row * PER_ROW]]
    for slot in range(1, PER_ROW):
        ends.append(ends[-1] + region_ref[row * PER_ROW + slot])
    return ends


def slot_of(places, ends):
    slot = (places >= ends[0]).astype(jnp.int32)
    for end in ends[1:]:
        slot = slot + (places >= end).astype(jnp.int32)
    return slot


def caption_rows(ref, captions, start, width):
    return jnp.concatenate(
        [ref[caption, :, start : start + width] for caption in captions], axis=0
    )


def co_forward_rows(bench, heads, rows_total):
    text_ref, image_ref = bench.co_t, bench.co_i
    inner = image_ref.shape[1] // 3
    size = inner // heads
    scaling = size ** (-0.5)
    span = PER_ROW * CAP_LEN
    per_step = 2
    order_ref, length_ref = bench.order, bench.lengths
    text_shares, image_shares = bench.cshare_t, bench.cshare_i
    text_out, image_out = bench.rctx_t, bench.ctx_i

    def step(index, carry):
        for member in range(per_step):
            row = index * per_step + member
            captions = [order_ref[row * PER_ROW + slot] for slot in range(PER_ROW)]
            ends = row_ends(bench.regions, row)
            token_slot = lax.broadcasted_iota(jnp.int32, (span, ROW_LEN), 0) // CAP_LEN
            to_image = token_slot == slot_of(
                lax.broadcasted_iota(jnp.int32, (span, ROW_LEN), 1), ends
            )
            spots = lax.broadcasted_iota(jnp.int32, (ROW_LEN, span), 1)
            length = jnp.full((ROW_LEN, span), length_ref[captions[0]], jnp.int32)
            for slot in range(1, PER_ROW):
                length = jnp.where(spots >= slot * CAP_LEN, length_ref[captions[slot]], length)
            to_text = (
                slot_of(lax.broadcasted_iota(jnp.int32, (ROW_LEN, span), 0), ends)
                == spots // CAP_LEN
            ) & (spots % CAP_LEN < length)
            rows = pl.ds(pl.multiple_of(row * ROW_LEN, ROW_LEN), ROW_LEN)
            texts = pl.ds(row * PER_ROW, PER_ROW)
            for head in range(heads):
                text = [
                    caption_rows(text_ref, captions, part * inner + head * size, size)
                    for part in range(3)
                ]
                image = [
                    image_ref[rows, part * inner + head * size : part * inner + (head + 1) * size]
                    for part in range(3)
                ]
                lanes = slice(head * size, (head + 1) * size)
                shares = softmax_block(product_nt(text[0], image[1]) * scaling, to_image)
                text_shares[row, head] = shares
                text_out[texts, :, lanes] = (
                    product(shares, image[2]).astype(BF).reshape(PER_ROW, CAP_LEN, size)
                )
                shares = softmax_block(product_nt(image[0], text[1]) * scaling, to_text)
                image_shares[row, head] = shares
                image_out[rows, lanes] = product(shares, text[2]).astype(BF)
        return carry

    lax.fori_loop(0, rows_total // per_step, step, 0)


def co_backward_rows(bench, heads, rows_total):
    text_ref, image_ref = bench.co_t, bench.co_i
    inner = image_ref.shape[1] // 3
    size = inner // heads
    scaling = size ** (-0.5)
    span = PER_ROW * CAP_LEN
    per_step = 2
    order_ref = bench.order
    text_shares, image_shares = bench.cshare_t, bench.cshare_i
    text_grad, image_grad = bench.cg_t, bench.cg_i
    text_out, image_out = bench.rgrad_t, bench.grad_i

    def step(index, carry):
        for member in range(per_step):
            row = index * per_step + member
            captions = [order_ref[row * PER_ROW + slot] for slot in range(PER_ROW)]
            rows = pl.ds(pl.multiple_of(row * ROW_LEN, ROW_LEN), ROW_LEN)
            texts = pl.ds(row * PER_ROW, PER_ROW)
            for head in range(heads):
                text = [
                    caption_rows(text_ref, captions, part * inner + head * size, size)
                    for part in range(3)
                ]
                image = [
                    image_ref[rows, part * inner + head * size : part * inner + (head + 1) * size]
                    for part in range(3)
                ]
                text_q, image_k, image_v = attend_back(
                    text_shares[row, head], scaling, text[0], image[1], image[2],
                    caption_rows(text_grad, captions, head * size, size),
                )
                image_q, text_k, text_v = attend_back(
                    image_shares[row, head], scaling, image[0], text[1], text[2],
                    image_grad[rows, head * size : (head + 1) * size],
                )
                for part, grad in enumerate((text_q, text_k, text_v)):
                    at = part * inner + head * size
                    text_out[texts, :, at : at + size] = grad.reshape(PER_ROW, CAP_LEN, size)
                for part, grad in enumerate((image_q, image_k, image_v)):
                    at = part * inner + head * size
                    image_out[rows, at : at + size] = grad
        return carry

    lax.fori_loop(0, rows_total // per_step, step, 0)


def in_caption_order(bench, source, target):
    for caption in range(source.shape[0]):
        rows = slice(caption * CAP_LEN, (caption + 1) * CAP_LEN)
        target[rows, :] = source[bench.inverse[caption]]


def self_mask_text(length_ref, block):
    shape = (2 * CAP_LEN, 2 * CAP_LEN)
    queries = lax.broadcasted_iota(jnp.int32, shape, 0)
    spots = lax.broadcasted_iota(jnp.int32, shape, 1)
    length = jnp.where(
        spots >= CAP_LEN, length_ref[block * 2 + 1] + CAP_LEN, length_ref[block * 2]
    )
    return (queries // CAP_LEN == spots // CAP_LEN) & (spots < length)


def self_mask_image(region_ref, row):
    ends = row_ends(region_ref, row)
    shape = (ROW_LEN, ROW_LEN)
    return slot_of(lax.broadcasted_iota(jnp.int32, shape, 0), ends) == slot_of(
        lax.broadcasted_iota(jnp.int32, shape, 1), ends
    )


def shape_of(shape, dtype=BF):
    return jax.ShapeDtypeStruct(shape, dtype)


def cost(flops, moved, exps):
    return pl.CostEstimate(flops=int(flops), bytes_accessed=int(moved), transcendentals=int(exps))


MESH = pl.DeviceIdType.MESH
BIG_LIMIT = 60 * 1024 * 1024


class Bench:
    def __init__(self, refs, fetched, flushed, counts):
        self.refs = refs
        self.fetches = {}
        self.flushes = []
        self.flush_index = {name: i for i, name in enumerate(flushed)}
        self.copies = 0
        for index, name in enumerate(fetched):
            copy = pltpu.make_async_copy(
                refs["src " + name], refs[name], refs["fetch_sems"].at[index]
            )
            copy.start()
            self.fetches[name] = copy

    def __getattr__(self, name):
        fetches = self.__dict__["fetches"]
        if name in fetches:
            fetches.pop(name).wait()
        return self.__dict__["refs"][name]

    def flush(self, *names):
        for name in names:
            copy = pltpu.make_async_copy(
                self.refs[name],
                self.refs["dst " + name],
                self.refs["flush_sems"].at[self.flush_index.pop(name)],
            )
            copy.start()
            self.flushes.append(copy)

    def remote(self, source, target, peer):
        index = self.copies
        assert index < self.refs["send_sems"].shape[0]
        self.copies += 1
        return pltpu.make_async_remote_copy(
            src_ref=source,
            dst_ref=target,
            send_sem=self.refs["send_sems"].at[index],
            recv_sem=self.refs["recv_sems"].at[index],
            device_id=peer,
            device_id_type=MESH,
        )

    def close(self):
        for name in list(self.flush_index):
            self.flush(name)
        for copy in self.flushes:
            copy.wait()


def exchange_kernel(body, name, collective, peers, inputs, outputs, scratch, copies, work):
    fetched = [key for key, (_, kind) in inputs.items() if kind == "hbm"]
    flushed = [key for key, (_, _, kind) in outputs.items() if kind == "hbm"]
    spaces = {"hbm": pl.ANY, "vmem": pltpu.VMEM, "smem": pltpu.SMEM}
    names = [("src " + key if kind == "hbm" else key) for key, (_, kind) in inputs.items()]
    names += [("dst " + key if kind == "hbm" else key) for key, (_, _, kind) in outputs.items()]
    shapes = []
    for key in fetched:
        names.append(key)
        shapes.append(pltpu.VMEM(inputs[key][0].shape, inputs[key][0].dtype))
    for key in flushed:
        names.append(key)
        shapes.append(pltpu.VMEM(outputs[key][0], outputs[key][1]))
    for key, (shape, dtype) in scratch.items():
        names.append(key)
        shapes.append(pltpu.VMEM(shape, dtype))
    for key, count in (
        ("fetch_sems", len(fetched)), ("flush_sems", len(flushed)),
        ("send_sems", copies), ("recv_sems", copies),
    ):
        names.append(key)
        shapes.append(pltpu.SemaphoreType.DMA((max(count, 1),)))

    def kernel(*refs):
        bench = Bench(dict(zip(names, refs)), fetched, flushed, copies)
        barrier = pltpu.get_barrier_semaphore()
        partners = peers()
        for partner in partners:
            pl.semaphore_signal(barrier, inc=1, device_id=partner, device_id_type=MESH)
        pl.semaphore_wait(barrier, len(partners))
        body(bench)
        bench.close()

    flops, moved, exps = work
    results = pl.pallas_call(
        kernel,
        in_specs=[pl.BlockSpec(memory_space=spaces[kind]) for _, kind in inputs.values()],
        out_specs=[pl.BlockSpec(memory_space=spaces[kind]) for _, _, kind in outputs.values()],
        out_shape=[shape_of(shape, dtype) for shape, dtype, _ in outputs.values()],
        scratch_shapes=shapes,
        compiler_params=pltpu.CompilerParams(
            collective_id=collective, has_side_effects=True, vmem_limit_bytes=BIG_LIMIT
        ),
        cost_estimate=cost(flops, moved, exps),
        name=name,
    )(*[array for array, _ in inputs.values()])
    return dict(zip(outputs, results))


def group_peers():
    spot = lax.axis_index("mp")
    core = lax.rem(spot, 2)
    chip = lax.div(spot, 2)
    return core, {"mp": spot + 1 - 2 * core}, {"mp": spot + 2 - 4 * chip}


class Gather:
    def __init__(self, bench, rows):
        self.bench = bench
        self.rows = rows
        self.core, self.core_peer, self.chip_peer = group_peers()
        self.other = 1 - self.core

    def place(self, half, core):
        step = self.rows & -self.rows
        return pl.ds(pl.multiple_of((2 * half + core) * self.rows, step), self.rows)

    def gather(self, full):
        own = full.at[self.place(0, self.core)]
        far = full.at[self.place(1, self.core)]
        self.across = self.bench.remote(own, far, self.chip_peer)
        self.near = self.bench.remote(own, own, self.core_peer)
        self.relay = self.bench.remote(far, far, self.core_peer)
        self.across.start()
        self.near.start()

    def arrive(self, half, project):
        if half == 0:
            project(0, self.core)
            self.near.wait_recv()
            project(0, self.other)
        else:
            self.across.wait_recv()
            self.relay.start()
            project(1, self.core)
            self.relay.wait_recv()
            project(1, self.other)

    def finish_gather(self):
        self.across.wait_send()
        self.near.wait_send()
        self.relay.wait_send()


class Stream(Gather):
    def __init__(self, bench, tag, rows):
        super().__init__(bench, rows)
        for key in ("give", "got", "send", "recv", "acc"):
            setattr(self, key, getattr(bench, tag + "_" + key))

    def open_sum(self):
        self.hand = [
            self.bench.remote(self.give.at[half], self.got.at[half], self.core_peer)
            for half in (0, 1)
        ]
        self.post = self.bench.remote(self.send, self.recv, self.chip_peer)

    def partial(self, half, output):
        self.give[half] = output(half, self.other).astype(BF)
        self.hand[half].start()
        self.acc[half] = output(half, self.core)
        if half == 1:
            self.hand[1].wait_recv()
            self.send[...] = (self.acc[1] + self.got[1].astype(F32)).astype(BF)
            self.post.start()

    def settle(self, gathered=True):
        self.hand[0].wait_recv()
        self.post.wait_recv()
        self.hand[0].wait_send()
        self.hand[1].wait_send()
        self.post.wait_send()
        if gathered:
            self.finish_gather()

    def piece(self, rows):
        return self.acc[0, rows] + self.got[0, rows].astype(F32) + self.recv[rows].astype(F32)


CHUNK = 32


def chunks(count, step, start):
    def once(index, carry):
        return step(pl.ds(pl.multiple_of(index * CHUNK, CHUNK), CHUNK), carry)

    return lax.fori_loop(0, count // CHUNK, once, start)


def folded(values):
    return jnp.sum(values.reshape(CHUNK // 8, 8, values.shape[-1]), axis=0)


def stream_scratch(tag, rows, width):
    return {
        tag + "_give": ((2, rows, width), BF),
        tag + "_got": ((2, rows, width), BF),
        tag + "_send": ((rows, width), BF),
        tag + "_recv": ((rows, width), BF),
        tag + "_acc": ((2, rows, width), F32),
    }


def at_offset(ref, offset, rows):
    return ref.at[pl.ds(pl.multiple_of(offset + rows.start, CHUNK), rows.size)]


def attend_many(parts_ref, share_ref, context_ref, base, first_block, blocks, heads, masker):
    inner = parts_ref.shape[1] // 3
    size = inner // heads
    scaling = size ** (-0.5)
    rows = [
        pl.ds(pl.multiple_of(base + block * ROW_LEN, CHUNK), ROW_LEN) for block in range(blocks)
    ]
    masks = [masker(first_block + block) for block in range(blocks)]
    scores = []
    for block in range(blocks):
        for head in range(heads):
            queries = parts_ref[rows[block], head * size : (head + 1) * size]
            keys = parts_ref[rows[block], inner + head * size : inner + (head + 1) * size]
            scores.append(jnp.where(masks[block], product_nt(queries, keys) * scaling, -1e9))
    scores = jnp.concatenate(scores, axis=0)
    exponent = jnp.exp(scores - jnp.max(scores, axis=-1, keepdims=True))
    shares = (exponent / jnp.sum(exponent, axis=-1, keepdims=True)).astype(BF)
    for block in range(blocks):
        contexts = []
        for head in range(heads):
            at = (block * heads + head) * ROW_LEN
            piece = shares[at : at + ROW_LEN]
            share_ref[first_block + block, head] = piece
            values = parts_ref[rows[block], 2 * inner + head * size : 2 * inner + (head + 1) * size]
            contexts.append(product(piece, values).astype(BF))
        context_ref[rows[block], :] = jnp.concatenate(contexts, axis=1)


def norm_chunk(values, gain, shift):
    centre = values - jnp.mean(values, axis=-1, keepdims=True)
    spread = jnp.mean(centre * centre, axis=-1, keepdims=True)
    return centre * lax.rsqrt(spread + epsilon) * gain + shift


def forward_kernel(ctx_t, ctx_i, text_in, image_in, weights, norms, text_g, image_g, lengths, regions,
                   text_local, image_local):
    (co_text_out, co_image_out, text_up, text_down, image_up, image_down,
     w_self_text, text_self_out, w_self_image, image_self_out) = weights
    n_t, d_t = text_in.shape
    n_i, d_i = image_in.shape
    ff_t, ff_i = text_up.shape[1], image_up.shape[1]
    in_t, in_i = text_self_out.shape[0], image_self_out.shape[0]
    inputs = {
        "lengths": (lengths, "smem"), "regions": (regions, "smem"),
        "gains_t": (norms[0], "vmem"), "shifts_t": (norms[1], "vmem"),
        "gains_i": (norms[2], "vmem"), "shifts_i": (norms[3], "vmem"),
        "ctx_i": (ctx_i, "hbm"), "w_co_i": (co_image_out, "hbm"),
        "ctx_t": (ctx_t, "hbm"), "w_co_t": (co_text_out, "hbm"),
        "x_i": (image_in, "hbm"), "x_t": (text_in, "hbm"),
        "up_i": (image_up, "hbm"), "down_i": (image_down, "hbm"),
        "up_t": (text_up, "hbm"), "down_t": (text_down, "hbm"),
        "qkv_i": (w_self_image, "hbm"), "so_i": (image_self_out, "hbm"),
        "qkv_t": (w_self_text, "hbm"), "so_t": (text_self_out, "hbm"),
        "g_i": (image_g, "hbm"), "g_t": (text_g, "hbm"),
    }
    outputs = {}
    scratch = {}
    for tag, n, d, ff, inner, heads in (
        ("t", n_t, d_t, ff_t, in_t, text_local), ("i", n_i, d_i, ff_i, in_i, image_local),
    ):
        outputs.update({
            "zero_" + tag: ((n, d), F32, "hbm"),
            "mid_" + tag: ((n, d), F32, "hbm"),
            "mlp_" + tag: ((4 * n, d), BF, "hbm"),
            "act_" + tag: ((4 * n, ff), BF, "hbm"),
            "slope_" + tag: ((4 * n, ff), BF, "hbm"),
            "self_" + tag: ((4 * n, d), BF, "hbm"),
            "parts_" + tag: ((4 * n, 3 * inner), BF, "hbm"),
            "share_" + tag: ((4 * n // ROW_LEN, heads, ROW_LEN, ROW_LEN), BF, "hbm"),
            "ctx2_" + tag: ((4 * n, inner), BF, "hbm"),
            "late_" + tag: ((n, d), F32, "hbm"),
            "result_" + tag: ((n, d), BF, "hbm"),
            "gain_" + tag: ((8, d), F32, "vmem"),
            "shift_" + tag: ((8, d), F32, "vmem"),
        })
        scratch.update(stream_scratch(tag, n, d))
        scratch["first_" + tag] = ((n, d), F32)

    def body(bench):
        streams = {tag: Stream(bench, tag, n) for tag, n in (("i", n_i), ("t", n_t))}
        get = lambda key, tag: getattr(bench, key + "_" + tag)

        for tag, stream in streams.items():
            context, weight = get("ctx", tag), get("w_co", tag)
            output = lambda half, core: product(context[stream.place(half, core)], weight[...])
            stream.open_sum()
            stream.partial(1, output)
            stream.partial(0, output)

        def settle(tag, stage, source, kept, resid, full):
            stream = streams[tag]
            stream.settle(gathered=stage > 0)
            gain = get("gains", tag)[stage : stage + 1]
            shift = get("shifts", tag)[stage : stage + 1]
            base = stream.core * stream.rows

            def step(rows, carry):
                values = source[rows].astype(F32) + stream.piece(rows)
                kept[rows] = values
                normed = norm_chunk(values, gain, shift)
                resid[rows] = normed
                at_offset(full, base, rows)[...] = normed.astype(BF)
                return carry

            chunks(stream.rows, step, 0)
            bench.flush({"zero": "zero_", "mid": "mid_"}["zero" if stage == 0 else "mid"] + tag)
            stream.gather(full)

        for tag in streams:
            settle(tag, 0, get("x", tag), get("zero", tag), get("first", tag), get("mlp", tag))

        def feeds(tag):
            stream = streams[tag]
            full, up, down = get("mlp", tag), get("up", tag), get("down", tag)
            act, slope = get("act", tag), get("slope", tag)

            def project(half, core):
                place = stream.place(half, core)
                pre = product(full[place], up[...])
                cube = GELU_A * (pre + GELU_B * pre * pre * pre)
                bent = jnp.tanh(cube)
                act[place] = (0.5 * pre * (1.0 + bent)).astype(BF)
                slope[place] = (
                    0.5 * (1.0 + bent)
                    + 0.5 * pre * (1.0 - bent * bent) * GELU_A * (1.0 + 3.0 * GELU_B * pre * pre)
                ).astype(BF)

            def output(half, core):
                return product(act[stream.place(half, core)], down[...])

            return project, output

        def layer(work):
            for half in (0, 1):
                for tag, stream in streams.items():
                    hooks = work[tag]
                    if half == 0:
                        stream.open_sum()
                    stream.arrive(half, hooks[0])
                    if len(hooks) > 2:
                        hooks[2](half)
                    stream.partial(half, hooks[1])

        layer({tag: feeds(tag) for tag in streams})
        for tag in streams:
            settle(tag, 1, get("first", tag), get("mid", tag), get("first", tag), get("self", tag))
            bench.flush("mlp_" + tag, "act_" + tag, "slope_" + tag)

        def attends(tag):
            stream = streams[tag]
            full, qkv, out = get("self", tag), get("qkv", tag), get("so", tag)
            parts, share, context = get("parts", tag), get("share", tag), get("ctx2", tag)

            def output(half, core):
                return product(context[stream.place(half, core)], out[...])

            if tag == "t":

                def project(half, core):
                    place = stream.place(half, core)
                    project_three(full[place], qkv, parts, place)
                    quad = 2 * half + core
                    attend_many(
                        parts, share, context, quad * n_t, quad * (n_t // ROW_LEN),
                        n_t // ROW_LEN, text_local,
                        functools.partial(self_mask_text, bench.lengths),
                    )

                return project, output

            def project_image(half, core):
                place = stream.place(half, core)
                project_three(full[place], qkv, parts, place)

            def middle(half):
                blocks = 2 * n_i // ROW_LEN
                attend_many(
                    parts, share, context, 2 * half * n_i, half * blocks, blocks, image_local,
                    functools.partial(self_mask_image, bench.regions),
                )

            return project_image, output, middle

        layer({tag: attends(tag) for tag in streams})
        for tag, stream in streams.items():
            stream.settle()
            bench.flush("self_" + tag, "parts_" + tag, "share_" + tag, "ctx2_" + tag)
            gain, shift = get("gains", tag)[2:3], get("shifts", tag)[2:3]
            second, result, late, grad = (
                get("first", tag), get("result", tag), get("late", tag), get("g", tag)
            )
            width = second.shape[1]

            def step(rows, carry):
                values = second[rows] + stream.piece(rows)
                back, normed, gains, shifts = norm_pull(values, gain, shift, grad[rows].astype(F32))
                result[rows] = normed.astype(BF)
                late[rows] = back
                return carry[0] + gains, carry[1] + shifts

            start = jnp.zeros((8, width), F32)
            gains, shifts = chunks(stream.rows, step, (start, start))
            get("gain", tag)[...] = gains
            get("shift", tag)[...] = shifts
            bench.flush("result_" + tag, "late_" + tag)

    return exchange_kernel(
        body, "forward_tail", 1, lambda: list(group_peers()[1:]), inputs, outputs, scratch, 32,
        (15e9, 40e6, 1e6),
    )


def norm_pull(values, gain, shift, gradient):
    centre = values - jnp.mean(values, axis=-1, keepdims=True)
    spread = jnp.mean(centre * centre, axis=-1, keepdims=True)
    inverse = lax.rsqrt(spread + epsilon)
    unit = centre * inverse
    scaled = gradient * gain
    back = inverse * (
        scaled
        - jnp.mean(scaled, axis=-1, keepdims=True)
        - unit * jnp.mean(scaled * unit, axis=-1, keepdims=True)
    )
    return back, unit * gain + shift, folded(gradient * unit), folded(gradient)


def attend_back_many(parts_ref, share_ref, grads, out_ref, base, first_block, blocks, heads):
    inner = parts_ref.shape[1] // 3
    size = inner // heads
    scaling = size ** (-0.5)
    rows = [
        pl.ds(pl.multiple_of(base + block * ROW_LEN, CHUNK), ROW_LEN) for block in range(blocks)
    ]
    context_grads = [grads(block) for block in range(blocks)]
    pairs = [(block, head) for block in range(blocks) for head in range(heads)]

    def piece(part, block, head):
        at = part * inner + head * size
        return parts_ref[rows[block], at : at + size]

    def grad_of(block, head):
        return context_grads[block][:, head * size : (head + 1) * size]

    narrow = [share_ref[first_block + block, head] for block, head in pairs]
    shares = jnp.concatenate(narrow, axis=0).astype(F32)
    share_grad = jnp.concatenate(
        [product_nt(grad_of(*pair), piece(2, *pair)) for pair in pairs], axis=0
    )
    total = jnp.sum(share_grad * shares, axis=-1, keepdims=True)
    score_grad = (shares * (share_grad - total) * scaling).astype(BF)
    for block in range(blocks):
        pieces = [[], [], []]
        for head in range(heads):
            index = block * heads + head
            scores = score_grad[index * ROW_LEN : (index + 1) * ROW_LEN]
            pieces[0].append(product(scores, piece(1, block, head)).astype(BF))
            pieces[1].append(product_tn(scores, piece(0, block, head)).astype(BF))
            pieces[2].append(product_tn(narrow[index], grad_of(block, head)).astype(BF))
        out_ref[rows[block], :] = jnp.concatenate(pieces[0] + pieces[1] + pieces[2], axis=1)


class Split:
    def __init__(self, group_count, rows, order):
        self.bits = group_count.bit_length() - 1
        ready = group_count == 1 << self.bits and (rows // group_count) % 32 == 0
        self.fast = ready and group_count > 1
        self.blocks = group_count if self.fast else 1
        self.part = rows // self.blocks
        self.order = order(self.bits) if self.fast else []

    def position(self, block):
        spot = 0
        for bit in self.order:
            spot = 2 * spot + ((block >> bit) & 1)
        return spot

    def shape(self, columns):
        return (self.blocks, self.part, columns)

    def spare(self, columns):
        return (max(self.blocks - 1, 1), self.part, columns)


def dp_peer(bit):
    place = lax.axis_index("dp")
    value = lax.rem(lax.div(place, 1 << bit), 2)
    return value, {"dp": place + (1 << bit) * (1 - 2 * value)}


def dp_peers(*splits):
    bits = sorted({bit for split in splits for bit in split.order})
    return [dp_peer(bit)[1] for bit in bits]


class GroupSum:
    def __init__(self, bench, split, stack, spare, first=0, last=None):
        self.bench, self.split, self.stack, self.spare = bench, split, stack, spare
        self.base = 0
        self.size = split.blocks
        self.at = 0
        self.left = list(split.order)[first:last]
        for bit in split.order[:first]:
            self.size //= 2
            self.base = self.base + dp_peer(bit)[0] * self.size

    def start(self):
        if not self.left:
            return
        bit = self.left.pop(0)
        self.size //= 2
        value, peer = dp_peer(bit)
        given = self.base + (1 - value) * self.size
        self.base = self.base + value * self.size
        self.copy = self.bench.remote(
            self.stack.at[pl.ds(given, self.size)],
            self.spare.at[pl.ds(self.at, self.size)],
            peer,
        )
        self.copy.start()
        self.pending = True

    def advance(self):
        if not getattr(self, "pending", False):
            return
        self.copy.wait_recv()
        self.copy.wait_send()
        self.pending = False

        def add(index, carry):
            mine = self.base + index
            self.stack[mine] = (
                self.stack[mine].astype(F32) + self.spare[self.at + index].astype(F32)
            ).astype(BF)
            return carry

        lax.fori_loop(0, self.size, add, 0)
        self.at += self.size
        self.start()

    def drain(self):
        while getattr(self, "pending", False):
            self.advance()

    def finish(self, out):
        self.drain()
        out[...] = self.stack[self.base]


def weight_grad(split, stack, column, left, right):
    rows, width = left.shape[1], right.shape[1]
    tile = rows // 2
    for start in (0, tile):
        value = product_tn(left[:, start : start + tile], right[...]).astype(BF)
        if split.blocks == 1:
            stack[0, start : start + tile, column : column + width] = value
            continue
        for index in range(tile // split.part):
            spot = split.position(start // split.part + index)
            stack[spot, :, column : column + width] = value[
                index * split.part : (index + 1) * split.part
            ]


def project_three(rows, weights, target, place):
    width = weights.shape[2]
    for part in range(3):
        target[place, part * width : (part + 1) * width] = product(rows, weights[part]).astype(BF)


def back_three(grads, place, weights):
    width = weights.shape[2]
    return (
        product_nt(grads[place, :width], weights[0])
        + product_nt(grads[place, width : 2 * width], weights[1])
        + product_nt(grads[place, 2 * width :], weights[2])
    )


def run_layer(streams, work):
    for half in (0, 1):
        for tag, stream in streams.items():
            hooks = work[tag]
            if half == 0:
                stream.open_sum()
            stream.arrive(half, hooks[0])
            if len(hooks) > 2:
                hooks[2](half)
            stream.partial(half, hooks[1])


def spread(stream, source, full):
    base = stream.core * stream.rows

    def step(rows, carry):
        at_offset(full, base, rows)[...] = source[rows].astype(BF)
        return carry

    chunks(stream.rows, step, 0)
    stream.gather(full)


def settle_back(stream, resid, values, gain, target, gain_out, shift_out, full=None):
    base = stream.core * stream.rows

    def step(rows, carry):
        gradient = resid[rows] + stream.piece(rows)
        back, _, gains, shifts = norm_pull(values[rows], gain, 0.0, gradient)
        target[rows] = back
        if full is not None:
            at_offset(full, base, rows)[...] = back.astype(BF)
        return carry[0] + gains, carry[1] + shifts

    start = jnp.zeros((8, resid.shape[1]), F32)
    gains, shifts = chunks(stream.rows, step, (start, start))
    gain_out[...] = gains
    shift_out[...] = shifts


def self_back_kernel(late, mid, tokens, parts, share, context, qkv, out, gains, splits):
    inputs, outputs, scratch = {}, {}, {}
    for index, tag in ((1, "i"), (0, "t")):
        n, d = late[index].shape
        width = parts[index].shape[1]
        inputs.update({
            "gains_" + tag: (gains[index], "vmem"),
            "late_" + tag: (late[index], "hbm"),
            "so_" + tag: (out[index], "hbm"),
            "parts_" + tag: (parts[index], "hbm"),
            "share_" + tag: (share[index], "hbm"),
            "qkv_" + tag: (qkv[index], "hbm"),
            "self_" + tag: (tokens[index], "hbm"),
            "ctx2_" + tag: (context[index], "hbm"),
            "mid_" + tag: (mid[index], "hbm"),
        })
        outputs.update({
            "back_" + tag: ((n, d), F32, "hbm"),
            "stack_" + tag: (splits[index].shape(width + width // 3), BF, "hbm"),
            "gain_" + tag: ((8, d), F32, "vmem"),
            "shift_" + tag: ((8, d), F32, "vmem"),
        })
        scratch.update(stream_scratch(tag, n, d))
        scratch["full_" + tag] = ((4 * n, d), BF)
        scratch["grad_" + tag] = ((4 * n, width), BF)
    n_t, n_i = late[0].shape[0], late[1].shape[0]
    scratch["cg_i"] = ((4 * n_i, parts[1].shape[1] // 3), BF)
    heads = {"t": share[0].shape[1], "i": share[1].shape[1]}

    def body(bench):
        streams = {tag: Stream(bench, tag, n) for tag, n in (("i", n_i), ("t", n_t))}
        get = lambda key, tag: getattr(bench, key + "_" + tag)
        for tag, stream in streams.items():
            spread(stream, get("late", tag), get("full", tag))

        def hooks(tag):
            stream = streams[tag]
            full, out_w, qkv_w = get("full", tag), get("so", tag), get("qkv", tag)
            parts_ref, share_ref, grad = get("parts", tag), get("share", tag), get("grad", tag)

            def output(half, core):
                return back_three(grad, stream.place(half, core), qkv_w)

            if tag == "t":

                def project(half, core):
                    context_grad = product_nt(full[stream.place(half, core)], out_w[...]).astype(BF)
                    quad = 2 * half + core
                    blocks = n_t // ROW_LEN
                    attend_back_many(
                        parts_ref, share_ref,
                        lambda block: context_grad[block * ROW_LEN : (block + 1) * ROW_LEN],
                        grad, quad * n_t, quad * blocks, blocks, heads[tag],
                    )

                return project, output
            context_grads = bench.cg_i

            def project_image(half, core):
                place = stream.place(half, core)
                context_grads[place] = product_nt(full[place], out_w[...]).astype(BF)

            def middle(half):
                blocks = 2 * n_i // ROW_LEN
                base = 2 * half * n_i
                attend_back_many(
                    parts_ref, share_ref,
                    lambda block: context_grads[
                        base + block * ROW_LEN : base + (block + 1) * ROW_LEN
                    ],
                    grad, base, half * blocks, blocks, heads[tag],
                )

            return project_image, output, middle

        run_layer(streams, {tag: hooks(tag) for tag in streams})
        for index, tag in ((1, "i"), (0, "t")):
            stack, grad = get("stack", tag), get("grad", tag)
            weight_grad(splits[index], stack, 0, get("self", tag), grad)
            weight_grad(splits[index], stack, grad.shape[1], get("full", tag), get("ctx2", tag))
            bench.flush("stack_" + tag)
            stream = streams[tag]
            stream.settle()
            settle_back(
                stream, get("late", tag), get("mid", tag), get("gains", tag)[1:2],
                get("back", tag), get("gain", tag), get("shift", tag),
            )
            bench.flush("back_" + tag)

    return exchange_kernel(
        body, "self_back", 2, lambda: list(group_peers()[1:]), inputs, outputs, scratch, 16,
        (12e9, 40e6, 1e6),
    )


def feed_back_kernel(mid_grad, zero, tokens, act, slope, up, down, context, co_out, gains, stacks,
                     splits):
    inputs, outputs, scratch = {}, {}, {}
    for index, tag in ((1, "i"), (0, "t")):
        n, d = mid_grad[index].shape
        ff = act[index].shape[1]
        inner = context[index].shape[1]
        split = splits[index]
        columns = stacks[index].shape[2]
        inputs.update({
            "gains_" + tag: (gains[index], "vmem"),
            "mg_" + tag: (mid_grad[index], "hbm"),
            "stack_" + tag: (stacks[index], "hbm"),
            "down_" + tag: (down[index], "hbm"),
            "slope_" + tag: (slope[index], "hbm"),
            "up_" + tag: (up[index], "hbm"),
            "mlp_" + tag: (tokens[index], "hbm"),
            "act_" + tag: (act[index], "hbm"),
            "zero_" + tag: (zero[index], "hbm"),
            "co_" + tag: (co_out[index], "hbm"),
            "ctx_" + tag: (context[index], "hbm"),
        })
        outputs.update({
            "back_" + tag: ((n, d), F32, "hbm"),
            "cg_" + tag: ((4 * n, inner), BF, "hbm"),
            "out_grad_" + tag: (split.shape(inner), BF, "hbm"),
            "gain_" + tag: ((8, d), F32, "vmem"),
            "shift_" + tag: ((8, d), F32, "vmem"),
            "self_sum_" + tag: ((split.part, columns), BF, "hbm"),
            "fstack_" + tag: (split.shape(2 * ff), BF, "hbm"),
        })
        scratch.update(stream_scratch(tag, n, d))
        scratch["spare_" + tag] = (split.spare(columns), BF)
        scratch["fspare_" + tag] = (split.spare(2 * ff), BF)
        scratch["full_" + tag] = ((4 * n, d), BF)
        scratch["full2_" + tag] = ((4 * n, d), BF)
        scratch["pre_" + tag] = ((4 * n, ff), BF)
    n_t, n_i = mid_grad[0].shape[0], mid_grad[1].shape[0]

    def body(bench):
        streams = {tag: Stream(bench, tag, n) for tag, n in (("i", n_i), ("t", n_t))}
        get = lambda key, tag: getattr(bench, key + "_" + tag)
        for tag, stream in streams.items():
            spread(stream, get("mg", tag), get("full", tag))
        self_sums = {
            tag: GroupSum(bench, splits[index], get("stack", tag), get("spare", tag))
            for index, tag in ((1, "i"), (0, "t"))
        }
        for total in self_sums.values():
            total.start()

        def hooks(tag):
            stream = streams[tag]
            full, up_w, down_w = get("full", tag), get("up", tag), get("down", tag)
            slope_ref, pre = get("slope", tag), get("pre", tag)

            def project(half, core):
                place = stream.place(half, core)
                grad = product_nt(full[place], down_w[...])
                pre[place] = (grad * slope_ref[place].astype(F32)).astype(BF)

            def output(half, core):
                return product_nt(pre[stream.place(half, core)], up_w[...])

            return project, output

        run_layer(streams, {tag: hooks(tag) for tag in streams})
        for total in self_sums.values():
            total.advance()
        feed_sums = {}
        for index, tag in ((1, "i"), (0, "t")):
            stack, pre = get("fstack", tag), get("pre", tag)
            weight_grad(splits[index], stack, 0, get("mlp", tag), pre)
            weight_grad(splits[index], stack, pre.shape[1], get("full", tag), get("act", tag))
            feed_sums[tag] = GroupSum(bench, splits[index], stack, get("fspare", tag), 0, 1)
            feed_sums[tag].start()
            stream = streams[tag]
            stream.settle()
            settle_back(
                stream, get("mg", tag), get("zero", tag), get("gains", tag)[0:1],
                get("back", tag), get("gain", tag), get("shift", tag), get("full2", tag),
            )
            bench.flush("back_" + tag)
            stream.gather(get("full2", tag))
        for total in self_sums.values():
            total.advance()
        for half in (0, 1):
            for tag, stream in streams.items():
                full, weight, target = get("full2", tag), get("co", tag), get("cg", tag)

                def project(half, core):
                    place = stream.place(half, core)
                    target[place] = product_nt(full[place], weight[...]).astype(BF)

                stream.arrive(half, project)
        for index, tag in ((1, "i"), (0, "t")):
            bench.flush("cg_" + tag)
            weight_grad(
                splits[index], get("out_grad", tag), 0, get("full2", tag), get("ctx", tag)
            )
            bench.flush("out_grad_" + tag)
            streams[tag].finish_gather()
        for tag in streams:
            self_sums[tag].finish(get("self_sum", tag))
            bench.flush("self_sum_" + tag)
        for tag in streams:
            feed_sums[tag].drain()
            bench.flush("fstack_" + tag)

    return exchange_kernel(
        body, "feed_back", 3, lambda: list(group_peers()[1:]) + dp_peers(*splits), inputs, outputs,
        scratch, 40, (12e9, 60e6, 1e6),
    )


def co_front_kernel(shards, weights, order, inverse, regions, lengths, heads):
    inputs = {
        "order": (order, "smem"), "inverse": (inverse, "smem"),
        "regions": (regions, "smem"), "lengths": (lengths, "smem"),
    }
    outputs, scratch = {}, {}
    for index, tag in ((0, "t"), (1, "i")):
        n, d = shards[index].shape
        width = weights[index].shape[2]
        inputs.update({"x_" + tag: (shards[index], "hbm"), "w_" + tag: (weights[index], "hbm")})
        outputs.update({
            "all_" + tag: ((4 * n, d), BF, "hbm"),
            "co_" + tag: ((4 * n, 3 * width), BF, "hbm"),
            "ctx_" + tag: ((4 * n, width), BF, "hbm"),
        })
    n_t, n_i = shards[0].shape[0], shards[1].shape[0]
    held, width = n_t // CAP_LEN, weights[0].shape[2]
    outputs["co_t"] = ((4 * held, CAP_LEN, 3 * width), BF, "hbm")
    rows = 4 * n_i // ROW_LEN
    span = PER_ROW * CAP_LEN
    outputs["cshare_t"] = ((rows, heads, span, ROW_LEN), BF, "hbm")
    outputs["cshare_i"] = ((rows, heads, ROW_LEN, span), BF, "hbm")
    scratch["rctx_t"] = ((4 * held, CAP_LEN, width), BF)

    def body(bench):
        streams = {tag: Gather(bench, n) for tag, n in (("t", n_t), ("i", n_i))}
        get = lambda key, tag: getattr(bench, key + "_" + tag)
        for tag, stream in streams.items():
            full = get("all", tag)
            full[stream.place(0, stream.core)] = get("x", tag)[...]
            stream.gather(full)
        for half in (0, 1):
            for tag, stream in streams.items():
                full, weight, target = get("all", tag), get("w", tag), get("co", tag)

                def project(half, core):
                    place = stream.place(half, core)
                    if tag == "i":
                        project_three(full[place], weight, target, place)
                        return
                    captions = pl.ds((2 * half + core) * held, held)
                    for part in range(3):
                        target[captions, :, part * width : (part + 1) * width] = (
                            product(full[place], weight[part])
                            .astype(BF)
                            .reshape(held, CAP_LEN, width)
                        )

                stream.arrive(half, project)
        for tag in streams:
            bench.flush("all_" + tag, "co_" + tag)
        co_forward_rows(bench, heads, rows)
        in_caption_order(bench, bench.rctx_t, bench.ctx_t)
        for stream in streams.values():
            stream.finish_gather()

    return exchange_kernel(
        body, "co_front", 5, lambda: list(group_peers()[1:]), inputs, outputs, scratch, 6,
        (4e9, 20e6, 1e6),
    )


class Total:
    def __init__(self, bench, held, landing, group_count):
        self.bench, self.held, self.landing = bench, held, landing
        self.peers = list(group_peers()[1:]) + [
            dp_peer(bit)[1] for bit in range(group_count.bit_length() - 1)
        ]
        self.step = 0
        self.start()

    def start(self):
        if self.step < len(self.peers):
            self.copy = self.bench.remote(
                self.held.at[self.step], self.landing.at[self.step], self.peers[self.step]
            )
            self.copy.start()

    def advance(self):
        if self.step < len(self.peers):
            self.copy.wait()
            self.held[self.step + 1] = self.held[self.step] + self.landing[self.step]
            self.step += 1
            self.start()

    def finish(self, out):
        while self.step < len(self.peers):
            self.advance()
        out[...] = self.held[self.step]


def co_back_kernel(zero_grad, context_grads, tokens, projected, shares, weights, out_grads,
                   feed_stacks, norms, order, inverse, splits, heads, group_count):
    inputs = {"order": (order, "smem"), "inverse": (inverse, "smem")}
    outputs, scratch = {}, {}
    steps = 2 + group_count.bit_length() - 1
    for index, tag in ((1, "i"), (0, "t")):
        n, d = zero_grad[index].shape
        width = projected[index].shape[-1]
        inner = out_grads[index].shape[2]
        split = splits[index]
        feeds = feed_stacks[index].shape[2]
        inputs.update({"norm%d_%s" % (k, tag): (v, "vmem") for k, v in enumerate(norms[index])})
        inputs.update({
            "co_" + tag: (projected[index], "hbm"),
            "cg_" + tag: (context_grads[index], "hbm"),
            "cshare_" + tag: (shares[index], "hbm"),
            "fstack_" + tag: (feed_stacks[index], "hbm"),
            "ostack_" + tag: (out_grads[index], "hbm"),
            "x_" + tag: (tokens[index], "hbm"),
            "w_" + tag: (weights[index], "hbm"),
            "zg_" + tag: (zero_grad[index], "hbm"),
        })
        outputs.update({
            "in_grad_" + tag: ((n, d), F32, "hbm"),
            "feed_sum_" + tag: ((split.part, feeds), BF, "hbm"),
            "out_sum_" + tag: ((split.part, inner), BF, "hbm"),
            "qkv_sum_" + tag: ((split.part, width), BF, "hbm"),
            "norm_" + tag: ((8, d), F32, "vmem"),
        })
        scratch.update(stream_scratch(tag, n, d))
        scratch["grad_" + tag] = ((4 * n, width), BF)
        scratch["stack_" + tag] = (split.shape(width), BF)
        scratch["spare_" + tag] = (split.spare(width), BF)
        scratch["fspare_" + tag] = (split.spare(feeds), BF)
        scratch["ospare_" + tag] = (split.spare(inner), BF)
        scratch["held_" + tag] = ((steps + 1, 8, d), F32)
        scratch["landing_" + tag] = ((steps, 8, d), F32)
    n_t, n_i = zero_grad[0].shape[0], zero_grad[1].shape[0]
    scratch["rgrad_t"] = (projected[0].shape, BF)

    def body(bench):
        streams = {tag: Stream(bench, tag, n) for tag, n in (("i", n_i), ("t", n_t))}
        get = lambda key, tag: getattr(bench, key + "_" + tag)
        totals, early, late = [], [], {}
        for index, tag in ((1, "i"), (0, "t")):
            held = get("held", tag)
            vectors = [
                jnp.sum(get("norm%d" % k, tag)[...], axis=0, keepdims=True) for k in range(6)
            ]
            held[0] = jnp.concatenate(vectors + [jnp.zeros_like(vectors[0])] * 2, axis=0)
            totals.append(Total(bench, held, get("landing", tag), group_count))
            early.append(
                GroupSum(bench, splits[index], get("fstack", tag), get("fspare", tag), 1)
            )
            early.append(GroupSum(bench, splits[index], get("ostack", tag), get("ospare", tag)))
        for total in early:
            total.start()
        co_backward_rows(bench, heads, 4 * n_i // ROW_LEN)
        in_caption_order(bench, bench.rgrad_t, bench.grad_t)
        for total in totals:
            total.advance()
        for index, tag in ((1, "i"), (0, "t")):
            stack = get("stack", tag)
            weight_grad(splits[index], stack, 0, get("x", tag), get("grad", tag))
            late[tag] = GroupSum(bench, splits[index], stack, get("spare", tag))
            late[tag].start()
            stream = streams[tag]
            grad, weight = get("grad", tag), get("w", tag)
            output = lambda half, core: back_three(grad, stream.place(half, core), weight)
            stream.open_sum()
            stream.partial(1, output)
            stream.partial(0, output)
            for total in totals + early:
                total.advance()
        for total in totals:
            total.advance()
        for tag, stream in streams.items():
            late[tag].advance()
            resid, target = get("zg", tag), get("in_grad", tag)
            stream.settle(gathered=False)

            def step(rows, carry):
                target[rows] = resid[rows] + stream.piece(rows)
                return carry

            chunks(stream.rows, step, 0)
            bench.flush("in_grad_" + tag)
            for total in totals:
                total.advance()
        for tag, total in zip(("i", "t"), totals):
            total.finish(get("norm", tag))
        for tag in ("i", "t"):
            late[tag].advance()
        for tag, total in zip(("feed_sum_i", "out_sum_i", "feed_sum_t", "out_sum_t"), early):
            total.finish(getattr(bench, tag))
            bench.flush(tag)
        for tag in ("t", "i"):
            late[tag].finish(get("qkv_sum", tag))
            bench.flush("qkv_sum_" + tag)

    return exchange_kernel(
        body, "co_back", 4,
        lambda: list(group_peers()[1:])
        + [dp_peer(bit)[1] for bit in range(group_count.bit_length() - 1)],
        inputs, outputs, scratch, 16 + 2 * steps + 20, (8e9, 50e6, 1e6),
    )


def finish_kernel(sums):
    flat = []
    shapes = []
    for qkv, out, own, feed, in_grad in sums:
        part = qkv.shape[0]
        inner = own.shape[1] // 4
        flat += [qkv, out, own, feed, in_grad]
        shapes += [
            shape_of((3, part, qkv.shape[1] // 3), F32),
            shape_of((out.shape[1], part), F32),
            shape_of((3, part, inner), F32),
            shape_of((inner, part), F32),
            shape_of((part, feed.shape[1] // 2), F32),
            shape_of((feed.shape[1] // 2, part), F32),
            shape_of(in_grad.shape, F32),
        ]

    def kernel(*refs):
        for stream in range(2):
            qkv, out, own, feed, in_grad = refs[5 * stream : 5 * stream + 5]
            results = refs[10 + 7 * stream : 17 + 7 * stream]
            width = qkv.shape[1] // 3
            inner = own.shape[1] // 4
            for part in range(3):
                results[0][part] = qkv[:, part * width : (part + 1) * width].astype(F32)
                results[2][part] = own[:, part * inner : (part + 1) * inner].astype(F32)
            results[1][...] = out[...].astype(F32).T
            results[3][...] = own[:, 3 * inner :].astype(F32).T
            ff = feed.shape[1] // 2
            results[4][...] = feed[:, :ff].astype(F32)
            results[5][...] = feed[:, ff:].astype(F32).T
            results[6][...] = in_grad[...]

    return pl.pallas_call(
        kernel,
        in_specs=[pl.BlockSpec(memory_space=pltpu.VMEM)] * len(flat),
        out_specs=[pl.BlockSpec(memory_space=pltpu.VMEM)] * len(shapes),
        out_shape=shapes,
        compiler_params=pltpu.CompilerParams(vmem_limit_bytes=32 * 1024 * 1024),
        name="finish",
    )(*flat)


def apart(grad):
    rows, columns = grad.shape
    return jnp.transpose(grad.reshape(rows, 3, columns // 3), (1, 0, 2))


def finish_plain(qkv, out, own, feed, in_grad):
    qkv, out, own, feed = [value.astype(F32) for value in (qkv, out, own, feed)]
    inner, ff = own.shape[1] // 4, feed.shape[1] // 2
    return (
        apart(qkv), out.T, apart(own[:, : 3 * inner]), own[:, 3 * inner :].T,
        feed[:, :ff], feed[:, ff:].T, in_grad,
    )


def per_device(
    text_in,
    image_in,
    caption_lengths,
    region_lengths,
    image_caption,
    co_text_qkv,
    co_image_qkv,
    co_text_out,
    co_image_out,
    text_up,
    text_down,
    image_up,
    image_down,
    text_self_qkv,
    text_self_out,
    image_self_qkv,
    image_self_out,
    text_gains,
    text_shifts,
    image_gains,
    image_shifts,
    text_grad_out,
    image_grad_out,
):
    captions = image_caption.shape[1]
    part_count = lax.axis_size("mp")
    group_count = lax.axis_size("dp")
    spot = lax.axis_index("mp")
    core = spot % 2
    chip = spot // 2
    co_local = CO_HEADS // part_count
    text_local = TEXT_HEADS // part_count
    image_local = IMAGE_HEADS // part_count

    half = captions // 2
    turned = chip == 1
    flip = lambda values: jnp.where(turned, jnp.roll(values, half), values)
    lengths = flip(caption_lengths)
    regions = flip(region_lengths.reshape(-1))
    order = flip(image_caption[0])
    order = jnp.where(turned, (order + half) % captions, order)

    labels = jnp.arange(captions, dtype=jnp.int32)
    inverse = jnp.sum(
        labels[None, :] * (order[None, :] == labels[:, None]).astype(jnp.int32), axis=1
    )

    front = co_front_kernel(
        (text_in, image_in), (co_text_qkv, co_image_qkv), order, inverse, regions, lengths,
        co_local,
    )
    text_ctx, image_ctx = front["ctx_t"], front["ctx_i"]
    ahead = forward_kernel(
        text_ctx, image_ctx, text_in, image_in,
        (co_text_out, co_image_out, text_up, text_down, image_up, image_down,
         text_self_qkv, text_self_out, image_self_qkv, image_self_out),
        (text_gains, text_shifts, image_gains, image_shifts),
        text_grad_out, image_grad_out, lengths, regions, text_local, image_local,
    )
    splits = (
        Split(group_count, text_in.shape[1], lambda bits: list(range(bits))),
        Split(group_count, image_in.shape[1], lambda bits: ([1, 0] + list(range(2, bits)))[:bits]),
    )
    gains = (text_gains, image_gains)
    first_back = self_back_kernel(
        (ahead["late_t"], ahead["late_i"]), (ahead["mid_t"], ahead["mid_i"]),
        (ahead["self_t"], ahead["self_i"]), (ahead["parts_t"], ahead["parts_i"]),
        (ahead["share_t"], ahead["share_i"]), (ahead["ctx2_t"], ahead["ctx2_i"]),
        (text_self_qkv, image_self_qkv), (text_self_out, image_self_out), gains, splits,
    )
    second_back = feed_back_kernel(
        (first_back["back_t"], first_back["back_i"]), (ahead["zero_t"], ahead["zero_i"]),
        (ahead["mlp_t"], ahead["mlp_i"]), (ahead["act_t"], ahead["act_i"]),
        (ahead["slope_t"], ahead["slope_i"]), (text_up, image_up), (text_down, image_down),
        (text_ctx, image_ctx), (co_text_out, co_image_out), gains,
        (first_back["stack_t"], first_back["stack_i"]), splits,
    )

    norms = [
        [stage[key + tag] for key in ("gain_", "shift_") for stage in (second_back, first_back, ahead)]
        for tag in "ti"
    ]
    last_back = co_back_kernel(
        (second_back["back_t"], second_back["back_i"]),
        (second_back["cg_t"].reshape(captions, CAP_LEN, -1), second_back["cg_i"]),
        (front["all_t"], front["all_i"]), (front["co_t"], front["co_i"]),
        (front["cshare_t"], front["cshare_i"]), (co_text_qkv, co_image_qkv),
        (second_back["out_grad_t"], second_back["out_grad_i"]),
        (second_back["fstack_t"], second_back["fstack_i"]),
        norms, order, inverse, splits, co_local, group_count,
    )

    def over_groups(summed, split):
        if not split.fast:
            summed = lax.psum_scatter(summed, "dp", scatter_dimension=0, tiled=True)
        return summed

    sums = [
        [
            over_groups(last_back["qkv_sum_" + tag], split),
            over_groups(last_back["out_sum_" + tag], split),
            over_groups(second_back["self_sum_" + tag], split),
            over_groups(last_back["feed_sum_" + tag], split),
            last_back["in_grad_" + tag],
        ]
        for tag, split in zip("ti", splits)
    ]
    if all(split.fast for split in splits):
        finished = finish_kernel(sums)
        text_grads, image_grads = finished[:7], finished[7:]
    else:
        text_grads, image_grads = [finish_plain(*stream) for stream in sums]

    def norm_part(total):
        columns = total.shape[1] // (group_count * part_count)
        place = lax.axis_index("dp") * part_count + spot
        mine = lax.dynamic_slice_in_dim(total, place * columns, columns, axis=1)
        return mine[:3], mine[3:6]

    text_gain_grad, text_shift_grad = norm_part(last_back["norm_t"])
    image_gain_grad, image_shift_grad = norm_part(last_back["norm_i"])
    return (
        ahead["result_t"],
        ahead["result_i"],
        text_grads[6],
        image_grads[6],
        text_grads[0],
        image_grads[0],
        text_grads[1],
        image_grads[1],
        text_grads[4],
        text_grads[5],
        image_grads[4],
        image_grads[5],
        text_grads[2],
        text_grads[3],
        image_grads[2],
        image_grads[3],
        text_gain_grad,
        text_shift_grad,
        image_gain_grad,
        image_shift_grad,
    )


def solution(mesh):
    tokens = P(("dp", "mp"), None)
    stack_in = P(None, None, "mp")
    rows_in = P("mp", None)
    columns_in = P(None, "mp")
    in_specs = (
        tokens, tokens, P("dp"), P("dp", None), P("dp", None),
        stack_in, stack_in, rows_in, rows_in,
        columns_in, rows_in, columns_in, rows_in,
        stack_in, rows_in, stack_in, rows_in,
        P(), P(), P(), P(),
        tokens, tokens,
    )
    stack_out = P(None, "dp", "mp")
    rows_out = P("mp", "dp")
    columns_out = P("dp", "mp")
    norm_out = P(None, ("dp", "mp"))
    out_specs = (
        tokens, tokens, tokens, tokens,
        stack_out, stack_out, rows_out, rows_out,
        columns_out, rows_out, columns_out, rows_out,
        stack_out, rows_out, stack_out, rows_out,
        norm_out, norm_out, norm_out, norm_out,
    )
    return jax.shard_map(
        per_device, mesh=mesh, in_specs=in_specs, out_specs=out_specs, check_vma=False
    )
```

```python
import functools

import jax
import jax.numpy as jnp
from jax import lax
from jax.experimental import pallas as pl
from jax.experimental.pallas import tpu as pltpu
from jax.sharding import PartitionSpec as P

CO_HEADS = 8
TEXT_HEADS = 12
IMAGE_HEADS = 8
CAP_LEN = 64
ROW_LEN = 128
PER_ROW = 4

epsilon = 1e-05
BF = jnp.bfloat16
F32 = jnp.float32
VMEM_LIMIT = 48 * 1024 * 1024


def product(former, latter):
    return jnp.dot(former, latter, preferred_element_type=F32)


def product_tn(former, latter):
    return lax.dot_general(former, latter, (((0,), (0,)), ((), ())), preferred_element_type=F32)


def product_nt(former, latter):
    return lax.dot_general(former, latter, (((1,), (1,)), ((), ())), preferred_element_type=F32)


GELU_A = 0.7978845608028654
GELU_B = 0.044715


def softmax_block(scores, mask):
    scores = jnp.where(mask, scores, -1000000000.0)
    exponent = jnp.exp(scores - jnp.max(scores, axis=-1, keepdims=True))
    return (exponent / jnp.sum(exponent, axis=-1, keepdims=True)).astype(BF)


def attend_back(shares, scaling, queries, keys, values, context_grad):
    wide = shares.astype(F32)
    share_grad = product_nt(context_grad, values)
    inner = jnp.sum(share_grad * wide, axis=-1, keepdims=True)
    score_grad = (wide * (share_grad - inner) * scaling).astype(BF)
    return (
        product(score_grad, keys).astype(BF),
        product_tn(score_grad, queries).astype(BF),
        product_tn(shares, context_grad).astype(BF),
    )


class Layout:
    def __init__(self, bench):
        self.bench = bench
        self.chip = lax.div(lax.axis_index("mp"), 2)

    def turn(self, index, count):
        return lax.rem(index + self.chip * (count // 2), count)

    def length(self, caption):
        lengths = self.bench.lengths
        return lengths[self.turn(caption, lengths.shape[0])]

    def caption_of(self, image):
        order = self.bench.order
        count = order.shape[0]
        return self.turn(order[self.turn(image, count)], count)

    def image_of(self, caption):
        inverse = self.bench.inverse
        count = inverse.shape[0]
        return self.turn(inverse[self.turn(caption, count)], count)

    def ends(self, row):
        regions = self.bench.regions
        place = self.turn(row, regions.shape[1])
        ends = [regions[0, place]]
        for slot in range(1, PER_ROW):
            ends.append(ends[-1] + regions[slot, place])
        return ends


def slot_of(places, ends):
    slot = (places >= ends[0]).astype(jnp.int32)
    for end in ends[1:]:
        slot = slot + (places >= end).astype(jnp.int32)
    return slot


def caption_rows(ref, captions, start, width):
    return jnp.concatenate(
        [ref[caption, :, start : start + width] for caption in captions], axis=0
    )


def co_forward_rows(bench, heads, rows_total):
    text_ref, image_ref = bench.co_t, bench.co_i
    inner = image_ref.shape[1] // 3
    size = inner // heads
    scaling = size ** (-0.5)
    span = PER_ROW * CAP_LEN
    per_step = 2
    layout = Layout(bench)
    text_shares, image_shares = bench.cshare_t, bench.cshare_i
    text_out, image_out = bench.rctx_t, bench.ctx_i

    def step(index, carry):
        for member in range(per_step):
            row = index * per_step + member
            captions = [layout.caption_of(row * PER_ROW + slot) for slot in range(PER_ROW)]
            ends = layout.ends(row)
            lengths = [layout.length(caption) for caption in captions]
            token_slot = lax.broadcasted_iota(jnp.int32, (span, ROW_LEN), 0) // CAP_LEN
            to_image = token_slot == slot_of(
                lax.broadcasted_iota(jnp.int32, (span, ROW_LEN), 1), ends
            )
            spots = lax.broadcasted_iota(jnp.int32, (ROW_LEN, span), 1)
            length = jnp.full((ROW_LEN, span), lengths[0], jnp.int32)
            for slot in range(1, PER_ROW):
                length = jnp.where(spots >= slot * CAP_LEN, lengths[slot], length)
            to_text = (
                slot_of(lax.broadcasted_iota(jnp.int32, (ROW_LEN, span), 0), ends)
                == spots // CAP_LEN
            ) & (spots % CAP_LEN < length)
            rows = pl.ds(pl.multiple_of(row * ROW_LEN, ROW_LEN), ROW_LEN)
            texts = pl.ds(row * PER_ROW, PER_ROW)
            for head in range(heads):
                text = [
                    caption_rows(text_ref, captions, part * inner + head * size, size)
                    for part in range(3)
                ]
                image = [
                    image_ref[rows, part * inner + head * size : part * inner + (head + 1) * size]
                    for part in range(3)
                ]
                lanes = slice(head * size, (head + 1) * size)
                shares = softmax_block(product_nt(text[0], image[1]) * scaling, to_image)
                text_shares[row, head] = shares
                text_out[texts, :, lanes] = (
                    product(shares, image[2]).astype(BF).reshape(PER_ROW, CAP_LEN, size)
                )
                shares = softmax_block(product_nt(image[0], text[1]) * scaling, to_text)
                image_shares[row, head] = shares
                image_out[rows, lanes] = product(shares, text[2]).astype(BF)
        return carry

    lax.fori_loop(0, rows_total // per_step, step, 0)


def co_backward_rows(bench, heads, first_row, last_row):
    text_ref, image_ref = bench.co_t, bench.co_i
    inner = image_ref.shape[1] // 3
    size = inner // heads
    scaling = size ** (-0.5)
    span = PER_ROW * CAP_LEN
    per_step = 2
    layout = Layout(bench)
    text_shares, image_shares = bench.cshare_t, bench.cshare_i
    text_grad, image_grad = bench.cg_t, bench.cg_i
    text_out, image_out = bench.rgrad_t, bench.grad_i

    def step(index, carry):
        for member in range(per_step):
            row = index * per_step + member
            captions = [layout.caption_of(row * PER_ROW + slot) for slot in range(PER_ROW)]
            rows = pl.ds(pl.multiple_of(row * ROW_LEN, ROW_LEN), ROW_LEN)
            texts = pl.ds(row * PER_ROW, PER_ROW)
            for head in range(heads):
                text = [
                    caption_rows(text_ref, captions, part * inner + head * size, size)
                    for part in range(3)
                ]
                image = [
                    image_ref[rows, part * inner + head * size : part * inner + (head + 1) * size]
                    for part in range(3)
                ]
                text_q, image_k, image_v = attend_back(
                    text_shares[row, head], scaling, text[0], image[1], image[2],
                    caption_rows(text_grad, captions, head * size, size),
                )
                image_q, text_k, text_v = attend_back(
                    image_shares[row, head], scaling, image[0], text[1], text[2],
                    image_grad[rows, head * size : (head + 1) * size],
                )
                for part, grad in enumerate((text_q, text_k, text_v)):
                    at = part * inner + head * size
                    text_out[texts, :, at : at + size] = grad.reshape(PER_ROW, CAP_LEN, size)
                for part, grad in enumerate((image_q, image_k, image_v)):
                    at = part * inner + head * size
                    image_out[rows, at : at + size] = grad
        return carry

    lax.fori_loop(first_row // per_step, last_row // per_step, step, 0)


def in_caption_order(bench, source, target):
    layout = Layout(bench)
    for caption in range(source.shape[0]):
        rows = slice(caption * CAP_LEN, (caption + 1) * CAP_LEN)
        target[rows, :] = source[layout.image_of(caption)]


def self_mask_text(layout, block):
    shape = (2 * CAP_LEN, 2 * CAP_LEN)
    queries = lax.broadcasted_iota(jnp.int32, shape, 0)
    spots = lax.broadcasted_iota(jnp.int32, shape, 1)
    length = jnp.where(
        spots >= CAP_LEN, layout.length(block * 2 + 1) + CAP_LEN, layout.length(block * 2)
    )
    return (queries // CAP_LEN == spots // CAP_LEN) & (spots < length)


def self_mask_image(layout, row):
    ends = layout.ends(row)
    shape = (ROW_LEN, ROW_LEN)
    return slot_of(lax.broadcasted_iota(jnp.int32, shape, 0), ends) == slot_of(
        lax.broadcasted_iota(jnp.int32, shape, 1), ends
    )


def shape_of(shape, dtype=BF):
    return jax.ShapeDtypeStruct(shape, dtype)


def cost(flops, moved, exps):
    return pl.CostEstimate(flops=int(flops), bytes_accessed=int(moved), transcendentals=int(exps))


MESH = pl.DeviceIdType.MESH
BIG_LIMIT = 60 * 1024 * 1024


class Bench:
    def __init__(self, refs, fetched, flushed, counts):
        self.refs = refs
        self.fetches = {}
        self.flushes = []
        self.flush_index = {name: i for i, name in enumerate(flushed)}
        self.copies = 0
        for index, name in enumerate(fetched):
            copy = pltpu.make_async_copy(
                refs["src " + name], refs[name], refs["fetch_sems"].at[index]
            )
            copy.start()
            self.fetches[name] = copy

    def __getattr__(self, name):
        fetches = self.__dict__["fetches"]
        if name in fetches:
            fetches.pop(name).wait()
        return self.__dict__["refs"][name]

    def flush(self, *names):
        for name in names:
            copy = pltpu.make_async_copy(
                self.refs[name],
                self.refs["dst " + name],
                self.refs["flush_sems"].at[self.flush_index.pop(name)],
            )
            copy.start()
            self.flushes.append(copy)

    def remote(self, source, target, peer):
        index = self.copies
        assert index < self.refs["send_sems"].shape[0]
        self.copies += 1
        return pltpu.make_async_remote_copy(
            src_ref=source,
            dst_ref=target,
            send_sem=self.refs["send_sems"].at[index],
            recv_sem=self.refs["recv_sems"].at[index],
            device_id=peer,
            device_id_type=MESH,
        )

    def close(self):
        for name in list(self.flush_index):
            self.flush(name)
        for copy in self.flushes:
            copy.wait()


def exchange_kernel(body, name, collective, peers, inputs, outputs, scratch, copies, work):
    fetched = [key for key, (_, kind) in inputs.items() if kind == "hbm"]
    flushed = [key for key, (_, _, kind) in outputs.items() if kind == "hbm"]
    spaces = {"hbm": pl.ANY, "vmem": pltpu.VMEM, "smem": pltpu.SMEM}
    names = [("src " + key if kind == "hbm" else key) for key, (_, kind) in inputs.items()]
    names += [("dst " + key if kind == "hbm" else key) for key, (_, _, kind) in outputs.items()]
    shapes = []
    for key in fetched:
        names.append(key)
        shapes.append(pltpu.VMEM(inputs[key][0].shape, inputs[key][0].dtype))
    for key in flushed:
        names.append(key)
        shapes.append(pltpu.VMEM(outputs[key][0], outputs[key][1]))
    for key, (shape, dtype) in scratch.items():
        names.append(key)
        shapes.append(pltpu.VMEM(shape, dtype))
    for key, count in (
        ("fetch_sems", len(fetched)), ("flush_sems", len(flushed)),
        ("send_sems", copies), ("recv_sems", copies),
    ):
        names.append(key)
        shapes.append(pltpu.SemaphoreType.DMA((max(count, 1),)))

    def kernel(*refs):
        bench = Bench(dict(zip(names, refs)), fetched, flushed, copies)
        barrier = pltpu.get_barrier_semaphore()
        partners = peers()
        for partner in partners:
            pl.semaphore_signal(barrier, inc=1, device_id=partner, device_id_type=MESH)
        pl.semaphore_wait(barrier, len(partners))
        body(bench)
        bench.close()

    flops, moved, exps = work
    results = pl.pallas_call(
        kernel,
        in_specs=[pl.BlockSpec(memory_space=spaces[kind]) for _, kind in inputs.values()],
        out_specs=[pl.BlockSpec(memory_space=spaces[kind]) for _, _, kind in outputs.values()],
        out_shape=[shape_of(shape, dtype) for shape, dtype, _ in outputs.values()],
        scratch_shapes=shapes,
        compiler_params=pltpu.CompilerParams(
            collective_id=collective, has_side_effects=True, vmem_limit_bytes=BIG_LIMIT
        ),
        cost_estimate=cost(flops, moved, exps),
        name=name,
    )(*[array for array, _ in inputs.values()])
    return dict(zip(outputs, results))


def group_peers():
    spot = lax.axis_index("mp")
    core = lax.rem(spot, 2)
    chip = lax.div(spot, 2)
    return core, {"mp": spot + 1 - 2 * core}, {"mp": spot + 2 - 4 * chip}


class Gather:
    def __init__(self, bench, rows):
        self.bench = bench
        self.rows = rows
        self.core, self.core_peer, self.chip_peer = group_peers()
        self.other = 1 - self.core

    def place(self, half, core):
        step = self.rows & -self.rows
        return pl.ds(pl.multiple_of((2 * half + core) * self.rows, step), self.rows)

    def gather(self, full):
        own = full.at[self.place(0, self.core)]
        far = full.at[self.place(1, self.core)]
        self.across = self.bench.remote(own, far, self.chip_peer)
        self.near = self.bench.remote(own, own, self.core_peer)
        self.relay = self.bench.remote(far, far, self.core_peer)
        self.across.start()
        self.near.start()

    def arrive(self, half, project):
        if half == 0:
            project(0, self.core)
            self.near.wait_recv()
            project(0, self.other)
        else:
            self.across.wait_recv()
            self.relay.start()
            project(1, self.core)
            self.relay.wait_recv()
            project(1, self.other)

    def finish_gather(self):
        self.across.wait_send()
        self.near.wait_send()
        self.relay.wait_send()


class Stream(Gather):
    def __init__(self, bench, tag, rows):
        super().__init__(bench, rows)
        for key in ("give", "got", "send", "recv", "acc"):
            setattr(self, key, getattr(bench, tag + "_" + key))

    def open_sum(self):
        self.hand = [
            self.bench.remote(self.give.at[half], self.got.at[half], self.core_peer)
            for half in (0, 1)
        ]
        self.post = self.bench.remote(self.send, self.recv, self.chip_peer)

    def partial(self, half, output):
        self.give[half] = output(half, self.other).astype(BF)
        self.hand[half].start()
        self.acc[half] = output(half, self.core)
        if half == 1:
            self.hand[1].wait_recv()
            self.send[...] = (self.acc[1] + self.got[1].astype(F32)).astype(BF)
            self.post.start()

    def settle(self, gathered=True):
        self.hand[0].wait_recv()
        self.post.wait_recv()
        self.hand[0].wait_send()
        self.hand[1].wait_send()
        self.post.wait_send()
        if gathered:
            self.finish_gather()

    def piece(self, rows):
        return self.acc[0, rows] + self.got[0, rows].astype(F32) + self.recv[rows].astype(F32)


class Near(Gather):
    def __init__(self, bench, tag, rows):
        super().__init__(bench, rows)
        for key in ("give", "got", "acc"):
            setattr(self, key, getattr(bench, tag + "_" + key))

    def gather(self, full):
        own = full.at[self.place(0, self.core)]
        self.near = self.bench.remote(own, own, self.core_peer)
        self.near.start()

    def open_sum(self):
        self.hand = self.bench.remote(self.give.at[0], self.got.at[0], self.core_peer)

    def partial(self, half, output):
        self.give[0] = output(0, self.other).astype(BF)
        self.hand.start()
        self.acc[0] = output(0, self.core)

    def settle(self):
        self.hand.wait_recv()
        self.hand.wait_send()
        self.near.wait_send()

    def piece(self, rows):
        return self.acc[0, rows] + self.got[0, rows].astype(F32)


class Weights:
    def __init__(self, bench, own, other, bits):
        self.bench, self.other, self.left = bench, other, list(bits)
        self.names = sorted(bits, reverse=True)
        self.lead = len(own.shape) - 2 - len(self.names)
        self.free = []
        self.copy = bench.remote(
            own.at[self.held()], other.at[self.held()], group_peers()[2]
        )
        self.copy.start()
        self.pending = True

    def held(self):
        kept = [slice(None) if bit in self.free else dp_peer(bit)[0] for bit in self.names]
        return (slice(None),) * self.lead + tuple(kept) + (slice(None), slice(None))

    def advance(self):
        if not self.pending:
            return
        self.copy.wait()
        self.pending = bool(self.left)
        if self.left:
            bit = self.left.pop(0)
            place = self.other.at[self.held()]
            self.copy = self.bench.remote(place, place, dp_peer(bit)[1])
            self.copy.start()
            self.free.append(bit)

    def finish(self):
        while self.pending:
            self.advance()


CHUNK = 32


def chunks(count, step, start):
    def once(index, carry):
        return step(pl.ds(pl.multiple_of(index * CHUNK, CHUNK), CHUNK), carry)

    return lax.fori_loop(0, count // CHUNK, once, start)


def folded(values):
    return jnp.sum(values.reshape(CHUNK // 8, 8, values.shape[-1]), axis=0)


def stream_scratch(tag, rows, width, halves=2):
    kinds = {
        tag + "_give": ((halves, rows, width), BF),
        tag + "_got": ((halves, rows, width), BF),
        tag + "_acc": ((halves, rows, width), F32),
    }
    if halves == 2:
        kinds[tag + "_send"] = ((rows, width), BF)
        kinds[tag + "_recv"] = ((rows, width), BF)
    return kinds


def at_offset(ref, offset, rows):
    return ref.at[pl.ds(pl.multiple_of(offset + rows.start, CHUNK), rows.size)]


def attend_many(parts_ref, share_ref, context_ref, base, first_block, blocks, heads, masker):
    inner = parts_ref.shape[1] // 3
    size = inner // heads
    scaling = size ** (-0.5)
    rows = [
        pl.ds(pl.multiple_of(base + block * ROW_LEN, CHUNK), ROW_LEN) for block in range(blocks)
    ]
    masks = [masker(first_block + block) for block in range(blocks)]
    scores = []
    for block in range(blocks):
        for head in range(heads):
            queries = parts_ref[rows[block], head * size : (head + 1) * size]
            keys = parts_ref[rows[block], inner + head * size : inner + (head + 1) * size]
            scores.append(jnp.where(masks[block], product_nt(queries, keys) * scaling, -1e9))
    scores = jnp.concatenate(scores, axis=0)
    exponent = jnp.exp(scores - jnp.max(scores, axis=-1, keepdims=True))
    shares = (exponent / jnp.sum(exponent, axis=-1, keepdims=True)).astype(BF)
    for block in range(blocks):
        contexts = []
        for head in range(heads):
            at = (block * heads + head) * ROW_LEN
            piece = shares[at : at + ROW_LEN]
            share_ref[first_block + block, head] = piece
            values = parts_ref[rows[block], 2 * inner + head * size : 2 * inner + (head + 1) * size]
            contexts.append(product(piece, values).astype(BF))
        context_ref[rows[block], :] = jnp.concatenate(contexts, axis=1)


def norm_chunk(values, gain, shift):
    centre = values - jnp.mean(values, axis=-1, keepdims=True)
    spread = jnp.mean(centre * centre, axis=-1, keepdims=True)
    return centre * lax.rsqrt(spread + epsilon) * gain + shift


def feed_forward(stream, full, ups, downs, act, slope):
    width = ups[0].shape[1]

    def project(half, core):
        place = stream.place(half, core)
        for share, up in enumerate(ups):
            lanes = slice(share * width, (share + 1) * width)
            pre = product(full[place], up[...])
            bent = jnp.tanh(GELU_A * (pre + GELU_B * pre * pre * pre))
            act[place, lanes] = (0.5 * pre * (1.0 + bent)).astype(BF)
            slope[place, lanes] = (
                0.5 * (1.0 + bent)
                + 0.5 * pre * (1.0 - bent * bent) * GELU_A * (1.0 + 3.0 * GELU_B * pre * pre)
            ).astype(BF)

    def output(half, core):
        place = stream.place(half, core)
        total = product(act[place, :width], downs[0][...])
        for share, down in enumerate(downs[1:], 1):
            total = total + product(act[place, share * width : (share + 1) * width], down[...])
        return total

    return project, output


def flat(ref, *lead):
    value = ref[lead] if lead else ref[...]
    return value.reshape(-1, value.shape[-1])


def forward_kernel(ctx_t, ctx_i, text_in, image_in, weights, others, norms, text_g, image_g,
                   lengths, regions, text_local, image_local, bits):
    (co_text_out, co_image_out, text_up, text_down, image_up, image_down,
     text_qkv, text_self_out, image_qkv, image_self_out) = weights
    n_t, d_t = text_in.shape
    n_i, d_i = image_in.shape
    ff_t, ff_i = text_up.shape[1], image_up.shape[1]
    in_t, in_i = ctx_inner(text_self_out), image_self_out.shape[0]
    inputs = {
        "lengths": (lengths, "smem"), "regions": (regions, "smem"),
        "gains_t": (norms[0], "vmem"), "shifts_t": (norms[1], "vmem"),
        "gains_i": (norms[2], "vmem"), "shifts_i": (norms[3], "vmem"),
        "ctx_t": (ctx_t, "hbm"), "w_co_t": (co_text_out, "hbm"),
        "ctx_i": (ctx_i, "hbm"), "w_co_i": (co_image_out, "hbm"),
        "qkv_t": (text_qkv, "hbm"), "so_t": (text_self_out, "hbm"),
        "x_t": (text_in, "hbm"), "x_i": (image_in, "hbm"),
        "up_t": (text_up, "hbm"), "down_t": (text_down, "hbm"),
        "up_i": (image_up, "hbm"), "down_i": (image_down, "hbm"),
        "upo_i": (others[0], "hbm"), "downo_i": (others[1], "hbm"),
        "qkv_i": (image_qkv, "hbm"), "so_i": (image_self_out, "hbm"),
        "g_i": (image_g, "hbm"), "g_t": (text_g, "hbm"),
    }
    outputs = {
        "mlp_t": ((4 * n_t, d_t), BF, "hbm"), "mlp_i": ((2 * n_i, d_i), BF, "hbm"),
        "act_t": ((4 * n_t, ff_t), BF, "hbm"), "act_i": ((2 * n_i, 2 * ff_i), BF, "hbm"),
        "slope_t": ((4 * n_t, ff_t), BF, "hbm"), "slope_i": ((2 * n_i, 2 * ff_i), BF, "hbm"),
        "self_t": ((2 * n_t, d_t), BF, "hbm"), "self_i": ((4 * n_i, d_i), BF, "hbm"),
        "parts_i": ((4 * n_i, 3 * in_i), BF, "hbm"),
        "share_i": ((4 * n_i // ROW_LEN, image_local, ROW_LEN, ROW_LEN), BF, "hbm"),
        "ctx2_i": ((4 * n_i, in_i), BF, "hbm"),
        "qkvo_t": (text_qkv.shape, BF, "hbm"), "soo_t": (text_self_out.shape, BF, "hbm"),
    }
    for share in "01":
        outputs["parts%s_t" % share] = ((2 * n_t, 3 * in_t), BF, "hbm")
        outputs["share%s_t" % share] = (
            (2 * n_t // ROW_LEN, text_local, ROW_LEN, ROW_LEN), BF, "hbm"
        )
        outputs["ctx2%s_t" % share] = ((2 * n_t, in_t), BF, "hbm")
    scratch = {}
    for tag, n, d in (("t", n_t, d_t), ("i", n_i, d_i)):
        outputs.update({
            "zero_" + tag: ((n, d), F32, "hbm"),
            "mid_" + tag: ((n, d), F32, "hbm"),
            "late_" + tag: ((n, d), F32, "hbm"),
            "result_" + tag: ((n, d), BF, "hbm"),
            "gain_" + tag: ((8, d), F32, "vmem"),
            "shift_" + tag: ((8, d), F32, "vmem"),
        })
        scratch.update(stream_scratch(tag, n, d))
        scratch["first_" + tag] = ((n, d), F32)

    def body(bench):
        wide = {tag: Stream(bench, tag, n) for tag, n in (("t", n_t), ("i", n_i))}
        near = {tag: Near(bench, tag, n) for tag, n in (("t", n_t), ("i", n_i))}
        get = lambda key, tag: getattr(bench, key + "_" + tag)

        for tag, stream in wide.items():
            context, weight = get("ctx", tag), get("w_co", tag)
            output = lambda half, core: product(context[stream.place(half, core)], weight[...])
            stream.open_sum()
            stream.partial(1, output)
            stream.partial(0, output)

        def settle(tag, stage, source, kept, resid, full, before, after):
            gain = get("gains", tag)[stage : stage + 1]
            shift = get("shifts", tag)[stage : stage + 1]
            base = after.core * after.rows

            def step(rows, carry):
                values = source[rows].astype(F32) + before.piece(rows)
                kept[rows] = values
                normed = norm_chunk(values, gain, shift)
                resid[rows] = normed
                at_offset(full, base, rows)[...] = normed.astype(BF)
                return carry

            chunks(after.rows, step, 0)
            after.gather(full)

        def first_norm(tag, after):
            wide[tag].settle(gathered=False)
            settle(
                tag, 0, get("x", tag), get("zero", tag), get("first", tag), get("mlp", tag),
                wide[tag], after,
            )
            bench.flush("zero_" + tag)

        first_norm("t", wide["t"])
        fetches = [
            Weights(bench, bench.qkv_t, bench.qkvo_t, bits),
            Weights(bench, bench.so_t, bench.soo_t, bits),
        ]
        text_feed = feed_forward(
            wide["t"], bench.mlp_t, [bench.up_t], [bench.down_t], bench.act_t, bench.slope_t
        )
        wide["t"].open_sum()
        wide["t"].arrive(0, text_feed[0])
        wide["t"].partial(0, text_feed[1])
        first_norm("i", near["i"])
        image_feed = feed_forward(
            near["i"], bench.mlp_i, [bench.up_i, bench.upo_i], [bench.down_i, bench.downo_i],
            bench.act_i, bench.slope_i,
        )
        near["i"].open_sum()
        near["i"].arrive(0, image_feed[0])
        near["i"].partial(0, image_feed[1])
        near["i"].settle()
        settle(
            "i", 1, bench.first_i, bench.mid_i, bench.first_i, bench.self_i, near["i"], wide["i"]
        )
        bench.flush("mid_i", "mlp_i", "act_i", "slope_i")
        for fetch in fetches:
            fetch.advance()

        stream_i = wide["i"]

        def project_image(half, core):
            place = stream_i.place(half, core)
            project_three(bench.self_i[place], bench.qkv_i, bench.parts_i, place)

        def middle(half):
            blocks = 2 * n_i // ROW_LEN
            attend_many(
                bench.parts_i, bench.share_i, bench.ctx2_i, 2 * half * n_i, half * blocks, blocks,
                image_local, functools.partial(self_mask_image, Layout(bench)),
            )

        def output_image(half, core):
            return product(bench.ctx2_i[stream_i.place(half, core)], bench.so_i[...])

        stream_i.open_sum()
        stream_i.arrive(0, project_image)
        middle(0)
        stream_i.partial(0, output_image)
        wide["t"].arrive(1, text_feed[0])
        wide["t"].partial(1, text_feed[1])
        for fetch in fetches:
            fetch.advance()
        stream_i.arrive(1, project_image)
        middle(1)
        stream_i.partial(1, output_image)
        bench.flush("act_t", "slope_t", "self_i", "parts_i", "share_i", "ctx2_i")
        for fetch in fetches:
            fetch.finish()
        bench.flush("qkvo_t", "soo_t")

        wide["t"].settle()
        settle(
            "t", 1, bench.first_t, bench.mid_t, bench.first_t, bench.self_t, wide["t"], near["t"]
        )
        bench.flush("mid_t", "mlp_t")
        stream_t = near["t"]
        shares = [
            (bench.qkv_t, bench.so_t, bench.parts0_t, bench.share0_t, bench.ctx20_t),
            (bench.qkvo_t, bench.soo_t, bench.parts1_t, bench.share1_t, bench.ctx21_t),
        ]

        def project_text(half, core):
            place = stream_t.place(half, core)
            for qkv, _, parts, share, context in shares:
                rows = bench.self_t[place]
                for part in range(3):
                    parts[place, part * in_t : (part + 1) * in_t] = product_nt(
                        rows, flat(qkv, part)
                    ).astype(BF)
                attend_many(
                    parts, share, context, core * n_t, core * (n_t // ROW_LEN), n_t // ROW_LEN,
                    text_local, functools.partial(self_mask_text, Layout(bench)),
                )

        def output_text(half, core):
            place = stream_t.place(half, core)
            return product(shares[0][4][place], flat(shares[0][1])) + product(
                shares[1][4][place], flat(shares[1][1])
            )

        stream_t.open_sum()
        stream_t.arrive(0, project_text)
        stream_t.partial(0, output_text)
        for share in "01":
            bench.flush("parts%s_t" % share, "share%s_t" % share, "ctx2%s_t" % share)
        bench.flush("self_t")

        for tag, stream in (("i", wide["i"]), ("t", near["t"])):
            stream.settle()
            gain, shift = get("gains", tag)[2:3], get("shifts", tag)[2:3]
            second, result, late, grad = (
                get("first", tag), get("result", tag), get("late", tag), get("g", tag)
            )
            width = second.shape[1]

            def step(rows, carry):
                values = second[rows] + stream.piece(rows)
                back, normed, gains, shifts = norm_pull(values, gain, shift, grad[rows].astype(F32))
                result[rows] = normed.astype(BF)
                late[rows] = back
                return carry[0] + gains, carry[1] + shifts

            start = jnp.zeros((8, width), F32)
            gains, shifts = chunks(stream.rows, step, (start, start))
            get("gain", tag)[...] = gains
            get("shift", tag)[...] = shifts
            bench.flush("result_" + tag, "late_" + tag)

    return exchange_kernel(
        body, "forward_tail", 1,
        lambda: list(group_peers()[1:]) + [dp_peer(bit)[1] for bit in bits],
        inputs, outputs, scratch, 40, (15e9, 40e6, 1e6),
    )


def ctx_inner(out_weight):
    rows = 1
    for size in out_weight.shape[:-1]:
        rows *= size
    return rows


def norm_pull(values, gain, shift, gradient):
    centre = values - jnp.mean(values, axis=-1, keepdims=True)
    spread = jnp.mean(centre * centre, axis=-1, keepdims=True)
    inverse = lax.rsqrt(spread + epsilon)
    unit = centre * inverse
    scaled = gradient * gain
    back = inverse * (
        scaled
        - jnp.mean(scaled, axis=-1, keepdims=True)
        - unit * jnp.mean(scaled * unit, axis=-1, keepdims=True)
    )
    return back, unit * gain + shift, folded(gradient * unit), folded(gradient)


def attend_back_many(parts_ref, share_ref, grads, out_ref, base, first_block, blocks, heads):
    inner = parts_ref.shape[1] // 3
    size = inner // heads
    scaling = size ** (-0.5)
    rows = [
        pl.ds(pl.multiple_of(base + block * ROW_LEN, CHUNK), ROW_LEN) for block in range(blocks)
    ]
    context_grads = [grads(block) for block in range(blocks)]
    pairs = [(block, head) for block in range(blocks) for head in range(heads)]

    def piece(part, block, head):
        at = part * inner + head * size
        return parts_ref[rows[block], at : at + size]

    def grad_of(block, head):
        return context_grads[block][:, head * size : (head + 1) * size]

    narrow = [share_ref[first_block + block, head] for block, head in pairs]
    shares = jnp.concatenate(narrow, axis=0).astype(F32)
    share_grad = jnp.concatenate(
        [product_nt(grad_of(*pair), piece(2, *pair)) for pair in pairs], axis=0
    )
    total = jnp.sum(share_grad * shares, axis=-1, keepdims=True)
    score_grad = (shares * (share_grad - total) * scaling).astype(BF)
    for block in range(blocks):
        pieces = [[], [], []]
        for head in range(heads):
            index = block * heads + head
            scores = score_grad[index * ROW_LEN : (index + 1) * ROW_LEN]
            pieces[0].append(product(scores, piece(1, block, head)).astype(BF))
            pieces[1].append(product_tn(scores, piece(0, block, head)).astype(BF))
            pieces[2].append(product_tn(narrow[index], grad_of(block, head)).astype(BF))
        out_ref[rows[block], :] = jnp.concatenate(pieces[0] + pieces[1] + pieces[2], axis=1)


class Split:
    def __init__(self, group_count, rows, order, shares=1, late=False):
        bits = group_count.bit_length() - 1
        ready = group_count == 1 << bits and (rows // group_count) % 32 == 0
        self.fast = ready and group_count > 1
        self.groups = group_count if self.fast else 1
        self.blocks = self.groups * shares
        self.part = rows // self.groups
        self.order = order(bits) if self.fast else []
        if shares == 2:
            at = len(self.order) if late else min(1, len(self.order))
            self.order = self.order[:at] + ["y"] + self.order[at:]

    def position(self, block, share=0):
        spot = 0
        for bit in self.order:
            spot = 2 * spot + (share if bit == "y" else (block >> bit) & 1)
        return spot

    def shape(self, columns):
        return (self.blocks, self.part, columns)

    def spare(self, columns):
        return (max(self.blocks - 1, 1), self.part, columns)


def dp_peer(bit):
    if bit == "y":
        return 0, group_peers()[2]
    place = lax.axis_index("dp")
    value = lax.rem(lax.div(place, 1 << bit), 2)
    return value, {"dp": place + (1 << bit) * (1 - 2 * value)}


def dp_peers(*splits):
    bits = sorted({bit for split in splits for bit in split.order if bit != "y"})
    return [dp_peer(bit)[1] for bit in bits]


class GroupSum:
    def __init__(self, bench, split, stack, spare, first=0, last=None, columns=slice(None)):
        self.bench, self.split, self.stack, self.spare = bench, split, stack, spare
        self.columns = columns
        self.base = 0
        self.size = split.blocks
        self.at = 0
        self.left = list(split.order)[first:last]
        self.pending = False
        for bit in split.order[:first]:
            self.size //= 2
            self.base = self.base + dp_peer(bit)[0] * self.size

    def start(self):
        if not self.left:
            return
        value, peer = dp_peer(self.left.pop(0))
        self.size //= 2
        given = self.base + (1 - value) * self.size
        self.base = self.base + value * self.size
        self.copy = self.bench.remote(
            self.stack.at[pl.ds(given, self.size), :, self.columns],
            self.spare.at[pl.ds(self.at, self.size), :, self.columns],
            peer,
        )
        self.copy.start()
        self.pending = True

    def advance(self):
        if not self.pending:
            return
        self.copy.wait_recv()
        self.copy.wait_send()
        self.pending = False

        def add(index, carry):
            mine = self.base + index
            self.stack[mine, :, self.columns] = (
                self.stack[mine, :, self.columns].astype(F32)
                + self.spare[self.at + index, :, self.columns].astype(F32)
            ).astype(BF)
            return carry

        lax.fori_loop(0, self.size, add, 0)
        self.at += self.size
        self.start()

    def drain(self):
        while self.pending:
            self.advance()

    def finish(self, out):
        self.drain()
        out[...] = self.stack[self.base]


def weight_grad(split, stack, column, left, right, share=0):
    rows, width = left.shape[1], right.shape[1]
    tile = rows // 2
    for start in (0, tile):
        value = product_tn(left[:, start : start + tile], right).astype(BF)
        lanes = slice(column, column + width)
        if split.groups == 1:
            stack[split.position(0, share), start : start + tile, lanes] = value
            continue
        for index in range(tile // split.part):
            spot = split.position(start // split.part + index, share)
            stack[spot, :, lanes] = value[index * split.part : (index + 1) * split.part]


def project_three(rows, weights, target, place):
    width = weights.shape[2]
    for part in range(3):
        target[place, part * width : (part + 1) * width] = product(rows, weights[part]).astype(BF)


def back_three(grads, place, weights):
    width = weights.shape[2]
    return (
        product_nt(grads[place, :width], weights[0])
        + product_nt(grads[place, width : 2 * width], weights[1])
        + product_nt(grads[place, 2 * width :], weights[2])
    )


def spread(stream, source, full):
    base = stream.core * stream.rows

    def step(rows, carry):
        at_offset(full, base, rows)[...] = source[rows].astype(BF)
        return carry

    chunks(stream.rows, step, 0)
    stream.gather(full)


def settle_back(stream, resid, values, gain, target, gain_out, shift_out, full=None):
    base = stream.core * stream.rows

    def step(rows, carry):
        gradient = resid[rows] + stream.piece(rows)
        back, _, gains, shifts = norm_pull(values[rows], gain, 0.0, gradient)
        target[rows] = back
        if full is not None:
            at_offset(full, base, rows)[...] = back.astype(BF)
        return carry[0] + gains, carry[1] + shifts

    start = jnp.zeros((8, resid.shape[1]), F32)
    gains, shifts = chunks(stream.rows, step, (start, start))
    gain_out[...] = gains
    shift_out[...] = shifts


def self_back_kernel(ahead, image_qkv, image_self_out, text_qkv, text_self_out, gains, splits):
    n_t, d_t = ahead["late_t"].shape
    n_i, d_i = ahead["late_i"].shape
    in_t, in_i = ctx_inner(text_self_out), image_self_out.shape[0]
    hbm = lambda *keys: {key: (ahead[key], "hbm") for key in keys}
    inputs = {"gains_t": (gains[0], "vmem"), "gains_i": (gains[1], "vmem")}
    inputs.update(hbm("late_i", "late_t"))
    inputs.update({"so_i": (image_self_out, "hbm")})
    inputs.update(hbm("parts_i", "share_i"))
    inputs.update({"so_t": (text_self_out, "hbm")})
    inputs.update(hbm("soo_t", "parts0_t", "share0_t", "parts1_t", "share1_t"))
    inputs.update({"qkv_i": (image_qkv, "hbm"), "qkv_t": (text_qkv, "hbm")})
    inputs.update(hbm("qkvo_t", "self_t", "ctx20_t", "ctx21_t", "mid_t", "self_i", "ctx2_i", "mid_i"))
    outputs, scratch = {}, {}
    for index, tag, n, d, inner in ((1, "i", n_i, d_i, in_i), (0, "t", n_t, d_t, in_t)):
        outputs.update({
            "back_" + tag: ((n, d), F32, "hbm"),
            "stack_" + tag: (splits[index].shape(4 * inner), BF, "hbm"),
            "gain_" + tag: ((8, d), F32, "vmem"),
            "shift_" + tag: ((8, d), F32, "vmem"),
        })
    scratch.update(stream_scratch("i", n_i, d_i))
    scratch.update(stream_scratch("t", n_t, d_t, 1))
    scratch.update({
        "full_i": ((4 * n_i, d_i), BF), "full_t": ((2 * n_t, d_t), BF),
        "grad_i": ((4 * n_i, 3 * in_i), BF), "cg_i": ((4 * n_i, in_i), BF),
        "grad0_t": ((2 * n_t, 3 * in_t), BF), "grad1_t": ((2 * n_t, 3 * in_t), BF),
    })
    heads = {"t": ahead["share0_t"].shape[1], "i": ahead["share_i"].shape[1]}

    def body(bench):
        image, text = Stream(bench, "i", n_i), Near(bench, "t", n_t)
        spread(image, bench.late_i, bench.full_i)
        spread(text, bench.late_t, bench.full_t)

        def project_image(half, core):
            place = image.place(half, core)
            bench.cg_i[place] = product_nt(bench.full_i[place], bench.so_i[...]).astype(BF)

        def middle(half):
            blocks = 2 * n_i // ROW_LEN
            base = 2 * half * n_i
            attend_back_many(
                bench.parts_i, bench.share_i,
                lambda block: bench.cg_i[base + block * ROW_LEN : base + (block + 1) * ROW_LEN],
                bench.grad_i, base, half * blocks, blocks, heads["i"],
            )

        def output_image(half, core):
            return back_three(bench.grad_i, image.place(half, core), bench.qkv_i)

        image.open_sum()
        image.arrive(0, project_image)
        middle(0)
        image.partial(0, output_image)
        shares = [
            (bench.so_t, bench.qkv_t, bench.parts0_t, bench.share0_t, bench.grad0_t),
            (bench.soo_t, bench.qkvo_t, bench.parts1_t, bench.share1_t, bench.grad1_t),
        ]

        def project_text(half, core):
            place = text.place(half, core)
            blocks = n_t // ROW_LEN
            for out, _, parts, share, grad in shares:
                context_grad = product_nt(bench.full_t[place], flat(out)).astype(BF)
                attend_back_many(
                    parts, share,
                    lambda block: context_grad[block * ROW_LEN : (block + 1) * ROW_LEN],
                    grad, core * n_t, core * blocks, blocks, heads["t"],
                )

        def output_text(half, core):
            place = text.place(half, core)
            total = None
            for _, qkv, _, _, grad in shares:
                for part in range(3):
                    term = product(grad[place, part * in_t : (part + 1) * in_t], flat(qkv, part))
                    total = term if total is None else total + term
            return total

        text.open_sum()
        text.arrive(0, project_text)
        image.arrive(1, project_image)
        middle(1)
        image.partial(1, output_image)
        text.partial(0, output_text)

        def close(index, tag, stream):
            stream.settle()
            get = lambda key: getattr(bench, key + "_" + tag)
            settle_back(
                stream, get("late"), get("mid"), get("gains")[1:2], get("back"), get("gain"),
                get("shift"),
            )
            bench.flush("back_" + tag)

        for share in (0, 1):
            grad, context = shares[share][4], getattr(bench, "ctx2%d_t" % share)
            weight_grad(splits[0], bench.stack_t, 0, bench.self_t, grad[...], share)
            weight_grad(splits[0], bench.stack_t, 3 * in_t, bench.full_t, context[...], share)
        bench.flush("stack_t")
        close(0, "t", text)
        weight_grad(splits[1], bench.stack_i, 0, bench.self_i, bench.grad_i[...])
        weight_grad(splits[1], bench.stack_i, 3 * in_i, bench.full_i, bench.ctx2_i[...])
        bench.flush("stack_i")
        close(1, "i", image)

    return exchange_kernel(
        body, "self_back", 2, lambda: list(group_peers()[1:]), inputs, outputs, scratch, 16,
        (12e9, 40e6, 1e6),
    )


def feed_back_kernel(first_back, ahead, ups, downs, others, contexts, co_out, gains, self_splits,
                     splits):
    n_t, d_t = first_back["back_t"].shape
    n_i, d_i = first_back["back_i"].shape
    ff = {"t": ups[0].shape[1], "i": ups[1].shape[1]}
    inputs, outputs, scratch = {}, {}, {}
    for index, tag in ((0, "t"), (1, "i")):
        n, d = first_back["back_" + tag].shape
        inner = contexts[index].shape[1]
        own = self_splits[index]
        stack = first_back["stack_" + tag]
        inputs.update({
            "gains_" + tag: (gains[index], "vmem"),
            "mg_" + tag: (first_back["back_" + tag], "hbm"),
            "down_" + tag: (downs[index], "hbm"),
            "slope_" + tag: (ahead["slope_" + tag], "hbm"),
            "up_" + tag: (ups[index], "hbm"),
        })
        if tag == "i":
            inputs.update({"upo_i": (others[0], "hbm"), "downo_i": (others[1], "hbm")})
        inputs.update({
            "stack_" + tag: (stack, "hbm"),
            "zero_" + tag: (ahead["zero_" + tag], "hbm"),
            "mlp_" + tag: (ahead["mlp_" + tag], "hbm"),
            "act_" + tag: (ahead["act_" + tag], "hbm"),
            "co_" + tag: (co_out[index], "hbm"),
            "ctx_" + tag: (contexts[index], "hbm"),
        })
        outputs.update({
            "back_" + tag: ((n, d), F32, "hbm"),
            "cg_" + tag: ((4 * n, inner), BF, "hbm"),
            "out_grad_" + tag: (Split.shape(plain_split(splits[index], d), inner), BF, "hbm"),
            "gain_" + tag: ((8, d), F32, "vmem"),
            "shift_" + tag: ((8, d), F32, "vmem"),
            "self_sum_" + tag: ((own.part, stack.shape[2]), BF, "hbm"),
            "fstack_" + tag: (splits[index].shape(2 * ff[tag]), BF, "hbm"),
        })
        scratch["spare_" + tag] = (own.spare(stack.shape[2]), BF)
        scratch["fspare_" + tag] = (splits[index].spare(2 * ff[tag]), BF)
        scratch["full2_" + tag] = ((4 * n, d), BF)
    scratch.update(stream_scratch("t", n_t, d_t))
    scratch.update(stream_scratch("i", n_i, d_i, 1))
    scratch.update({
        "full_t": ((4 * n_t, d_t), BF), "full_i": ((2 * n_i, d_i), BF),
        "pre_t": ((4 * n_t, ff["t"]), BF), "pre_i": ((2 * n_i, 2 * ff["i"]), BF),
    })

    def body(bench):
        text, image = Stream(bench, "t", n_t), Near(bench, "i", n_i)
        last = {"t": Gather(bench, n_t), "i": Gather(bench, n_i)}
        get = lambda key, tag: getattr(bench, key + "_" + tag)
        spread(text, bench.mg_t, bench.full_t)
        spread(image, bench.mg_i, bench.full_i)

        def hooks(stream, tag, up_w, down_w):
            full, slope, pre = get("full", tag), get("slope", tag), get("pre", tag)
            width = ff[tag]

            def project(half, core):
                place = stream.place(half, core)
                for share, down in enumerate(down_w):
                    lanes = slice(share * width, (share + 1) * width)
                    grad = product_nt(full[place], down[...])
                    pre[place, lanes] = (grad * slope[place, lanes].astype(F32)).astype(BF)

            def output(half, core):
                place = stream.place(half, core)
                total = product_nt(pre[place, :width], up_w[0][...])
                for share, up in enumerate(up_w[1:], 1):
                    total = total + product_nt(
                        pre[place, share * width : (share + 1) * width], up[...]
                    )
                return total

            return project, output

        text_hooks = hooks(text, "t", [bench.up_t], [bench.down_t])
        text.open_sum()
        text.arrive(0, text_hooks[0])
        text.partial(0, text_hooks[1])
        sums = {
            tag: GroupSum(bench, self_splits[index], get("stack", tag), get("spare", tag))
            for index, tag in ((1, "i"), (0, "t"))
        }
        for total in sums.values():
            total.start()
        image_hooks = hooks(
            image, "i", [bench.up_i, bench.upo_i], [bench.down_i, bench.downo_i]
        )
        image.open_sum()
        image.arrive(0, image_hooks[0])
        image.partial(0, image_hooks[1])

        def close(tag, stream):
            stream.settle()
            settle_back(
                stream, get("mg", tag), get("zero", tag), get("gains", tag)[0:1],
                get("back", tag), get("gain", tag), get("shift", tag), get("full2", tag),
            )
            bench.flush("back_" + tag)
            last[tag].gather(get("full2", tag))

        feed_sums = {"t": [], "i": []}

        def feed_grads(index, tag, key, left, right, column):
            stack, width = get("fstack", tag), ff[tag]
            for share in range(1 + index):
                lanes = slice(share * width, (share + 1) * width)
                weight_grad(splits[index], stack, column, left, right[:, lanes], share)
            columns = pl.ds(column, width)
            total = GroupSum(
                bench, splits[index], stack, get("fspare", tag), 0, 1, columns
            )
            total.start()
            feed_sums[tag].append(total)

        def co_project(tag):
            full, weight, target = get("full2", tag), get("co", tag), get("cg", tag)

            def project(half, core):
                place = last[tag].place(half, core)
                target[place] = product_nt(full[place], weight[...]).astype(BF)

            return project

        close("i", image)
        text.arrive(1, text_hooks[0])
        text.partial(1, text_hooks[1])
        feed_grads(1, "i", "up", bench.mlp_i, bench.pre_i, 0)
        feed_grads(1, "i", "down", bench.full_i, bench.act_i, ff["i"])
        last["i"].arrive(0, co_project("i"))
        sums["i"].advance()
        feed_grads(0, "t", "up", bench.mlp_t, bench.pre_t, 0)
        sums["t"].advance()
        feed_grads(0, "t", "down", bench.full_t, bench.act_t, ff["t"])
        close("t", text)
        last["i"].arrive(1, co_project("i"))
        bench.flush("cg_i")
        last["t"].arrive(0, co_project("t"))
        plain = plain_split(splits[1], d_i)
        weight_grad(plain, bench.out_grad_i, 0, bench.full2_i, bench.ctx_i[...])
        bench.flush("out_grad_i")
        sums["i"].advance()
        sums["t"].advance()
        last["t"].arrive(1, co_project("t"))
        bench.flush("cg_t")
        plain = plain_split(splits[0], d_t)
        weight_grad(plain, bench.out_grad_t, 0, bench.full2_t, bench.ctx_t[...])
        bench.flush("out_grad_t")
        for stream in last.values():
            stream.finish_gather()
        sums["t"].advance()
        sums["i"].finish(bench.self_sum_i)
        bench.flush("self_sum_i")
        for tag in ("i", "t"):
            for total in feed_sums[tag]:
                total.drain()
            bench.flush("fstack_" + tag)
        sums["t"].finish(bench.self_sum_t)
        bench.flush("self_sum_t")

    return exchange_kernel(
        body, "feed_back", 3,
        lambda: list(group_peers()[1:]) + dp_peers(*self_splits, *splits), inputs, outputs,
        scratch, 40, (12e9, 60e6, 1e6),
    )


def plain_split(split, rows):
    order = [bit for bit in split.order if bit != "y"]
    return Split(split.groups, rows, lambda bits: order)


def co_front_kernel(shards, weights, feeds, order, inverse, regions, lengths, heads, bits):
    inputs = {
        "order": (order, "smem"), "inverse": (inverse, "smem"),
        "regions": (regions, "smem"), "lengths": (lengths, "smem"),
    }
    outputs, scratch = {}, {}
    for key, weight in zip(("up", "down"), feeds):
        inputs[key + "_i"] = (weight, "hbm")
        outputs[key + "o_i"] = (weight.shape, BF, "hbm")
    for index, tag in ((0, "t"), (1, "i")):
        n, d = shards[index].shape
        width = weights[index].shape[2]
        inputs.update({"x_" + tag: (shards[index], "hbm"), "w_" + tag: (weights[index], "hbm")})
        outputs.update({
            "all_" + tag: ((4 * n, d), BF, "hbm"),
            "co_" + tag: ((4 * n, 3 * width), BF, "hbm"),
            "ctx_" + tag: ((4 * n, width), BF, "hbm"),
        })
    n_t, n_i = shards[0].shape[0], shards[1].shape[0]
    held, width = n_t // CAP_LEN, weights[0].shape[2]
    outputs["co_t"] = ((4 * held, CAP_LEN, 3 * width), BF, "hbm")
    rows = 4 * n_i // ROW_LEN
    span = PER_ROW * CAP_LEN
    outputs["cshare_t"] = ((rows, heads, span, ROW_LEN), BF, "hbm")
    outputs["cshare_i"] = ((rows, heads, ROW_LEN, span), BF, "hbm")
    scratch["rctx_t"] = ((4 * held, CAP_LEN, width), BF)

    def body(bench):
        streams = {tag: Gather(bench, n) for tag, n in (("t", n_t), ("i", n_i))}
        get = lambda key, tag: getattr(bench, key + "_" + tag)
        fetches = [
            Weights(bench, bench.up_i, bench.upo_i, bits),
            Weights(bench, bench.down_i, bench.downo_i, bits[:-2] + bits[:-3:-1]),
        ]
        for tag, stream in streams.items():
            full = get("all", tag)
            full[stream.place(0, stream.core)] = get("x", tag)[...]
            stream.gather(full)
        for half in (0, 1):
            for tag, stream in streams.items():
                full, weight, target = get("all", tag), get("w", tag), get("co", tag)

                def project(half, core):
                    place = stream.place(half, core)
                    if tag == "i":
                        project_three(full[place], weight, target, place)
                        return
                    captions = pl.ds((2 * half + core) * held, held)
                    for part in range(3):
                        target[captions, :, part * width : (part + 1) * width] = (
                            product(full[place], weight[part])
                            .astype(BF)
                            .reshape(held, CAP_LEN, width)
                        )

                stream.arrive(half, project)
            if half == 0:
                for fetch in fetches * len(bits):
                    fetch.advance()
        for tag in streams:
            bench.flush("all_" + tag, "co_" + tag)
        co_forward_rows(bench, heads, rows)
        in_caption_order(bench, bench.rctx_t, bench.ctx_t)
        for fetch in fetches:
            fetch.finish()
        for stream in streams.values():
            stream.finish_gather()

    return exchange_kernel(
        body, "co_front", 5,
        lambda: list(group_peers()[1:]) + [dp_peer(bit)[1] for bit in bits],
        inputs, outputs, scratch, 16,
        (4e9, 20e6, 1e6),
    )


class Total:
    def __init__(self, bench, held, landing, group_count):
        self.bench, self.held, self.landing = bench, held, landing
        self.peers = list(group_peers()[1:]) + [
            dp_peer(bit)[1] for bit in range(group_count.bit_length() - 1)
        ]
        self.step = 0
        self.start()

    def start(self):
        if self.step < len(self.peers):
            self.copy = self.bench.remote(
                self.held.at[self.step], self.landing.at[self.step], self.peers[self.step]
            )
            self.copy.start()

    def advance(self):
        if self.step < len(self.peers):
            self.copy.wait()
            self.held[self.step + 1] = self.held[self.step] + self.landing[self.step]
            self.step += 1
            self.start()

    def finish(self, out):
        while self.step < len(self.peers):
            self.advance()
        out[...] = self.held[self.step]


def co_back_kernel(zero_grad, context_grads, tokens, projected, shares, weights, out_grads,
                   feed_stacks, norms, order, inverse, splits, feed_splits, heads, group_count):
    inputs = {"order": (order, "smem"), "inverse": (inverse, "smem")}
    outputs, scratch = {}, {}
    steps = 2 + group_count.bit_length() - 1
    for index, tag in ((1, "i"), (0, "t")):
        n, d = zero_grad[index].shape
        width = projected[index].shape[-1]
        inner = out_grads[index].shape[2]
        split = splits[index]
        feeds = feed_stacks[index].shape[2]
        inputs.update({"norm%d_%s" % (k, tag): (v, "vmem") for k, v in enumerate(norms[index])})
        inputs.update({
            "co_" + tag: (projected[index], "hbm"),
            "cg_" + tag: (context_grads[index], "hbm"),
            "cshare_" + tag: (shares[index], "hbm"),
            "fstack_" + tag: (feed_stacks[index], "hbm"),
            "ostack_" + tag: (out_grads[index], "hbm"),
            "x_" + tag: (tokens[index], "hbm"),
            "w_" + tag: (weights[index], "hbm"),
            "zg_" + tag: (zero_grad[index], "hbm"),
        })
        outputs.update({
            "in_grad_" + tag: ((n, d), F32, "hbm"),
            "feed_sum_" + tag: ((split.part, feeds), BF, "hbm"),
            "out_sum_" + tag: ((split.part, inner), BF, "hbm"),
            "qkv_sum_" + tag: ((split.part, width), BF, "hbm"),
            "norm_" + tag: ((8, d), F32, "vmem"),
        })
        scratch.update(stream_scratch(tag, n, d))
        scratch["grad_" + tag] = ((4 * n, width), BF)
        scratch["stack_" + tag] = (split.shape(width), BF)
        scratch["spare_" + tag] = (split.spare(width), BF)
        scratch["fspare_" + tag] = (feed_splits[index].spare(feeds), BF)
        scratch["ospare_" + tag] = (split.spare(inner), BF)
        scratch["held_" + tag] = ((steps + 1, 8, d), F32)
        scratch["landing_" + tag] = ((steps, 8, d), F32)
    n_t, n_i = zero_grad[0].shape[0], zero_grad[1].shape[0]
    scratch["rgrad_t"] = (projected[0].shape, BF)

    def body(bench):
        streams = {tag: Stream(bench, tag, n) for tag, n in (("i", n_i), ("t", n_t))}
        get = lambda key, tag: getattr(bench, key + "_" + tag)
        feeds, outs, late, totals = {}, {}, {}, {}
        for index, tag in ((0, "t"), (1, "i")):
            feeds[tag] = GroupSum(
                bench, feed_splits[index], get("fstack", tag), get("fspare", tag), 1
            )
            outs[tag] = GroupSum(bench, splits[index], get("ostack", tag), get("ospare", tag))
            feeds[tag].start()
            outs[tag].start()
        for tag in ("t", "i"):
            held = get("held", tag)
            vectors = [
                jnp.sum(get("norm%d" % k, tag)[...], axis=0, keepdims=True) for k in range(6)
            ]
            held[0] = jnp.concatenate(vectors + [jnp.zeros_like(vectors[0])] * 2, axis=0)
            totals[tag] = Total(bench, held, get("landing", tag), group_count)
        rows = 4 * n_i // ROW_LEN
        for step in range(3):
            co_backward_rows(bench, heads, rows * step // 3, rows * (step + 1) // 3)
            for total in totals.values():
                total.advance()
            if step == 1:
                outs["t"].advance()
        in_caption_order(bench, bench.rgrad_t, bench.grad_t)
        feeds["i"].advance()

        def finish_stream(index, tag):
            stack = get("stack", tag)
            weight_grad(splits[index], stack, 0, get("x", tag), get("grad", tag)[...])
            late[tag] = GroupSum(bench, splits[index], stack, get("spare", tag))
            late[tag].start()
            stream = streams[tag]
            grad, weight = get("grad", tag), get("w", tag)
            output = lambda half, core: back_three(grad, stream.place(half, core), weight)
            stream.open_sum()
            stream.partial(1, output)
            feeds["t"].advance()
            outs["i"].advance()
            for total in totals.values():
                total.advance()
            stream.partial(0, output)

        def close(tag):
            stream = streams[tag]
            resid, target = get("zg", tag), get("in_grad", tag)
            stream.settle(gathered=False)

            def step(rows, carry):
                target[rows] = resid[rows] + stream.piece(rows)
                return carry

            chunks(stream.rows, step, 0)
            bench.flush("in_grad_" + tag)

        finish_stream(1, "i")
        outs["t"].advance()
        feeds["i"].advance()
        finish_stream(0, "t")
        for tag, total in totals.items():
            total.advance()
        late["i"].advance()
        late["t"].advance()
        close("i")
        for tag, total in totals.items():
            total.finish(get("norm", tag))
        late["i"].advance()
        late["t"].advance()
        close("t")
        for tag in ("t", "i"):
            feeds[tag].finish(get("feed_sum", tag))
            outs[tag].finish(get("out_sum", tag))
            bench.flush("feed_sum_" + tag, "out_sum_" + tag)
        for tag in ("t", "i"):
            late[tag].finish(get("qkv_sum", tag))
            bench.flush("qkv_sum_" + tag)

    return exchange_kernel(
        body, "co_back", 4,
        lambda: list(group_peers()[1:])
        + [dp_peer(bit)[1] for bit in range(group_count.bit_length() - 1)],
        inputs, outputs, scratch, 16 + 2 * steps + 20, (8e9, 50e6, 1e6),
    )


def finish_kernel(sums, norms, kept):
    arrays, shapes = [], []
    for stream, (qkv, out, own, feed) in enumerate(sums):
        part = qkv.shape[0]
        inner, ff = own.shape[1] // 4, feed.shape[1] // 2
        arrays += [qkv, out, own, feed]
        turned = lambda rows: (part, rows) if stream == 0 else (rows, part)
        shapes += [
            (3, part, qkv.shape[1] // 3), turned(out.shape[1]), (3, part, inner), (inner, part),
            (part, ff), turned(ff),
        ]
    devices = lax.axis_size("dp") * lax.axis_size("mp")
    columns = [norm.shape[1] // devices for norm in norms]
    count, made = len(arrays), len(shapes)
    outs = [shape_of(shape, F32) for shape in shapes]
    for width in columns:
        outs += [shape_of((3, width), F32)] * 2
    outs += [shape_of(array.shape, array.dtype) for array in kept]
    any_spec, vmem_spec = pl.BlockSpec(memory_space=pl.ANY), pl.BlockSpec(memory_space=pltpu.VMEM)

    def kernel(*refs):
        refs = list(refs)
        take = lambda number: [refs.pop(0) for _ in range(number)]
        sources, totals, whole = take(count), take(2), take(len(kept))
        results, parts, copies = take(made), take(4), take(len(kept))
        held, built = take(count), take(made)
        in_sems, out_sems, keep_sems = take(3)
        fetches = [
            pltpu.make_async_copy(source, target, in_sems.at[index])
            for index, (source, target) in enumerate(zip(sources, held))
        ]
        moves = [
            pltpu.make_async_copy(source, target, keep_sems.at[index])
            for index, (source, target) in enumerate(zip(whole, copies))
        ]
        for copy in fetches + moves:
            copy.start()
        place = lax.axis_index("dp") * lax.axis_size("mp") + lax.axis_index("mp")
        for stream in range(2):
            total, width = totals[stream][...], columns[stream]
            mine = pltpu.roll(total, total.shape[1] - place * width, 1)[:, :width]
            parts[2 * stream][...] = mine[:3]
            parts[2 * stream + 1][...] = mine[3:6]
        stores = []

        def store(index, values):
            for part, value in enumerate(values):
                target = built[index].at[part] if len(values) > 1 else built[index]
                target[...] = value
            stores.append(
                pltpu.make_async_copy(built[index], results[index], out_sems.at[index])
            )
            stores[-1].start()

        for stream in range(2):
            qkv, out, own, feed = held[4 * stream : 4 * stream + 4]
            at = 6 * stream
            width, inner, ff = qkv.shape[1] // 3, own.shape[1] // 4, feed.shape[1] // 2
            turned = (lambda value: value) if stream == 0 else (lambda value: value.T)
            fetches[4 * stream].wait()
            store(at, [qkv[:, k * width : (k + 1) * width].astype(F32) for k in range(3)])
            fetches[4 * stream + 1].wait()
            store(at + 1, [turned(out[...].astype(F32))])
            fetches[4 * stream + 2].wait()
            store(at + 2, [own[:, k * inner : (k + 1) * inner].astype(F32) for k in range(3)])
            store(at + 3, [own[:, 3 * inner :].astype(F32).T])
            fetches[4 * stream + 3].wait()
            store(at + 4, [feed[:, :ff].astype(F32)])
            store(at + 5, [turned(feed[:, ff:].astype(F32))])
        for copy in stores + moves:
            copy.wait()

    return pl.pallas_call(
        kernel,
        in_specs=[any_spec] * count + [vmem_spec] * 2 + [any_spec] * len(kept),
        out_specs=[any_spec] * made + [vmem_spec] * 4 + [any_spec] * len(kept),
        out_shape=outs,
        scratch_shapes=[pltpu.VMEM(array.shape, array.dtype) for array in arrays]
        + [pltpu.VMEM(shape, F32) for shape in shapes]
        + [pltpu.SemaphoreType.DMA((number,)) for number in (count, made, len(kept))],
        compiler_params=pltpu.CompilerParams(vmem_limit_bytes=32 * 1024 * 1024),
        name="finish",
    )(*arrays, *norms, *kept)


def apart(grad):
    rows, columns = grad.shape
    return jnp.transpose(grad.reshape(rows, 3, columns // 3), (1, 0, 2))


def finish_plain(sums, norms, kept):
    place = lax.axis_index("dp") * lax.axis_size("mp") + lax.axis_index("mp")
    outs, parts = [], []
    for stream, values in enumerate(sums):
        qkv, out, own, feed = [value.astype(F32) for value in values]
        inner, ff = own.shape[1] // 4, feed.shape[1] // 2
        turned = (lambda value: value) if stream == 0 else (lambda value: value.T)
        outs += [
            apart(qkv), turned(out), apart(own[:, : 3 * inner]), own[:, 3 * inner :].T,
            feed[:, :ff], turned(feed[:, ff:]),
        ]
        columns = norms[stream].shape[1] // (lax.axis_size("dp") * lax.axis_size("mp"))
        mine = lax.dynamic_slice_in_dim(norms[stream], place * columns, columns, axis=1)
        parts += [mine[:3], mine[3:6]]
    return outs + parts + list(kept)


def per_device(
    text_in,
    image_in,
    caption_lengths,
    region_lengths,
    image_caption,
    co_text_qkv,
    co_image_qkv,
    co_text_out,
    co_image_out,
    text_up,
    text_down,
    image_up,
    image_down,
    text_self_qkv,
    text_self_out,
    image_self_qkv,
    image_self_out,
    text_gains,
    text_shifts,
    image_gains,
    image_shifts,
    text_grad_out,
    image_grad_out,
):
    captions = image_caption.shape[1]
    part_count = lax.axis_size("mp")
    group_count = lax.axis_size("dp")
    spot = lax.axis_index("mp")
    core = spot % 2
    chip = spot // 2
    co_local = CO_HEADS // part_count
    text_local = TEXT_HEADS // part_count
    image_local = IMAGE_HEADS // part_count

    lengths = caption_lengths
    regions = region_lengths.T
    order = image_caption[0]
    labels = jnp.arange(captions, dtype=jnp.int32)
    inverse = jnp.sum(
        jnp.where(order[None, :] == labels[:, None], labels[None, :], 0), axis=1, dtype=jnp.int32
    )

    power = group_count.bit_length() - 1 if group_count & (group_count - 1) == 0 else 0

    def fold(weight, bits):
        return weight.reshape(
            weight.shape[:-2] + (2,) * bits + (weight.shape[-2] >> bits, weight.shape[-1])
        )

    feed_bits, self_bits = list(range(min(power, 3)))[::-1], list(range(min(power, 2)))[::-1]
    text_qkv = fold(jnp.swapaxes(text_self_qkv, 1, 2), len(self_bits))
    text_self_blocks = fold(text_self_out, len(self_bits))

    front = co_front_kernel(
        (text_in, image_in), (co_text_qkv, co_image_qkv),
        (fold(image_up, len(feed_bits)), fold(image_down, len(feed_bits))),
        order, inverse, regions, lengths, co_local, feed_bits,
    )
    others = (
        front["upo_i"].reshape(image_up.shape), front["downo_i"].reshape(image_down.shape)
    )
    text_ctx, image_ctx = front["ctx_t"], front["ctx_i"]
    ahead = forward_kernel(
        text_ctx, image_ctx, text_in, image_in,
        (co_text_out, co_image_out, text_up, text_down, image_up, image_down,
         text_qkv, text_self_blocks, image_self_qkv, image_self_out),
        others, (text_gains, text_shifts, image_gains, image_shifts),
        text_grad_out, image_grad_out, lengths, regions, text_local, image_local, self_bits,
    )
    widths = (text_in.shape[1], image_in.shape[1])
    orders = (
        lambda bits: list(range(bits)),
        lambda bits: ([1, 0] + list(range(2, bits)))[:bits],
    )

    def split_of(text_shares, image_shares):
        return tuple(
            Split(group_count, width, sort, shares, text_shares == 2)
            for width, sort, shares in zip(widths, orders, (text_shares, image_shares))
        )

    splits, self_splits, feed_splits = split_of(1, 1), split_of(2, 1), split_of(1, 2)
    gains = (text_gains, image_gains)
    first_back = self_back_kernel(
        ahead, image_self_qkv, image_self_out, text_qkv, text_self_blocks, gains, self_splits
    )
    second_back = feed_back_kernel(
        first_back, ahead, (text_up, image_up), (text_down, image_down), others,
        (text_ctx, image_ctx), (co_text_out, co_image_out), gains, self_splits, feed_splits,
    )
    norms = [
        [stage[key + tag] for key in ("gain_", "shift_") for stage in (second_back, first_back, ahead)]
        for tag in "ti"
    ]
    last_back = co_back_kernel(
        (second_back["back_t"], second_back["back_i"]),
        (second_back["cg_t"].reshape(captions, CAP_LEN, -1), second_back["cg_i"]),
        (front["all_t"], front["all_i"]), (front["co_t"], front["co_i"]),
        (front["cshare_t"], front["cshare_i"]), (co_text_qkv, co_image_qkv),
        (second_back["out_grad_t"], second_back["out_grad_i"]),
        (second_back["fstack_t"], second_back["fstack_i"]),
        norms, order, inverse, splits, feed_splits, co_local, group_count,
    )

    def over_groups(summed, split):
        if not split.fast:
            summed = lax.psum_scatter(summed, "dp", scatter_dimension=0, tiled=True)
        return summed

    sums = [
        [
            over_groups(last_back["qkv_sum_" + tag], split),
            over_groups(last_back["out_sum_" + tag], split),
            over_groups(second_back["self_sum_" + tag], split),
            over_groups(last_back["feed_sum_" + tag], split),
        ]
        for tag, split in zip("ti", splits)
    ]
    finish = finish_kernel if all(split.fast for split in splits) else finish_plain
    outs = finish(
        sums,
        (last_back["norm_t"], last_back["norm_i"]),
        (ahead["result_t"], ahead["result_i"], last_back["in_grad_t"], last_back["in_grad_i"]),
    )
    text_grads, image_grads, norm_grads, kept = outs[:6], outs[6:12], outs[12:16], outs[16:]
    return (
        *kept,
        text_grads[0],
        image_grads[0],
        text_grads[1].T,
        image_grads[1],
        text_grads[4],
        text_grads[5].T,
        image_grads[4],
        image_grads[5],
        text_grads[2],
        text_grads[3],
        image_grads[2],
        image_grads[3],
        *norm_grads,
    )


def solution(mesh):
    tokens = P(("dp", "mp"), None)
    stack_in = P(None, None, "mp")
    rows_in = P("mp", None)
    columns_in = P(None, "mp")
    in_specs = (
        tokens, tokens, P("dp"), P("dp", None), P("dp", None),
        stack_in, stack_in, rows_in, rows_in,
        columns_in, rows_in, columns_in, rows_in,
        stack_in, rows_in, stack_in, rows_in,
        P(), P(), P(), P(),
        tokens, tokens,
    )
    stack_out = P(None, "dp", "mp")
    rows_out = P("mp", "dp")
    columns_out = P("dp", "mp")
    norm_out = P(None, ("dp", "mp"))
    out_specs = (
        tokens, tokens, tokens, tokens,
        stack_out, stack_out, rows_out, rows_out,
        columns_out, rows_out, columns_out, rows_out,
        stack_out, rows_out, stack_out, rows_out,
        norm_out, norm_out, norm_out, norm_out,
    )
    return jax.shard_map(
        per_device, mesh=mesh, in_specs=in_specs, out_specs=out_specs, check_vma=False
    )
```

```python
import functools

import jax
import jax.numpy as jnp
from jax import lax
from jax.experimental import pallas as pl
from jax.experimental.pallas import tpu as pltpu
from jax.sharding import PartitionSpec as P

CO_HEADS = 8
TEXT_HEADS = 12
IMAGE_HEADS = 8
CAP_LEN = 64
ROW_LEN = 128
PER_ROW = 4

epsilon = 1e-05
BF = jnp.bfloat16
F32 = jnp.float32
VMEM_LIMIT = 48 * 1024 * 1024


def product(former, latter):
    return jnp.dot(former, latter, preferred_element_type=F32)


def product_tn(former, latter):
    return lax.dot_general(former, latter, (((0,), (0,)), ((), ())), preferred_element_type=F32)


def product_nt(former, latter):
    return lax.dot_general(former, latter, (((1,), (1,)), ((), ())), preferred_element_type=F32)


GELU_A = 0.7978845608028654
GELU_B = 0.044715


def softmax_block(scores, mask):
    scores = jnp.where(mask, scores, -1000000000.0)
    exponent = jnp.exp(scores - jnp.max(scores, axis=-1, keepdims=True))
    return (exponent / jnp.sum(exponent, axis=-1, keepdims=True)).astype(BF)


def attend_back(shares, scaling, queries, keys, values, context_grad):
    wide = shares.astype(F32)
    share_grad = product_nt(context_grad, values)
    inner = jnp.sum(share_grad * wide, axis=-1, keepdims=True)
    score_grad = (wide * (share_grad - inner) * scaling).astype(BF)
    return (
        product(score_grad, keys).astype(BF),
        product_tn(score_grad, queries).astype(BF),
        product_tn(shares, context_grad).astype(BF),
    )


class Layout:
    def __init__(self, bench):
        self.bench = bench
        self.chip = lax.div(lax.axis_index("mp"), 2)

    def turn(self, index, count):
        return lax.rem(index + self.chip * (count // 2), count)

    def length(self, caption):
        lengths = self.bench.lengths
        return lengths[self.turn(caption, lengths.shape[0])]

    def caption_of(self, image):
        order = self.bench.order
        count = order.shape[0]
        return self.turn(order[self.turn(image, count)], count)

    def image_of(self, caption):
        inverse = self.bench.inverse
        count = inverse.shape[0]
        return self.turn(inverse[self.turn(caption, count)], count)

    def ends(self, row):
        regions = self.bench.regions
        place = self.turn(row, regions.shape[1])
        ends = [regions[0, place]]
        for slot in range(1, PER_ROW):
            ends.append(ends[-1] + regions[slot, place])
        return ends


def slot_of(places, ends):
    slot = (places >= ends[0]).astype(jnp.int32)
    for end in ends[1:]:
        slot = slot + (places >= end).astype(jnp.int32)
    return slot


def caption_rows(ref, captions, start, width):
    return jnp.concatenate(
        [ref[caption, :, start : start + width] for caption in captions], axis=0
    )


def co_forward_rows(bench, heads, rows_total):
    text_ref, image_ref = bench.co_t, bench.co_i
    inner = image_ref.shape[1] // 3
    size = inner // heads
    scaling = size ** (-0.5)
    span = PER_ROW * CAP_LEN
    per_step = 2
    layout = Layout(bench)
    text_shares, image_shares = bench.cshare_t, bench.cshare_i
    text_out, image_out = bench.rctx_t, bench.ctx_i

    def step(index, carry):
        for member in range(per_step):
            row = index * per_step + member
            captions = [layout.caption_of(row * PER_ROW + slot) for slot in range(PER_ROW)]
            ends = layout.ends(row)
            lengths = [layout.length(caption) for caption in captions]
            token_slot = lax.broadcasted_iota(jnp.int32, (span, ROW_LEN), 0) // CAP_LEN
            to_image = token_slot == slot_of(
                lax.broadcasted_iota(jnp.int32, (span, ROW_LEN), 1), ends
            )
            spots = lax.broadcasted_iota(jnp.int32, (ROW_LEN, span), 1)
            length = jnp.full((ROW_LEN, span), lengths[0], jnp.int32)
            for slot in range(1, PER_ROW):
                length = jnp.where(spots >= slot * CAP_LEN, lengths[slot], length)
            to_text = (
                slot_of(lax.broadcasted_iota(jnp.int32, (ROW_LEN, span), 0), ends)
                == spots // CAP_LEN
            ) & (spots % CAP_LEN < length)
            rows = pl.ds(pl.multiple_of(row * ROW_LEN, ROW_LEN), ROW_LEN)
            texts = pl.ds(row * PER_ROW, PER_ROW)
            for head in range(heads):
                text = [
                    caption_rows(text_ref, captions, part * inner + head * size, size)
                    for part in range(3)
                ]
                image = [
                    image_ref[rows, part * inner + head * size : part * inner + (head + 1) * size]
                    for part in range(3)
                ]
                lanes = slice(head * size, (head + 1) * size)
                shares = softmax_block(product_nt(text[0], image[1]) * scaling, to_image)
                text_shares[row, head] = shares
                text_out[texts, :, lanes] = (
                    product(shares, image[2]).astype(BF).reshape(PER_ROW, CAP_LEN, size)
                )
                shares = softmax_block(product_nt(image[0], text[1]) * scaling, to_text)
                image_shares[row, head] = shares
                image_out[rows, lanes] = product(shares, text[2]).astype(BF)
        return carry

    lax.fori_loop(0, rows_total // per_step, step, 0)


def co_backward_rows(bench, heads, first_row, last_row):
    text_ref, image_ref = bench.co_t, bench.co_i
    inner = image_ref.shape[1] // 3
    size = inner // heads
    scaling = size ** (-0.5)
    span = PER_ROW * CAP_LEN
    per_step = 2
    layout = Layout(bench)
    text_shares, image_shares = bench.cshare_t, bench.cshare_i
    text_grad, image_grad = bench.cg_t, bench.cg_i
    text_out, image_out = bench.rgrad_t, bench.grad_i

    def step(index, carry):
        for member in range(per_step):
            row = index * per_step + member
            captions = [layout.caption_of(row * PER_ROW + slot) for slot in range(PER_ROW)]
            rows = pl.ds(pl.multiple_of(row * ROW_LEN, ROW_LEN), ROW_LEN)
            texts = pl.ds(row * PER_ROW, PER_ROW)
            for head in range(heads):
                text = [
                    caption_rows(text_ref, captions, part * inner + head * size, size)
                    for part in range(3)
                ]
                image = [
                    image_ref[rows, part * inner + head * size : part * inner + (head + 1) * size]
                    for part in range(3)
                ]
                text_q, image_k, image_v = attend_back(
                    text_shares[row, head], scaling, text[0], image[1], image[2],
                    caption_rows(text_grad, captions, head * size, size),
                )
                image_q, text_k, text_v = attend_back(
                    image_shares[row, head], scaling, image[0], text[1], text[2],
                    image_grad[rows, head * size : (head + 1) * size],
                )
                for part, grad in enumerate((text_q, text_k, text_v)):
                    at = part * inner + head * size
                    text_out[texts, :, at : at + size] = grad.reshape(PER_ROW, CAP_LEN, size)
                for part, grad in enumerate((image_q, image_k, image_v)):
                    at = part * inner + head * size
                    image_out[rows, at : at + size] = grad
        return carry

    lax.fori_loop(first_row // per_step, last_row // per_step, step, 0)


def in_caption_order(bench, source, target):
    layout = Layout(bench)
    for caption in range(source.shape[0]):
        rows = slice(caption * CAP_LEN, (caption + 1) * CAP_LEN)
        target[rows, :] = source[layout.image_of(caption)]


def self_mask_text(layout, block):
    shape = (2 * CAP_LEN, 2 * CAP_LEN)
    queries = lax.broadcasted_iota(jnp.int32, shape, 0)
    spots = lax.broadcasted_iota(jnp.int32, shape, 1)
    length = jnp.where(
        spots >= CAP_LEN, layout.length(block * 2 + 1) + CAP_LEN, layout.length(block * 2)
    )
    return (queries // CAP_LEN == spots // CAP_LEN) & (spots < length)


def self_mask_image(layout, row):
    ends = layout.ends(row)
    shape = (ROW_LEN, ROW_LEN)
    return slot_of(lax.broadcasted_iota(jnp.int32, shape, 0), ends) == slot_of(
        lax.broadcasted_iota(jnp.int32, shape, 1), ends
    )


def shape_of(shape, dtype=BF):
    return jax.ShapeDtypeStruct(shape, dtype)


def cost(flops, moved, exps):
    return pl.CostEstimate(flops=int(flops), bytes_accessed=int(moved), transcendentals=int(exps))


MESH = pl.DeviceIdType.MESH
BIG_LIMIT = 60 * 1024 * 1024


class Bench:
    def __init__(self, refs, fetched, flushed, counts):
        self.refs = refs
        self.fetches = {}
        self.flushes = []
        self.flush_index = {name: i for i, name in enumerate(flushed)}
        self.copies = 0
        self.waiting = []
        for index, (name, stage) in enumerate(fetched.items()):
            copy = pltpu.make_async_copy(
                refs["src " + name], refs[name], refs["fetch_sems"].at[index]
            )
            self.fetches[name] = copy
            self.waiting.append((stage, copy))
        self.release(0)

    def release(self, stage):
        for due, copy in self.waiting:
            if due <= stage:
                copy.start()
        self.waiting = [(due, copy) for due, copy in self.waiting if due > stage]

    def __getattr__(self, name):
        fetches = self.__dict__["fetches"]
        if name in fetches:
            copy = fetches.pop(name)
            if any(copy is late for _, late in self.waiting):
                copy.start()
                self.waiting = [pair for pair in self.waiting if pair[1] is not copy]
            copy.wait()
        return self.__dict__["refs"][name]

    def flush(self, *names):
        for name in names:
            copy = pltpu.make_async_copy(
                self.refs[name],
                self.refs["dst " + name],
                self.refs["flush_sems"].at[self.flush_index.pop(name)],
            )
            copy.start()
            self.flushes.append(copy)

    def remote(self, source, target, peer):
        index = self.copies
        assert index < self.refs["send_sems"].shape[0]
        self.copies += 1
        return pltpu.make_async_remote_copy(
            src_ref=source,
            dst_ref=target,
            send_sem=self.refs["send_sems"].at[index],
            recv_sem=self.refs["recv_sems"].at[index],
            device_id=peer,
            device_id_type=MESH,
        )

    def close(self):
        for name in list(self.fetches):
            getattr(self, name)
        for name in list(self.flush_index):
            self.flush(name)
        for copy in self.flushes:
            copy.wait()


def exchange_kernel(body, name, collective, peers, inputs, outputs, scratch, copies, work):
    fetched = {
        key: int(kind[3:] or 0) for key, (_, kind) in inputs.items() if kind.startswith("hbm")
    }
    inputs = {key: (array, kind[:3] if key in fetched else kind)
              for key, (array, kind) in inputs.items()}
    flushed = [key for key, (_, _, kind) in outputs.items() if kind == "hbm"]
    spaces = {"hbm": pl.ANY, "vmem": pltpu.VMEM, "smem": pltpu.SMEM}
    names = [("src " + key if kind == "hbm" else key) for key, (_, kind) in inputs.items()]
    names += [("dst " + key if kind == "hbm" else key) for key, (_, _, kind) in outputs.items()]
    shapes = []
    for key in fetched:
        names.append(key)
        shapes.append(pltpu.VMEM(inputs[key][0].shape, inputs[key][0].dtype))
    for key in flushed:
        names.append(key)
        shapes.append(pltpu.VMEM(outputs[key][0], outputs[key][1]))
    for key, (shape, dtype) in scratch.items():
        names.append(key)
        shapes.append(pltpu.VMEM(shape, dtype))
    for key, count in (
        ("fetch_sems", len(fetched)), ("flush_sems", len(flushed)),
        ("send_sems", copies), ("recv_sems", copies),
    ):
        names.append(key)
        shapes.append(pltpu.SemaphoreType.DMA((max(count, 1),)))

    def kernel(*refs):
        bench = Bench(dict(zip(names, refs)), fetched, flushed, copies)
        barrier = pltpu.get_barrier_semaphore()
        partners = peers()
        for partner in partners:
            pl.semaphore_signal(barrier, inc=1, device_id=partner, device_id_type=MESH)
        pl.semaphore_wait(barrier, len(partners))
        body(bench)
        bench.close()

    flops, moved, exps = work
    results = pl.pallas_call(
        kernel,
        in_specs=[pl.BlockSpec(memory_space=spaces[kind]) for _, kind in inputs.values()],
        out_specs=[pl.BlockSpec(memory_space=spaces[kind]) for _, _, kind in outputs.values()],
        out_shape=[shape_of(shape, dtype) for shape, dtype, _ in outputs.values()],
        scratch_shapes=shapes,
        compiler_params=pltpu.CompilerParams(
            collective_id=collective, has_side_effects=True, vmem_limit_bytes=BIG_LIMIT
        ),
        cost_estimate=cost(flops, moved, exps),
        name=name,
    )(*[array for array, _ in inputs.values()])
    return dict(zip(outputs, results))


def group_peers():
    spot = lax.axis_index("mp")
    core = lax.rem(spot, 2)
    chip = lax.div(spot, 2)
    return core, {"mp": spot + 1 - 2 * core}, {"mp": spot + 2 - 4 * chip}


class Gather:
    def __init__(self, bench, rows):
        self.bench = bench
        self.rows = rows
        self.core, self.core_peer, self.chip_peer = group_peers()
        self.other = 1 - self.core

    def place(self, half, core):
        step = self.rows & -self.rows
        return pl.ds(pl.multiple_of((2 * half + core) * self.rows, step), self.rows)

    def gather(self, full):
        own = full.at[self.place(0, self.core)]
        far = full.at[self.place(1, self.core)]
        self.across = self.bench.remote(own, far, self.chip_peer)
        self.near = self.bench.remote(own, own, self.core_peer)
        self.relay = self.bench.remote(far, far, self.core_peer)
        self.across.start()
        self.near.start()

    def arrive(self, half, project):
        if half == 0:
            project(0, self.core)
            self.near.wait_recv()
            project(0, self.other)
        else:
            self.across.wait_recv()
            self.relay.start()
            project(1, self.core)
            self.relay.wait_recv()
            project(1, self.other)

    def finish_gather(self):
        self.across.wait_send()
        self.near.wait_send()
        self.relay.wait_send()


class Stream(Gather):
    def __init__(self, bench, tag, rows):
        super().__init__(bench, rows)
        for key in ("give", "got", "send", "recv", "acc"):
            setattr(self, key, getattr(bench, tag + "_" + key))

    def open_sum(self):
        self.hand = [
            self.bench.remote(self.give.at[half], self.got.at[half], self.core_peer)
            for half in (0, 1)
        ]
        self.post = self.bench.remote(self.send, self.recv, self.chip_peer)

    def partial(self, half, output):
        self.give[half] = output(half, self.other).astype(BF)
        self.hand[half].start()
        self.acc[half] = output(half, self.core)
        if half == 1:
            self.hand[1].wait_recv()
            self.send[...] = (self.acc[1] + self.got[1].astype(F32)).astype(BF)
            self.post.start()

    def settle(self, gathered=True):
        self.hand[0].wait_recv()
        self.post.wait_recv()
        self.hand[0].wait_send()
        self.hand[1].wait_send()
        self.post.wait_send()
        if gathered:
            self.finish_gather()

    def piece(self, rows):
        return self.acc[0, rows] + self.got[0, rows].astype(F32) + self.recv[rows].astype(F32)


class Near(Gather):
    def __init__(self, bench, tag, rows):
        super().__init__(bench, rows)
        for key in ("give", "got", "acc"):
            setattr(self, key, getattr(bench, tag + "_" + key))

    def gather(self, full):
        own = full.at[self.place(0, self.core)]
        self.near = self.bench.remote(own, own, self.core_peer)
        self.near.start()

    def open_sum(self):
        self.hand = self.bench.remote(self.give.at[0], self.got.at[0], self.core_peer)

    def partial(self, half, output):
        self.give[0] = output(0, self.other).astype(BF)
        self.hand.start()
        self.acc[0] = output(0, self.core)

    def settle(self):
        self.hand.wait_recv()
        self.hand.wait_send()
        self.near.wait_send()

    def piece(self, rows):
        return self.acc[0, rows] + self.got[0, rows].astype(F32)


class Weights:
    def __init__(self, bench, own, other, bits):
        self.bench, self.other, self.left = bench, other, list(bits)
        self.names = sorted(bits, reverse=True)
        self.lead = len(own.shape) - 2 - len(self.names)
        self.free = []
        self.copy = bench.remote(
            own.at[self.held()], other.at[self.held()], group_peers()[2]
        )
        self.copy.start()
        self.pending = True

    def held(self):
        kept = [slice(None) if bit in self.free else dp_peer(bit)[0] for bit in self.names]
        return (slice(None),) * self.lead + tuple(kept) + (slice(None), slice(None))

    def advance(self):
        if not self.pending:
            return
        self.copy.wait()
        self.pending = bool(self.left)
        if self.left:
            bit = self.left.pop(0)
            place = self.other.at[self.held()]
            self.copy = self.bench.remote(place, place, dp_peer(bit)[1])
            self.copy.start()
            self.free.append(bit)

    def finish(self):
        while self.pending:
            self.advance()


CHUNK = 32


def chunks(count, step, start):
    def once(index, carry):
        return step(pl.ds(pl.multiple_of(index * CHUNK, CHUNK), CHUNK), carry)

    return lax.fori_loop(0, count // CHUNK, once, start)


def folded(values):
    return jnp.sum(values.reshape(CHUNK // 8, 8, values.shape[-1]), axis=0)


def stream_scratch(tag, rows, width, halves=2):
    kinds = {
        tag + "_give": ((halves, rows, width), BF),
        tag + "_got": ((halves, rows, width), BF),
        tag + "_acc": ((halves, rows, width), F32),
    }
    if halves == 2:
        kinds[tag + "_send"] = ((rows, width), BF)
        kinds[tag + "_recv"] = ((rows, width), BF)
    return kinds


def at_offset(ref, offset, rows):
    return ref.at[pl.ds(pl.multiple_of(offset + rows.start, CHUNK), rows.size)]


def attend_many(parts_ref, share_ref, context_ref, base, first_block, blocks, heads, masker):
    inner = parts_ref.shape[1] // 3
    size = inner // heads
    scaling = size ** (-0.5)
    rows = [
        pl.ds(pl.multiple_of(base + block * ROW_LEN, CHUNK), ROW_LEN) for block in range(blocks)
    ]
    masks = [masker(first_block + block) for block in range(blocks)]
    scores = []
    for block in range(blocks):
        for head in range(heads):
            queries = parts_ref[rows[block], head * size : (head + 1) * size]
            keys = parts_ref[rows[block], inner + head * size : inner + (head + 1) * size]
            scores.append(jnp.where(masks[block], product_nt(queries, keys) * scaling, -1e9))
    scores = jnp.concatenate(scores, axis=0)
    exponent = jnp.exp(scores - jnp.max(scores, axis=-1, keepdims=True))
    shares = (exponent / jnp.sum(exponent, axis=-1, keepdims=True)).astype(BF)
    for block in range(blocks):
        contexts = []
        for head in range(heads):
            at = (block * heads + head) * ROW_LEN
            piece = shares[at : at + ROW_LEN]
            share_ref[first_block + block, head] = piece
            values = parts_ref[rows[block], 2 * inner + head * size : 2 * inner + (head + 1) * size]
            contexts.append(product(piece, values).astype(BF))
        context_ref[rows[block], :] = jnp.concatenate(contexts, axis=1)


def norm_chunk(values, gain, shift):
    centre = values - jnp.mean(values, axis=-1, keepdims=True)
    spread = jnp.mean(centre * centre, axis=-1, keepdims=True)
    return centre * lax.rsqrt(spread + epsilon) * gain + shift


def feed_forward(stream, full, ups, downs, act, slope):
    width = ups[0].shape[1]

    def project(half, core):
        place = stream.place(half, core)
        for share, up in enumerate(ups):
            lanes = slice(share * width, (share + 1) * width)
            pre = product(full[place], up[...])
            bent = jnp.tanh(GELU_A * (pre + GELU_B * pre * pre * pre))
            act[place, lanes] = (0.5 * pre * (1.0 + bent)).astype(BF)
            slope[place, lanes] = (
                0.5 * (1.0 + bent)
                + 0.5 * pre * (1.0 - bent * bent) * GELU_A * (1.0 + 3.0 * GELU_B * pre * pre)
            ).astype(BF)

    def output(half, core):
        place = stream.place(half, core)
        total = product(act[place, :width], downs[0][...])
        for share, down in enumerate(downs[1:], 1):
            total = total + product(act[place, share * width : (share + 1) * width], down[...])
        return total

    return project, output


def flat(ref, *lead):
    value = ref[lead] if lead else ref[...]
    return value.reshape(-1, value.shape[-1])


def forward_kernel(ctx_t, ctx_i, text_in, image_in, weights, others, norms, text_g, image_g,
                   lengths, regions, text_local, image_local, bits):
    (co_text_out, co_image_out, text_up, text_down, image_up, image_down,
     text_qkv, text_self_out, image_qkv, image_self_out) = weights
    n_t, d_t = text_in.shape
    n_i, d_i = image_in.shape
    ff_t, ff_i = text_up.shape[1], image_up.shape[1]
    in_t, in_i = ctx_inner(text_self_out), image_self_out.shape[0]
    inputs = {
        "lengths": (lengths, "smem"), "regions": (regions, "smem"),
        "gains_t": (norms[0], "hbm"), "shifts_t": (norms[1], "hbm"),
        "gains_i": (norms[2], "hbm"), "shifts_i": (norms[3], "hbm"),
        "ctx_t": (ctx_t, "hbm"), "w_co_t": (co_text_out, "hbm"),
        "ctx_i": (ctx_i, "hbm"), "w_co_i": (co_image_out, "hbm"),
        "qkv_t": (text_qkv, "hbm1"), "so_t": (text_self_out, "hbm1"),
        "x_t": (text_in, "hbm1"), "x_i": (image_in, "hbm1"),
        "up_t": (text_up, "hbm1"), "down_t": (text_down, "hbm1"),
        "up_i": (image_up, "hbm2"), "down_i": (image_down, "hbm2"),
        "upo_i": (others[0], "hbm2"), "downo_i": (others[1], "hbm2"),
        "qkv_i": (image_qkv, "hbm2"), "so_i": (image_self_out, "hbm2"),
        "g_i": (image_g, "hbm2"), "g_t": (text_g, "hbm2"),
    }
    outputs = {
        "mlp_t": ((4 * n_t, d_t), BF, "hbm"), "mlp_i": ((2 * n_i, d_i), BF, "hbm"),
        "act_t": ((4 * n_t, ff_t), BF, "hbm"), "act_i": ((2 * n_i, 2 * ff_i), BF, "hbm"),
        "slope_t": ((4 * n_t, ff_t), BF, "hbm"), "slope_i": ((2 * n_i, 2 * ff_i), BF, "hbm"),
        "self_t": ((2 * n_t, d_t), BF, "hbm"), "self_i": ((4 * n_i, d_i), BF, "hbm"),
        "parts_i": ((4 * n_i, 3 * in_i), BF, "hbm"),
        "share_i": ((4 * n_i // ROW_LEN, image_local, ROW_LEN, ROW_LEN), BF, "hbm"),
        "ctx2_i": ((4 * n_i, in_i), BF, "hbm"),
        "qkvo_t": (text_qkv.shape, BF, "hbm"), "soo_t": (text_self_out.shape, BF, "hbm"),
    }
    for share in "01":
        outputs["parts%s_t" % share] = ((2 * n_t, 3 * in_t), BF, "hbm")
        outputs["share%s_t" % share] = (
            (2 * n_t // ROW_LEN, text_local, ROW_LEN, ROW_LEN), BF, "hbm"
        )
        outputs["ctx2%s_t" % share] = ((2 * n_t, in_t), BF, "hbm")
    scratch = {}
    for tag, n, d in (("t", n_t, d_t), ("i", n_i, d_i)):
        outputs.update({
            "zero_" + tag: ((n, d), F32, "hbm"),
            "mid_" + tag: ((n, d), F32, "hbm"),
            "late_" + tag: ((n, d), F32, "hbm"),
            "result_" + tag: ((n, d), BF, "hbm"),
            "gain_" + tag: ((8, d), F32, "hbm"),
            "shift_" + tag: ((8, d), F32, "hbm"),
        })
        scratch.update(stream_scratch(tag, n, d))
        scratch["first_" + tag] = ((n, d), F32)

    def body(bench):
        wide = {tag: Stream(bench, tag, n) for tag, n in (("t", n_t), ("i", n_i))}
        near = {tag: Near(bench, tag, n) for tag, n in (("t", n_t), ("i", n_i))}
        get = lambda key, tag: getattr(bench, key + "_" + tag)

        for tag, stream in wide.items():
            context, weight = get("ctx", tag), get("w_co", tag)
            output = lambda half, core: product(context[stream.place(half, core)], weight[...])
            stream.open_sum()
            stream.partial(1, output)
            bench.release(1)
            stream.partial(0, output)
        bench.release(2)

        def settle(tag, stage, source, kept, resid, full, before, after):
            gain = get("gains", tag)[stage : stage + 1]
            shift = get("shifts", tag)[stage : stage + 1]
            base = after.core * after.rows

            def step(rows, carry):
                values = source[rows].astype(F32) + before.piece(rows)
                kept[rows] = values
                normed = norm_chunk(values, gain, shift)
                resid[rows] = normed
                at_offset(full, base, rows)[...] = normed.astype(BF)
                return carry

            chunks(after.rows, step, 0)
            after.gather(full)

        def first_norm(tag, after):
            wide[tag].settle(gathered=False)
            settle(
                tag, 0, get("x", tag), get("zero", tag), get("first", tag), get("mlp", tag),
                wide[tag], after,
            )
            bench.flush("zero_" + tag)

        first_norm("t", wide["t"])
        fetches = [
            Weights(bench, bench.qkv_t, bench.qkvo_t, bits),
            Weights(bench, bench.so_t, bench.soo_t, bits),
        ]
        text_feed = feed_forward(
            wide["t"], bench.mlp_t, [bench.up_t], [bench.down_t], bench.act_t, bench.slope_t
        )
        wide["t"].open_sum()
        wide["t"].arrive(0, text_feed[0])
        wide["t"].partial(0, text_feed[1])
        first_norm("i", near["i"])
        image_feed = feed_forward(
            near["i"], bench.mlp_i, [bench.up_i, bench.upo_i], [bench.down_i, bench.downo_i],
            bench.act_i, bench.slope_i,
        )
        near["i"].open_sum()
        near["i"].arrive(0, image_feed[0])
        near["i"].partial(0, image_feed[1])
        near["i"].settle()
        settle(
            "i", 1, bench.first_i, bench.mid_i, bench.first_i, bench.self_i, near["i"], wide["i"]
        )
        bench.flush("mid_i", "mlp_i", "act_i", "slope_i")
        for fetch in fetches:
            fetch.advance()

        stream_i = wide["i"]

        def project_image(half, core):
            place = stream_i.place(half, core)
            project_three(bench.self_i[place], bench.qkv_i, bench.parts_i, place)

        def middle(half):
            blocks = 2 * n_i // ROW_LEN
            attend_many(
                bench.parts_i, bench.share_i, bench.ctx2_i, 2 * half * n_i, half * blocks, blocks,
                image_local, functools.partial(self_mask_image, Layout(bench)),
            )

        def output_image(half, core):
            return product(bench.ctx2_i[stream_i.place(half, core)], bench.so_i[...])

        stream_i.open_sum()
        stream_i.arrive(0, project_image)
        middle(0)
        stream_i.partial(0, output_image)
        wide["t"].arrive(1, text_feed[0])
        wide["t"].partial(1, text_feed[1])
        for fetch in fetches:
            fetch.advance()
        stream_i.arrive(1, project_image)
        middle(1)
        stream_i.partial(1, output_image)
        bench.flush("act_t", "slope_t", "self_i", "parts_i", "share_i", "ctx2_i")
        for fetch in fetches:
            fetch.finish()
        bench.flush("qkvo_t", "soo_t")

        wide["t"].settle()
        settle(
            "t", 1, bench.first_t, bench.mid_t, bench.first_t, bench.self_t, wide["t"], near["t"]
        )
        bench.flush("mid_t", "mlp_t")
        stream_t = near["t"]
        shares = [
            (bench.qkv_t, bench.so_t, bench.parts0_t, bench.share0_t, bench.ctx20_t),
            (bench.qkvo_t, bench.soo_t, bench.parts1_t, bench.share1_t, bench.ctx21_t),
        ]

        def project_text(half, core):
            place = stream_t.place(half, core)
            for qkv, _, parts, share, context in shares:
                rows = bench.self_t[place]
                for part in range(3):
                    parts[place, part * in_t : (part + 1) * in_t] = product_nt(
                        rows, flat(qkv, part)
                    ).astype(BF)
                attend_many(
                    parts, share, context, core * n_t, core * (n_t // ROW_LEN), n_t // ROW_LEN,
                    text_local, functools.partial(self_mask_text, Layout(bench)),
                )

        def output_text(half, core):
            place = stream_t.place(half, core)
            return product(shares[0][4][place], flat(shares[0][1])) + product(
                shares[1][4][place], flat(shares[1][1])
            )

        stream_t.open_sum()
        stream_t.arrive(0, project_text)
        stream_t.partial(0, output_text)
        for share in "01":
            bench.flush("parts%s_t" % share, "share%s_t" % share, "ctx2%s_t" % share)
        bench.flush("self_t")

        for tag, stream in (("i", wide["i"]), ("t", near["t"])):
            stream.settle()
            gain, shift = get("gains", tag)[2:3], get("shifts", tag)[2:3]
            second, result, late, grad = (
                get("first", tag), get("result", tag), get("late", tag), get("g", tag)
            )
            width = second.shape[1]

            def step(rows, carry):
                values = second[rows] + stream.piece(rows)
                back, normed, gains, shifts = norm_pull(values, gain, shift, grad[rows].astype(F32))
                result[rows] = normed.astype(BF)
                late[rows] = back
                return carry[0] + gains, carry[1] + shifts

            start = jnp.zeros((8, width), F32)
            gains, shifts = chunks(stream.rows, step, (start, start))
            get("gain", tag)[...] = gains
            get("shift", tag)[...] = shifts
            bench.flush("result_" + tag, "late_" + tag)

    return exchange_kernel(
        body, "forward_tail", 1,
        lambda: list(group_peers()[1:]) + [dp_peer(bit)[1] for bit in bits],
        inputs, outputs, scratch, 40, (15e9, 40e6, 1e6),
    )


def ctx_inner(out_weight):
    rows = 1
    for size in out_weight.shape[:-1]:
        rows *= size
    return rows


def norm_pull(values, gain, shift, gradient):
    centre = values - jnp.mean(values, axis=-1, keepdims=True)
    spread = jnp.mean(centre * centre, axis=-1, keepdims=True)
    inverse = lax.rsqrt(spread + epsilon)
    unit = centre * inverse
    scaled = gradient * gain
    back = inverse * (
        scaled
        - jnp.mean(scaled, axis=-1, keepdims=True)
        - unit * jnp.mean(scaled * unit, axis=-1, keepdims=True)
    )
    return back, unit * gain + shift, folded(gradient * unit), folded(gradient)


def attend_back_many(parts_ref, share_ref, grads, out_ref, base, first_block, blocks, heads):
    inner = parts_ref.shape[1] // 3
    size = inner // heads
    scaling = size ** (-0.5)
    rows = [
        pl.ds(pl.multiple_of(base + block * ROW_LEN, CHUNK), ROW_LEN) for block in range(blocks)
    ]
    context_grads = [grads(block) for block in range(blocks)]
    pairs = [(block, head) for block in range(blocks) for head in range(heads)]

    def piece(part, block, head):
        at = part * inner + head * size
        return parts_ref[rows[block], at : at + size]

    def grad_of(block, head):
        return context_grads[block][:, head * size : (head + 1) * size]

    narrow = [share_ref[first_block + block, head] for block, head in pairs]
    shares = jnp.concatenate(narrow, axis=0).astype(F32)
    share_grad = jnp.concatenate(
        [product_nt(grad_of(*pair), piece(2, *pair)) for pair in pairs], axis=0
    )
    total = jnp.sum(share_grad * shares, axis=-1, keepdims=True)
    score_grad = (shares * (share_grad - total) * scaling).astype(BF)
    for block in range(blocks):
        pieces = [[], [], []]
        for head in range(heads):
            index = block * heads + head
            scores = score_grad[index * ROW_LEN : (index + 1) * ROW_LEN]
            pieces[0].append(product(scores, piece(1, block, head)).astype(BF))
            pieces[1].append(product_tn(scores, piece(0, block, head)).astype(BF))
            pieces[2].append(product_tn(narrow[index], grad_of(block, head)).astype(BF))
        out_ref[rows[block], :] = jnp.concatenate(pieces[0] + pieces[1] + pieces[2], axis=1)


class Split:
    def __init__(self, group_count, rows, order, shares=1, across=0):
        bits = group_count.bit_length() - 1
        ready = group_count == 1 << bits and (rows // group_count) % 32 == 0
        self.fast = ready and group_count > 1
        self.groups = group_count if self.fast else 1
        self.blocks = self.groups * shares
        self.part = rows // self.groups
        self.order = order(bits) if self.fast else []
        if shares == 2:
            at = min(across, len(self.order))
            self.order = self.order[:at] + ["y"] + self.order[at:]

    def position(self, block, share=0):
        spot = 0
        for bit in self.order:
            spot = 2 * spot + (share if bit == "y" else (block >> bit) & 1)
        return spot

    def shape(self, columns):
        return (self.blocks, self.part, columns)

    def spare(self, columns):
        return (max(self.blocks - 1, 1), self.part, columns)


def dp_peer(bit):
    if bit == "y":
        return 0, group_peers()[2]
    place = lax.axis_index("dp")
    value = lax.rem(lax.div(place, 1 << bit), 2)
    return value, {"dp": place + (1 << bit) * (1 - 2 * value)}


def dp_peers(*splits):
    bits = sorted({bit for split in splits for bit in split.order if bit != "y"})
    return [dp_peer(bit)[1] for bit in bits]


class GroupSum:
    def __init__(self, bench, split, key, spare, first=0, last=None, columns=slice(None),
                 source=None):
        self.bench, self.split, self.key, self.spare = bench, split, key, spare
        self.source = source
        self.columns = columns
        self.base = 0
        self.size = split.blocks
        self.at = 0
        self.left = list(split.order)[first:last]
        self.pending = False
        for bit in split.order[:first]:
            self.size //= 2
            self.base = self.base + dp_peer(bit)[0] * self.size

    @property
    def stack(self):
        return getattr(self.bench, self.key)

    def start(self):
        if not self.left:
            return
        value, peer = dp_peer(self.left.pop(0))
        self.size //= 2
        given = self.base + (1 - value) * self.size
        self.base = self.base + value * self.size
        source, self.source = self.source, None
        self.copy = self.bench.remote(
            (self.stack if source is None else source).at[pl.ds(given, self.size), :, self.columns],
            self.spare.at[pl.ds(self.at, self.size), :, self.columns],
            peer,
        )
        self.copy.start()
        self.pending = True

    def advance(self):
        if not self.pending:
            return
        self.copy.wait_recv()
        self.copy.wait_send()
        self.pending = False

        stack = self.stack

        def add(index, carry):
            mine = self.base + index
            stack[mine, :, self.columns] = (
                stack[mine, :, self.columns].astype(F32)
                + self.spare[self.at + index, :, self.columns].astype(F32)
            ).astype(BF)
            return carry

        lax.fori_loop(0, self.size, add, 0)
        self.at += self.size
        self.start()

    def drain(self):
        while self.pending:
            self.advance()

    def finish(self, out):
        self.drain()
        out[:, self.columns] = self.stack[self.base, :, self.columns]


def weight_grad(split, stack, column, left, right, share=0):
    rows, width = left.shape[1], right.shape[1]
    tile = rows // 2
    for start in (0, tile):
        value = product_tn(left[:, start : start + tile], right).astype(BF)
        lanes = slice(column, column + width)
        if split.groups == 1:
            stack[split.position(0, share), start : start + tile, lanes] = value
            continue
        for index in range(tile // split.part):
            spot = split.position(start // split.part + index, share)
            stack[spot, :, lanes] = value[index * split.part : (index + 1) * split.part]


def project_three(rows, weights, target, place):
    width = weights.shape[2]
    for part in range(3):
        target[place, part * width : (part + 1) * width] = product(rows, weights[part]).astype(BF)


def back_three(grads, place, weights):
    width = weights.shape[2]
    return (
        product_nt(grads[place, :width], weights[0])
        + product_nt(grads[place, width : 2 * width], weights[1])
        + product_nt(grads[place, 2 * width :], weights[2])
    )


def spread(stream, source, full):
    base = stream.core * stream.rows

    def step(rows, carry):
        at_offset(full, base, rows)[...] = source[rows].astype(BF)
        return carry

    chunks(stream.rows, step, 0)
    stream.gather(full)


def settle_back(stream, resid, values, gain, target, gain_out, shift_out, full=None):
    base = stream.core * stream.rows

    def step(rows, carry):
        gradient = resid[rows] + stream.piece(rows)
        back, _, gains, shifts = norm_pull(values[rows], gain, 0.0, gradient)
        target[rows] = back
        if full is not None:
            at_offset(full, base, rows)[...] = back.astype(BF)
        return carry[0] + gains, carry[1] + shifts

    start = jnp.zeros((8, resid.shape[1]), F32)
    gains, shifts = chunks(stream.rows, step, (start, start))
    gain_out[...] = gains
    shift_out[...] = shifts


def self_back_kernel(ahead, image_qkv, image_self_out, text_qkv, text_self_out, gains, splits):
    n_t, d_t = ahead["late_t"].shape
    n_i, d_i = ahead["late_i"].shape
    in_t, in_i = ctx_inner(text_self_out), image_self_out.shape[0]
    hbm = lambda *keys, kind="hbm1": {key: (ahead[key], kind) for key in keys}
    inputs = {"gains_t": (gains[0], "hbm"), "gains_i": (gains[1], "hbm")}
    inputs.update(hbm("late_i", "late_t", kind="hbm"))
    inputs.update({"so_i": (image_self_out, "hbm")})
    inputs.update(hbm("parts_i", "share_i"))
    inputs.update({"so_t": (text_self_out, "hbm1")})
    inputs.update(hbm("soo_t", "parts0_t", "share0_t", "parts1_t", "share1_t"))
    inputs.update({"qkv_i": (image_qkv, "hbm1"), "qkv_t": (text_qkv, "hbm1")})
    inputs.update(hbm("qkvo_t"))
    inputs.update(hbm("self_t", "ctx20_t", "ctx21_t", "mid_t", "self_i", "ctx2_i", "mid_i", kind="hbm2"))
    outputs, scratch = {}, {}
    for index, tag, n, d, inner in ((1, "i", n_i, d_i, in_i), (0, "t", n_t, d_t, in_t)):
        outputs.update({
            "back_" + tag: ((n, d), F32, "hbm"),
            "stack_" + tag: (splits[index].shape(4 * inner), BF, "hbm"),
            "gain_" + tag: ((8, d), F32, "hbm"),
            "shift_" + tag: ((8, d), F32, "hbm"),
        })
    scratch.update(stream_scratch("i", n_i, d_i))
    scratch.update(stream_scratch("t", n_t, d_t, 1))
    scratch.update({
        "full_i": ((4 * n_i, d_i), BF), "full_t": ((2 * n_t, d_t), BF),
        "grad_i": ((4 * n_i, 3 * in_i), BF), "cg_i": ((4 * n_i, in_i), BF),
        "grad0_t": ((2 * n_t, 3 * in_t), BF), "grad1_t": ((2 * n_t, 3 * in_t), BF),
    })
    scratch["spare_t"] = (
        (max(splits[0].blocks // 2, 1),) + splits[0].shape(4 * in_t)[1:], BF
    )
    heads = {"t": ahead["share0_t"].shape[1], "i": ahead["share_i"].shape[1]}

    def body(bench):
        image, text = Stream(bench, "i", n_i), Near(bench, "t", n_t)
        spread(image, bench.late_i, bench.full_i)
        bench.release(1)
        spread(text, bench.late_t, bench.full_t)

        def project_image(half, core):
            place = image.place(half, core)
            bench.cg_i[place] = product_nt(bench.full_i[place], bench.so_i[...]).astype(BF)

        def middle(half):
            blocks = 2 * n_i // ROW_LEN
            base = 2 * half * n_i
            attend_back_many(
                bench.parts_i, bench.share_i,
                lambda block: bench.cg_i[base + block * ROW_LEN : base + (block + 1) * ROW_LEN],
                bench.grad_i, base, half * blocks, blocks, heads["i"],
            )

        def output_image(half, core):
            return back_three(bench.grad_i, image.place(half, core), bench.qkv_i)

        bench.release(2)
        shares = [
            (bench.so_t, bench.qkv_t, bench.parts0_t, bench.share0_t, bench.grad0_t),
            (bench.soo_t, bench.qkvo_t, bench.parts1_t, bench.share1_t, bench.grad1_t),
        ]

        def project_text(half, core):
            place = text.place(half, core)
            blocks = n_t // ROW_LEN
            for out, _, parts, share, grad in shares:
                context_grad = product_nt(bench.full_t[place], flat(out)).astype(BF)
                attend_back_many(
                    parts, share,
                    lambda block: context_grad[block * ROW_LEN : (block + 1) * ROW_LEN],
                    grad, core * n_t, core * blocks, blocks, heads["t"],
                )

        def output_text(half, core):
            place = text.place(half, core)
            total = None
            for _, qkv, _, _, grad in shares:
                for part in range(3):
                    term = product(grad[place, part * in_t : (part + 1) * in_t], flat(qkv, part))
                    total = term if total is None else total + term
            return total

        text.open_sum()
        text.arrive(0, project_text)
        text.partial(0, output_text)
        for share in (0, 1):
            grad, context = shares[share][4], getattr(bench, "ctx2%d_t" % share)
            weight_grad(splits[0], bench.stack_t, 0, bench.self_t, grad[...], share)
            weight_grad(splits[0], bench.stack_t, 3 * in_t, bench.full_t, context[...], share)
        total = GroupSum(bench, splits[0], "stack_t", bench.spare_t, 0, 1)
        total.start()
        image.open_sum()
        for half in (0, 1):
            image.arrive(half, project_image)
            middle(half)
            image.partial(half, output_image)

        def close(index, tag, stream):
            stream.settle()
            get = lambda key: getattr(bench, key + "_" + tag)
            settle_back(
                stream, get("late"), get("mid"), get("gains")[1:2], get("back"), get("gain"),
                get("shift"),
            )
            bench.flush("back_" + tag)

        close(0, "t", text)
        weight_grad(splits[1], bench.stack_i, 0, bench.self_i, bench.grad_i[...])
        weight_grad(splits[1], bench.stack_i, 3 * in_i, bench.full_i, bench.ctx2_i[...])
        bench.flush("stack_i")
        close(1, "i", image)
        total.drain()

    return exchange_kernel(
        body, "self_back", 2,
        lambda: list(group_peers()[1:]) + [dp_peer(bit)[1] for bit in splits[0].order[:1] if bit != "y"],
        inputs, outputs, scratch, 16,
        (12e9, 40e6, 1e6),
    )


def feed_back_kernel(first_back, ahead, ups, downs, others, contexts, co_out, gains, self_splits,
                     splits, co_splits):
    n_t, d_t = first_back["back_t"].shape
    n_i, d_i = first_back["back_i"].shape
    ff = {"t": ups[0].shape[1], "i": ups[1].shape[1]}
    inputs, outputs, scratch = {}, {}, {}
    for index, tag in ((0, "t"), (1, "i")):
        n, d = first_back["back_" + tag].shape
        inner = contexts[index].shape[1]
        own = self_splits[index]
        stack = first_back["stack_" + tag]
        inputs.update({
            "gains_" + tag: (gains[index], "hbm"),
            "mg_" + tag: (first_back["back_" + tag], "hbm"),
            "down_" + tag: (downs[index], "hbm" if tag == "t" else "hbm1"),
            "slope_" + tag: (ahead["slope_" + tag], "hbm1"),
            "up_" + tag: (ups[index], "hbm1"),
        })
        if tag == "i":
            inputs.update({"upo_i": (others[0], "hbm1"), "downo_i": (others[1], "hbm1")})
        inputs.update({
            "stack_" + tag: (stack, "hbm2"),
            "zero_" + tag: (ahead["zero_" + tag], "hbm2"),
            "mlp_" + tag: (ahead["mlp_" + tag], "hbm2"),
            "act_" + tag: (ahead["act_" + tag], "hbm2"),
            "co_" + tag: (co_out[index], "hbm2"),
            "ctx_" + tag: (contexts[index], "hbm2"),
        })
        outputs.update({
            "back_" + tag: ((n, d), F32, "hbm"),
            "cg_" + tag: ((4 * n, inner), BF, "hbm"),
            "out_grad_" + tag: (co_splits[index].shape(inner), BF, "hbm"),
            "gain_" + tag: ((8, d), F32, "hbm"),
            "shift_" + tag: ((8, d), F32, "hbm"),
            "self_sum_" + tag: ((own.part, stack.shape[2]), BF, "hbm"),
            "fstack_" + tag: (splits[index].shape(2 * ff[tag]), BF, "hbm"),
        })
        steps = own.blocks // (2 if tag == "t" else 1)
        scratch["spare_" + tag] = ((max(steps - 1, 1),) + own.shape(stack.shape[2])[1:], BF)
        scratch["fspare_" + tag] = (
            (max(splits[index].blocks // 2, 1),) + splits[index].shape(2 * ff[tag])[1:], BF
        )
        scratch["full2_" + tag] = ((4 * n, d), BF)
    scratch.update(stream_scratch("t", n_t, d_t))
    scratch.update(stream_scratch("i", n_i, d_i, 1))
    scratch.update({
        "full_t": ((4 * n_t, d_t), BF), "full_i": ((2 * n_i, d_i), BF),
        "pre_t": ((4 * n_t, ff["t"]), BF), "pre_i": ((2 * n_i, 2 * ff["i"]), BF),
    })

    def body(bench):
        text, image = Stream(bench, "t", n_t), Near(bench, "i", n_i)
        last = {"t": Gather(bench, n_t), "i": Gather(bench, n_i)}
        get = lambda key, tag: getattr(bench, key + "_" + tag)
        spread(text, bench.mg_t, bench.full_t)
        bench.release(1)
        sums = {
            tag: GroupSum(
                bench, self_splits[index], "stack_" + tag, get("spare", tag),
                1 if tag == "t" else 0, source=bench.refs["src stack_" + tag],
            )
            for index, tag in ((1, "i"), (0, "t"))
        }
        for total in sums.values():
            total.start()
        spread(image, bench.mg_i, bench.full_i)

        def hooks(stream, tag, up_w, down_w):
            full, slope, pre = get("full", tag), get("slope", tag), get("pre", tag)
            width = ff[tag]

            def project(half, core):
                place = stream.place(half, core)
                for share, down in enumerate(down_w):
                    lanes = slice(share * width, (share + 1) * width)
                    grad = product_nt(full[place], down[...])
                    pre[place, lanes] = (grad * slope[place, lanes].astype(F32)).astype(BF)

            def output(half, core):
                place = stream.place(half, core)
                total = product_nt(pre[place, :width], up_w[0][...])
                for share, up in enumerate(up_w[1:], 1):
                    total = total + product_nt(
                        pre[place, share * width : (share + 1) * width], up[...]
                    )
                return total

            return project, output

        text_hooks = hooks(text, "t", [bench.up_t], [bench.down_t])
        text.open_sum()
        text.arrive(0, text_hooks[0])
        text.partial(0, text_hooks[1])
        bench.release(2)
        image_hooks = hooks(
            image, "i", [bench.up_i, bench.upo_i], [bench.down_i, bench.downo_i]
        )
        image.open_sum()
        image.arrive(0, image_hooks[0])
        image.partial(0, image_hooks[1])

        def close(tag, stream):
            stream.settle()
            settle_back(
                stream, get("mg", tag), get("zero", tag), get("gains", tag)[0:1],
                get("back", tag), get("gain", tag), get("shift", tag), get("full2", tag),
            )
            bench.flush("back_" + tag)
            last[tag].gather(get("full2", tag))

        feed_sums = {"t": [], "i": []}

        def feed_grads(index, tag, key, left, right, column):
            stack, width = get("fstack", tag), ff[tag]
            for share in range(1 + index):
                lanes = slice(share * width, (share + 1) * width)
                weight_grad(splits[index], stack, column, left, right[:, lanes], share)
            columns = pl.ds(column, width)
            total = GroupSum(
                bench, splits[index], "fstack_" + tag, get("fspare", tag), 0, 1, columns
            )
            total.start()
            feed_sums[tag].append(total)

        def co_project(tag):
            full, weight, target = get("full2", tag), get("co", tag), get("cg", tag)

            def project(half, core):
                place = last[tag].place(half, core)
                target[place] = product_nt(full[place], weight[...]).astype(BF)

            return project

        close("i", image)
        sums["t"].advance()
        text.arrive(1, text_hooks[0])
        text.partial(1, text_hooks[1])
        sums["i"].advance()
        feed_grads(1, "i", "up", bench.mlp_i, bench.pre_i, 0)
        sums["t"].advance()
        feed_grads(1, "i", "down", bench.full_i, bench.act_i, ff["i"])
        last["i"].arrive(0, co_project("i"))
        feed_grads(0, "t", "up", bench.mlp_t, bench.pre_t, 0)
        sums["t"].finish(bench.self_sum_t)
        bench.flush("self_sum_t")
        feed_grads(0, "t", "down", bench.full_t, bench.act_t, ff["t"])
        close("t", text)
        last["i"].arrive(1, co_project("i"))
        bench.flush("cg_i")
        sums["i"].advance()
        last["t"].arrive(0, co_project("t"))
        weight_grad(co_splits[1], bench.out_grad_i, 0, bench.full2_i, bench.ctx_i[...])
        bench.flush("out_grad_i")
        last["t"].arrive(1, co_project("t"))
        bench.flush("cg_t")
        weight_grad(co_splits[0], bench.out_grad_t, 0, bench.full2_t, bench.ctx_t[...])
        bench.flush("out_grad_t")
        for stream in last.values():
            stream.finish_gather()
        sums["i"].finish(bench.self_sum_i)
        bench.flush("self_sum_i")
        for tag in ("i", "t"):
            for total in feed_sums[tag]:
                total.drain()
            bench.flush("fstack_" + tag)
    return exchange_kernel(
        body, "feed_back", 3,
        lambda: list(group_peers()[1:]) + dp_peers(*self_splits, *splits), inputs, outputs,
        scratch, 40, (12e9, 60e6, 1e6),
    )


def co_front_kernel(shards, weights, feeds, order, inverse, regions, lengths, heads, bits):
    inputs = {
        "order": (order, "smem"), "inverse": (inverse, "smem"),
        "regions": (regions, "smem"), "lengths": (lengths, "smem"),
    }
    outputs, scratch = {}, {}
    for key, weight in zip(("up", "down"), feeds):
        inputs[key + "_i"] = (weight, "hbm")
        outputs[key + "o_i"] = (weight.shape, BF, "hbm")
    for index, tag in ((0, "t"), (1, "i")):
        n, d = shards[index].shape
        width = weights[index].shape[2]
        inputs.update({"x_" + tag: (shards[index], "hbm"), "w_" + tag: (weights[index], "hbm")})
        outputs.update({
            "all_" + tag: ((4 * n, d), BF, "hbm"),
            "co_" + tag: ((4 * n, 3 * width), BF, "hbm"),
            "ctx_" + tag: ((4 * n, width), BF, "hbm"),
        })
    n_t, n_i = shards[0].shape[0], shards[1].shape[0]
    held, width = n_t // CAP_LEN, weights[0].shape[2]
    outputs["co_t"] = ((4 * held, CAP_LEN, 3 * width), BF, "hbm")
    rows = 4 * n_i // ROW_LEN
    span = PER_ROW * CAP_LEN
    outputs["cshare_t"] = ((rows, heads, span, ROW_LEN), BF, "hbm")
    outputs["cshare_i"] = ((rows, heads, ROW_LEN, span), BF, "hbm")
    scratch["rctx_t"] = ((4 * held, CAP_LEN, width), BF)

    def body(bench):
        streams = {tag: Gather(bench, n) for tag, n in (("t", n_t), ("i", n_i))}
        get = lambda key, tag: getattr(bench, key + "_" + tag)
        fetches = [
            Weights(bench, bench.up_i, bench.upo_i, bits),
            Weights(bench, bench.down_i, bench.downo_i, bits[:-2] + bits[:-3:-1]),
        ]
        for tag, stream in streams.items():
            full = get("all", tag)
            full[stream.place(0, stream.core)] = get("x", tag)[...]
            stream.gather(full)
        for half in (0, 1):
            for tag, stream in streams.items():
                full, weight, target = get("all", tag), get("w", tag), get("co", tag)

                def project(half, core):
                    place = stream.place(half, core)
                    if tag == "i":
                        project_three(full[place], weight, target, place)
                        return
                    captions = pl.ds((2 * half + core) * held, held)
                    for part in range(3):
                        target[captions, :, part * width : (part + 1) * width] = (
                            product(full[place], weight[part])
                            .astype(BF)
                            .reshape(held, CAP_LEN, width)
                        )

                stream.arrive(half, project)
            if half == 0:
                for fetch in fetches * len(bits):
                    fetch.advance()
        for tag in streams:
            bench.flush("all_" + tag, "co_" + tag)
        co_forward_rows(bench, heads, rows)
        in_caption_order(bench, bench.rctx_t, bench.ctx_t)
        for fetch in fetches:
            fetch.finish()
        for stream in streams.values():
            stream.finish_gather()

    return exchange_kernel(
        body, "co_front", 5,
        lambda: list(group_peers()[1:]) + [dp_peer(bit)[1] for bit in bits],
        inputs, outputs, scratch, 16,
        (4e9, 20e6, 1e6),
    )


class Total:
    def __init__(self, bench, held, landing, group_count):
        self.bench, self.held, self.landing = bench, held, landing
        self.peers = list(group_peers()[1:]) + [
            dp_peer(bit)[1] for bit in range(group_count.bit_length() - 1)
        ]
        self.step = 0
        self.start()

    def start(self):
        if self.step < len(self.peers):
            self.copy = self.bench.remote(
                self.held.at[self.step], self.landing.at[self.step], self.peers[self.step]
            )
            self.copy.start()

    def advance(self):
        if self.step < len(self.peers):
            self.copy.wait()
            self.held[self.step + 1] = self.held[self.step] + self.landing[self.step]
            self.step += 1
            self.start()

    def finish(self, out):
        while self.step < len(self.peers):
            self.advance()
        out[...] = self.held[self.step]


def co_back_kernel(zero_grad, context_grads, tokens, projected, shares, weights, out_grads,
                   feed_stacks, norms, order, inverse, splits, feed_splits, late_splits, heads,
                   group_count):
    inputs = {"order": (order, "smem"), "inverse": (inverse, "smem")}
    outputs, scratch = {}, {}
    steps = 2 + group_count.bit_length() - 1
    for index, tag in ((1, "i"), (0, "t")):
        n, d = zero_grad[index].shape
        width = projected[index].shape[-1]
        inner = out_grads[index].shape[2]
        split = splits[index]
        feeds = feed_stacks[index].shape[2]
        inputs.update({"norm%d_%s" % (k, tag): (v, "hbm") for k, v in enumerate(norms[index])})
        inputs.update({
            "co_" + tag: (projected[index], "hbm"),
            "cg_" + tag: (context_grads[index], "hbm"),
            "cshare_" + tag: (shares[index], "hbm"),
            "fstack_" + tag: (feed_stacks[index], "hbm1"),
            "ostack_" + tag: (out_grads[index], "hbm1"),
            "x_" + tag: (tokens[index], "hbm1"),
            "w_" + tag: (weights[index], "hbm1"),
            "zg_" + tag: (zero_grad[index], "hbm1"),
        })
        outputs.update({
            "in_grad_" + tag: ((n, d), F32, "hbm"),
            "feed_sum_" + tag: ((split.part, feeds), BF, "hbm"),
            "out_sum_" + tag: ((split.part, inner), BF, "hbm"),
            "qkv_sum_" + tag: ((split.part, width), BF, "hbm"),
            "norm_" + tag: ((8, d), F32, "hbm"),
        })
        scratch.update(stream_scratch(tag, n, d))
        scratch["grad_" + tag] = ((4 * n, width), BF)
        scratch["stack_" + tag] = (split.shape(width), BF)
        scratch["spare_" + tag] = (split.spare(width), BF)
        scratch["fspare_" + tag] = (feed_splits[index].spare(feeds), BF)
        scratch["ospare_" + tag] = (split.spare(inner), BF)
        scratch["held_" + tag] = ((steps + 1, 8, d), F32)
        scratch["landing_" + tag] = ((steps, 8, d), F32)
    n_t, n_i = zero_grad[0].shape[0], zero_grad[1].shape[0]
    scratch["rgrad_t"] = (projected[0].shape, BF)

    def body(bench):
        streams = {tag: Stream(bench, tag, n) for tag, n in (("i", n_i), ("t", n_t))}
        get = lambda key, tag: getattr(bench, key + "_" + tag)
        feeds, outs, late, totals = {}, {}, {}, {}
        for index, tag in ((0, "t"), (1, "i")):
            feeds[tag] = GroupSum(
                bench, feed_splits[index], "fstack_" + tag, get("fspare", tag),
                1, source=bench.refs["src fstack_" + tag],
            )
            outs[tag] = GroupSum(
                bench, splits[index], "ostack_" + tag, get("ospare", tag),
                source=bench.refs["src ostack_" + tag],
            )
            feeds[tag].start()
            outs[tag].start()
        bench.release(1)
        for tag in ("t", "i"):
            held = get("held", tag)
            vectors = [
                jnp.sum(get("norm%d" % k, tag)[...], axis=0, keepdims=True) for k in range(6)
            ]
            held[0] = jnp.concatenate(vectors + [jnp.zeros_like(vectors[0])] * 2, axis=0)
            totals[tag] = Total(bench, held, get("landing", tag), group_count)
        rows = 4 * n_i // ROW_LEN
        for step in range(3):
            co_backward_rows(bench, heads, rows * step // 3, rows * (step + 1) // 3)
            for total in totals.values():
                total.advance()
            if step > 0:
                outs["t" if step == 1 else "i"].advance()
        in_caption_order(bench, bench.rgrad_t, bench.grad_t)
        feeds["i"].advance()

        def finish_stream(index, tag):
            stack = get("stack", tag)
            weight_grad(late_splits[index], stack, 0, get("x", tag), get("grad", tag)[...])
            late[tag] = GroupSum(bench, late_splits[index], "stack_" + tag, get("spare", tag))
            late[tag].start()
            stream = streams[tag]
            grad, weight = get("grad", tag), get("w", tag)
            output = lambda half, core: back_three(grad, stream.place(half, core), weight)
            stream.open_sum()
            stream.partial(1, output)
            if tag == "i":
                feeds["t"].advance()
            outs["i"].advance()
            for total in totals.values():
                total.advance()
            stream.partial(0, output)

        def close(tag):
            stream = streams[tag]
            resid, target = get("zg", tag), get("in_grad", tag)
            stream.settle(gathered=False)

            def step(rows, carry):
                target[rows] = resid[rows] + stream.piece(rows)
                return carry

            chunks(stream.rows, step, 0)
            bench.flush("in_grad_" + tag)

        finish_stream(1, "i")
        outs["t"].advance()
        feeds["i"].advance()
        finish_stream(0, "t")
        close("i")
        late["i"].advance()
        late["t"].advance()
        for tag, total in totals.items():
            total.finish(get("norm", tag))
        feeds["t"].finish(bench.feed_sum_t)
        bench.flush("feed_sum_t")
        feeds["i"].advance()
        late["i"].advance()
        close("t")
        late["t"].advance()
        feeds["i"].advance()
        for tag in ("t", "i"):
            outs[tag].finish(get("out_sum", tag))
        feeds["i"].finish(bench.feed_sum_i)
        bench.flush("out_sum_t", "out_sum_i", "feed_sum_i")
        for tag in ("t", "i"):
            late[tag].finish(get("qkv_sum", tag))
            bench.flush("qkv_sum_" + tag)

    return exchange_kernel(
        body, "co_back", 4,
        lambda: list(group_peers()[1:])
        + [dp_peer(bit)[1] for bit in range(group_count.bit_length() - 1)],
        inputs, outputs, scratch, 16 + 2 * steps + 20, (8e9, 50e6, 1e6),
    )


def finish_kernel(sums, norms, kept):
    arrays, shapes = [], []
    for stream, (qkv, out, own, feed) in enumerate(sums):
        part = qkv.shape[0]
        inner, ff = own.shape[1] // 4, feed.shape[1] // 2
        arrays += [qkv, out, own, feed]
        turned = lambda rows: (part, rows) if stream == 0 else (rows, part)
        shapes += [
            (3, part, qkv.shape[1] // 3), turned(out.shape[1]), (3, part, inner), (inner, part),
            (part, ff), turned(ff),
        ]
    devices = lax.axis_size("dp") * lax.axis_size("mp")
    columns = [norm.shape[1] // devices for norm in norms]
    count, made = len(arrays), len(shapes)
    outs = [shape_of(shape, F32) for shape in shapes]
    for width in columns:
        outs += [shape_of((3, width), F32)] * 2
    outs += [shape_of(array.shape, array.dtype) for array in kept]
    any_spec, vmem_spec = pl.BlockSpec(memory_space=pl.ANY), pl.BlockSpec(memory_space=pltpu.VMEM)

    def kernel(*refs):
        refs = list(refs)
        take = lambda number: [refs.pop(0) for _ in range(number)]
        sources, totals, whole = take(count), take(2), take(len(kept))
        results, parts, copies = take(made), take(4), take(len(kept))
        held, built, through = take(count), take(made), take(len(kept))
        in_sems, out_sems, keep_sems = take(3)
        fetches = [
            pltpu.make_async_copy(source, target, in_sems.at[index])
            for index, (source, target) in enumerate(zip(sources, held))
        ]
        moves = [
            pltpu.make_async_copy(source, target, keep_sems.at[index])
            for index, (source, target) in enumerate(zip(whole, through))
        ]
        for copy in fetches + moves:
            copy.start()
        place = lax.axis_index("dp") * lax.axis_size("mp") + lax.axis_index("mp")
        for stream in range(2):
            total, width = totals[stream][...], columns[stream]
            mine = pltpu.roll(total, total.shape[1] - place * width, 1)[:, :width]
            parts[2 * stream][...] = mine[:3]
            parts[2 * stream + 1][...] = mine[3:6]
        stores = []
        for index, copy in enumerate(moves):
            copy.wait()
            stores.append(
                pltpu.make_async_copy(through[index], copies[index], keep_sems.at[index])
            )
            stores[-1].start()

        def store(index, values):
            for part, value in enumerate(values):
                target = built[index].at[part] if len(values) > 1 else built[index]
                target[...] = value
            stores.append(
                pltpu.make_async_copy(built[index], results[index], out_sems.at[index])
            )
            stores[-1].start()

        for stream in range(2):
            qkv, out, own, feed = held[4 * stream : 4 * stream + 4]
            at = 6 * stream
            width, inner, ff = qkv.shape[1] // 3, own.shape[1] // 4, feed.shape[1] // 2
            turned = (lambda value: value) if stream == 0 else (lambda value: value.T)
            fetches[4 * stream].wait()
            store(at, [qkv[:, k * width : (k + 1) * width].astype(F32) for k in range(3)])
            fetches[4 * stream + 1].wait()
            store(at + 1, [turned(out[...].astype(F32))])
            fetches[4 * stream + 2].wait()
            store(at + 2, [own[:, k * inner : (k + 1) * inner].astype(F32) for k in range(3)])
            store(at + 3, [own[:, 3 * inner :].astype(F32).T])
            fetches[4 * stream + 3].wait()
            store(at + 4, [feed[:, :ff].astype(F32)])
            store(at + 5, [turned(feed[:, ff:].astype(F32))])
        for copy in stores:
            copy.wait()

    return pl.pallas_call(
        kernel,
        in_specs=[any_spec] * count + [vmem_spec] * 2 + [any_spec] * len(kept),
        out_specs=[any_spec] * made + [vmem_spec] * 4 + [any_spec] * len(kept),
        out_shape=outs,
        scratch_shapes=[pltpu.VMEM(array.shape, array.dtype) for array in arrays]
        + [pltpu.VMEM(shape, F32) for shape in shapes]
        + [pltpu.VMEM(array.shape, array.dtype) for array in kept]
        + [pltpu.SemaphoreType.DMA((number,)) for number in (count, made, len(kept))],
        compiler_params=pltpu.CompilerParams(vmem_limit_bytes=BIG_LIMIT),
        name="finish",
    )(*arrays, *norms, *kept)


def apart(grad):
    rows, columns = grad.shape
    return jnp.transpose(grad.reshape(rows, 3, columns // 3), (1, 0, 2))


def finish_plain(sums, norms, kept):
    place = lax.axis_index("dp") * lax.axis_size("mp") + lax.axis_index("mp")
    outs, parts = [], []
    for stream, values in enumerate(sums):
        qkv, out, own, feed = [value.astype(F32) for value in values]
        inner, ff = own.shape[1] // 4, feed.shape[1] // 2
        turned = (lambda value: value) if stream == 0 else (lambda value: value.T)
        outs += [
            apart(qkv), turned(out), apart(own[:, : 3 * inner]), own[:, 3 * inner :].T,
            feed[:, :ff], turned(feed[:, ff:]),
        ]
        columns = norms[stream].shape[1] // (lax.axis_size("dp") * lax.axis_size("mp"))
        mine = lax.dynamic_slice_in_dim(norms[stream], place * columns, columns, axis=1)
        parts += [mine[:3], mine[3:6]]
    return outs + parts + list(kept)


def per_device(
    text_in,
    image_in,
    caption_lengths,
    region_lengths,
    image_caption,
    co_text_qkv,
    co_image_qkv,
    co_text_out,
    co_image_out,
    text_up,
    text_down,
    image_up,
    image_down,
    text_self_qkv,
    text_self_out,
    image_self_qkv,
    image_self_out,
    text_gains,
    text_shifts,
    image_gains,
    image_shifts,
    text_grad_out,
    image_grad_out,
):
    captions = image_caption.shape[1]
    part_count = lax.axis_size("mp")
    group_count = lax.axis_size("dp")
    spot = lax.axis_index("mp")
    core = spot % 2
    chip = spot // 2
    co_local = CO_HEADS // part_count
    text_local = TEXT_HEADS // part_count
    image_local = IMAGE_HEADS // part_count

    lengths = caption_lengths
    regions = region_lengths.T
    order = image_caption[0]
    labels = jnp.arange(captions, dtype=jnp.int32)
    inverse = jnp.sum(
        jnp.where(order[None, :] == labels[:, None], labels[None, :], 0), axis=1, dtype=jnp.int32
    )

    power = group_count.bit_length() - 1 if group_count & (group_count - 1) == 0 else 0

    def fold(weight, bits):
        return weight.reshape(
            weight.shape[:-2] + (2,) * bits + (weight.shape[-2] >> bits, weight.shape[-1])
        )

    feed_bits, self_bits = list(range(min(power, 3)))[::-1], list(range(min(power, 2)))[::-1]
    text_qkv = fold(jnp.swapaxes(text_self_qkv, 1, 2), len(self_bits))
    text_self_blocks = fold(text_self_out, len(self_bits))

    front = co_front_kernel(
        (text_in, image_in), (co_text_qkv, co_image_qkv),
        (fold(image_up, len(feed_bits)), fold(image_down, len(feed_bits))),
        order, inverse, regions, lengths, co_local, feed_bits,
    )
    others = (
        front["upo_i"].reshape(image_up.shape), front["downo_i"].reshape(image_down.shape)
    )
    text_ctx, image_ctx = front["ctx_t"], front["ctx_i"]
    ahead = forward_kernel(
        text_ctx, image_ctx, text_in, image_in,
        (co_text_out, co_image_out, text_up, text_down, image_up, image_down,
         text_qkv, text_self_blocks, image_self_qkv, image_self_out),
        others, (text_gains, text_shifts, image_gains, image_shifts),
        text_grad_out, image_grad_out, lengths, regions, text_local, image_local, self_bits,
    )
    widths = (text_in.shape[1], image_in.shape[1])
    upward = lambda bits: list(range(bits))
    second_first = lambda bits: ([1, 0] + list(range(2, bits)))[:bits]
    text_width, image_width = widths
    splits = (
        Split(group_count, text_width, upward), Split(group_count, image_width, upward)
    )
    self_splits = (
        Split(group_count, text_width, upward, 2, power),
        splits[1],
    )
    late_splits = (Split(group_count, text_width, second_first), splits[1])
    feed_splits = (splits[0], Split(group_count, image_width, second_first, 2, 1))
    gains = (text_gains, image_gains)
    first_back = self_back_kernel(
        ahead, image_self_qkv, image_self_out, text_qkv, text_self_blocks, gains, self_splits
    )
    second_back = feed_back_kernel(
        first_back, ahead, (text_up, image_up), (text_down, image_down), others,
        (text_ctx, image_ctx), (co_text_out, co_image_out), gains, self_splits, feed_splits,
        splits,
    )
    norms = [
        [stage[key + tag] for key in ("gain_", "shift_") for stage in (second_back, first_back, ahead)]
        for tag in "ti"
    ]
    last_back = co_back_kernel(
        (second_back["back_t"], second_back["back_i"]),
        (second_back["cg_t"].reshape(captions, CAP_LEN, -1), second_back["cg_i"]),
        (front["all_t"], front["all_i"]), (front["co_t"], front["co_i"]),
        (front["cshare_t"], front["cshare_i"]), (co_text_qkv, co_image_qkv),
        (second_back["out_grad_t"], second_back["out_grad_i"]),
        (second_back["fstack_t"], second_back["fstack_i"]),
        norms, order, inverse, splits, feed_splits, late_splits, co_local, group_count,
    )

    def over_groups(summed, split):
        if not split.fast:
            summed = lax.psum_scatter(summed, "dp", scatter_dimension=0, tiled=True)
        return summed

    sums = [
        [
            over_groups(last_back["qkv_sum_" + tag], split),
            over_groups(last_back["out_sum_" + tag], split),
            over_groups(second_back["self_sum_" + tag], split),
            over_groups(last_back["feed_sum_" + tag], split),
        ]
        for tag, split in zip("ti", splits)
    ]
    finish = finish_kernel if all(split.fast for split in splits) else finish_plain
    outs = finish(
        sums,
        (last_back["norm_t"], last_back["norm_i"]),
        (ahead["result_t"], ahead["result_i"], last_back["in_grad_t"], last_back["in_grad_i"]),
    )
    text_grads, image_grads, norm_grads, kept = outs[:6], outs[6:12], outs[12:16], outs[16:]
    return (
        *kept,
        text_grads[0],
        image_grads[0],
        text_grads[1].T,
        image_grads[1],
        text_grads[4],
        text_grads[5].T,
        image_grads[4],
        image_grads[5],
        text_grads[2],
        text_grads[3],
        image_grads[2],
        image_grads[3],
        *norm_grads,
    )


def solution(mesh):
    tokens = P(("dp", "mp"), None)
    stack_in = P(None, None, "mp")
    rows_in = P("mp", None)
    columns_in = P(None, "mp")
    in_specs = (
        tokens, tokens, P("dp"), P("dp", None), P("dp", None),
        stack_in, stack_in, rows_in, rows_in,
        columns_in, rows_in, columns_in, rows_in,
        stack_in, rows_in, stack_in, rows_in,
        P(), P(), P(), P(),
        tokens, tokens,
    )
    stack_out = P(None, "dp", "mp")
    rows_out = P("mp", "dp")
    columns_out = P("dp", "mp")
    norm_out = P(None, ("dp", "mp"))
    out_specs = (
        tokens, tokens, tokens, tokens,
        stack_out, stack_out, rows_out, rows_out,
        columns_out, rows_out, columns_out, rows_out,
        stack_out, rows_out, stack_out, rows_out,
        norm_out, norm_out, norm_out, norm_out,
    )
    return jax.shard_map(
        per_device, mesh=mesh, in_specs=in_specs, out_specs=out_specs, check_vma=False
    )
```

```python
import functools

import jax
import jax.numpy as jnp
from jax import lax
from jax.experimental import pallas as pl
from jax.experimental.pallas import tpu as pltpu
from jax.sharding import PartitionSpec as P

CO_HEADS = 8
TEXT_HEADS = 12
IMAGE_HEADS = 8
CAP_LEN = 64
ROW_LEN = 128
PER_ROW = 4

epsilon = 1e-05
BF = jnp.bfloat16
F32 = jnp.float32
VMEM_LIMIT = 48 * 1024 * 1024


def product(former, latter):
    return jnp.dot(former, latter, preferred_element_type=F32)


def product_tn(former, latter):
    return lax.dot_general(former, latter, (((0,), (0,)), ((), ())), preferred_element_type=F32)


def product_nt(former, latter):
    return lax.dot_general(former, latter, (((1,), (1,)), ((), ())), preferred_element_type=F32)


GELU_A = 0.7978845608028654
GELU_B = 0.044715


def softmax_block(scores, mask):
    scores = jnp.where(mask, scores, -1000000000.0)
    exponent = jnp.exp(scores - jnp.max(scores, axis=-1, keepdims=True))
    return (exponent / jnp.sum(exponent, axis=-1, keepdims=True)).astype(BF)


def attend_back(shares, scaling, queries, keys, values, context_grad):
    wide = shares.astype(F32)
    share_grad = product_nt(context_grad, values)
    inner = jnp.sum(share_grad * wide, axis=-1, keepdims=True)
    score_grad = (wide * (share_grad - inner) * scaling).astype(BF)
    return (
        product(score_grad, keys).astype(BF),
        product_tn(score_grad, queries).astype(BF),
        product_tn(shares, context_grad).astype(BF),
    )


class Layout:
    def __init__(self, bench):
        self.bench = bench
        self.chip = lax.div(lax.axis_index("mp"), 2)

    def turn(self, index, count):
        return lax.rem(index + self.chip * (count // 2), count)

    def length(self, caption):
        lengths = self.bench.lengths
        return lengths[self.turn(caption, lengths.shape[0])]

    def caption_of(self, image):
        order = self.bench.order
        count = order.shape[0]
        return self.turn(order[self.turn(image, count)], count)

    def image_of(self, caption):
        inverse = self.bench.inverse
        count = inverse.shape[0]
        return self.turn(inverse[self.turn(caption, count)], count)

    def ends(self, row):
        regions = self.bench.regions
        place = self.turn(row, regions.shape[1])
        ends = [regions[0, place]]
        for slot in range(1, PER_ROW):
            ends.append(ends[-1] + regions[slot, place])
        return ends


def slot_of(places, ends):
    slot = (places >= ends[0]).astype(jnp.int32)
    for end in ends[1:]:
        slot = slot + (places >= end).astype(jnp.int32)
    return slot


def caption_rows(ref, captions, start, width):
    return jnp.concatenate(
        [ref[caption, :, start : start + width] for caption in captions], axis=0
    )


def co_forward_rows(bench, heads, rows_total):
    text_ref, image_ref = bench.co_t, bench.co_i
    inner = image_ref.shape[1] // 3
    size = inner // heads
    scaling = size ** (-0.5)
    span = PER_ROW * CAP_LEN
    per_step = 2
    layout = Layout(bench)
    text_shares, image_shares = bench.cshare_t, bench.cshare_i
    text_out, image_out = bench.rctx_t, bench.ctx_i

    def step(index, carry):
        for member in range(per_step):
            row = index * per_step + member
            captions = [layout.caption_of(row * PER_ROW + slot) for slot in range(PER_ROW)]
            ends = layout.ends(row)
            lengths = [layout.length(caption) for caption in captions]
            token_slot = lax.broadcasted_iota(jnp.int32, (span, ROW_LEN), 0) // CAP_LEN
            to_image = token_slot == slot_of(
                lax.broadcasted_iota(jnp.int32, (span, ROW_LEN), 1), ends
            )
            spots = lax.broadcasted_iota(jnp.int32, (ROW_LEN, span), 1)
            length = jnp.full((ROW_LEN, span), lengths[0], jnp.int32)
            for slot in range(1, PER_ROW):
                length = jnp.where(spots >= slot * CAP_LEN, lengths[slot], length)
            to_text = (
                slot_of(lax.broadcasted_iota(jnp.int32, (ROW_LEN, span), 0), ends)
                == spots // CAP_LEN
            ) & (spots % CAP_LEN < length)
            rows = pl.ds(pl.multiple_of(row * ROW_LEN, ROW_LEN), ROW_LEN)
            texts = pl.ds(row * PER_ROW, PER_ROW)
            for head in range(heads):
                text = [
                    caption_rows(text_ref, captions, part * inner + head * size, size)
                    for part in range(3)
                ]
                image = [
                    image_ref[rows, part * inner + head * size : part * inner + (head + 1) * size]
                    for part in range(3)
                ]
                lanes = slice(head * size, (head + 1) * size)
                shares = softmax_block(product_nt(text[0], image[1]) * scaling, to_image)
                text_shares[row, head] = shares
                text_out[texts, :, lanes] = (
                    product(shares, image[2]).astype(BF).reshape(PER_ROW, CAP_LEN, size)
                )
                shares = softmax_block(product_nt(image[0], text[1]) * scaling, to_text)
                image_shares[row, head] = shares
                image_out[rows, lanes] = product(shares, text[2]).astype(BF)
        return carry

    lax.fori_loop(0, rows_total // per_step, step, 0)


def co_backward_rows(bench, heads, first_row, last_row):
    text_ref, image_ref = bench.co_t, bench.co_i
    inner = image_ref.shape[1] // 3
    size = inner // heads
    scaling = size ** (-0.5)
    span = PER_ROW * CAP_LEN
    per_step = 2
    layout = Layout(bench)
    text_shares, image_shares = bench.cshare_t, bench.cshare_i
    text_grad, image_grad = bench.cg_t, bench.cg_i
    text_out, image_out = bench.rgrad_t, bench.grad_i

    def step(index, carry):
        for member in range(per_step):
            row = index * per_step + member
            captions = [layout.caption_of(row * PER_ROW + slot) for slot in range(PER_ROW)]
            rows = pl.ds(pl.multiple_of(row * ROW_LEN, ROW_LEN), ROW_LEN)
            texts = pl.ds(row * PER_ROW, PER_ROW)
            for head in range(heads):
                text = [
                    caption_rows(text_ref, captions, part * inner + head * size, size)
                    for part in range(3)
                ]
                image = [
                    image_ref[rows, part * inner + head * size : part * inner + (head + 1) * size]
                    for part in range(3)
                ]
                text_q, image_k, image_v = attend_back(
                    text_shares[row, head], scaling, text[0], image[1], image[2],
                    caption_rows(text_grad, captions, head * size, size),
                )
                image_q, text_k, text_v = attend_back(
                    image_shares[row, head], scaling, image[0], text[1], text[2],
                    image_grad[rows, head * size : (head + 1) * size],
                )
                for part, grad in enumerate((text_q, text_k, text_v)):
                    at = part * inner + head * size
                    text_out[texts, :, at : at + size] = grad.reshape(PER_ROW, CAP_LEN, size)
                for part, grad in enumerate((image_q, image_k, image_v)):
                    at = part * inner + head * size
                    image_out[rows, at : at + size] = grad
        return carry

    lax.fori_loop(first_row // per_step, last_row // per_step, step, 0)


def in_caption_order(bench, source, target):
    layout = Layout(bench)
    for caption in range(source.shape[0]):
        rows = slice(caption * CAP_LEN, (caption + 1) * CAP_LEN)
        target[rows, :] = source[layout.image_of(caption)]


def self_mask_text(layout, block):
    shape = (2 * CAP_LEN, 2 * CAP_LEN)
    queries = lax.broadcasted_iota(jnp.int32, shape, 0)
    spots = lax.broadcasted_iota(jnp.int32, shape, 1)
    length = jnp.where(
        spots >= CAP_LEN, layout.length(block * 2 + 1) + CAP_LEN, layout.length(block * 2)
    )
    return (queries // CAP_LEN == spots // CAP_LEN) & (spots < length)


def self_mask_image(layout, row):
    ends = layout.ends(row)
    shape = (ROW_LEN, ROW_LEN)
    return slot_of(lax.broadcasted_iota(jnp.int32, shape, 0), ends) == slot_of(
        lax.broadcasted_iota(jnp.int32, shape, 1), ends
    )


def shape_of(shape, dtype=BF):
    return jax.ShapeDtypeStruct(shape, dtype)


def cost(flops, moved, exps):
    return pl.CostEstimate(flops=int(flops), bytes_accessed=int(moved), transcendentals=int(exps))


MESH = pl.DeviceIdType.MESH
BIG_LIMIT = 60 * 1024 * 1024


class Bench:
    def __init__(self, refs, fetched, flushed, counts):
        self.refs = refs
        self.fetches = {}
        self.flushes = []
        self.flush_index = {name: i for i, name in enumerate(flushed)}
        self.copies = 0
        self.waiting = []
        for index, (name, stage) in enumerate(fetched.items()):
            copy = pltpu.make_async_copy(
                refs["src " + name], refs[name], refs["fetch_sems"].at[index]
            )
            self.fetches[name] = copy
            self.waiting.append((stage, copy))
        self.release(0)

    def release(self, stage):
        for due, copy in self.waiting:
            if due <= stage:
                copy.start()
        self.waiting = [(due, copy) for due, copy in self.waiting if due > stage]

    def __getattr__(self, name):
        fetches = self.__dict__["fetches"]
        if name in fetches:
            copy = fetches.pop(name)
            if any(copy is late for _, late in self.waiting):
                copy.start()
                self.waiting = [pair for pair in self.waiting if pair[1] is not copy]
            copy.wait()
        return self.__dict__["refs"][name]

    def flush(self, *names):
        for name in names:
            copy = pltpu.make_async_copy(
                self.refs[name],
                self.refs["dst " + name],
                self.refs["flush_sems"].at[self.flush_index.pop(name)],
            )
            copy.start()
            self.flushes.append(copy)

    def remote(self, source, target, peer):
        index = self.copies
        assert index < self.refs["send_sems"].shape[0]
        self.copies += 1
        return pltpu.make_async_remote_copy(
            src_ref=source,
            dst_ref=target,
            send_sem=self.refs["send_sems"].at[index],
            recv_sem=self.refs["recv_sems"].at[index],
            device_id=peer,
            device_id_type=MESH,
        )

    def local(self, source, target):
        index = self.copies
        self.copies += 1
        return pltpu.make_async_copy(source, target, self.refs["send_sems"].at[index])

    def close(self):
        for name in list(self.fetches):
            getattr(self, name)
        for name in list(self.flush_index):
            self.flush(name)
        for copy in self.flushes:
            copy.wait()


def exchange_kernel(body, name, collective, peers, inputs, outputs, scratch, copies, work):
    fetched = {
        key: int(kind[3:] or 0) for key, (_, kind) in inputs.items() if kind.startswith("hbm")
    }
    inputs = {key: (array, kind[:3] if key in fetched else kind)
              for key, (array, kind) in inputs.items()}
    flushed = [key for key, (_, _, kind) in outputs.items() if kind == "hbm"]
    spaces = {"hbm": pl.ANY, "any": pl.ANY, "vmem": pltpu.VMEM, "smem": pltpu.SMEM}
    names = [("src " + key if kind == "hbm" else key) for key, (_, kind) in inputs.items()]
    names += [("dst " + key if kind == "hbm" else key) for key, (_, _, kind) in outputs.items()]
    shapes = []
    for key in fetched:
        names.append(key)
        shapes.append(pltpu.VMEM(inputs[key][0].shape, inputs[key][0].dtype))
    for key in flushed:
        names.append(key)
        shapes.append(pltpu.VMEM(outputs[key][0], outputs[key][1]))
    for key, (shape, dtype) in scratch.items():
        names.append(key)
        shapes.append(pltpu.VMEM(shape, dtype))
    for key, count in (
        ("fetch_sems", len(fetched)), ("flush_sems", len(flushed)),
        ("send_sems", copies), ("recv_sems", copies),
    ):
        names.append(key)
        shapes.append(pltpu.SemaphoreType.DMA((max(count, 1),)))

    def kernel(*refs):
        bench = Bench(dict(zip(names, refs)), fetched, flushed, copies)
        barrier = pltpu.get_barrier_semaphore()
        partners = peers()
        for partner in partners:
            pl.semaphore_signal(barrier, inc=1, device_id=partner, device_id_type=MESH)
        pl.semaphore_wait(barrier, len(partners))
        body(bench)
        bench.close()

    flops, moved, exps = work
    results = pl.pallas_call(
        kernel,
        in_specs=[pl.BlockSpec(memory_space=spaces[kind]) for _, kind in inputs.values()],
        out_specs=[pl.BlockSpec(memory_space=spaces[kind]) for _, _, kind in outputs.values()],
        out_shape=[shape_of(shape, dtype) for shape, dtype, _ in outputs.values()],
        scratch_shapes=shapes,
        compiler_params=pltpu.CompilerParams(
            collective_id=collective, has_side_effects=True, vmem_limit_bytes=BIG_LIMIT
        ),
        cost_estimate=cost(flops, moved, exps),
        name=name,
    )(*[array for array, _ in inputs.values()])
    return dict(zip(outputs, results))


def group_peers():
    spot = lax.axis_index("mp")
    core = lax.rem(spot, 2)
    chip = lax.div(spot, 2)
    return core, {"mp": spot + 1 - 2 * core}, {"mp": spot + 2 - 4 * chip}


class Gather:
    def __init__(self, bench, rows):
        self.bench = bench
        self.rows = rows
        self.core, self.core_peer, self.chip_peer = group_peers()
        self.other = 1 - self.core

    def place(self, half, core):
        step = self.rows & -self.rows
        return pl.ds(pl.multiple_of((2 * half + core) * self.rows, step), self.rows)

    def gather(self, full):
        own = full.at[self.place(0, self.core)]
        far = full.at[self.place(1, self.core)]
        self.across = self.bench.remote(own, far, self.chip_peer)
        self.near = self.bench.remote(own, own, self.core_peer)
        self.relay = self.bench.remote(far, far, self.core_peer)
        self.across.start()
        self.near.start()

    def arrive(self, half, project):
        if half == 0:
            project(0, self.core)
            self.near.wait_recv()
            project(0, self.other)
        else:
            self.across.wait_recv()
            self.relay.start()
            project(1, self.core)
            self.relay.wait_recv()
            project(1, self.other)

    def finish_gather(self):
        self.across.wait_send()
        self.near.wait_send()
        self.relay.wait_send()


class Stream(Gather):
    def __init__(self, bench, tag, rows):
        super().__init__(bench, rows)
        for key in ("give", "got", "send", "recv", "acc"):
            setattr(self, key, getattr(bench, tag + "_" + key))

    def open_sum(self):
        self.hand = [
            self.bench.remote(self.give.at[half], self.got.at[half], self.core_peer)
            for half in (0, 1)
        ]
        self.post = self.bench.remote(self.send, self.recv, self.chip_peer)

    def partial(self, half, output):
        self.give[half] = output(half, self.other).astype(BF)
        self.hand[half].start()
        self.acc[half] = output(half, self.core)
        if half == 1:
            self.hand[1].wait_recv()
            self.send[...] = (self.acc[1] + self.got[1].astype(F32)).astype(BF)
            self.post.start()

    def settle(self, gathered=True):
        self.hand[0].wait_recv()
        self.post.wait_recv()
        self.hand[0].wait_send()
        self.hand[1].wait_send()
        self.post.wait_send()
        if gathered:
            self.finish_gather()

    def piece(self, rows):
        return self.acc[0, rows] + self.got[0, rows].astype(F32) + self.recv[rows].astype(F32)


class Near(Gather):
    def __init__(self, bench, tag, rows):
        super().__init__(bench, rows)
        for key in ("give", "got", "acc"):
            setattr(self, key, getattr(bench, tag + "_" + key))

    def gather(self, full):
        own = full.at[self.place(0, self.core)]
        self.near = self.bench.remote(own, own, self.core_peer)
        self.near.start()

    def open_sum(self):
        self.hand = self.bench.remote(self.give.at[0], self.got.at[0], self.core_peer)

    def partial(self, half, output):
        self.give[0] = output(0, self.other).astype(BF)
        self.hand.start()
        self.acc[0] = output(0, self.core)

    def settle(self):
        self.hand.wait_recv()
        self.hand.wait_send()
        self.near.wait_send()

    def piece(self, rows):
        return self.acc[0, rows] + self.got[0, rows].astype(F32)


class Weights:
    def __init__(self, bench, own, other, bits, ready=None):
        self.bench, self.other, self.left = bench, other, list(bits)
        self.names = sorted(bits, reverse=True)
        self.lead = len(own.shape) - 2 - len(self.names)
        self.free = []
        if ready is None:
            self.copy = bench.remote(
                own.at[self.held()], other.at[self.held()], group_peers()[2]
            )
        else:
            self.copy = bench.local(ready, other.at[self.held()])
        self.copy.start()
        self.pending = True

    def held(self):
        kept = [slice(None) if bit in self.free else dp_peer(bit)[0] for bit in self.names]
        return (slice(None),) * self.lead + tuple(kept) + (slice(None), slice(None))

    def advance(self):
        if not self.pending:
            return
        self.copy.wait()
        self.pending = bool(self.left)
        if self.left:
            bit = self.left.pop(0)
            place = self.other.at[self.held()]
            self.copy = self.bench.remote(place, place, dp_peer(bit)[1])
            self.copy.start()
            self.free.append(bit)

    def finish(self):
        while self.pending:
            self.advance()


CHUNK = 32


def chunks(count, step, start):
    def once(index, carry):
        return step(pl.ds(pl.multiple_of(index * CHUNK, CHUNK), CHUNK), carry)

    return lax.fori_loop(0, count // CHUNK, once, start)


def folded(values):
    return jnp.sum(values.reshape(CHUNK // 8, 8, values.shape[-1]), axis=0)


def stream_scratch(tag, rows, width, halves=2):
    kinds = {
        tag + "_give": ((halves, rows, width), BF),
        tag + "_got": ((halves, rows, width), BF),
        tag + "_acc": ((halves, rows, width), F32),
    }
    if halves == 2:
        kinds[tag + "_send"] = ((rows, width), BF)
        kinds[tag + "_recv"] = ((rows, width), BF)
    return kinds


def at_offset(ref, offset, rows):
    return ref.at[pl.ds(pl.multiple_of(offset + rows.start, CHUNK), rows.size)]


def attend_many(parts_ref, share_ref, context_ref, base, first_block, blocks, heads, masker):
    inner = parts_ref.shape[1] // 3
    size = inner // heads
    scaling = size ** (-0.5)
    rows = [
        pl.ds(pl.multiple_of(base + block * ROW_LEN, CHUNK), ROW_LEN) for block in range(blocks)
    ]
    masks = [masker(first_block + block) for block in range(blocks)]
    scores = []
    for block in range(blocks):
        for head in range(heads):
            queries = parts_ref[rows[block], head * size : (head + 1) * size]
            keys = parts_ref[rows[block], inner + head * size : inner + (head + 1) * size]
            scores.append(jnp.where(masks[block], product_nt(queries, keys) * scaling, -1e9))
    scores = jnp.concatenate(scores, axis=0)
    exponent = jnp.exp(scores - jnp.max(scores, axis=-1, keepdims=True))
    shares = (exponent / jnp.sum(exponent, axis=-1, keepdims=True)).astype(BF)
    for block in range(blocks):
        contexts = []
        for head in range(heads):
            at = (block * heads + head) * ROW_LEN
            piece = shares[at : at + ROW_LEN]
            share_ref[first_block + block, head] = piece
            values = parts_ref[rows[block], 2 * inner + head * size : 2 * inner + (head + 1) * size]
            contexts.append(product(piece, values).astype(BF))
        context_ref[rows[block], :] = jnp.concatenate(contexts, axis=1)


def norm_chunk(values, gain, shift):
    centre = values - jnp.mean(values, axis=-1, keepdims=True)
    spread = jnp.mean(centre * centre, axis=-1, keepdims=True)
    return centre * lax.rsqrt(spread + epsilon) * gain + shift


def feed_forward(stream, full, ups, downs, act, slope):
    width = ups[0].shape[1]

    def project(half, core):
        place = stream.place(half, core)
        for share, up in enumerate(ups):
            lanes = slice(share * width, (share + 1) * width)
            pre = product(full[place], up[...])
            bent = jnp.tanh(GELU_A * (pre + GELU_B * pre * pre * pre))
            act[place, lanes] = (0.5 * pre * (1.0 + bent)).astype(BF)
            slope[place, lanes] = (
                0.5 * (1.0 + bent)
                + 0.5 * pre * (1.0 - bent * bent) * GELU_A * (1.0 + 3.0 * GELU_B * pre * pre)
            ).astype(BF)

    def output(half, core):
        place = stream.place(half, core)
        total = product(act[place, :width], downs[0][...])
        for share, down in enumerate(downs[1:], 1):
            total = total + product(act[place, share * width : (share + 1) * width], down[...])
        return total

    return project, output


def flat(ref, *lead):
    value = ref[lead] if lead else ref[...]
    return value.reshape(-1, value.shape[-1])


def forward_kernel(ctx_t, ctx_i, text_in, image_in, weights, others, norms, text_g, image_g,
                   lengths, regions, text_local, image_local, bits):
    (co_text_out, co_image_out, text_up, text_down, image_up, image_down,
     text_qkv, text_self_out, image_qkv, image_self_out) = weights
    n_t, d_t = text_in.shape
    n_i, d_i = image_in.shape
    ff_t, ff_i = text_up.shape[1], image_up.shape[1]
    in_t, in_i = ctx_inner(text_self_out), image_self_out.shape[0]
    inputs = {
        "lengths": (lengths, "smem"), "regions": (regions, "smem"),
        "gains_t": (norms[0], "hbm"), "shifts_t": (norms[1], "hbm"),
        "gains_i": (norms[2], "hbm"), "shifts_i": (norms[3], "hbm"),
        "ctx_t": (ctx_t, "hbm"), "w_co_t": (co_text_out, "hbm"),
        "ctx_i": (ctx_i, "hbm"), "w_co_i": (co_image_out, "hbm"),
        "qkv_t": (text_qkv, "hbm1"), "so_t": (text_self_out, "hbm1"),
        "x_t": (text_in, "hbm1"), "x_i": (image_in, "hbm1"),
        "up_t": (text_up, "hbm1"), "down_t": (text_down, "hbm1"),
        "up_i": (image_up, "hbm2"), "down_i": (image_down, "hbm2"),
        "upo_i": (others[0], "hbm2"), "downo_i": (others[1], "hbm2"),
        "qkvb_t": (others[2], "any"), "sob_t": (others[3], "any"),
        "qkv_i": (image_qkv, "hbm2"), "so_i": (image_self_out, "hbm2"),
        "g_i": (image_g, "hbm2"), "g_t": (text_g, "hbm2"),
    }
    outputs = {
        "mlp_t": ((4 * n_t, d_t), BF, "hbm"), "mlp_i": ((2 * n_i, d_i), BF, "hbm"),
        "act_t": ((4 * n_t, ff_t), BF, "hbm"), "act_i": ((2 * n_i, 2 * ff_i), BF, "hbm"),
        "slope_t": ((4 * n_t, ff_t), BF, "hbm"), "slope_i": ((2 * n_i, 2 * ff_i), BF, "hbm"),
        "self_t": ((2 * n_t, d_t), BF, "hbm"), "self_i": ((4 * n_i, d_i), BF, "hbm"),
        "parts_i": ((4 * n_i, 3 * in_i), BF, "hbm"),
        "share_i": ((4 * n_i // ROW_LEN, image_local, ROW_LEN, ROW_LEN), BF, "hbm"),
        "ctx2_i": ((4 * n_i, in_i), BF, "hbm"),
        "qkvo_t": (text_qkv.shape, BF, "hbm"), "soo_t": (text_self_out.shape, BF, "hbm"),
    }
    for share in "01":
        outputs["parts%s_t" % share] = ((2 * n_t, 3 * in_t), BF, "hbm")
        outputs["share%s_t" % share] = (
            (2 * n_t // ROW_LEN, text_local, ROW_LEN, ROW_LEN), BF, "hbm"
        )
        outputs["ctx2%s_t" % share] = ((2 * n_t, in_t), BF, "hbm")
    scratch = {}
    for tag, n, d in (("t", n_t, d_t), ("i", n_i, d_i)):
        outputs.update({
            "zero_" + tag: ((n, d), F32, "hbm"),
            "mid_" + tag: ((n, d), F32, "hbm"),
            "late_" + tag: ((n, d), F32, "hbm"),
            "result_" + tag: ((n, d), BF, "hbm"),
            "gain_" + tag: ((8, d), F32, "hbm"),
            "shift_" + tag: ((8, d), F32, "hbm"),
        })
        scratch.update(stream_scratch(tag, n, d))
        scratch["first_" + tag] = ((n, d), F32)

    def body(bench):
        wide = {tag: Stream(bench, tag, n) for tag, n in (("t", n_t), ("i", n_i))}
        near = {tag: Near(bench, tag, n) for tag, n in (("t", n_t), ("i", n_i))}
        get = lambda key, tag: getattr(bench, key + "_" + tag)

        for tag, stream in wide.items():
            context, weight = get("ctx", tag), get("w_co", tag)
            output = lambda half, core: product(context[stream.place(half, core)], weight[...])
            stream.open_sum()
            stream.partial(1, output)
            bench.release(1)
            stream.partial(0, output)
        bench.release(2)

        def settle(tag, stage, source, kept, resid, full, before, after):
            gain = get("gains", tag)[stage : stage + 1]
            shift = get("shifts", tag)[stage : stage + 1]
            base = after.core * after.rows

            def step(rows, carry):
                values = source[rows].astype(F32) + before.piece(rows)
                kept[rows] = values
                normed = norm_chunk(values, gain, shift)
                resid[rows] = normed
                at_offset(full, base, rows)[...] = normed.astype(BF)
                return carry

            chunks(after.rows, step, 0)
            after.gather(full)

        def first_norm(tag, after):
            wide[tag].settle(gathered=False)
            settle(
                tag, 0, get("x", tag), get("zero", tag), get("first", tag), get("mlp", tag),
                wide[tag], after,
            )
            bench.flush("zero_" + tag)

        first_norm("t", wide["t"])
        fetches = [
            Weights(bench, bench.qkv_t, bench.qkvo_t, bits, bench.qkvb_t),
            Weights(bench, bench.so_t, bench.soo_t, bits, bench.sob_t),
        ]
        text_feed = feed_forward(
            wide["t"], bench.mlp_t, [bench.up_t], [bench.down_t], bench.act_t, bench.slope_t
        )
        wide["t"].open_sum()
        wide["t"].arrive(0, text_feed[0])
        wide["t"].partial(0, text_feed[1])
        first_norm("i", near["i"])
        image_feed = feed_forward(
            near["i"], bench.mlp_i, [bench.up_i, bench.upo_i], [bench.down_i, bench.downo_i],
            bench.act_i, bench.slope_i,
        )
        near["i"].open_sum()
        near["i"].arrive(0, image_feed[0])
        near["i"].partial(0, image_feed[1])
        near["i"].settle()
        settle(
            "i", 1, bench.first_i, bench.mid_i, bench.first_i, bench.self_i, near["i"], wide["i"]
        )
        bench.flush("mid_i", "mlp_i", "act_i", "slope_i")
        for fetch in fetches:
            fetch.advance()

        stream_i = wide["i"]

        def project_image(half, core):
            place = stream_i.place(half, core)
            project_three(bench.self_i[place], bench.qkv_i, bench.parts_i, place)

        def middle(half):
            blocks = 2 * n_i // ROW_LEN
            attend_many(
                bench.parts_i, bench.share_i, bench.ctx2_i, 2 * half * n_i, half * blocks, blocks,
                image_local, functools.partial(self_mask_image, Layout(bench)),
            )

        def output_image(half, core):
            return product(bench.ctx2_i[stream_i.place(half, core)], bench.so_i[...])

        stream_i.open_sum()
        stream_i.arrive(0, project_image)
        middle(0)
        stream_i.partial(0, output_image)
        wide["t"].arrive(1, text_feed[0])
        wide["t"].partial(1, text_feed[1])
        for fetch in fetches:
            fetch.advance()
        stream_i.arrive(1, project_image)
        middle(1)
        stream_i.partial(1, output_image)
        bench.flush("act_t", "slope_t", "self_i", "parts_i", "share_i", "ctx2_i")
        for fetch in fetches:
            fetch.finish()
        bench.flush("qkvo_t", "soo_t")

        wide["t"].settle()
        settle(
            "t", 1, bench.first_t, bench.mid_t, bench.first_t, bench.self_t, wide["t"], near["t"]
        )
        bench.flush("mid_t", "mlp_t")
        stream_t = near["t"]
        shares = [
            (bench.qkv_t, bench.so_t, bench.parts0_t, bench.share0_t, bench.ctx20_t),
            (bench.qkvo_t, bench.soo_t, bench.parts1_t, bench.share1_t, bench.ctx21_t),
        ]

        def project_text(half, core):
            place = stream_t.place(half, core)
            for qkv, _, parts, share, context in shares:
                rows = bench.self_t[place]
                for part in range(3):
                    parts[place, part * in_t : (part + 1) * in_t] = product_nt(
                        rows, flat(qkv, part)
                    ).astype(BF)
                attend_many(
                    parts, share, context, core * n_t, core * (n_t // ROW_LEN), n_t // ROW_LEN,
                    text_local, functools.partial(self_mask_text, Layout(bench)),
                )

        def output_text(half, core):
            place = stream_t.place(half, core)
            return product(shares[0][4][place], flat(shares[0][1])) + product(
                shares[1][4][place], flat(shares[1][1])
            )

        stream_t.open_sum()
        stream_t.arrive(0, project_text)
        stream_t.partial(0, output_text)
        for share in "01":
            bench.flush("parts%s_t" % share, "share%s_t" % share, "ctx2%s_t" % share)
        bench.flush("self_t")

        for tag, stream in (("i", wide["i"]), ("t", near["t"])):
            stream.settle()
            gain, shift = get("gains", tag)[2:3], get("shifts", tag)[2:3]
            second, result, late, grad = (
                get("first", tag), get("result", tag), get("late", tag), get("g", tag)
            )
            width = second.shape[1]

            def step(rows, carry):
                values = second[rows] + stream.piece(rows)
                back, normed, gains, shifts = norm_pull(values, gain, shift, grad[rows].astype(F32))
                result[rows] = normed.astype(BF)
                late[rows] = back
                return carry[0] + gains, carry[1] + shifts

            start = jnp.zeros((8, width), F32)
            gains, shifts = chunks(stream.rows, step, (start, start))
            get("gain", tag)[...] = gains
            get("shift", tag)[...] = shifts
            bench.flush("result_" + tag, "late_" + tag)

    return exchange_kernel(
        body, "forward_tail", 1,
        lambda: list(group_peers()[1:]) + [dp_peer(bit)[1] for bit in bits],
        inputs, outputs, scratch, 40, (15e9, 40e6, 1e6),
    )


def ctx_inner(out_weight):
    rows = 1
    for size in out_weight.shape[:-1]:
        rows *= size
    return rows


def norm_pull(values, gain, shift, gradient):
    centre = values - jnp.mean(values, axis=-1, keepdims=True)
    spread = jnp.mean(centre * centre, axis=-1, keepdims=True)
    inverse = lax.rsqrt(spread + epsilon)
    unit = centre * inverse
    scaled = gradient * gain
    back = inverse * (
        scaled
        - jnp.mean(scaled, axis=-1, keepdims=True)
        - unit * jnp.mean(scaled * unit, axis=-1, keepdims=True)
    )
    return back, unit * gain + shift, folded(gradient * unit), folded(gradient)


def attend_back_many(parts_ref, share_ref, grads, out_ref, base, first_block, blocks, heads):
    inner = parts_ref.shape[1] // 3
    size = inner // heads
    scaling = size ** (-0.5)
    rows = [
        pl.ds(pl.multiple_of(base + block * ROW_LEN, CHUNK), ROW_LEN) for block in range(blocks)
    ]
    context_grads = [grads(block) for block in range(blocks)]
    pairs = [(block, head) for block in range(blocks) for head in range(heads)]

    def piece(part, block, head):
        at = part * inner + head * size
        return parts_ref[rows[block], at : at + size]

    def grad_of(block, head):
        return context_grads[block][:, head * size : (head + 1) * size]

    narrow = [share_ref[first_block + block, head] for block, head in pairs]
    shares = jnp.concatenate(narrow, axis=0).astype(F32)
    share_grad = jnp.concatenate(
        [product_nt(grad_of(*pair), piece(2, *pair)) for pair in pairs], axis=0
    )
    total = jnp.sum(share_grad * shares, axis=-1, keepdims=True)
    score_grad = (shares * (share_grad - total) * scaling).astype(BF)
    for block in range(blocks):
        pieces = [[], [], []]
        for head in range(heads):
            index = block * heads + head
            scores = score_grad[index * ROW_LEN : (index + 1) * ROW_LEN]
            pieces[0].append(product(scores, piece(1, block, head)).astype(BF))
            pieces[1].append(product_tn(scores, piece(0, block, head)).astype(BF))
            pieces[2].append(product_tn(narrow[index], grad_of(block, head)).astype(BF))
        out_ref[rows[block], :] = jnp.concatenate(pieces[0] + pieces[1] + pieces[2], axis=1)


class Split:
    def __init__(self, group_count, rows, order, shares=1, across=0):
        bits = group_count.bit_length() - 1
        ready = group_count == 1 << bits and (rows // group_count) % 32 == 0
        self.fast = ready and group_count > 1
        self.groups = group_count if self.fast else 1
        self.blocks = self.groups * shares
        self.part = rows // self.groups
        self.order = order(bits) if self.fast else []
        if shares == 2:
            at = min(across, len(self.order))
            self.order = self.order[:at] + ["y"] + self.order[at:]

    def position(self, block, share=0):
        spot = 0
        for bit in self.order:
            spot = 2 * spot + (share if bit == "y" else (block >> bit) & 1)
        return spot

    def shape(self, columns):
        return (self.blocks, self.part, columns)

    def spare(self, columns):
        return (max(self.blocks - 1, 1), self.part, columns)


def dp_peer(bit):
    if bit == "y":
        return 0, group_peers()[2]
    place = lax.axis_index("dp")
    value = lax.rem(lax.div(place, 1 << bit), 2)
    return value, {"dp": place + (1 << bit) * (1 - 2 * value)}


def dp_peers(*splits):
    bits = sorted({bit for split in splits for bit in split.order if bit != "y"})
    return [dp_peer(bit)[1] for bit in bits]


class GroupSum:
    def __init__(self, bench, split, key, spare, first=0, last=None, columns=slice(None),
                 source=None):
        self.bench, self.split, self.key, self.spare = bench, split, key, spare
        self.source = source
        self.columns = columns
        self.base = 0
        self.size = split.blocks
        self.at = 0
        self.left = list(split.order)[first:last]
        self.pending = False
        for bit in split.order[:first]:
            self.size //= 2
            self.base = self.base + dp_peer(bit)[0] * self.size

    @property
    def stack(self):
        return getattr(self.bench, self.key)

    def start(self):
        if not self.left:
            return
        value, peer = dp_peer(self.left.pop(0))
        self.size //= 2
        given = self.base + (1 - value) * self.size
        self.base = self.base + value * self.size
        source, self.source = self.source, None
        self.copy = self.bench.remote(
            (self.stack if source is None else source).at[pl.ds(given, self.size), :, self.columns],
            self.spare.at[pl.ds(self.at, self.size), :, self.columns],
            peer,
        )
        self.copy.start()
        self.pending = True

    def advance(self):
        if not self.pending:
            return
        self.copy.wait_recv()
        self.copy.wait_send()
        self.pending = False

        stack = self.stack

        def add(index, carry):
            mine = self.base + index
            stack[mine, :, self.columns] = (
                stack[mine, :, self.columns].astype(F32)
                + self.spare[self.at + index, :, self.columns].astype(F32)
            ).astype(BF)
            return carry

        lax.fori_loop(0, self.size, add, 0)
        self.at += self.size
        self.start()

    def drain(self):
        while self.pending:
            self.advance()

    def finish(self, out):
        self.drain()
        out[:, self.columns] = self.stack[self.base, :, self.columns]


def weight_grad(split, stack, column, left, right, share=0):
    rows, width = left.shape[1], right.shape[1]
    tile = rows // 2
    for start in (0, tile):
        value = product_tn(left[:, start : start + tile], right).astype(BF)
        lanes = slice(column, column + width)
        if split.groups == 1:
            stack[split.position(0, share), start : start + tile, lanes] = value
            continue
        for index in range(tile // split.part):
            spot = split.position(start // split.part + index, share)
            stack[spot, :, lanes] = value[index * split.part : (index + 1) * split.part]


def project_three(rows, weights, target, place):
    width = weights.shape[2]
    for part in range(3):
        target[place, part * width : (part + 1) * width] = product(rows, weights[part]).astype(BF)


def back_three(grads, place, weights):
    width = weights.shape[2]
    return (
        product_nt(grads[place, :width], weights[0])
        + product_nt(grads[place, width : 2 * width], weights[1])
        + product_nt(grads[place, 2 * width :], weights[2])
    )


def spread(stream, source, full):
    base = stream.core * stream.rows

    def step(rows, carry):
        at_offset(full, base, rows)[...] = source[rows].astype(BF)
        return carry

    chunks(stream.rows, step, 0)
    stream.gather(full)


def settle_back(stream, resid, values, gain, target, gain_out, shift_out, full=None):
    base = stream.core * stream.rows

    def step(rows, carry):
        gradient = resid[rows] + stream.piece(rows)
        back, _, gains, shifts = norm_pull(values[rows], gain, 0.0, gradient)
        target[rows] = back
        if full is not None:
            at_offset(full, base, rows)[...] = back.astype(BF)
        return carry[0] + gains, carry[1] + shifts

    start = jnp.zeros((8, resid.shape[1]), F32)
    gains, shifts = chunks(stream.rows, step, (start, start))
    gain_out[...] = gains
    shift_out[...] = shifts


def self_back_kernel(ahead, image_qkv, image_self_out, text_qkv, text_self_out, gains, splits):
    n_t, d_t = ahead["late_t"].shape
    n_i, d_i = ahead["late_i"].shape
    in_t, in_i = ctx_inner(text_self_out), image_self_out.shape[0]
    hbm = lambda *keys, kind="hbm1": {key: (ahead[key], kind) for key in keys}
    inputs = {"gains_t": (gains[0], "hbm"), "gains_i": (gains[1], "hbm")}
    inputs.update(hbm("late_i", "late_t", kind="hbm"))
    inputs.update({"so_i": (image_self_out, "hbm")})
    inputs.update(hbm("parts_i", "share_i"))
    inputs.update({"so_t": (text_self_out, "hbm1")})
    inputs.update(hbm("soo_t", "parts0_t", "share0_t", "parts1_t", "share1_t"))
    inputs.update({"qkv_i": (image_qkv, "hbm1"), "qkv_t": (text_qkv, "hbm1")})
    inputs.update(hbm("qkvo_t"))
    inputs.update(hbm("self_t", "ctx20_t", "ctx21_t", "mid_t", "self_i", "ctx2_i", "mid_i", kind="hbm2"))
    outputs, scratch = {}, {}
    for index, tag, n, d, inner in ((1, "i", n_i, d_i, in_i), (0, "t", n_t, d_t, in_t)):
        outputs.update({
            "back_" + tag: ((n, d), F32, "hbm"),
            "stack_" + tag: (splits[index].shape(4 * inner), BF, "hbm"),
            "gain_" + tag: ((8, d), F32, "hbm"),
            "shift_" + tag: ((8, d), F32, "hbm"),
        })
    scratch.update(stream_scratch("i", n_i, d_i))
    scratch.update(stream_scratch("t", n_t, d_t, 1))
    scratch.update({
        "full_i": ((4 * n_i, d_i), BF), "full_t": ((2 * n_t, d_t), BF),
        "grad_i": ((4 * n_i, 3 * in_i), BF), "cg_i": ((4 * n_i, in_i), BF),
        "grad0_t": ((2 * n_t, 3 * in_t), BF), "grad1_t": ((2 * n_t, 3 * in_t), BF),
    })
    scratch["spare_t"] = (
        (max(splits[0].blocks // 2, 1),) + splits[0].shape(4 * in_t)[1:], BF
    )
    heads = {"t": ahead["share0_t"].shape[1], "i": ahead["share_i"].shape[1]}

    def body(bench):
        image, text = Stream(bench, "i", n_i), Near(bench, "t", n_t)
        spread(image, bench.late_i, bench.full_i)
        bench.release(1)
        spread(text, bench.late_t, bench.full_t)

        def project_image(half, core):
            place = image.place(half, core)
            bench.cg_i[place] = product_nt(bench.full_i[place], bench.so_i[...]).astype(BF)

        def middle(half):
            blocks = 2 * n_i // ROW_LEN
            base = 2 * half * n_i
            attend_back_many(
                bench.parts_i, bench.share_i,
                lambda block: bench.cg_i[base + block * ROW_LEN : base + (block + 1) * ROW_LEN],
                bench.grad_i, base, half * blocks, blocks, heads["i"],
            )

        def output_image(half, core):
            return back_three(bench.grad_i, image.place(half, core), bench.qkv_i)

        bench.release(2)
        shares = [
            (bench.so_t, bench.qkv_t, bench.parts0_t, bench.share0_t, bench.grad0_t),
            (bench.soo_t, bench.qkvo_t, bench.parts1_t, bench.share1_t, bench.grad1_t),
        ]

        def project_text(half, core):
            place = text.place(half, core)
            blocks = n_t // ROW_LEN
            for out, _, parts, share, grad in shares:
                context_grad = product_nt(bench.full_t[place], flat(out)).astype(BF)
                attend_back_many(
                    parts, share,
                    lambda block: context_grad[block * ROW_LEN : (block + 1) * ROW_LEN],
                    grad, core * n_t, core * blocks, blocks, heads["t"],
                )

        def output_text(half, core):
            place = text.place(half, core)
            total = None
            for _, qkv, _, _, grad in shares:
                for part in range(3):
                    term = product(grad[place, part * in_t : (part + 1) * in_t], flat(qkv, part))
                    total = term if total is None else total + term
            return total

        text.open_sum()
        text.arrive(0, project_text)
        text.partial(0, output_text)
        for share in (0, 1):
            grad, context = shares[share][4], getattr(bench, "ctx2%d_t" % share)
            weight_grad(splits[0], bench.stack_t, 0, bench.self_t, grad[...], share)
            weight_grad(splits[0], bench.stack_t, 3 * in_t, bench.full_t, context[...], share)
        total = GroupSum(bench, splits[0], "stack_t", bench.spare_t, 0, 1)
        total.start()
        image.open_sum()
        for half in (0, 1):
            image.arrive(half, project_image)
            middle(half)
            image.partial(half, output_image)

        def close(index, tag, stream):
            stream.settle()
            get = lambda key: getattr(bench, key + "_" + tag)
            settle_back(
                stream, get("late"), get("mid"), get("gains")[1:2], get("back"), get("gain"),
                get("shift"),
            )
            bench.flush("back_" + tag)

        close(0, "t", text)
        weight_grad(splits[1], bench.stack_i, 0, bench.self_i, bench.grad_i[...])
        weight_grad(splits[1], bench.stack_i, 3 * in_i, bench.full_i, bench.ctx2_i[...])
        bench.flush("stack_i")
        close(1, "i", image)
        total.drain()

    return exchange_kernel(
        body, "self_back", 2,
        lambda: list(group_peers()[1:]) + [dp_peer(bit)[1] for bit in splits[0].order[:1] if bit != "y"],
        inputs, outputs, scratch, 16,
        (12e9, 40e6, 1e6),
    )


def feed_back_kernel(first_back, ahead, ups, downs, others, contexts, co_out, gains, self_splits,
                     splits, co_splits):
    n_t, d_t = first_back["back_t"].shape
    n_i, d_i = first_back["back_i"].shape
    ff = {"t": ups[0].shape[1], "i": ups[1].shape[1]}
    inputs, outputs, scratch = {}, {}, {}
    for index, tag in ((0, "t"), (1, "i")):
        n, d = first_back["back_" + tag].shape
        inner = contexts[index].shape[1]
        own = self_splits[index]
        stack = first_back["stack_" + tag]
        inputs.update({
            "gains_" + tag: (gains[index], "hbm"),
            "mg_" + tag: (first_back["back_" + tag], "hbm"),
            "down_" + tag: (downs[index], "hbm" if tag == "t" else "hbm1"),
            "slope_" + tag: (ahead["slope_" + tag], "hbm1"),
            "up_" + tag: (ups[index], "hbm1"),
        })
        if tag == "i":
            inputs.update({"upo_i": (others[0], "hbm1"), "downo_i": (others[1], "hbm1")})
        inputs.update({
            "stack_" + tag: (stack, "hbm2"),
            "zero_" + tag: (ahead["zero_" + tag], "hbm2"),
            "mlp_" + tag: (ahead["mlp_" + tag], "hbm2"),
            "act_" + tag: (ahead["act_" + tag], "hbm2"),
            "co_" + tag: (co_out[index], "hbm2"),
            "ctx_" + tag: (contexts[index], "hbm2"),
        })
        outputs.update({
            "back_" + tag: ((n, d), F32, "hbm"),
            "cg_" + tag: ((4 * n, inner), BF, "hbm"),
            "out_grad_" + tag: (co_splits[index].shape(inner), BF, "hbm"),
            "gain_" + tag: ((8, d), F32, "hbm"),
            "shift_" + tag: ((8, d), F32, "hbm"),
            "self_sum_" + tag: ((own.part, stack.shape[2]), BF, "hbm"),
            "fstack_" + tag: (splits[index].shape(2 * ff[tag]), BF, "hbm"),
        })
        steps = own.blocks // (2 if tag == "t" else 1)
        scratch["spare_" + tag] = ((max(steps - 1, 1),) + own.shape(stack.shape[2])[1:], BF)
        scratch["fspare_" + tag] = (
            (max(splits[index].blocks // 2, 1),) + splits[index].shape(2 * ff[tag])[1:], BF
        )
        scratch["full2_" + tag] = ((4 * n, d), BF)
    scratch.update(stream_scratch("t", n_t, d_t))
    scratch.update(stream_scratch("i", n_i, d_i, 1))
    scratch.update({
        "full_t": ((4 * n_t, d_t), BF), "full_i": ((2 * n_i, d_i), BF),
        "pre_t": ((4 * n_t, ff["t"]), BF), "pre_i": ((2 * n_i, 2 * ff["i"]), BF),
    })

    def body(bench):
        text, image = Stream(bench, "t", n_t), Near(bench, "i", n_i)
        last = {"t": Gather(bench, n_t), "i": Gather(bench, n_i)}
        get = lambda key, tag: getattr(bench, key + "_" + tag)
        spread(text, bench.mg_t, bench.full_t)
        bench.release(1)
        sums = {
            tag: GroupSum(
                bench, self_splits[index], "stack_" + tag, get("spare", tag),
                1 if tag == "t" else 0, source=bench.refs["src stack_" + tag],
            )
            for index, tag in ((1, "i"), (0, "t"))
        }
        for total in sums.values():
            total.start()
        spread(image, bench.mg_i, bench.full_i)

        def hooks(stream, tag, up_w, down_w):
            full, slope, pre = get("full", tag), get("slope", tag), get("pre", tag)
            width = ff[tag]

            def project(half, core):
                place = stream.place(half, core)
                for share, down in enumerate(down_w):
                    lanes = slice(share * width, (share + 1) * width)
                    grad = product_nt(full[place], down[...])
                    pre[place, lanes] = (grad * slope[place, lanes].astype(F32)).astype(BF)

            def output(half, core):
                place = stream.place(half, core)
                total = product_nt(pre[place, :width], up_w[0][...])
                for share, up in enumerate(up_w[1:], 1):
                    total = total + product_nt(
                        pre[place, share * width : (share + 1) * width], up[...]
                    )
                return total

            return project, output

        text_hooks = hooks(text, "t", [bench.up_t], [bench.down_t])
        text.open_sum()
        text.arrive(0, text_hooks[0])
        text.partial(0, text_hooks[1])
        bench.release(2)
        image_hooks = hooks(
            image, "i", [bench.up_i, bench.upo_i], [bench.down_i, bench.downo_i]
        )
        image.open_sum()
        image.arrive(0, image_hooks[0])
        image.partial(0, image_hooks[1])

        def close(tag, stream):
            stream.settle()
            settle_back(
                stream, get("mg", tag), get("zero", tag), get("gains", tag)[0:1],
                get("back", tag), get("gain", tag), get("shift", tag), get("full2", tag),
            )
            bench.flush("back_" + tag)
            last[tag].gather(get("full2", tag))

        feed_sums = {"t": [], "i": []}

        def feed_grads(index, tag, key, left, right, column):
            stack, width = get("fstack", tag), ff[tag]
            for share in range(1 + index):
                lanes = slice(share * width, (share + 1) * width)
                weight_grad(splits[index], stack, column, left, right[:, lanes], share)
            columns = pl.ds(column, width)
            total = GroupSum(
                bench, splits[index], "fstack_" + tag, get("fspare", tag), 0, 1, columns
            )
            total.start()
            feed_sums[tag].append(total)

        def co_project(tag):
            full, weight, target = get("full2", tag), get("co", tag), get("cg", tag)

            def project(half, core):
                place = last[tag].place(half, core)
                target[place] = product_nt(full[place], weight[...]).astype(BF)

            return project

        close("i", image)
        sums["t"].advance()
        text.arrive(1, text_hooks[0])
        text.partial(1, text_hooks[1])
        sums["i"].advance()
        feed_grads(1, "i", "up", bench.mlp_i, bench.pre_i, 0)
        sums["t"].advance()
        feed_grads(1, "i", "down", bench.full_i, bench.act_i, ff["i"])
        last["i"].arrive(0, co_project("i"))
        feed_grads(0, "t", "up", bench.mlp_t, bench.pre_t, 0)
        sums["t"].finish(bench.self_sum_t)
        bench.flush("self_sum_t")
        feed_grads(0, "t", "down", bench.full_t, bench.act_t, ff["t"])
        close("t", text)
        last["i"].arrive(1, co_project("i"))
        bench.flush("cg_i")
        sums["i"].advance()
        last["t"].arrive(0, co_project("t"))
        weight_grad(co_splits[1], bench.out_grad_i, 0, bench.full2_i, bench.ctx_i[...])
        bench.flush("out_grad_i")
        last["t"].arrive(1, co_project("t"))
        bench.flush("cg_t")
        weight_grad(co_splits[0], bench.out_grad_t, 0, bench.full2_t, bench.ctx_t[...])
        bench.flush("out_grad_t")
        for stream in last.values():
            stream.finish_gather()
        sums["i"].finish(bench.self_sum_i)
        bench.flush("self_sum_i")
        for tag in ("i", "t"):
            for total in feed_sums[tag]:
                total.drain()
            bench.flush("fstack_" + tag)
    return exchange_kernel(
        body, "feed_back", 3,
        lambda: list(group_peers()[1:]) + dp_peers(*self_splits, *splits), inputs, outputs,
        scratch, 40, (12e9, 60e6, 1e6),
    )


def co_front_kernel(shards, weights, feeds, attentions, order, inverse, regions, lengths, heads, bits):
    inputs = {
        "order": (order, "smem"), "inverse": (inverse, "smem"),
        "regions": (regions, "smem"), "lengths": (lengths, "smem"),
    }
    outputs, scratch = {}, {}
    for key, weight in zip(("up", "down"), feeds):
        inputs[key + "_i"] = (weight, "hbm")
        outputs[key + "o_i"] = (weight.shape, BF, "hbm")
    for key, weight in zip(("qkv", "so"), attentions):
        lead = weight.shape[:1] if key == "qkv" else ()
        inputs[key + "_t"] = (weight, "any")
        outputs[key + "b_t"] = (lead + weight.shape[-2:], BF, "hbm")
    for index, tag in ((0, "t"), (1, "i")):
        n, d = shards[index].shape
        width = weights[index].shape[2]
        inputs.update({"x_" + tag: (shards[index], "hbm"), "w_" + tag: (weights[index], "hbm")})
        outputs.update({
            "all_" + tag: ((4 * n, d), BF, "hbm"),
            "co_" + tag: ((4 * n, 3 * width), BF, "hbm"),
            "ctx_" + tag: ((4 * n, width), BF, "hbm"),
        })
    n_t, n_i = shards[0].shape[0], shards[1].shape[0]
    held, width = n_t // CAP_LEN, weights[0].shape[2]
    outputs["co_t"] = ((4 * held, CAP_LEN, 3 * width), BF, "hbm")
    rows = 4 * n_i // ROW_LEN
    span = PER_ROW * CAP_LEN
    outputs["cshare_t"] = ((rows, heads, span, ROW_LEN), BF, "hbm")
    outputs["cshare_i"] = ((rows, heads, ROW_LEN, span), BF, "hbm")
    scratch["rctx_t"] = ((4 * held, CAP_LEN, width), BF)

    def body(bench):
        streams = {tag: Gather(bench, n) for tag, n in (("t", n_t), ("i", n_i))}
        get = lambda key, tag: getattr(bench, key + "_" + tag)
        fetches = [
            Weights(bench, bench.up_i, bench.upo_i, bits),
            Weights(bench, bench.down_i, bench.downo_i, bits[:-2] + bits[:-3:-1]),
        ]
        for tag, stream in streams.items():
            full = get("all", tag)
            full[stream.place(0, stream.core)] = get("x", tag)[...]
            stream.gather(full)
        blocks, moves = [], []
        for key, weight in zip(("qkv", "so"), attentions):
            lead = 1 if key == "qkv" else 0
            names = range(len(weight.shape) - 2 - lead)[::-1]
            block = (slice(None),) * lead + tuple(dp_peer(bit)[0] for bit in names)
            moves.append(
                bench.remote(
                    getattr(bench, key + "_t").at[block + (slice(None), slice(None))],
                    getattr(bench, key + "b_t"), group_peers()[2],
                )
            )
        blocks += moves
        for half in (0, 1):
            for tag, stream in streams.items():
                full, weight, target = get("all", tag), get("w", tag), get("co", tag)

                due = blocks if (half, tag) == (1, "t") else []

                def project(half, core):
                    while due:
                        due.pop(0).start()
                    place = stream.place(half, core)
                    if tag == "i":
                        project_three(full[place], weight, target, place)
                        return
                    captions = pl.ds((2 * half + core) * held, held)
                    for part in range(3):
                        target[captions, :, part * width : (part + 1) * width] = (
                            product(full[place], weight[part])
                            .astype(BF)
                            .reshape(held, CAP_LEN, width)
                        )

                stream.arrive(half, project)
            if half == 0:
                for fetch in fetches * len(bits):
                    fetch.advance()
        for tag in streams:
            bench.flush("all_" + tag, "co_" + tag)
        co_forward_rows(bench, heads, rows)
        in_caption_order(bench, bench.rctx_t, bench.ctx_t)
        for fetch in fetches:
            fetch.finish()
        for block in moves:
            block.wait()
        for stream in streams.values():
            stream.finish_gather()

    return exchange_kernel(
        body, "co_front", 5,
        lambda: list(group_peers()[1:]) + [dp_peer(bit)[1] for bit in bits],
        inputs, outputs, scratch, 16,
        (4e9, 20e6, 1e6),
    )


class Total:
    def __init__(self, bench, held, landing, group_count):
        self.bench, self.held, self.landing = bench, held, landing
        self.peers = list(group_peers()[1:]) + [
            dp_peer(bit)[1] for bit in range(group_count.bit_length() - 1)
        ]
        self.step = 0
        self.start()

    def start(self):
        if self.step < len(self.peers):
            self.copy = self.bench.remote(
                self.held.at[self.step], self.landing.at[self.step], self.peers[self.step]
            )
            self.copy.start()

    def advance(self):
        if self.step < len(self.peers):
            self.copy.wait()
            self.held[self.step + 1] = self.held[self.step] + self.landing[self.step]
            self.step += 1
            self.start()

    def finish(self, out):
        while self.step < len(self.peers):
            self.advance()
        out[...] = self.held[self.step]


def co_back_kernel(zero_grad, context_grads, tokens, projected, shares, weights, out_grads,
                   feed_stacks, norms, order, inverse, splits, feed_splits, late_splits, heads,
                   group_count):
    inputs = {"order": (order, "smem"), "inverse": (inverse, "smem")}
    outputs, scratch = {}, {}
    steps = 2 + group_count.bit_length() - 1
    for index, tag in ((1, "i"), (0, "t")):
        n, d = zero_grad[index].shape
        width = projected[index].shape[-1]
        inner = out_grads[index].shape[2]
        split = splits[index]
        feeds = feed_stacks[index].shape[2]
        inputs.update({"norm%d_%s" % (k, tag): (v, "hbm") for k, v in enumerate(norms[index])})
        inputs.update({
            "co_" + tag: (projected[index], "hbm"),
            "cg_" + tag: (context_grads[index], "hbm"),
            "cshare_" + tag: (shares[index], "hbm"),
            "fstack_" + tag: (feed_stacks[index], "hbm1"),
            "ostack_" + tag: (out_grads[index], "hbm1"),
            "x_" + tag: (tokens[index], "hbm1"),
            "w_" + tag: (weights[index], "hbm1"),
            "zg_" + tag: (zero_grad[index], "hbm1"),
        })
        outputs.update({
            "in_grad_" + tag: ((n, d), F32, "hbm"),
            "feed_sum_" + tag: ((split.part, feeds), BF, "hbm"),
            "out_sum_" + tag: ((split.part, inner), BF, "hbm"),
            "qkv_sum_" + tag: ((split.part, width), BF, "hbm"),
            "norm_" + tag: ((8, d), F32, "hbm"),
        })
        scratch.update(stream_scratch(tag, n, d))
        scratch["grad_" + tag] = ((4 * n, width), BF)
        scratch["stack_" + tag] = (split.shape(width), BF)
        scratch["spare_" + tag] = (split.spare(width), BF)
        scratch["fspare_" + tag] = (feed_splits[index].spare(feeds), BF)
        scratch["ospare_" + tag] = (split.spare(inner), BF)
        scratch["held_" + tag] = ((steps + 1, 8, d), F32)
        scratch["landing_" + tag] = ((steps, 8, d), F32)
    n_t, n_i = zero_grad[0].shape[0], zero_grad[1].shape[0]
    scratch["rgrad_t"] = (projected[0].shape, BF)

    def body(bench):
        streams = {tag: Stream(bench, tag, n) for tag, n in (("i", n_i), ("t", n_t))}
        get = lambda key, tag: getattr(bench, key + "_" + tag)
        feeds, outs, late, totals = {}, {}, {}, {}
        for index, tag in ((0, "t"), (1, "i")):
            feeds[tag] = GroupSum(
                bench, feed_splits[index], "fstack_" + tag, get("fspare", tag),
                1, source=bench.refs["src fstack_" + tag],
            )
            outs[tag] = GroupSum(
                bench, splits[index], "ostack_" + tag, get("ospare", tag),
                source=bench.refs["src ostack_" + tag],
            )
            feeds[tag].start()
            outs[tag].start()
        bench.release(1)
        for tag in ("t", "i"):
            held = get("held", tag)
            vectors = [
                jnp.sum(get("norm%d" % k, tag)[...], axis=0, keepdims=True) for k in range(6)
            ]
            held[0] = jnp.concatenate(vectors + [jnp.zeros_like(vectors[0])] * 2, axis=0)
            totals[tag] = Total(bench, held, get("landing", tag), group_count)
        rows = 4 * n_i // ROW_LEN
        for step in range(3):
            co_backward_rows(bench, heads, rows * step // 3, rows * (step + 1) // 3)
            for total in totals.values():
                total.advance()
            if step > 0:
                outs["t" if step == 1 else "i"].advance()
        def open_late(index, tag):
            stack = get("stack", tag)
            weight_grad(late_splits[index], stack, 0, get("x", tag), get("grad", tag)[...])
            late[tag] = GroupSum(bench, late_splits[index], "stack_" + tag, get("spare", tag))
            late[tag].start()

        def finish_stream(tag):
            stream = streams[tag]
            grad, weight = get("grad", tag), get("w", tag)
            output = lambda half, core: back_three(grad, stream.place(half, core), weight)
            stream.open_sum()
            stream.partial(1, output)
            if tag == "i":
                feeds["t"].advance()
            outs["i"].advance()
            for total in totals.values():
                total.advance()
            stream.partial(0, output)

        def close(tag):
            stream = streams[tag]
            resid, target = get("zg", tag), get("in_grad", tag)
            stream.settle(gathered=False)

            def step(rows, carry):
                target[rows] = resid[rows] + stream.piece(rows)
                return carry

            chunks(stream.rows, step, 0)
            bench.flush("in_grad_" + tag)

        open_late(1, "i")
        in_caption_order(bench, bench.rgrad_t, bench.grad_t)
        feeds["i"].advance()
        open_late(0, "t")
        finish_stream("i")
        outs["t"].advance()
        feeds["i"].advance()
        finish_stream("t")
        close("i")
        late["i"].advance()
        late["t"].advance()
        for tag, total in totals.items():
            total.finish(get("norm", tag))
        feeds["t"].finish(bench.feed_sum_t)
        bench.flush("feed_sum_t")
        feeds["i"].advance()
        late["i"].advance()
        close("t")
        late["t"].advance()
        feeds["i"].advance()
        for tag in ("t", "i"):
            outs[tag].finish(get("out_sum", tag))
        feeds["i"].finish(bench.feed_sum_i)
        bench.flush("out_sum_t", "out_sum_i", "feed_sum_i")
        for tag in ("t", "i"):
            late[tag].finish(get("qkv_sum", tag))
            bench.flush("qkv_sum_" + tag)

    return exchange_kernel(
        body, "co_back", 4,
        lambda: list(group_peers()[1:])
        + [dp_peer(bit)[1] for bit in range(group_count.bit_length() - 1)],
        inputs, outputs, scratch, 16 + 2 * steps + 20, (8e9, 50e6, 1e6),
    )


def finish_kernel(sums, norms, kept):
    arrays, shapes = [], []
    for stream, (qkv, out, own, feed) in enumerate(sums):
        part = qkv.shape[0]
        inner, ff = own.shape[1] // 4, feed.shape[1] // 2
        arrays += [qkv, out, own, feed]
        turned = lambda rows: (part, rows) if stream == 0 else (rows, part)
        shapes += [
            (3, part, qkv.shape[1] // 3), turned(out.shape[1]), (3, part, inner), (inner, part),
            (part, ff), turned(ff),
        ]
    devices = lax.axis_size("dp") * lax.axis_size("mp")
    columns = [norm.shape[1] // devices for norm in norms]
    count, made = len(arrays), len(shapes)
    outs = [shape_of(shape, F32) for shape in shapes]
    for width in columns:
        outs += [shape_of((3, width), F32)] * 2
    outs += [shape_of(array.shape, array.dtype) for array in kept]
    any_spec, vmem_spec = pl.BlockSpec(memory_space=pl.ANY), pl.BlockSpec(memory_space=pltpu.VMEM)

    def kernel(*refs):
        refs = list(refs)
        take = lambda number: [refs.pop(0) for _ in range(number)]
        sources, totals, whole = take(count), take(2), take(len(kept))
        results, parts, copies = take(made), take(4), take(len(kept))
        held, built, through = take(count), take(made), take(len(kept))
        in_sems, out_sems, keep_sems = take(3)
        fetches = [
            pltpu.make_async_copy(source, target, in_sems.at[index])
            for index, (source, target) in enumerate(zip(sources, held))
        ]
        moves = [
            pltpu.make_async_copy(source, target, keep_sems.at[index])
            for index, (source, target) in enumerate(zip(whole, through))
        ]
        for copy in fetches + moves:
            copy.start()
        place = lax.axis_index("dp") * lax.axis_size("mp") + lax.axis_index("mp")
        for stream in range(2):
            total, width = totals[stream][...], columns[stream]
            mine = pltpu.roll(total, total.shape[1] - place * width, 1)[:, :width]
            parts[2 * stream][...] = mine[:3]
            parts[2 * stream + 1][...] = mine[3:6]
        stores = []
        for index, copy in enumerate(moves):
            copy.wait()
            stores.append(
                pltpu.make_async_copy(through[index], copies[index], keep_sems.at[index])
            )
            stores[-1].start()

        def store(index, values):
            for part, value in enumerate(values):
                target = built[index].at[part] if len(values) > 1 else built[index]
                target[...] = value
            stores.append(
                pltpu.make_async_copy(built[index], results[index], out_sems.at[index])
            )
            stores[-1].start()

        for stream in range(2):
            qkv, out, own, feed = held[4 * stream : 4 * stream + 4]
            at = 6 * stream
            width, inner, ff = qkv.shape[1] // 3, own.shape[1] // 4, feed.shape[1] // 2
            turned = (lambda value: value) if stream == 0 else (lambda value: value.T)
            fetches[4 * stream].wait()
            store(at, [qkv[:, k * width : (k + 1) * width].astype(F32) for k in range(3)])
            fetches[4 * stream + 1].wait()
            store(at + 1, [turned(out[...].astype(F32))])
            fetches[4 * stream + 2].wait()
            store(at + 2, [own[:, k * inner : (k + 1) * inner].astype(F32) for k in range(3)])
            store(at + 3, [own[:, 3 * inner :].astype(F32).T])
            fetches[4 * stream + 3].wait()
            store(at + 4, [feed[:, :ff].astype(F32)])
            store(at + 5, [turned(feed[:, ff:].astype(F32))])
        for copy in stores:
            copy.wait()

    return pl.pallas_call(
        kernel,
        in_specs=[any_spec] * count + [vmem_spec] * 2 + [any_spec] * len(kept),
        out_specs=[any_spec] * made + [vmem_spec] * 4 + [any_spec] * len(kept),
        out_shape=outs,
        scratch_shapes=[pltpu.VMEM(array.shape, array.dtype) for array in arrays]
        + [pltpu.VMEM(shape, F32) for shape in shapes]
        + [pltpu.VMEM(array.shape, array.dtype) for array in kept]
        + [pltpu.SemaphoreType.DMA((number,)) for number in (count, made, len(kept))],
        compiler_params=pltpu.CompilerParams(vmem_limit_bytes=BIG_LIMIT),
        name="finish",
    )(*arrays, *norms, *kept)


def apart(grad):
    rows, columns = grad.shape
    return jnp.transpose(grad.reshape(rows, 3, columns // 3), (1, 0, 2))


def finish_plain(sums, norms, kept):
    place = lax.axis_index("dp") * lax.axis_size("mp") + lax.axis_index("mp")
    outs, parts = [], []
    for stream, values in enumerate(sums):
        qkv, out, own, feed = [value.astype(F32) for value in values]
        inner, ff = own.shape[1] // 4, feed.shape[1] // 2
        turned = (lambda value: value) if stream == 0 else (lambda value: value.T)
        outs += [
            apart(qkv), turned(out), apart(own[:, : 3 * inner]), own[:, 3 * inner :].T,
            feed[:, :ff], turned(feed[:, ff:]),
        ]
        columns = norms[stream].shape[1] // (lax.axis_size("dp") * lax.axis_size("mp"))
        mine = lax.dynamic_slice_in_dim(norms[stream], place * columns, columns, axis=1)
        parts += [mine[:3], mine[3:6]]
    return outs + parts + list(kept)


def per_device(
    text_in,
    image_in,
    caption_lengths,
    region_lengths,
    image_caption,
    co_text_qkv,
    co_image_qkv,
    co_text_out,
    co_image_out,
    text_up,
    text_down,
    image_up,
    image_down,
    text_self_qkv,
    text_self_out,
    image_self_qkv,
    image_self_out,
    text_gains,
    text_shifts,
    image_gains,
    image_shifts,
    text_grad_out,
    image_grad_out,
):
    captions = image_caption.shape[1]
    part_count = lax.axis_size("mp")
    group_count = lax.axis_size("dp")
    spot = lax.axis_index("mp")
    core = spot % 2
    chip = spot // 2
    co_local = CO_HEADS // part_count
    text_local = TEXT_HEADS // part_count
    image_local = IMAGE_HEADS // part_count

    lengths = caption_lengths
    regions = region_lengths.T
    order = image_caption[0]
    labels = jnp.arange(captions, dtype=jnp.int32)
    inverse = jnp.sum(
        jnp.where(order[None, :] == labels[:, None], labels[None, :], 0), axis=1, dtype=jnp.int32
    )

    power = group_count.bit_length() - 1 if group_count & (group_count - 1) == 0 else 0

    def fold(weight, bits):
        return weight.reshape(
            weight.shape[:-2] + (2,) * bits + (weight.shape[-2] >> bits, weight.shape[-1])
        )

    feed_bits, self_bits = list(range(min(power, 3)))[::-1], list(range(min(power, 2)))[::-1]
    text_qkv = fold(jnp.swapaxes(text_self_qkv, 1, 2), len(self_bits))
    text_self_blocks = fold(text_self_out, len(self_bits))

    front = co_front_kernel(
        (text_in, image_in), (co_text_qkv, co_image_qkv),
        (fold(image_up, len(feed_bits)), fold(image_down, len(feed_bits))),
        (text_qkv, text_self_blocks), order, inverse, regions, lengths, co_local, feed_bits,
    )
    others = (
        front["upo_i"].reshape(image_up.shape), front["downo_i"].reshape(image_down.shape),
        front["qkvb_t"], front["sob_t"],
    )
    text_ctx, image_ctx = front["ctx_t"], front["ctx_i"]
    ahead = forward_kernel(
        text_ctx, image_ctx, text_in, image_in,
        (co_text_out, co_image_out, text_up, text_down, image_up, image_down,
         text_qkv, text_self_blocks, image_self_qkv, image_self_out),
        others, (text_gains, text_shifts, image_gains, image_shifts),
        text_grad_out, image_grad_out, lengths, regions, text_local, image_local, self_bits,
    )
    widths = (text_in.shape[1], image_in.shape[1])
    upward = lambda bits: list(range(bits))
    second_first = lambda bits: ([1, 0] + list(range(2, bits)))[:bits]
    text_width, image_width = widths
    splits = (
        Split(group_count, text_width, upward), Split(group_count, image_width, upward)
    )
    self_splits = (
        Split(group_count, text_width, upward, 2, power),
        splits[1],
    )
    late_splits = (Split(group_count, text_width, second_first), splits[1])
    feed_splits = (splits[0], Split(group_count, image_width, second_first, 2, 1))
    gains = (text_gains, image_gains)
    first_back = self_back_kernel(
        ahead, image_self_qkv, image_self_out, text_qkv, text_self_blocks, gains, self_splits
    )
    second_back = feed_back_kernel(
        first_back, ahead, (text_up, image_up), (text_down, image_down), others,
        (text_ctx, image_ctx), (co_text_out, co_image_out), gains, self_splits, feed_splits,
        splits,
    )
    norms = [
        [stage[key + tag] for key in ("gain_", "shift_") for stage in (second_back, first_back, ahead)]
        for tag in "ti"
    ]
    last_back = co_back_kernel(
        (second_back["back_t"], second_back["back_i"]),
        (second_back["cg_t"].reshape(captions, CAP_LEN, -1), second_back["cg_i"]),
        (front["all_t"], front["all_i"]), (front["co_t"], front["co_i"]),
        (front["cshare_t"], front["cshare_i"]), (co_text_qkv, co_image_qkv),
        (second_back["out_grad_t"], second_back["out_grad_i"]),
        (second_back["fstack_t"], second_back["fstack_i"]),
        norms, order, inverse, splits, feed_splits, late_splits, co_local, group_count,
    )

    def over_groups(summed, split):
        if not split.fast:
            summed = lax.psum_scatter(summed, "dp", scatter_dimension=0, tiled=True)
        return summed

    sums = [
        [
            over_groups(last_back["qkv_sum_" + tag], split),
            over_groups(last_back["out_sum_" + tag], split),
            over_groups(second_back["self_sum_" + tag], split),
            over_groups(last_back["feed_sum_" + tag], split),
        ]
        for tag, split in zip("ti", splits)
    ]
    finish = finish_kernel if all(split.fast for split in splits) else finish_plain
    outs = finish(
        sums,
        (last_back["norm_t"], last_back["norm_i"]),
        (ahead["result_t"], ahead["result_i"], last_back["in_grad_t"], last_back["in_grad_i"]),
    )
    text_grads, image_grads, norm_grads, kept = outs[:6], outs[6:12], outs[12:16], outs[16:]
    return (
        *kept,
        text_grads[0],
        image_grads[0],
        text_grads[1].T,
        image_grads[1],
        text_grads[4],
        text_grads[5].T,
        image_grads[4],
        image_grads[5],
        text_grads[2],
        text_grads[3],
        image_grads[2],
        image_grads[3],
        *norm_grads,
    )


def solution(mesh):
    tokens = P(("dp", "mp"), None)
    stack_in = P(None, None, "mp")
    rows_in = P("mp", None)
    columns_in = P(None, "mp")
    in_specs = (
        tokens, tokens, P("dp"), P("dp", None), P("dp", None),
        stack_in, stack_in, rows_in, rows_in,
        columns_in, rows_in, columns_in, rows_in,
        stack_in, rows_in, stack_in, rows_in,
        P(), P(), P(), P(),
        tokens, tokens,
    )
    stack_out = P(None, "dp", "mp")
    rows_out = P("mp", "dp")
    columns_out = P("dp", "mp")
    norm_out = P(None, ("dp", "mp"))
    out_specs = (
        tokens, tokens, tokens, tokens,
        stack_out, stack_out, rows_out, rows_out,
        columns_out, rows_out, columns_out, rows_out,
        stack_out, rows_out, stack_out, rows_out,
        norm_out, norm_out, norm_out, norm_out,
    )
    return jax.shard_map(
        per_device, mesh=mesh, in_specs=in_specs, out_specs=out_specs, check_vma=False
    )
```

```python
import functools

import jax
import jax.numpy as jnp
from jax import lax
from jax.experimental import pallas as pl
from jax.experimental.pallas import tpu as pltpu
from jax.sharding import PartitionSpec as P

CO_HEADS = 8
TEXT_HEADS = 12
IMAGE_HEADS = 8
CAP_LEN = 64
ROW_LEN = 128
PER_ROW = 4

epsilon = 1e-05
BF = jnp.bfloat16
F32 = jnp.float32
VMEM_LIMIT = 48 * 1024 * 1024


def product(former, latter):
    return jnp.dot(former, latter, preferred_element_type=F32)


def product_tn(former, latter):
    return lax.dot_general(former, latter, (((0,), (0,)), ((), ())), preferred_element_type=F32)


def product_nt(former, latter):
    return lax.dot_general(former, latter, (((1,), (1,)), ((), ())), preferred_element_type=F32)


GELU_A = 0.7978845608028654
GELU_B = 0.044715


def softmax_block(scores, mask):
    scores = jnp.where(mask, scores, -1000000000.0)
    exponent = jnp.exp(scores - jnp.max(scores, axis=-1, keepdims=True))
    return (exponent / jnp.sum(exponent, axis=-1, keepdims=True)).astype(BF)


def attend_back(shares, scaling, queries, keys, values, context_grad):
    wide = shares.astype(F32)
    share_grad = product_nt(context_grad, values)
    inner = jnp.sum(share_grad * wide, axis=-1, keepdims=True)
    score_grad = (wide * (share_grad - inner) * scaling).astype(BF)
    return (
        product(score_grad, keys).astype(BF),
        product_tn(score_grad, queries).astype(BF),
        product_tn(shares, context_grad).astype(BF),
    )


class Layout:
    def __init__(self, bench):
        self.bench = bench
        self.chip = lax.div(lax.axis_index("mp"), 2)

    def turn(self, index, count):
        return lax.rem(index + self.chip * (count // 2), count)

    def length(self, caption):
        lengths = self.bench.lengths
        return lengths[self.turn(caption, lengths.shape[0])]

    def caption_of(self, image):
        order = self.bench.order
        count = order.shape[0]
        return self.turn(order[self.turn(image, count)], count)

    def image_of(self, caption):
        inverse = self.bench.inverse
        count = inverse.shape[0]
        return self.turn(inverse[self.turn(caption, count)], count)

    def ends(self, row):
        regions = self.bench.regions
        place = self.turn(row, regions.shape[1])
        ends = [regions[0, place]]
        for slot in range(1, PER_ROW):
            ends.append(ends[-1] + regions[slot, place])
        return ends


def slot_of(places, ends):
    slot = (places >= ends[0]).astype(jnp.int32)
    for end in ends[1:]:
        slot = slot + (places >= end).astype(jnp.int32)
    return slot


def caption_rows(ref, captions, start, width):
    return jnp.concatenate(
        [ref[caption, :, start : start + width] for caption in captions], axis=0
    )


def co_forward_rows(bench, heads, rows_total):
    text_ref, image_ref = bench.co_t, bench.co_i
    inner = image_ref.shape[1] // 3
    size = inner // heads
    scaling = size ** (-0.5)
    span = PER_ROW * CAP_LEN
    per_step = 2
    layout = Layout(bench)
    text_shares, image_shares = bench.cshare_t, bench.cshare_i
    text_out, image_out = bench.rctx_t, bench.ctx_i

    def step(index, carry):
        for member in range(per_step):
            row = index * per_step + member
            captions = [layout.caption_of(row * PER_ROW + slot) for slot in range(PER_ROW)]
            ends = layout.ends(row)
            lengths = [layout.length(caption) for caption in captions]
            token_slot = lax.broadcasted_iota(jnp.int32, (span, ROW_LEN), 0) // CAP_LEN
            to_image = token_slot == slot_of(
                lax.broadcasted_iota(jnp.int32, (span, ROW_LEN), 1), ends
            )
            spots = lax.broadcasted_iota(jnp.int32, (ROW_LEN, span), 1)
            length = jnp.full((ROW_LEN, span), lengths[0], jnp.int32)
            for slot in range(1, PER_ROW):
                length = jnp.where(spots >= slot * CAP_LEN, lengths[slot], length)
            to_text = (
                slot_of(lax.broadcasted_iota(jnp.int32, (ROW_LEN, span), 0), ends)
                == spots // CAP_LEN
            ) & (spots % CAP_LEN < length)
            rows = pl.ds(pl.multiple_of(row * ROW_LEN, ROW_LEN), ROW_LEN)
            texts = pl.ds(row * PER_ROW, PER_ROW)
            for head in range(heads):
                text = [
                    caption_rows(text_ref, captions, part * inner + head * size, size)
                    for part in range(3)
                ]
                image = [
                    image_ref[rows, part * inner + head * size : part * inner + (head + 1) * size]
                    for part in range(3)
                ]
                lanes = slice(head * size, (head + 1) * size)
                shares = softmax_block(product_nt(text[0], image[1]) * scaling, to_image)
                text_shares[row, head] = shares
                text_out[texts, :, lanes] = (
                    product(shares, image[2]).astype(BF).reshape(PER_ROW, CAP_LEN, size)
                )
                shares = softmax_block(product_nt(image[0], text[1]) * scaling, to_text)
                image_shares[row, head] = shares
                image_out[rows, lanes] = product(shares, text[2]).astype(BF)
        return carry

    lax.fori_loop(0, rows_total // per_step, step, 0)


def co_backward_rows(bench, heads, first_row, last_row):
    text_ref, image_ref = bench.co_t, bench.co_i
    inner = image_ref.shape[1] // 3
    size = inner // heads
    scaling = size ** (-0.5)
    span = PER_ROW * CAP_LEN
    per_step = 2
    layout = Layout(bench)
    text_shares, image_shares = bench.cshare_t, bench.cshare_i
    text_grad, image_grad = bench.cg_t, bench.cg_i
    text_out, image_out = bench.rgrad_t, bench.grad_i

    def step(index, carry):
        for member in range(per_step):
            row = index * per_step + member
            captions = [layout.caption_of(row * PER_ROW + slot) for slot in range(PER_ROW)]
            rows = pl.ds(pl.multiple_of(row * ROW_LEN, ROW_LEN), ROW_LEN)
            texts = pl.ds(row * PER_ROW, PER_ROW)
            for head in range(heads):
                text = [
                    caption_rows(text_ref, captions, part * inner + head * size, size)
                    for part in range(3)
                ]
                image = [
                    image_ref[rows, part * inner + head * size : part * inner + (head + 1) * size]
                    for part in range(3)
                ]
                text_q, image_k, image_v = attend_back(
                    text_shares[row, head], scaling, text[0], image[1], image[2],
                    caption_rows(text_grad, captions, head * size, size),
                )
                image_q, text_k, text_v = attend_back(
                    image_shares[row, head], scaling, image[0], text[1], text[2],
                    image_grad[rows, head * size : (head + 1) * size],
                )
                for part, grad in enumerate((text_q, text_k, text_v)):
                    at = part * inner + head * size
                    text_out[texts, :, at : at + size] = grad.reshape(PER_ROW, CAP_LEN, size)
                for part, grad in enumerate((image_q, image_k, image_v)):
                    at = part * inner + head * size
                    image_out[rows, at : at + size] = grad
        return carry

    lax.fori_loop(first_row // per_step, last_row // per_step, step, 0)


def in_caption_order(bench, source, target):
    layout = Layout(bench)
    for caption in range(source.shape[0]):
        rows = slice(caption * CAP_LEN, (caption + 1) * CAP_LEN)
        target[rows, :] = source[layout.image_of(caption)]


def self_mask_text(layout, block):
    shape = (2 * CAP_LEN, 2 * CAP_LEN)
    queries = lax.broadcasted_iota(jnp.int32, shape, 0)
    spots = lax.broadcasted_iota(jnp.int32, shape, 1)
    length = jnp.where(
        spots >= CAP_LEN, layout.length(block * 2 + 1) + CAP_LEN, layout.length(block * 2)
    )
    return (queries // CAP_LEN == spots // CAP_LEN) & (spots < length)


def self_mask_image(layout, row):
    ends = layout.ends(row)
    shape = (ROW_LEN, ROW_LEN)
    return slot_of(lax.broadcasted_iota(jnp.int32, shape, 0), ends) == slot_of(
        lax.broadcasted_iota(jnp.int32, shape, 1), ends
    )


def shape_of(shape, dtype=BF):
    return jax.ShapeDtypeStruct(shape, dtype)


def cost(flops, moved, exps):
    return pl.CostEstimate(flops=int(flops), bytes_accessed=int(moved), transcendentals=int(exps))


MESH = pl.DeviceIdType.MESH
BIG_LIMIT = 60 * 1024 * 1024


class Bench:
    def __init__(self, refs, fetched, flushed, counts):
        self.refs = refs
        self.fetches = {}
        self.flushes = []
        self.flush_index = {name: i for i, name in enumerate(flushed)}
        self.copies = 0
        self.waiting = []
        for index, (name, stage) in enumerate(fetched.items()):
            copy = pltpu.make_async_copy(
                refs["src " + name], refs[name], refs["fetch_sems"].at[index]
            )
            self.fetches[name] = copy
            self.waiting.append((stage, copy))
        self.release(0)

    def release(self, stage):
        for due, copy in self.waiting:
            if due <= stage:
                copy.start()
        self.waiting = [(due, copy) for due, copy in self.waiting if due > stage]

    def __getattr__(self, name):
        fetches = self.__dict__["fetches"]
        if name in fetches:
            copy = fetches.pop(name)
            if any(copy is late for _, late in self.waiting):
                copy.start()
                self.waiting = [pair for pair in self.waiting if pair[1] is not copy]
            copy.wait()
        return self.__dict__["refs"][name]

    def flush(self, *names):
        for name in names:
            copy = pltpu.make_async_copy(
                self.refs[name],
                self.refs["dst " + name],
                self.refs["flush_sems"].at[self.flush_index.pop(name)],
            )
            copy.start()
            self.flushes.append(copy)

    def remote(self, source, target, peer):
        index = self.copies
        assert index < self.refs["send_sems"].shape[0]
        self.copies += 1
        return pltpu.make_async_remote_copy(
            src_ref=source,
            dst_ref=target,
            send_sem=self.refs["send_sems"].at[index],
            recv_sem=self.refs["recv_sems"].at[index],
            device_id=peer,
            device_id_type=MESH,
        )

    def local(self, source, target):
        index = self.copies
        self.copies += 1
        return pltpu.make_async_copy(source, target, self.refs["send_sems"].at[index])

    def close(self):
        for name in list(self.fetches):
            getattr(self, name)
        for name in list(self.flush_index):
            self.flush(name)
        for copy in self.flushes:
            copy.wait()


def exchange_kernel(body, name, collective, peers, inputs, outputs, scratch, copies, work):
    fetched = {
        key: int(kind[3:] or 0) for key, (_, kind) in inputs.items() if kind.startswith("hbm")
    }
    inputs = {key: (array, kind[:3] if key in fetched else kind)
              for key, (array, kind) in inputs.items()}
    flushed = [key for key, (_, _, kind) in outputs.items() if kind == "hbm"]
    spaces = {"hbm": pl.ANY, "any": pl.ANY, "vmem": pltpu.VMEM, "smem": pltpu.SMEM}
    names = [("src " + key if kind == "hbm" else key) for key, (_, kind) in inputs.items()]
    names += [("dst " + key if kind == "hbm" else key) for key, (_, _, kind) in outputs.items()]
    shapes = []
    for key in fetched:
        names.append(key)
        shapes.append(pltpu.VMEM(inputs[key][0].shape, inputs[key][0].dtype))
    for key in flushed:
        names.append(key)
        shapes.append(pltpu.VMEM(outputs[key][0], outputs[key][1]))
    for key, (shape, dtype) in scratch.items():
        names.append(key)
        shapes.append(pltpu.VMEM(shape, dtype))
    for key, count in (
        ("fetch_sems", len(fetched)), ("flush_sems", len(flushed)),
        ("send_sems", copies), ("recv_sems", copies),
    ):
        names.append(key)
        shapes.append(pltpu.SemaphoreType.DMA((max(count, 1),)))

    def kernel(*refs):
        bench = Bench(dict(zip(names, refs)), fetched, flushed, copies)
        barrier = pltpu.get_barrier_semaphore()
        partners = peers()
        for partner in partners:
            pl.semaphore_signal(barrier, inc=1, device_id=partner, device_id_type=MESH)
        pl.semaphore_wait(barrier, len(partners))
        body(bench)
        bench.close()

    flops, moved, exps = work
    results = pl.pallas_call(
        kernel,
        in_specs=[pl.BlockSpec(memory_space=spaces[kind]) for _, kind in inputs.values()],
        out_specs=[pl.BlockSpec(memory_space=spaces[kind]) for _, _, kind in outputs.values()],
        out_shape=[shape_of(shape, dtype) for shape, dtype, _ in outputs.values()],
        scratch_shapes=shapes,
        compiler_params=pltpu.CompilerParams(
            collective_id=collective, has_side_effects=True, vmem_limit_bytes=BIG_LIMIT
        ),
        cost_estimate=cost(flops, moved, exps),
        name=name,
    )(*[array for array, _ in inputs.values()])
    return dict(zip(outputs, results))


def group_peers():
    spot = lax.axis_index("mp")
    core = lax.rem(spot, 2)
    chip = lax.div(spot, 2)
    return core, {"mp": spot + 1 - 2 * core}, {"mp": spot + 2 - 4 * chip}


class Gather:
    def __init__(self, bench, rows):
        self.bench = bench
        self.rows = rows
        self.core, self.core_peer, self.chip_peer = group_peers()
        self.other = 1 - self.core

    def place(self, half, core):
        step = self.rows & -self.rows
        return pl.ds(pl.multiple_of((2 * half + core) * self.rows, step), self.rows)

    def gather(self, full):
        own = full.at[self.place(0, self.core)]
        far = full.at[self.place(1, self.core)]
        self.across = self.bench.remote(own, far, self.chip_peer)
        self.near = self.bench.remote(own, own, self.core_peer)
        self.relay = self.bench.remote(far, far, self.core_peer)
        self.across.start()
        self.near.start()

    def arrive(self, half, project):
        if half == 0:
            project(0, self.core)
            self.near.wait_recv()
            project(0, self.other)
        else:
            self.across.wait_recv()
            self.relay.start()
            project(1, self.core)
            self.relay.wait_recv()
            project(1, self.other)

    def finish_gather(self):
        self.across.wait_send()
        self.near.wait_send()
        self.relay.wait_send()


class Stream(Gather):
    def __init__(self, bench, tag, rows):
        super().__init__(bench, rows)
        for key in ("give", "got", "send", "recv", "acc"):
            setattr(self, key, getattr(bench, tag + "_" + key))

    def open_sum(self):
        self.hand = [
            self.bench.remote(self.give.at[half], self.got.at[half], self.core_peer)
            for half in (0, 1)
        ]
        self.post = self.bench.remote(self.send, self.recv, self.chip_peer)

    def partial(self, half, output):
        self.give[half] = output(half, self.other).astype(BF)
        self.hand[half].start()
        self.acc[half] = output(half, self.core)
        if half == 1:
            self.hand[1].wait_recv()
            self.send[...] = (self.acc[1] + self.got[1].astype(F32)).astype(BF)
            self.post.start()

    def settle(self, gathered=True):
        self.hand[0].wait_recv()
        self.post.wait_recv()
        self.hand[0].wait_send()
        self.hand[1].wait_send()
        self.post.wait_send()
        if gathered:
            self.finish_gather()

    def piece(self, rows):
        return self.acc[0, rows] + self.got[0, rows].astype(F32) + self.recv[rows].astype(F32)


class Near(Gather):
    def __init__(self, bench, tag, rows):
        super().__init__(bench, rows)
        for key in ("give", "got", "acc"):
            setattr(self, key, getattr(bench, tag + "_" + key))

    def gather(self, full):
        own = full.at[self.place(0, self.core)]
        self.near = self.bench.remote(own, own, self.core_peer)
        self.near.start()

    def open_sum(self):
        self.hand = self.bench.remote(self.give.at[0], self.got.at[0], self.core_peer)

    def partial(self, half, output):
        self.give[0] = output(0, self.other).astype(BF)
        self.hand.start()
        self.acc[0] = output(0, self.core)

    def settle(self):
        self.hand.wait_recv()
        self.hand.wait_send()
        self.near.wait_send()

    def piece(self, rows):
        return self.acc[0, rows] + self.got[0, rows].astype(F32)


class Weights:
    def __init__(self, bench, own, other, bits, ready=None):
        self.bench, self.other, self.left = bench, other, list(bits)
        self.names = sorted(bits, reverse=True)
        self.lead = len(own.shape) - 2 - len(self.names)
        self.free = []
        if ready is None:
            self.copy = bench.remote(
                own.at[self.held()], other.at[self.held()], group_peers()[2]
            )
        else:
            self.copy = bench.local(ready, other.at[self.held()])
        self.copy.start()
        self.pending = True

    def held(self):
        kept = [slice(None) if bit in self.free else dp_peer(bit)[0] for bit in self.names]
        return (slice(None),) * self.lead + tuple(kept) + (slice(None), slice(None))

    def advance(self):
        if not self.pending:
            return
        self.copy.wait()
        self.pending = bool(self.left)
        if self.left:
            bit = self.left.pop(0)
            place = self.other.at[self.held()]
            self.copy = self.bench.remote(place, place, dp_peer(bit)[1])
            self.copy.start()
            self.free.append(bit)

    def finish(self):
        while self.pending:
            self.advance()


CHUNK = 32


def chunks(count, step, start):
    def once(index, carry):
        return step(pl.ds(pl.multiple_of(index * CHUNK, CHUNK), CHUNK), carry)

    return lax.fori_loop(0, count // CHUNK, once, start)


def folded(values):
    return jnp.sum(values.reshape(CHUNK // 8, 8, values.shape[-1]), axis=0)


def stream_scratch(tag, rows, width, halves=2):
    kinds = {
        tag + "_give": ((halves, rows, width), BF),
        tag + "_got": ((halves, rows, width), BF),
        tag + "_acc": ((halves, rows, width), F32),
    }
    if halves == 2:
        kinds[tag + "_send"] = ((rows, width), BF)
        kinds[tag + "_recv"] = ((rows, width), BF)
    return kinds


def at_offset(ref, offset, rows):
    return ref.at[pl.ds(pl.multiple_of(offset + rows.start, CHUNK), rows.size)]


def attend_many(parts_ref, share_ref, context_ref, base, first_block, blocks, heads, masker):
    inner = parts_ref.shape[1] // 3
    size = inner // heads
    scaling = size ** (-0.5)
    rows = [
        pl.ds(pl.multiple_of(base + block * ROW_LEN, CHUNK), ROW_LEN) for block in range(blocks)
    ]
    masks = [masker(first_block + block) for block in range(blocks)]
    scores = []
    for block in range(blocks):
        for head in range(heads):
            queries = parts_ref[rows[block], head * size : (head + 1) * size]
            keys = parts_ref[rows[block], inner + head * size : inner + (head + 1) * size]
            scores.append(jnp.where(masks[block], product_nt(queries, keys) * scaling, -1e9))
    scores = jnp.concatenate(scores, axis=0)
    exponent = jnp.exp(scores - jnp.max(scores, axis=-1, keepdims=True))
    shares = (exponent / jnp.sum(exponent, axis=-1, keepdims=True)).astype(BF)
    for block in range(blocks):
        contexts = []
        for head in range(heads):
            at = (block * heads + head) * ROW_LEN
            piece = shares[at : at + ROW_LEN]
            share_ref[first_block + block, head] = piece
            values = parts_ref[rows[block], 2 * inner + head * size : 2 * inner + (head + 1) * size]
            contexts.append(product(piece, values).astype(BF))
        context_ref[rows[block], :] = jnp.concatenate(contexts, axis=1)


def norm_chunk(values, gain, shift):
    centre = values - jnp.mean(values, axis=-1, keepdims=True)
    spread = jnp.mean(centre * centre, axis=-1, keepdims=True)
    return centre * lax.rsqrt(spread + epsilon) * gain + shift


def feed_forward(stream, full, ups, downs, act, slope):
    width = ups[0].shape[1]

    def project(half, core):
        place = stream.place(half, core)
        for share, up in enumerate(ups):
            lanes = slice(share * width, (share + 1) * width)
            pre = product(full[place], up[...])
            bent = jnp.tanh(GELU_A * (pre + GELU_B * pre * pre * pre))
            act[place, lanes] = (0.5 * pre * (1.0 + bent)).astype(BF)
            slope[place, lanes] = (
                0.5 * (1.0 + bent)
                + 0.5 * pre * (1.0 - bent * bent) * GELU_A * (1.0 + 3.0 * GELU_B * pre * pre)
            ).astype(BF)

    def output(half, core):
        place = stream.place(half, core)
        total = product(act[place, :width], downs[0][...])
        for share, down in enumerate(downs[1:], 1):
            total = total + product(act[place, share * width : (share + 1) * width], down[...])
        return total

    return project, output


def flat(ref, *lead):
    value = ref[lead] if lead else ref[...]
    return value.reshape(-1, value.shape[-1])


def forward_kernel(ctx_t, ctx_i, text_in, image_in, weights, others, norms, text_g, image_g,
                   lengths, regions, text_local, image_local, bits):
    (co_text_out, co_image_out, text_up, text_down, image_up, image_down,
     text_qkv, text_self_out, image_qkv, image_self_out) = weights
    n_t, d_t = text_in.shape
    n_i, d_i = image_in.shape
    ff_t, ff_i = text_up.shape[1], image_up.shape[1]
    in_t, in_i = ctx_inner(text_self_out), image_self_out.shape[0]
    inputs = {
        "lengths": (lengths, "smem"), "regions": (regions, "smem"),
        "gains_t": (norms[0], "hbm"), "shifts_t": (norms[1], "hbm"),
        "gains_i": (norms[2], "hbm"), "shifts_i": (norms[3], "hbm"),
        "ctx_t": (ctx_t, "hbm"), "w_co_t": (co_text_out, "hbm"),
        "ctx_i": (ctx_i, "hbm"), "w_co_i": (co_image_out, "hbm"),
        "qkv_t": (text_qkv, "hbm1"), "so_t": (text_self_out, "hbm1"),
        "x_t": (text_in, "hbm1"), "x_i": (image_in, "hbm1"),
        "up_t": (text_up, "hbm1"), "down_t": (text_down, "hbm1"),
        "up_i": (image_up, "hbm2"), "down_i": (image_down, "hbm2"),
        "upo_i": (others[0], "hbm2"), "downo_i": (others[1], "hbm2"),
        "qkvb_t": (others[2], "any"), "sob_t": (others[3], "any"),
        "qkv_i": (image_qkv, "hbm2"), "so_i": (image_self_out, "hbm2"),
        "g_i": (image_g, "hbm2"), "g_t": (text_g, "hbm2"),
    }
    outputs = {
        "mlp_t": ((4 * n_t, d_t), BF, "hbm"), "mlp_i": ((2 * n_i, d_i), BF, "hbm"),
        "act_t": ((4 * n_t, ff_t), BF, "hbm"), "act_i": ((2 * n_i, 2 * ff_i), BF, "hbm"),
        "slope_t": ((4 * n_t, ff_t), BF, "hbm"), "slope_i": ((2 * n_i, 2 * ff_i), BF, "hbm"),
        "self_t": ((2 * n_t, d_t), BF, "hbm"), "self_i": ((4 * n_i, d_i), BF, "hbm"),
        "parts_i": ((4 * n_i, 3 * in_i), BF, "hbm"),
        "share_i": ((4 * n_i // ROW_LEN, image_local, ROW_LEN, ROW_LEN), BF, "hbm"),
        "ctx2_i": ((4 * n_i, in_i), BF, "hbm"),
        "qkvo_t": (text_qkv.shape, BF, "hbm"), "soo_t": (text_self_out.shape, BF, "hbm"),
    }
    for share in "01":
        outputs["parts%s_t" % share] = ((2 * n_t, 3 * in_t), BF, "hbm")
        outputs["share%s_t" % share] = (
            (2 * n_t // ROW_LEN, text_local, ROW_LEN, ROW_LEN), BF, "hbm"
        )
        outputs["ctx2%s_t" % share] = ((2 * n_t, in_t), BF, "hbm")
    scratch = {}
    for tag, n, d in (("t", n_t, d_t), ("i", n_i, d_i)):
        outputs.update({
            "zero_" + tag: ((n, d), F32, "hbm"),
            "mid_" + tag: ((n, d), F32, "hbm"),
            "late_" + tag: ((n, d), F32, "hbm"),
            "result_" + tag: ((n, d), BF, "hbm"),
            "gain_" + tag: ((8, d), F32, "hbm"),
            "shift_" + tag: ((8, d), F32, "hbm"),
        })
        scratch.update(stream_scratch(tag, n, d))
        scratch["first_" + tag] = ((n, d), F32)

    def body(bench):
        wide = {tag: Stream(bench, tag, n) for tag, n in (("t", n_t), ("i", n_i))}
        near = {tag: Near(bench, tag, n) for tag, n in (("t", n_t), ("i", n_i))}
        get = lambda key, tag: getattr(bench, key + "_" + tag)

        for tag, stream in wide.items():
            context, weight = get("ctx", tag), get("w_co", tag)
            output = lambda half, core: product(context[stream.place(half, core)], weight[...])
            stream.open_sum()
            stream.partial(1, output)
            bench.release(1)
            stream.partial(0, output)
        bench.release(2)

        def settle(tag, stage, source, kept, resid, full, before, after):
            gain = get("gains", tag)[stage : stage + 1]
            shift = get("shifts", tag)[stage : stage + 1]
            base = after.core * after.rows

            def step(rows, carry):
                values = source[rows].astype(F32) + before.piece(rows)
                kept[rows] = values
                normed = norm_chunk(values, gain, shift)
                resid[rows] = normed
                at_offset(full, base, rows)[...] = normed.astype(BF)
                return carry

            chunks(after.rows, step, 0)
            after.gather(full)

        def first_norm(tag, after):
            wide[tag].settle(gathered=False)
            settle(
                tag, 0, get("x", tag), get("zero", tag), get("first", tag), get("mlp", tag),
                wide[tag], after,
            )
            bench.flush("zero_" + tag)

        first_norm("t", wide["t"])
        fetches = [
            Weights(bench, bench.qkv_t, bench.qkvo_t, bits, bench.qkvb_t),
            Weights(bench, bench.so_t, bench.soo_t, bits, bench.sob_t),
        ]
        text_feed = feed_forward(
            wide["t"], bench.mlp_t, [bench.up_t], [bench.down_t], bench.act_t, bench.slope_t
        )
        wide["t"].open_sum()
        wide["t"].arrive(0, text_feed[0])
        wide["t"].partial(0, text_feed[1])
        first_norm("i", near["i"])
        image_feed = feed_forward(
            near["i"], bench.mlp_i, [bench.up_i, bench.upo_i], [bench.down_i, bench.downo_i],
            bench.act_i, bench.slope_i,
        )
        near["i"].open_sum()
        near["i"].arrive(0, image_feed[0])
        near["i"].partial(0, image_feed[1])
        near["i"].settle()
        settle(
            "i", 1, bench.first_i, bench.mid_i, bench.first_i, bench.self_i, near["i"], wide["i"]
        )
        bench.flush("mid_i", "mlp_i", "act_i", "slope_i")
        for fetch in fetches:
            fetch.advance()

        stream_i = wide["i"]

        def project_image(half, core):
            place = stream_i.place(half, core)
            project_three(bench.self_i[place], bench.qkv_i, bench.parts_i, place)

        def middle(half):
            blocks = 2 * n_i // ROW_LEN
            attend_many(
                bench.parts_i, bench.share_i, bench.ctx2_i, 2 * half * n_i, half * blocks, blocks,
                image_local, functools.partial(self_mask_image, Layout(bench)),
            )

        def output_image(half, core):
            return product(bench.ctx2_i[stream_i.place(half, core)], bench.so_i[...])

        stream_i.open_sum()
        stream_i.arrive(0, project_image)
        middle(0)
        stream_i.partial(0, output_image)
        wide["t"].arrive(1, text_feed[0])
        wide["t"].partial(1, text_feed[1])
        for fetch in fetches:
            fetch.advance()
        stream_i.arrive(1, project_image)
        middle(1)
        stream_i.partial(1, output_image)
        bench.flush("act_t", "slope_t", "self_i", "parts_i", "share_i", "ctx2_i")
        for fetch in fetches:
            fetch.finish()
        bench.flush("qkvo_t", "soo_t")

        wide["t"].settle()
        settle(
            "t", 1, bench.first_t, bench.mid_t, bench.first_t, bench.self_t, wide["t"], near["t"]
        )
        bench.flush("mid_t", "mlp_t")
        stream_t = near["t"]
        shares = [
            (bench.qkv_t, bench.so_t, bench.parts0_t, bench.share0_t, bench.ctx20_t),
            (bench.qkvo_t, bench.soo_t, bench.parts1_t, bench.share1_t, bench.ctx21_t),
        ]

        def project_text(half, core):
            place = stream_t.place(half, core)
            for qkv, _, parts, share, context in shares:
                rows = bench.self_t[place]
                for part in range(3):
                    parts[place, part * in_t : (part + 1) * in_t] = product_nt(
                        rows, flat(qkv, part)
                    ).astype(BF)
                attend_many(
                    parts, share, context, core * n_t, core * (n_t // ROW_LEN), n_t // ROW_LEN,
                    text_local, functools.partial(self_mask_text, Layout(bench)),
                )

        def output_text(half, core):
            place = stream_t.place(half, core)
            return product(shares[0][4][place], flat(shares[0][1])) + product(
                shares[1][4][place], flat(shares[1][1])
            )

        stream_t.open_sum()
        stream_t.arrive(0, project_text)
        stream_t.partial(0, output_text)
        for share in "01":
            bench.flush("parts%s_t" % share, "share%s_t" % share, "ctx2%s_t" % share)
        bench.flush("self_t")

        for tag, stream in (("i", wide["i"]), ("t", near["t"])):
            stream.settle()
            gain, shift = get("gains", tag)[2:3], get("shifts", tag)[2:3]
            second, result, late, grad = (
                get("first", tag), get("result", tag), get("late", tag), get("g", tag)
            )
            width = second.shape[1]

            def step(rows, carry):
                values = second[rows] + stream.piece(rows)
                back, normed, gains, shifts = norm_pull(values, gain, shift, grad[rows].astype(F32))
                result[rows] = normed.astype(BF)
                late[rows] = back
                return carry[0] + gains, carry[1] + shifts

            start = jnp.zeros((8, width), F32)
            gains, shifts = chunks(stream.rows, step, (start, start))
            get("gain", tag)[...] = gains
            get("shift", tag)[...] = shifts
            bench.flush("result_" + tag, "late_" + tag)

    return exchange_kernel(
        body, "forward_tail", 1,
        lambda: list(group_peers()[1:]) + [dp_peer(bit)[1] for bit in bits],
        inputs, outputs, scratch, 40, (15e9, 40e6, 1e6),
    )


def ctx_inner(out_weight):
    rows = 1
    for size in out_weight.shape[:-1]:
        rows *= size
    return rows


def norm_pull(values, gain, shift, gradient):
    centre = values - jnp.mean(values, axis=-1, keepdims=True)
    spread = jnp.mean(centre * centre, axis=-1, keepdims=True)
    inverse = lax.rsqrt(spread + epsilon)
    unit = centre * inverse
    scaled = gradient * gain
    back = inverse * (
        scaled
        - jnp.mean(scaled, axis=-1, keepdims=True)
        - unit * jnp.mean(scaled * unit, axis=-1, keepdims=True)
    )
    return back, unit * gain + shift, folded(gradient * unit), folded(gradient)


def attend_back_many(parts_ref, share_ref, grads, out_ref, base, first_block, blocks, heads):
    inner = parts_ref.shape[1] // 3
    size = inner // heads
    scaling = size ** (-0.5)
    rows = [
        pl.ds(pl.multiple_of(base + block * ROW_LEN, CHUNK), ROW_LEN) for block in range(blocks)
    ]
    context_grads = [grads(block) for block in range(blocks)]
    pairs = [(block, head) for block in range(blocks) for head in range(heads)]

    def piece(part, block, head):
        at = part * inner + head * size
        return parts_ref[rows[block], at : at + size]

    def grad_of(block, head):
        return context_grads[block][:, head * size : (head + 1) * size]

    narrow = [share_ref[first_block + block, head] for block, head in pairs]
    shares = jnp.concatenate(narrow, axis=0).astype(F32)
    share_grad = jnp.concatenate(
        [product_nt(grad_of(*pair), piece(2, *pair)) for pair in pairs], axis=0
    )
    total = jnp.sum(share_grad * shares, axis=-1, keepdims=True)
    score_grad = (shares * (share_grad - total) * scaling).astype(BF)
    for block in range(blocks):
        pieces = [[], [], []]
        for head in range(heads):
            index = block * heads + head
            scores = score_grad[index * ROW_LEN : (index + 1) * ROW_LEN]
            pieces[0].append(product(scores, piece(1, block, head)).astype(BF))
            pieces[1].append(product_tn(scores, piece(0, block, head)).astype(BF))
            pieces[2].append(product_tn(narrow[index], grad_of(block, head)).astype(BF))
        out_ref[rows[block], :] = jnp.concatenate(pieces[0] + pieces[1] + pieces[2], axis=1)


class Split:
    def __init__(self, group_count, rows, order, shares=1, across=0):
        bits = group_count.bit_length() - 1
        ready = group_count == 1 << bits and (rows // group_count) % 32 == 0
        self.fast = ready and group_count > 1
        self.groups = group_count if self.fast else 1
        self.blocks = self.groups * shares
        self.part = rows // self.groups
        self.order = order(bits) if self.fast else []
        if shares == 2:
            at = min(across, len(self.order))
            self.order = self.order[:at] + ["y"] + self.order[at:]

    def position(self, block, share=0):
        spot = 0
        for bit in self.order:
            spot = 2 * spot + (share if bit == "y" else (block >> bit) & 1)
        return spot

    def shape(self, columns):
        return (self.blocks, self.part, columns)

    def spare(self, columns):
        return (max(self.blocks - 1, 1), self.part, columns)


def dp_peer(bit):
    if bit == "y":
        return 0, group_peers()[2]
    place = lax.axis_index("dp")
    value = lax.rem(lax.div(place, 1 << bit), 2)
    return value, {"dp": place + (1 << bit) * (1 - 2 * value)}


def dp_peers(*splits):
    bits = sorted({bit for split in splits for bit in split.order if bit != "y"})
    return [dp_peer(bit)[1] for bit in bits]


class GroupSum:
    def __init__(self, bench, split, key, spare, first=0, last=None, columns=slice(None),
                 source=None):
        self.bench, self.split, self.key, self.spare = bench, split, key, spare
        self.source = source
        self.columns = columns
        self.base = 0
        self.size = split.blocks
        self.at = 0
        self.left = list(split.order)[first:last]
        self.pending = False
        for bit in split.order[:first]:
            self.size //= 2
            self.base = self.base + dp_peer(bit)[0] * self.size

    @property
    def stack(self):
        return getattr(self.bench, self.key)

    def start(self):
        if not self.left:
            return
        value, peer = dp_peer(self.left.pop(0))
        self.size //= 2
        given = self.base + (1 - value) * self.size
        self.base = self.base + value * self.size
        source, self.source = self.source, None
        self.copy = self.bench.remote(
            (self.stack if source is None else source).at[pl.ds(given, self.size), :, self.columns],
            self.spare.at[pl.ds(self.at, self.size), :, self.columns],
            peer,
        )
        self.copy.start()
        self.pending = True

    def advance(self):
        if not self.pending:
            return
        self.copy.wait_recv()
        self.copy.wait_send()
        self.pending = False

        stack = self.stack

        def add(index, carry):
            mine = self.base + index
            stack[mine, :, self.columns] = (
                stack[mine, :, self.columns].astype(F32)
                + self.spare[self.at + index, :, self.columns].astype(F32)
            ).astype(BF)
            return carry

        lax.fori_loop(0, self.size, add, 0)
        self.at += self.size
        self.start()

    def drain(self):
        while self.pending:
            self.advance()

    def finish(self, out):
        self.drain()
        out[:, self.columns] = self.stack[self.base, :, self.columns]


def weight_grad(split, stack, column, left, right, share=0):
    rows, width = left.shape[1], right.shape[1]
    tile = rows // 2
    for start in (0, tile):
        value = product_tn(left[:, start : start + tile], right).astype(BF)
        lanes = slice(column, column + width)
        if split.groups == 1:
            stack[split.position(0, share), start : start + tile, lanes] = value
            continue
        for index in range(tile // split.part):
            spot = split.position(start // split.part + index, share)
            stack[spot, :, lanes] = value[index * split.part : (index + 1) * split.part]


def project_three(rows, weights, target, place):
    width = weights.shape[2]
    for part in range(3):
        target[place, part * width : (part + 1) * width] = product(rows, weights[part]).astype(BF)


def back_three(grads, place, weights):
    width = weights.shape[2]
    return (
        product_nt(grads[place, :width], weights[0])
        + product_nt(grads[place, width : 2 * width], weights[1])
        + product_nt(grads[place, 2 * width :], weights[2])
    )


def spread(stream, source, full):
    base = stream.core * stream.rows

    def step(rows, carry):
        at_offset(full, base, rows)[...] = source[rows].astype(BF)
        return carry

    chunks(stream.rows, step, 0)
    stream.gather(full)


def settle_back(stream, resid, values, gain, target, gain_out, shift_out, full=None):
    base = stream.core * stream.rows

    def step(rows, carry):
        gradient = resid[rows] + stream.piece(rows)
        back, _, gains, shifts = norm_pull(values[rows], gain, 0.0, gradient)
        target[rows] = back
        if full is not None:
            at_offset(full, base, rows)[...] = back.astype(BF)
        return carry[0] + gains, carry[1] + shifts

    start = jnp.zeros((8, resid.shape[1]), F32)
    gains, shifts = chunks(stream.rows, step, (start, start))
    gain_out[...] = gains
    shift_out[...] = shifts


def self_back_kernel(ahead, image_qkv, image_self_out, text_qkv, text_self_out, gains, splits):
    n_t, d_t = ahead["late_t"].shape
    n_i, d_i = ahead["late_i"].shape
    in_t, in_i = ctx_inner(text_self_out), image_self_out.shape[0]
    hbm = lambda *keys, kind="hbm1": {key: (ahead[key], kind) for key in keys}
    inputs = {"gains_t": (gains[0], "hbm"), "gains_i": (gains[1], "hbm")}
    inputs.update(hbm("late_t", "late_i", kind="hbm"))
    inputs.update({"so_i": (image_self_out, "hbm2")})
    inputs.update(hbm("parts_i", "share_i", kind="hbm2"))
    inputs.update({"so_t": (text_self_out, "hbm1")})
    inputs.update(hbm("soo_t", "parts0_t", "share0_t", "parts1_t", "share1_t"))
    inputs.update({"qkv_i": (image_qkv, "hbm2"), "qkv_t": (text_qkv, "hbm1")})
    inputs.update(hbm("qkvo_t"))
    inputs.update(hbm("self_t", "ctx20_t", "ctx21_t", "mid_t", "self_i", "ctx2_i", "mid_i", kind="hbm2"))
    outputs, scratch = {}, {}
    for index, tag, n, d, inner in ((1, "i", n_i, d_i, in_i), (0, "t", n_t, d_t, in_t)):
        outputs.update({
            "back_" + tag: ((n, d), F32, "hbm"),
            "stack_" + tag: (splits[index].shape(4 * inner), BF, "hbm"),
            "gain_" + tag: ((8, d), F32, "hbm"),
            "shift_" + tag: ((8, d), F32, "hbm"),
        })
    scratch.update(stream_scratch("i", n_i, d_i))
    scratch.update(stream_scratch("t", n_t, d_t, 1))
    scratch.update({
        "full_i": ((4 * n_i, d_i), BF), "full_t": ((2 * n_t, d_t), BF),
        "grad_i": ((4 * n_i, 3 * in_i), BF), "cg_i": ((4 * n_i, in_i), BF),
        "grad0_t": ((2 * n_t, 3 * in_t), BF), "grad1_t": ((2 * n_t, 3 * in_t), BF),
    })
    scratch["spare_t"] = (
        (max(splits[0].blocks // 2, 1),) + splits[0].shape(4 * in_t)[1:], BF
    )
    heads = {"t": ahead["share0_t"].shape[1], "i": ahead["share_i"].shape[1]}

    def body(bench):
        image, text = Stream(bench, "i", n_i), Near(bench, "t", n_t)
        spread(text, bench.late_t, bench.full_t)
        bench.release(1)
        spread(image, bench.late_i, bench.full_i)

        def project_image(half, core):
            place = image.place(half, core)
            bench.cg_i[place] = product_nt(bench.full_i[place], bench.so_i[...]).astype(BF)

        def middle(half):
            blocks = 2 * n_i // ROW_LEN
            base = 2 * half * n_i
            attend_back_many(
                bench.parts_i, bench.share_i,
                lambda block: bench.cg_i[base + block * ROW_LEN : base + (block + 1) * ROW_LEN],
                bench.grad_i, base, half * blocks, blocks, heads["i"],
            )

        def output_image(half, core):
            return back_three(bench.grad_i, image.place(half, core), bench.qkv_i)

        shares = [
            (bench.so_t, bench.qkv_t, bench.parts0_t, bench.share0_t, bench.grad0_t),
            (bench.soo_t, bench.qkvo_t, bench.parts1_t, bench.share1_t, bench.grad1_t),
        ]

        def project_text(half, core):
            place = text.place(half, core)
            blocks = n_t // ROW_LEN
            for out, _, parts, share, grad in shares:
                context_grad = product_nt(bench.full_t[place], flat(out)).astype(BF)
                attend_back_many(
                    parts, share,
                    lambda block: context_grad[block * ROW_LEN : (block + 1) * ROW_LEN],
                    grad, core * n_t, core * blocks, blocks, heads["t"],
                )

        def output_text(half, core):
            place = text.place(half, core)
            total = None
            for _, qkv, _, _, grad in shares:
                for part in range(3):
                    term = product(grad[place, part * in_t : (part + 1) * in_t], flat(qkv, part))
                    total = term if total is None else total + term
            return total

        text.open_sum()
        text.arrive(0, project_text)
        bench.release(2)
        for share in (0, 1):
            grad, context = shares[share][4], getattr(bench, "ctx2%d_t" % share)
            weight_grad(splits[0], bench.stack_t, 0, bench.self_t, grad[...], share)
            weight_grad(splits[0], bench.stack_t, 3 * in_t, bench.full_t, context[...], share)
        total = GroupSum(bench, splits[0], "stack_t", bench.spare_t, 0, 1)
        total.start()
        text.partial(0, output_text)
        image.open_sum()
        for half in (0, 1):
            image.arrive(half, project_image)
            middle(half)
            image.partial(half, output_image)

        def close(index, tag, stream):
            stream.settle()
            get = lambda key: getattr(bench, key + "_" + tag)
            settle_back(
                stream, get("late"), get("mid"), get("gains")[1:2], get("back"), get("gain"),
                get("shift"),
            )
            bench.flush("back_" + tag)

        close(0, "t", text)
        weight_grad(splits[1], bench.stack_i, 0, bench.self_i, bench.grad_i[...])
        weight_grad(splits[1], bench.stack_i, 3 * in_i, bench.full_i, bench.ctx2_i[...])
        bench.flush("stack_i")
        close(1, "i", image)
        total.drain()

    return exchange_kernel(
        body, "self_back", 2,
        lambda: list(group_peers()[1:]) + [dp_peer(bit)[1] for bit in splits[0].order[:1] if bit != "y"],
        inputs, outputs, scratch, 16,
        (12e9, 40e6, 1e6),
    )


def feed_back_kernel(first_back, ahead, ups, downs, others, contexts, co_out, gains, self_splits,
                     splits, co_splits):
    n_t, d_t = first_back["back_t"].shape
    n_i, d_i = first_back["back_i"].shape
    ff = {"t": ups[0].shape[1], "i": ups[1].shape[1]}
    inputs, outputs, scratch = {}, {}, {}
    for index, tag in ((0, "t"), (1, "i")):
        n, d = first_back["back_" + tag].shape
        inner = contexts[index].shape[1]
        own = self_splits[index]
        stack = first_back["stack_" + tag]
        inputs.update({
            "gains_" + tag: (gains[index], "hbm"),
            "mg_" + tag: (first_back["back_" + tag], "hbm"),
            "down_" + tag: (downs[index], "hbm" if tag == "t" else "hbm1"),
            "slope_" + tag: (ahead["slope_" + tag], "hbm1"),
            "up_" + tag: (ups[index], "hbm1"),
        })
        if tag == "i":
            inputs.update({"upo_i": (others[0], "hbm1"), "downo_i": (others[1], "hbm1")})
        inputs.update({
            "stack_" + tag: (stack, "hbm2"),
            "zero_" + tag: (ahead["zero_" + tag], "hbm2"),
            "mlp_" + tag: (ahead["mlp_" + tag], "hbm2"),
            "act_" + tag: (ahead["act_" + tag], "hbm2"),
            "co_" + tag: (co_out[index], "hbm2"),
            "ctx_" + tag: (contexts[index], "hbm2"),
        })
        outputs.update({
            "back_" + tag: ((n, d), F32, "hbm"),
            "cg_" + tag: ((4 * n, inner), BF, "hbm"),
            "out_grad_" + tag: (co_splits[index].shape(inner), BF, "hbm"),
            "gain_" + tag: ((8, d), F32, "hbm"),
            "shift_" + tag: ((8, d), F32, "hbm"),
            "self_sum_" + tag: ((own.part, stack.shape[2]), BF, "hbm"),
            "fstack_" + tag: (splits[index].shape(2 * ff[tag]), BF, "hbm"),
        })
        steps = own.blocks // (2 if tag == "t" else 1)
        scratch["spare_" + tag] = ((max(steps - 1, 1),) + own.shape(stack.shape[2])[1:], BF)
        scratch["fspare_" + tag] = (
            (max(splits[index].blocks // 2, 1),) + splits[index].shape(2 * ff[tag])[1:], BF
        )
        scratch["full2_" + tag] = ((4 * n, d), BF)
    scratch.update(stream_scratch("t", n_t, d_t))
    scratch.update(stream_scratch("i", n_i, d_i, 1))
    scratch.update({
        "full_t": ((4 * n_t, d_t), BF), "full_i": ((2 * n_i, d_i), BF),
        "pre_t": ((4 * n_t, ff["t"]), BF), "pre_i": ((2 * n_i, 2 * ff["i"]), BF),
    })

    def body(bench):
        text, image = Stream(bench, "t", n_t), Near(bench, "i", n_i)
        last = {"t": Gather(bench, n_t), "i": Gather(bench, n_i)}
        get = lambda key, tag: getattr(bench, key + "_" + tag)
        spread(text, bench.mg_t, bench.full_t)
        bench.release(1)
        sums = {
            tag: GroupSum(
                bench, self_splits[index], "stack_" + tag, get("spare", tag),
                1 if tag == "t" else 0, source=bench.refs["src stack_" + tag],
            )
            for index, tag in ((1, "i"), (0, "t"))
        }
        for total in sums.values():
            total.start()
        spread(image, bench.mg_i, bench.full_i)

        def hooks(stream, tag, up_w, down_w):
            full, slope, pre = get("full", tag), get("slope", tag), get("pre", tag)
            width = ff[tag]

            def project(half, core):
                place = stream.place(half, core)
                for share, down in enumerate(down_w):
                    lanes = slice(share * width, (share + 1) * width)
                    grad = product_nt(full[place], down[...])
                    pre[place, lanes] = (grad * slope[place, lanes].astype(F32)).astype(BF)

            def output(half, core):
                place = stream.place(half, core)
                total = product_nt(pre[place, :width], up_w[0][...])
                for share, up in enumerate(up_w[1:], 1):
                    total = total + product_nt(
                        pre[place, share * width : (share + 1) * width], up[...]
                    )
                return total

            return project, output

        text_hooks = hooks(text, "t", [bench.up_t], [bench.down_t])
        text.open_sum()
        text.arrive(0, text_hooks[0])
        text.partial(0, text_hooks[1])
        bench.release(2)
        image_hooks = hooks(
            image, "i", [bench.up_i, bench.upo_i], [bench.down_i, bench.downo_i]
        )
        image.open_sum()
        image.arrive(0, image_hooks[0])
        image.partial(0, image_hooks[1])

        def close(tag, stream):
            stream.settle()
            settle_back(
                stream, get("mg", tag), get("zero", tag), get("gains", tag)[0:1],
                get("back", tag), get("gain", tag), get("shift", tag), get("full2", tag),
            )
            bench.flush("back_" + tag)
            last[tag].gather(get("full2", tag))

        feed_sums = {"t": [], "i": []}

        def feed_grads(index, tag, key, left, right, column):
            stack, width = get("fstack", tag), ff[tag]
            for share in range(1 + index):
                lanes = slice(share * width, (share + 1) * width)
                weight_grad(splits[index], stack, column, left, right[:, lanes], share)
            columns = pl.ds(column, width)
            total = GroupSum(
                bench, splits[index], "fstack_" + tag, get("fspare", tag), 0, 1, columns
            )
            total.start()
            feed_sums[tag].append(total)

        def co_project(tag):
            full, weight, target = get("full2", tag), get("co", tag), get("cg", tag)

            def project(half, core):
                place = last[tag].place(half, core)
                target[place] = product_nt(full[place], weight[...]).astype(BF)

            return project

        close("i", image)
        sums["t"].advance()
        text.arrive(1, text_hooks[0])
        text.partial(1, text_hooks[1])
        sums["i"].advance()
        feed_grads(1, "i", "up", bench.mlp_i, bench.pre_i, 0)
        sums["t"].advance()
        feed_grads(1, "i", "down", bench.full_i, bench.act_i, ff["i"])
        last["i"].arrive(0, co_project("i"))
        feed_grads(0, "t", "up", bench.mlp_t, bench.pre_t, 0)
        sums["t"].finish(bench.self_sum_t)
        bench.flush("self_sum_t")
        feed_grads(0, "t", "down", bench.full_t, bench.act_t, ff["t"])
        close("t", text)
        last["i"].arrive(1, co_project("i"))
        bench.flush("cg_i")
        sums["i"].advance()
        last["t"].arrive(0, co_project("t"))
        weight_grad(co_splits[1], bench.out_grad_i, 0, bench.full2_i, bench.ctx_i[...])
        bench.flush("out_grad_i")
        last["t"].arrive(1, co_project("t"))
        bench.flush("cg_t")
        weight_grad(co_splits[0], bench.out_grad_t, 0, bench.full2_t, bench.ctx_t[...])
        bench.flush("out_grad_t")
        for stream in last.values():
            stream.finish_gather()
        sums["i"].finish(bench.self_sum_i)
        bench.flush("self_sum_i")
        for tag in ("i", "t"):
            for total in feed_sums[tag]:
                total.drain()
            bench.flush("fstack_" + tag)
    return exchange_kernel(
        body, "feed_back", 3,
        lambda: list(group_peers()[1:]) + dp_peers(*self_splits, *splits), inputs, outputs,
        scratch, 40, (12e9, 60e6, 1e6),
    )


def co_front_kernel(shards, weights, feeds, attentions, order, inverse, regions, lengths, heads, bits):
    inputs = {
        "order": (order, "smem"), "inverse": (inverse, "smem"),
        "regions": (regions, "smem"), "lengths": (lengths, "smem"),
    }
    outputs, scratch = {}, {}
    for key, weight in zip(("up", "down"), feeds):
        inputs[key + "_i"] = (weight, "hbm")
        outputs[key + "o_i"] = (weight.shape, BF, "hbm")
    for key, weight in zip(("qkv", "so"), attentions):
        lead = weight.shape[:1] if key == "qkv" else ()
        inputs[key + "_t"] = (weight, "any")
        outputs[key + "b_t"] = (lead + weight.shape[-2:], BF, "hbm")
    for index, tag in ((0, "t"), (1, "i")):
        n, d = shards[index].shape
        width = weights[index].shape[2]
        inputs.update({"x_" + tag: (shards[index], "hbm"), "w_" + tag: (weights[index], "hbm")})
        outputs.update({
            "all_" + tag: ((4 * n, d), BF, "hbm"),
            "co_" + tag: ((4 * n, 3 * width), BF, "hbm"),
            "ctx_" + tag: ((4 * n, width), BF, "hbm"),
        })
    n_t, n_i = shards[0].shape[0], shards[1].shape[0]
    held, width = n_t // CAP_LEN, weights[0].shape[2]
    outputs["co_t"] = ((4 * held, CAP_LEN, 3 * width), BF, "hbm")
    rows = 4 * n_i // ROW_LEN
    span = PER_ROW * CAP_LEN
    outputs["cshare_t"] = ((rows, heads, span, ROW_LEN), BF, "hbm")
    outputs["cshare_i"] = ((rows, heads, ROW_LEN, span), BF, "hbm")
    scratch["rctx_t"] = ((4 * held, CAP_LEN, width), BF)

    def body(bench):
        streams = {tag: Gather(bench, n) for tag, n in (("t", n_t), ("i", n_i))}
        get = lambda key, tag: getattr(bench, key + "_" + tag)
        fetches = [
            Weights(bench, bench.up_i, bench.upo_i, bits),
            Weights(bench, bench.down_i, bench.downo_i, bits[:-2] + bits[:-3:-1]),
        ]
        for tag, stream in streams.items():
            full = get("all", tag)
            full[stream.place(0, stream.core)] = get("x", tag)[...]
            stream.gather(full)
        blocks, moves = [], []
        for key, weight in zip(("qkv", "so"), attentions):
            lead = 1 if key == "qkv" else 0
            names = range(len(weight.shape) - 2 - lead)[::-1]
            block = (slice(None),) * lead + tuple(dp_peer(bit)[0] for bit in names)
            moves.append(
                bench.remote(
                    getattr(bench, key + "_t").at[block + (slice(None), slice(None))],
                    getattr(bench, key + "b_t"), group_peers()[2],
                )
            )
        blocks += moves
        for half in (0, 1):
            for tag, stream in streams.items():
                full, weight, target = get("all", tag), get("w", tag), get("co", tag)

                due = blocks if (half, tag) == (1, "t") else []

                def project(half, core):
                    while due:
                        due.pop(0).start()
                    place = stream.place(half, core)
                    if tag == "i":
                        project_three(full[place], weight, target, place)
                        return
                    captions = pl.ds((2 * half + core) * held, held)
                    for part in range(3):
                        target[captions, :, part * width : (part + 1) * width] = (
                            product(full[place], weight[part])
                            .astype(BF)
                            .reshape(held, CAP_LEN, width)
                        )

                stream.arrive(half, project)
            if half == 0:
                for fetch in fetches * len(bits):
                    fetch.advance()
        for tag in streams:
            bench.flush("all_" + tag, "co_" + tag)
        co_forward_rows(bench, heads, rows)
        in_caption_order(bench, bench.rctx_t, bench.ctx_t)
        for fetch in fetches:
            fetch.finish()
        for block in moves:
            block.wait()
        for stream in streams.values():
            stream.finish_gather()

    return exchange_kernel(
        body, "co_front", 5,
        lambda: list(group_peers()[1:]) + [dp_peer(bit)[1] for bit in bits],
        inputs, outputs, scratch, 16,
        (4e9, 20e6, 1e6),
    )


class Total:
    def __init__(self, bench, held, landing, group_count):
        self.bench, self.held, self.landing = bench, held, landing
        self.peers = list(group_peers()[1:]) + [
            dp_peer(bit)[1] for bit in range(group_count.bit_length() - 1)
        ]
        self.step = 0
        self.start()

    def start(self):
        if self.step < len(self.peers):
            self.copy = self.bench.remote(
                self.held.at[self.step], self.landing.at[self.step], self.peers[self.step]
            )
            self.copy.start()

    def advance(self):
        if self.step < len(self.peers):
            self.copy.wait()
            self.held[self.step + 1] = self.held[self.step] + self.landing[self.step]
            self.step += 1
            self.start()

    def finish(self, out):
        while self.step < len(self.peers):
            self.advance()
        out[...] = self.held[self.step]


def co_back_kernel(zero_grad, context_grads, tokens, projected, shares, weights, out_grads,
                   feed_stacks, norms, order, inverse, splits, feed_splits, late_splits, heads,
                   group_count):
    inputs = {"order": (order, "smem"), "inverse": (inverse, "smem")}
    outputs, scratch = {}, {}
    steps = 2 + group_count.bit_length() - 1
    for index, tag in ((1, "i"), (0, "t")):
        n, d = zero_grad[index].shape
        width = projected[index].shape[-1]
        inner = out_grads[index].shape[2]
        split = splits[index]
        feeds = feed_stacks[index].shape[2]
        inputs.update({"norm%d_%s" % (k, tag): (v, "hbm") for k, v in enumerate(norms[index])})
        inputs.update({
            "co_" + tag: (projected[index], "hbm"),
            "cg_" + tag: (context_grads[index], "hbm"),
            "cshare_" + tag: (shares[index], "hbm"),
            "fstack_" + tag: (feed_stacks[index], "hbm1"),
            "ostack_" + tag: (out_grads[index], "hbm1"),
            "x_" + tag: (tokens[index], "hbm1"),
            "w_" + tag: (weights[index], "hbm1"),
            "zg_" + tag: (zero_grad[index], "hbm1"),
        })
        outputs.update({
            "in_grad_" + tag: ((n, d), F32, "hbm"),
            "feed_sum_" + tag: ((split.part, feeds), BF, "hbm"),
            "out_sum_" + tag: ((split.part, inner), BF, "hbm"),
            "qkv_sum_" + tag: ((split.part, width), BF, "hbm"),
            "norm_" + tag: ((8, d), F32, "hbm"),
        })
        scratch.update(stream_scratch(tag, n, d))
        scratch["grad_" + tag] = ((4 * n, width), BF)
        scratch["stack_" + tag] = (split.shape(width), BF)
        scratch["spare_" + tag] = (split.spare(width), BF)
        scratch["fspare_" + tag] = (feed_splits[index].spare(feeds), BF)
        scratch["ospare_" + tag] = (split.spare(inner), BF)
        scratch["held_" + tag] = ((steps + 1, 8, d), F32)
        scratch["landing_" + tag] = ((steps, 8, d), F32)
    n_t, n_i = zero_grad[0].shape[0], zero_grad[1].shape[0]
    scratch["rgrad_t"] = (projected[0].shape, BF)

    def body(bench):
        streams = {tag: Stream(bench, tag, n) for tag, n in (("i", n_i), ("t", n_t))}
        get = lambda key, tag: getattr(bench, key + "_" + tag)
        feeds, outs, late, totals = {}, {}, {}, {}
        for index, tag in ((0, "t"), (1, "i")):
            feeds[tag] = GroupSum(
                bench, feed_splits[index], "fstack_" + tag, get("fspare", tag),
                1, source=bench.refs["src fstack_" + tag],
            )
            outs[tag] = GroupSum(
                bench, splits[index], "ostack_" + tag, get("ospare", tag),
                source=bench.refs["src ostack_" + tag],
            )
            feeds[tag].start()
            outs[tag].start()
        bench.release(1)
        for tag in ("t", "i"):
            held = get("held", tag)
            vectors = [
                jnp.sum(get("norm%d" % k, tag)[...], axis=0, keepdims=True) for k in range(6)
            ]
            held[0] = jnp.concatenate(vectors + [jnp.zeros_like(vectors[0])] * 2, axis=0)
            totals[tag] = Total(bench, held, get("landing", tag), group_count)
        rows = 4 * n_i // ROW_LEN
        for step in range(3):
            co_backward_rows(bench, heads, rows * step // 3, rows * (step + 1) // 3)
            for total in totals.values():
                total.advance()
            if step > 0:
                outs["t" if step == 1 else "i"].advance()
        def open_late(index, tag):
            stack = get("stack", tag)
            weight_grad(late_splits[index], stack, 0, get("x", tag), get("grad", tag)[...])
            late[tag] = GroupSum(bench, late_splits[index], "stack_" + tag, get("spare", tag))
            late[tag].start()

        def finish_stream(tag):
            stream = streams[tag]
            grad, weight = get("grad", tag), get("w", tag)
            output = lambda half, core: back_three(grad, stream.place(half, core), weight)
            stream.open_sum()
            stream.partial(1, output)
            if tag == "i":
                feeds["t"].advance()
            outs["i"].advance()
            for total in totals.values():
                total.advance()
            stream.partial(0, output)

        def close(tag):
            stream = streams[tag]
            resid, target = get("zg", tag), get("in_grad", tag)
            stream.settle(gathered=False)

            def step(rows, carry):
                target[rows] = resid[rows] + stream.piece(rows)
                return carry

            chunks(stream.rows, step, 0)
            bench.flush("in_grad_" + tag)

        open_late(1, "i")
        in_caption_order(bench, bench.rgrad_t, bench.grad_t)
        feeds["i"].advance()
        open_late(0, "t")
        finish_stream("i")
        outs["t"].advance()
        feeds["i"].advance()
        finish_stream("t")
        close("i")
        late["i"].advance()
        late["t"].advance()
        for tag, total in totals.items():
            total.finish(get("norm", tag))
        feeds["t"].finish(bench.feed_sum_t)
        bench.flush("feed_sum_t")
        feeds["i"].advance()
        late["i"].advance()
        close("t")
        late["t"].advance()
        feeds["i"].advance()
        for tag in ("t", "i"):
            outs[tag].finish(get("out_sum", tag))
        feeds["i"].finish(bench.feed_sum_i)
        bench.flush("out_sum_t", "out_sum_i", "feed_sum_i")
        for tag in ("t", "i"):
            late[tag].finish(get("qkv_sum", tag))
            bench.flush("qkv_sum_" + tag)

    return exchange_kernel(
        body, "co_back", 4,
        lambda: list(group_peers()[1:])
        + [dp_peer(bit)[1] for bit in range(group_count.bit_length() - 1)],
        inputs, outputs, scratch, 16 + 2 * steps + 20, (8e9, 50e6, 1e6),
    )


def finish_kernel(sums, norms, kept):
    arrays, shapes = [], []
    for stream, (qkv, out, own, feed) in enumerate(sums):
        part = qkv.shape[0]
        inner, ff = own.shape[1] // 4, feed.shape[1] // 2
        arrays += [qkv, out, own, feed]
        turned = lambda rows: (part, rows) if stream == 0 else (rows, part)
        shapes += [
            (3, part, qkv.shape[1] // 3), turned(out.shape[1]), (3, part, inner), (inner, part),
            (part, ff), turned(ff),
        ]
    devices = lax.axis_size("dp") * lax.axis_size("mp")
    columns = [norm.shape[1] // devices for norm in norms]
    count, made = len(arrays), len(shapes)
    outs = [shape_of(shape, F32) for shape in shapes]
    for width in columns:
        outs += [shape_of((3, width), F32)] * 2
    outs += [shape_of(array.shape, array.dtype) for array in kept]
    any_spec, vmem_spec = pl.BlockSpec(memory_space=pl.ANY), pl.BlockSpec(memory_space=pltpu.VMEM)

    def kernel(*refs):
        refs = list(refs)
        take = lambda number: [refs.pop(0) for _ in range(number)]
        sources, totals, whole = take(count), take(2), take(len(kept))
        results, parts, copies = take(made), take(4), take(len(kept))
        held, built, through = take(count), take(made), take(len(kept))
        in_sems, out_sems, keep_sems = take(3)
        fetches = [
            pltpu.make_async_copy(source, target, in_sems.at[index])
            for index, (source, target) in enumerate(zip(sources, held))
        ]
        moves = [
            pltpu.make_async_copy(source, target, keep_sems.at[index])
            for index, (source, target) in enumerate(zip(whole, through))
        ]
        for copy in fetches + moves:
            copy.start()
        place = lax.axis_index("dp") * lax.axis_size("mp") + lax.axis_index("mp")
        for stream in range(2):
            total, width = totals[stream][...], columns[stream]
            mine = pltpu.roll(total, total.shape[1] - place * width, 1)[:, :width]
            parts[2 * stream][...] = mine[:3]
            parts[2 * stream + 1][...] = mine[3:6]
        stores = []
        for index, copy in enumerate(moves):
            copy.wait()
            stores.append(
                pltpu.make_async_copy(through[index], copies[index], keep_sems.at[index])
            )
            stores[-1].start()

        def store(index, values):
            for part, value in enumerate(values):
                target = built[index].at[part] if len(values) > 1 else built[index]
                target[...] = value
            stores.append(
                pltpu.make_async_copy(built[index], results[index], out_sems.at[index])
            )
            stores[-1].start()

        for stream in range(2):
            qkv, out, own, feed = held[4 * stream : 4 * stream + 4]
            at = 6 * stream
            width, inner, ff = qkv.shape[1] // 3, own.shape[1] // 4, feed.shape[1] // 2
            turned = (lambda value: value) if stream == 0 else (lambda value: value.T)
            fetches[4 * stream].wait()
            store(at, [qkv[:, k * width : (k + 1) * width].astype(F32) for k in range(3)])
            fetches[4 * stream + 1].wait()
            store(at + 1, [turned(out[...].astype(F32))])
            fetches[4 * stream + 2].wait()
            store(at + 2, [own[:, k * inner : (k + 1) * inner].astype(F32) for k in range(3)])
            store(at + 3, [own[:, 3 * inner :].astype(F32).T])
            fetches[4 * stream + 3].wait()
            store(at + 4, [feed[:, :ff].astype(F32)])
            store(at + 5, [turned(feed[:, ff:].astype(F32))])
        for copy in stores:
            copy.wait()

    return pl.pallas_call(
        kernel,
        in_specs=[any_spec] * count + [vmem_spec] * 2 + [any_spec] * len(kept),
        out_specs=[any_spec] * made + [vmem_spec] * 4 + [any_spec] * len(kept),
        out_shape=outs,
        scratch_shapes=[pltpu.VMEM(array.shape, array.dtype) for array in arrays]
        + [pltpu.VMEM(shape, F32) for shape in shapes]
        + [pltpu.VMEM(array.shape, array.dtype) for array in kept]
        + [pltpu.SemaphoreType.DMA((number,)) for number in (count, made, len(kept))],
        compiler_params=pltpu.CompilerParams(vmem_limit_bytes=BIG_LIMIT),
        name="finish",
    )(*arrays, *norms, *kept)


def apart(grad):
    rows, columns = grad.shape
    return jnp.transpose(grad.reshape(rows, 3, columns // 3), (1, 0, 2))


def finish_plain(sums, norms, kept):
    place = lax.axis_index("dp") * lax.axis_size("mp") + lax.axis_index("mp")
    outs, parts = [], []
    for stream, values in enumerate(sums):
        qkv, out, own, feed = [value.astype(F32) for value in values]
        inner, ff = own.shape[1] // 4, feed.shape[1] // 2
        turned = (lambda value: value) if stream == 0 else (lambda value: value.T)
        outs += [
            apart(qkv), turned(out), apart(own[:, : 3 * inner]), own[:, 3 * inner :].T,
            feed[:, :ff], turned(feed[:, ff:]),
        ]
        columns = norms[stream].shape[1] // (lax.axis_size("dp") * lax.axis_size("mp"))
        mine = lax.dynamic_slice_in_dim(norms[stream], place * columns, columns, axis=1)
        parts += [mine[:3], mine[3:6]]
    return outs + parts + list(kept)


def per_device(
    text_in,
    image_in,
    caption_lengths,
    region_lengths,
    image_caption,
    co_text_qkv,
    co_image_qkv,
    co_text_out,
    co_image_out,
    text_up,
    text_down,
    image_up,
    image_down,
    text_self_qkv,
    text_self_out,
    image_self_qkv,
    image_self_out,
    text_gains,
    text_shifts,
    image_gains,
    image_shifts,
    text_grad_out,
    image_grad_out,
):
    captions = image_caption.shape[1]
    part_count = lax.axis_size("mp")
    group_count = lax.axis_size("dp")
    spot = lax.axis_index("mp")
    core = spot % 2
    chip = spot // 2
    co_local = CO_HEADS // part_count
    text_local = TEXT_HEADS // part_count
    image_local = IMAGE_HEADS // part_count

    lengths = caption_lengths
    regions = region_lengths.T
    order = image_caption[0]
    labels = jnp.arange(captions, dtype=jnp.int32)
    inverse = jnp.sum(
        jnp.where(order[None, :] == labels[:, None], labels[None, :], 0), axis=1, dtype=jnp.int32
    )

    power = group_count.bit_length() - 1 if group_count & (group_count - 1) == 0 else 0

    def fold(weight, bits):
        return weight.reshape(
            weight.shape[:-2] + (2,) * bits + (weight.shape[-2] >> bits, weight.shape[-1])
        )

    feed_bits, self_bits = list(range(min(power, 3)))[::-1], list(range(min(power, 2)))[::-1]
    text_qkv = fold(jnp.swapaxes(text_self_qkv, 1, 2), len(self_bits))
    text_self_blocks = fold(text_self_out, len(self_bits))

    front = co_front_kernel(
        (text_in, image_in), (co_text_qkv, co_image_qkv),
        (fold(image_up, len(feed_bits)), fold(image_down, len(feed_bits))),
        (text_qkv, text_self_blocks), order, inverse, regions, lengths, co_local, feed_bits,
    )
    others = (
        front["upo_i"].reshape(image_up.shape), front["downo_i"].reshape(image_down.shape),
        front["qkvb_t"], front["sob_t"],
    )
    text_ctx, image_ctx = front["ctx_t"], front["ctx_i"]
    ahead = forward_kernel(
        text_ctx, image_ctx, text_in, image_in,
        (co_text_out, co_image_out, text_up, text_down, image_up, image_down,
         text_qkv, text_self_blocks, image_self_qkv, image_self_out),
        others, (text_gains, text_shifts, image_gains, image_shifts),
        text_grad_out, image_grad_out, lengths, regions, text_local, image_local, self_bits,
    )
    widths = (text_in.shape[1], image_in.shape[1])
    upward = lambda bits: list(range(bits))
    second_first = lambda bits: ([1, 0] + list(range(2, bits)))[:bits]
    text_width, image_width = widths
    splits = (
        Split(group_count, text_width, upward), Split(group_count, image_width, upward)
    )
    self_splits = (
        Split(group_count, text_width, upward, 2, power),
        splits[1],
    )
    late_splits = (Split(group_count, text_width, second_first), splits[1])
    feed_splits = (splits[0], Split(group_count, image_width, second_first, 2, 1))
    gains = (text_gains, image_gains)
    first_back = self_back_kernel(
        ahead, image_self_qkv, image_self_out, text_qkv, text_self_blocks, gains, self_splits
    )
    second_back = feed_back_kernel(
        first_back, ahead, (text_up, image_up), (text_down, image_down), others,
        (text_ctx, image_ctx), (co_text_out, co_image_out), gains, self_splits, feed_splits,
        splits,
    )
    norms = [
        [stage[key + tag] for key in ("gain_", "shift_") for stage in (second_back, first_back, ahead)]
        for tag in "ti"
    ]
    last_back = co_back_kernel(
        (second_back["back_t"], second_back["back_i"]),
        (second_back["cg_t"].reshape(captions, CAP_LEN, -1), second_back["cg_i"]),
        (front["all_t"], front["all_i"]), (front["co_t"], front["co_i"]),
        (front["cshare_t"], front["cshare_i"]), (co_text_qkv, co_image_qkv),
        (second_back["out_grad_t"], second_back["out_grad_i"]),
        (second_back["fstack_t"], second_back["fstack_i"]),
        norms, order, inverse, splits, feed_splits, late_splits, co_local, group_count,
    )

    def over_groups(summed, split):
        if not split.fast:
            summed = lax.psum_scatter(summed, "dp", scatter_dimension=0, tiled=True)
        return summed

    sums = [
        [
            over_groups(last_back["qkv_sum_" + tag], split),
            over_groups(last_back["out_sum_" + tag], split),
            over_groups(second_back["self_sum_" + tag], split),
            over_groups(last_back["feed_sum_" + tag], split),
        ]
        for tag, split in zip("ti", splits)
    ]
    finish = finish_kernel if all(split.fast for split in splits) else finish_plain
    outs = finish(
        sums,
        (last_back["norm_t"], last_back["norm_i"]),
        (ahead["result_t"], ahead["result_i"], last_back["in_grad_t"], last_back["in_grad_i"]),
    )
    text_grads, image_grads, norm_grads, kept = outs[:6], outs[6:12], outs[12:16], outs[16:]
    return (
        *kept,
        text_grads[0],
        image_grads[0],
        text_grads[1].T,
        image_grads[1],
        text_grads[4],
        text_grads[5].T,
        image_grads[4],
        image_grads[5],
        text_grads[2],
        text_grads[3],
        image_grads[2],
        image_grads[3],
        *norm_grads,
    )


def solution(mesh):
    tokens = P(("dp", "mp"), None)
    stack_in = P(None, None, "mp")
    rows_in = P("mp", None)
    columns_in = P(None, "mp")
    in_specs = (
        tokens, tokens, P("dp"), P("dp", None), P("dp", None),
        stack_in, stack_in, rows_in, rows_in,
        columns_in, rows_in, columns_in, rows_in,
        stack_in, rows_in, stack_in, rows_in,
        P(), P(), P(), P(),
        tokens, tokens,
    )
    stack_out = P(None, "dp", "mp")
    rows_out = P("mp", "dp")
    columns_out = P("dp", "mp")
    norm_out = P(None, ("dp", "mp"))
    out_specs = (
        tokens, tokens, tokens, tokens,
        stack_out, stack_out, rows_out, rows_out,
        columns_out, rows_out, columns_out, rows_out,
        stack_out, rows_out, stack_out, rows_out,
        norm_out, norm_out, norm_out, norm_out,
    )
    return jax.shard_map(
        per_device, mesh=mesh, in_specs=in_specs, out_specs=out_specs, check_vma=False
    )
```
